32 devices in a mesh: section: 2 (over x), dp: 16 (over z, y, core).
Axes of the slice: x: 2, y: 2, z: 4, core: 2. Of those that a mesh axis runs over, the one named last changes fastest.
Arguments:
- cells: float32 [32, 24, 19, 512], P('dp'), may hold values from -6 to 6
- missing_mask: int32 [32, 24, 19], P('dp'), may hold values 0 or 1
- missing_embed: float32 [512], replicated, may hold values from -6 to 6
- context_rows: int32 [32], P('dp'), may hold values from 2 to 24
- norm_gains: float32 [2, 3, 512], P('section'), may hold values from 0.25 to 1.75
- attn_in: float32 [2, 2, 512, 1536], P('section'), may hold values from -0.375 to 0.375
- attn_out: float32 [2, 2, 512, 512], P('section'), may hold values from -0.75 to 0.75
- mlp_up: float32 [2, 512, 2048], P('section'), may hold values from -0.25 to 0.25
- mlp_down: float32 [2, 2048, 512], P('section'), may hold values from -0.1875 to 0.1875
- cotangent: float32 [32, 24, 19, 512], P('dp'), may hold values from -6 to 6
Outputs:
- layer_outputs: float32 [2, 32, 24, 19, 512], P('section', 'dp')
- input_grads: float32 [2, 32, 24, 19, 512], P('section', 'dp')
- gain_grads: float32 [2, 3, 512], P('section')
- attn_in_grads: float32 [2, 2, 512, 1536], P('section')
- attn_out_grads: float32 [2, 2, 512, 512], P('section')
- up_grads: float32 [2, 512, 2048], P('section')
- down_grads: float32 [2, 2048, 512], P('section')
- missing_grad: float32 [512], replicated
The draws below stay inside these ranges and needn't reach their ends.
Inputs may be any that keep to these rules, and one draw needn't show every extreme that they name: Only the first context_rows rows of a table are attended to in column attention; every row attends to them.
All inputs are finite; a program needn't handle non-finite values. No bound on the sum of `missing_mask` on one device may be relied on, other than what follows from the above.
Results may differ from the reference program's by a relative error of at most 0.0003.
Values sent between devices are 32-bit elements; how exact they have to be, the bound alone decides.
A program may use at most 192 MiB of HBM per device.

```python
import jax
import jax.numpy as jnp
from jax import lax

D = 512
HEADS = 4
FF = 2048
ROWS = 24
FEAT = 19
TAB_DEV = 2
TABLES = 32
N_SECTION = 2


def place_ends(array, stream_key, smallest, high):
    longest = array.shape.index(max(array.shape))
    spots = []
    for shift in (0, 1):
        where = [jax.random.randint(jax.random.fold_in(stream_key, axis), (), 0, length) for axis, length in enumerate(array.shape)]
        where[longest] = (where[longest] + shift) % array.shape[longest]
        spots.append(tuple(where))
    return array.at[spots[0]].set(smallest).at[spots[1]].set(high)


def block_scale(key, shape, shards, low, top_value):
    def one(position, shards_of):
        draws = jax.random.uniform(jax.random.fold_in(jax.random.fold_in(key, 6), position), (shards_of,), jnp.float32, low / len(shards), top_value / len(shards))
        return jnp.repeat(jnp.exp(draws), shape[position] // shards_of).reshape((-1,) + (1,) * (len(shape) - position - 1))

    level = one(*shards[0])
    for cut in shards[1:]:
        level = level * one(*cut)
    return level


def bell_draw(own_key, shape, width, bound, shards=(), dtype=jnp.bfloat16):
    level = block_scale(own_key, shape, shards, -0.22, 0.18) if shards else 1.0
    result = jax.random.normal(own_key, shape, jnp.float32) * width * level
    return jnp.minimum(jnp.maximum(result, -bound), bound).astype(dtype)


def setup_inputs(seed: int = 0) -> dict:
    seeds = jax.random.split(jax.random.key(seed), 11)
    return {
        "cells": bell_draw(seeds[0], (TABLES, ROWS, FEAT, D), 1.0, 6.0, ((0, 16),), jnp.float32),
        "missing_mask": place_ends((jax.random.randint(seeds[1], (TABLES, ROWS, FEAT), 0, 5) < 1).astype(jnp.int32), jax.random.fold_in(seeds[1], 1), 0, 1),
        "missing_embed": bell_draw(seeds[2], (D,), 1.0, 6.0, (), jnp.float32),
        "context_rows": place_ends(jax.random.randint(seeds[3], (TABLES,), 2, ROWS + 1), jax.random.fold_in(seeds[3], 1), 2, ROWS).astype(jnp.int32),
        "norm_gains": jnp.clip(1.0 + 0.15 * jax.random.normal(seeds[4], (N_SECTION, 3, D), jnp.float32), 0.25, 1.75),
        "attn_in": bell_draw(seeds[5], (N_SECTION, 2, D, 3 * D), (D // 2) ** -0.5, 0.375, ((0, 2),), jnp.float32),
        "attn_out": bell_draw(seeds[6], (N_SECTION, 2, D, D), (D // 8) ** -0.5, 0.75, ((0, 2),), jnp.float32),
        "mlp_up": bell_draw(seeds[7], (N_SECTION, D, FF), D ** -0.5, 0.25, ((0, 2),), jnp.float32),
        "mlp_down": bell_draw(seeds[8], (N_SECTION, FF, D), (FF // 2) ** -0.5, 0.1875, ((0, 2),), jnp.float32),
        "cotangent": bell_draw(seeds[9], (TABLES, ROWS, FEAT, D), 1.0, 6.0, ((0, 16),), jnp.float32),
    }


epsilon = 1e-05
exact_mode = lax.Precision.HIGHEST

@jax.custom_vjp
def low(v):
    return lax.optimization_barrier(v.astype(jnp.bfloat16)).astype(jnp.float32)

@jax.custom_vjp
def low_back(v):
    return v

def low_keep(v):
    return (low(v), None)

def low_pass(kept, grad):
    return (grad,)

def back_keep(v):
    return (v, None)

def back_low(kept, grad):
    return (low(grad),)
low.defvjp(low_keep, low_pass)
low_back.defvjp(back_keep, back_low)

def layer_norm(hidden, gain):
    centred = hidden - lax.optimization_barrier(jnp.mean(hidden, axis=-1, keepdims=True))
    spread = lax.optimization_barrier(jnp.mean(centred * centred, axis=-1, keepdims=True))
    return centred * lax.rsqrt(spread + epsilon) * gain

def project(inputs, matrix):
    return jnp.einsum('rfd,de->rfe', inputs, matrix, precision=exact_mode)

def split_heads(packed, which):
    model_width = packed.shape[2] // 3
    part = packed[:, :, which * model_width:(which + 1) * model_width]
    return part.reshape(packed.shape[0], packed.shape[1], HEADS, model_width // HEADS)

def row_attention(normed, w_in, w_out):
    packed = project(normed, w_in)
    query_part = split_heads(packed, 0)
    key_part = split_heads(packed, 1)
    value_part = split_heads(packed, 2)
    factor = query_part.shape[3] ** (-0.5)
    scores = jnp.einsum('rfhd,rghd->rhfg', query_part, key_part, precision=exact_mode) * factor
    weights = jax.nn.softmax(scores, axis=-1)
    blended = jnp.einsum('rhfg,rghd->rfhd', weights, value_part, precision=exact_mode)
    return project(blended.reshape(normed.shape), w_out)

def column_attention(normed, context, w_in, w_out):
    packed = project(normed, w_in)
    query_part = split_heads(packed, 0)
    key_part = split_heads(packed, 1)
    value_part = split_heads(packed, 2)
    factor = query_part.shape[3] ** (-0.5)
    scores = jnp.einsum('rfhd,sfhd->fhrs', query_part, key_part, precision=exact_mode) * factor
    usable = jnp.arange(normed.shape[0]).astype(jnp.int32) < context
    scores = jnp.where(usable, scores, -1e+30)
    weights = jax.nn.softmax(scores, axis=-1)
    blended = jnp.einsum('fhrs,sfhd->rfhd', weights, value_part, precision=exact_mode)
    return project(blended.reshape(normed.shape), w_out)

def attention_part(hidden, context, gains, w_in, w_out):
    first = hidden + row_attention(layer_norm(hidden, gains[0]), w_in[0], w_out[0])
    return first + column_attention(layer_norm(first, gains[1]), context, w_in[1], w_out[1])

def feed_forward(hidden, gains, w_up, w_down):
    normed = layer_norm(hidden, gains[2])
    inner = jax.nn.gelu(project(normed, w_up), approximate=False)
    return hidden + project(inner, w_down)

def whole_layer(hidden, context, gains, w_in, w_out, w_up, w_down):
    return feed_forward(attention_part(hidden, context, gains, w_in, w_out), gains, w_up, w_down)

def reference(cells, missing_mask, missing_embed, context_rows, norm_gains, attn_in, attn_out, mlp_up, mlp_down, cotangent):
    group_count = TABLES // TAB_DEV
    grouped_ctx = context_rows.reshape(group_count, TAB_DEV)

    def all_tables(hidden, params):

        def one_group(pair):
            return jax.vmap(lambda table, context: whole_layer(table, context, *params))(pair[0], pair[1])
        stepped = lax.map(jax.checkpoint(one_group), (hidden.reshape(group_count, TAB_DEV, ROWS, FEAT, D), grouped_ctx))
        return stepped.reshape(hidden.shape)

    def first_layer(raw, embed, gains, w_in, w_out, w_up, w_down):
        filled = jnp.where((missing_mask == 1)[..., None], embed, raw)
        return all_tables(filled, (gains, w_in, w_out, w_up, w_down))

    def second_layer(hidden, gains, w_in, w_out, w_up, w_down):
        return all_tables(hidden, (gains, w_in, w_out, w_up, w_down))
    section_one = (norm_gains[0], attn_in[0], attn_out[0], mlp_up[0], mlp_down[0])
    section_two = (norm_gains[1], attn_in[1], attn_out[1], mlp_up[1], mlp_down[1])
    hidden, first_back = jax.vjp(first_layer, cells, missing_embed, *section_one)
    output, second_back = jax.vjp(second_layer, hidden, *section_two)
    grads_two = second_back(cotangent)
    grads_one = first_back(grads_two[0])
    layer_outputs = jnp.stack([hidden, output])
    input_grads = jnp.stack([grads_one[0], grads_two[0]])
    stacked = [jnp.stack([grads_one[member + 2], grads_two[member + 1]]) for member in range(5)]
    return (layer_outputs, input_grads, stacked[0], stacked[1], stacked[2], stacked[3], stacked[4], grads_one[1])
```

```python
import functools

import jax
import jax.numpy as jnp
from jax import lax
from jax.experimental import pallas as pl
from jax.experimental.pallas import tpu as pltpu
from jax.sharding import PartitionSpec as P

HEADS = 4
EPSILON = 1e-05
NEG = -1e30
INV_SQRT2 = 0.7071067811865476
INV_SQRT2PI = 0.3989422804014327
PREC = lax.Precision.HIGH
VMEM_LIMIT = 62 * 1024 * 1024


def mm(a, b):
    return lax.dot_general(a, b, (((1,), (0,)), ((), ())), precision=PREC, preferred_element_type=jnp.float32)


def mm_nt(a, b):
    return lax.dot_general(a, b, (((1,), (1,)), ((), ())), precision=PREC, preferred_element_type=jnp.float32)


def mm_tn(a, b):
    return lax.dot_general(a, b, (((0,), (0,)), ((), ())), precision=PREC, preferred_element_type=jnp.float32)


def normalized(h):
    centred = h - jnp.mean(h, axis=-1, keepdims=True)
    rstd = lax.rsqrt(jnp.mean(centred * centred, axis=-1, keepdims=True) + EPSILON)
    return centred * rstd, rstd


def norm_back(h, gain, da):
    n, rstd = normalized(h)
    dgain = jnp.sum(da * n, axis=0, keepdims=True)
    dn = da * gain
    dh = rstd * (dn - jnp.mean(dn, axis=-1, keepdims=True) - n * jnp.mean(dn * n, axis=-1, keepdims=True))
    return dh, n * gain, dgain


def cell_ids(start, count, feat, along):
    shape = (count, 1) if along == 0 else (1, count)
    at = lax.broadcasted_iota(jnp.int32, shape, along) + start
    mult = (1 << 20) // feat + 1
    row = lax.shift_right_logical(at * mult, 20)
    return row, at - row * feat


def row_blocks(rows, feat):
    cells = rows * feat
    half = ((rows // 2) * feat + 7) // 8 * 8
    first_keys = min(cells, ((((half - 1) // feat) + 1) * feat + 7) // 8 * 8)
    second_keys = ((half // feat) * feat) // 8 * 8
    return (((0, half), (0, first_keys)), ((half, cells), (second_keys, cells)))


def probs(q, k, mask, scale):
    s = jnp.where(mask, mm_nt(q, k) * scale, NEG)
    e = jnp.exp(s - jnp.max(s, axis=-1, keepdims=True))
    return e / jnp.sum(e, axis=-1, keepdims=True)


def row_mask(block, feat):
    (q0, q1), (k0, k1) = block
    return cell_ids(q0, q1 - q0, feat, 0)[0] == cell_ids(k0, k1 - k0, feat, 1)[0]


def col_mask(cells, feat, context):
    key_row, key_feat = cell_ids(0, cells, feat, 1)
    return (cell_ids(0, cells, feat, 0)[1] == key_feat) & (key_row < context)


def lanes(j, width):
    return pl.ds(pl.multiple_of(j * width, width), width)


def start(src, dst, sem):
    copy = pltpu.make_async_copy(src, dst, sem)
    copy.start()
    return copy


def fwd_kernel(rows, feat, first, *refs):
    ctl, ctx, x_hbm, gains, win, wout, wup, wdown = refs[:8]
    refs = refs[8:] if first else refs[12:]
    y_hbm, hs, qkvs, os, zs = refs[:5]
    win_v, wout_v, wup_v, wdown_v, h_v, qkv_v, o_v, z_v, g_v, a_v, y_v, sem_in, sem_out = refs[5:]
    cells, width = a_v.shape
    ff = z_v.shape[1]
    hd = width // HEADS
    scale = hd ** (-0.5)
    tile = 256

    @pl.when(ctl[0] == 1)
    def _():
        table = ctl[1]
        c_x = start(x_hbm, h_v.at[0], sem_in.at[0])
        c_win0 = start(win.at[0], win_v.at[0], sem_in.at[1])
        c_wout0 = start(wout.at[0], wout_v.at[0], sem_in.at[2])
        c_win1 = start(win.at[1], win_v.at[1], sem_in.at[3])
        c_wout1 = start(wout.at[1], wout_v.at[1], sem_in.at[4])
        c_up = start(wup, wup_v, sem_in.at[5])
        c_down = start(wdown, wdown_v, sem_in.at[6])
        outs = []
        c_x.wait()
        outs.append(start(h_v.at[0], hs.at[table, 0], sem_out.at[0]))
        for site in range(2):
            a_v[...] = normalized(h_v[site])[0] * gains[site : site + 1, :]
            (c_win0, c_win1)[site].wait()

            @pl.loop(0, 3 * width // tile)
            def _(j):
                qkv_v[site, :, lanes(j, tile)] = mm(a_v[...], win_v[site, :, lanes(j, tile)])

            outs.append(start(qkv_v.at[site], qkvs.at[table, site], sem_out.at[1 + site]))
            if site == 0:
                blocks = row_blocks(rows, feat)
                masks = [row_mask(block, feat) for block in blocks]
            else:
                blocks = (((0, cells), (0, cells)),)
                masks = [col_mask(cells, feat, ctx[table])]

            @pl.loop(0, HEADS)
            def _(head):
                for ((q0, q1), (k0, k1)), mask in zip(blocks, masks):
                    q = qkv_v[site, q0:q1, lanes(head, hd)]
                    k = qkv_v[site, k0:k1, lanes(HEADS + head, hd)]
                    v = qkv_v[site, k0:k1, lanes(2 * HEADS + head, hd)]
                    o_v[site, q0:q1, lanes(head, hd)] = mm(probs(q, k, mask, scale), v)

            outs.append(start(o_v.at[site], os.at[table, site], sem_out.at[3 + site]))
            (c_wout0, c_wout1)[site].wait()

            @pl.loop(0, width // tile)
            def _(j):
                at = lanes(j, tile)
                h_v[site + 1, :, at] = h_v[site, :, at] + mm(o_v[site], wout_v[site, :, at])

            outs.append(start(h_v.at[site + 1], hs.at[table, site + 1], sem_out.at[5 + site]))
        a_v[...] = normalized(h_v[2])[0] * gains[2:3, :]
        c_up.wait()

        @pl.loop(0, ff // tile)
        def _(j):
            at = lanes(j, tile)
            z = mm(a_v[...], wup_v[:, at])
            z_v[:, at] = z
            g_v[:, at] = 0.5 * z * (1.0 + lax.erf(z * INV_SQRT2))

        outs.append(start(z_v, zs.at[table], sem_out.at[7]))
        c_down.wait()

        @pl.loop(0, width // tile)
        def _(j):
            at = lanes(j, tile)
            y_v[:, at] = h_v[2, :, at] + mm(g_v[...], wdown_v[:, at])

        outs.append(start(y_v, y_hbm, sem_out.at[8]))
        for copy in outs:
            copy.wait()


def bwd_kernel(rows, feat, first, *refs):
    ctl, ctx, dy_a, dy_b, gains, win, wout, wup, wdown, hs, qkvs, zs = refs[:12]
    refs = refs[12:] if first else refs[17:]
    dx_hbm, dgain, as_, dqkvs, dhs, gs, dzs = refs[:7]
    win_v, wout_v, wup_v, wdown_v, h_v, qkv_v, z_v, a_v, dqkv_v, dh_v, g_v, do_v, sem_in, sem_out = refs[7:]
    cells, width = do_v.shape
    ff = z_v.shape[1]
    hd = width // HEADS
    scale = hd ** (-0.5)
    tile = 256

    @pl.when(ctl[0] == 1)
    def _():
        table = ctl[1]

        @pl.when(ctl[2] == 0)
        def _():
            start(dy_a, dh_v.at[2], sem_in.at[0]).wait()

        @pl.when(ctl[2] == 1)
        def _():
            start(dy_b, dh_v.at[2], sem_in.at[0]).wait()

        c_down = start(wdown, wdown_v, sem_in.at[1])
        c_z = start(zs.at[table], z_v, sem_in.at[2])
        c_up = start(wup, wup_v, sem_in.at[3])
        c_h = start(hs.at[table], h_v, sem_in.at[4])
        c_wout = start(wout, wout_v, sem_in.at[5])
        c_qkv = start(qkvs.at[table], qkv_v, sem_in.at[6])
        c_win = start(win, win_v, sem_in.at[7])
        outs = []
        outs.append(start(dh_v.at[2], dhs.at[table, 2], sem_out.at[0]))
        c_down.wait()
        c_z.wait()

        @pl.loop(0, ff // tile)
        def _(j):
            at = lanes(j, tile)
            dg = mm_nt(dh_v[2], wdown_v[at, :])
            z = z_v[:, at]
            phi = 0.5 * (1.0 + lax.erf(z * INV_SQRT2))
            g_v[:, at] = z * phi
            z_v[:, at] = dg * (phi + z * (INV_SQRT2PI * jnp.exp(-0.5 * z * z)))

        outs.append(start(g_v, gs.at[table], sem_out.at[1]))
        outs.append(start(z_v, dzs.at[table], sem_out.at[2]))
        c_up.wait()

        @pl.loop(0, width // tile)
        def _(j):
            at = lanes(j, tile)
            do_v[:, at] = mm_nt(z_v[...], wup_v[at, :])

        c_h.wait()
        for site in (1, 0):
            dh, a, dg_row = norm_back(h_v[site + 1], gains[site + 1 : site + 2, :], do_v[...])
            dh_v[site] = dh_v[site + 1] + dh
            a_v[site + 1] = a
            dgain[site + 1 : site + 2, :] = dg_row
            outs.append(start(dh_v.at[site], dhs.at[table, site], sem_out.at[3 + site]))
            outs.append(start(a_v.at[site + 1], as_.at[table, site + 1], sem_out.at[5 + site]))
            if site == 1:
                c_wout.wait()

            @pl.loop(0, width // tile)
            def _(j):
                at = lanes(j, tile)
                do_v[:, at] = mm_nt(dh_v[site], wout_v[site, at, :])

            if site == 1:
                c_qkv.wait()
            if site == 0:
                blocks = row_blocks(rows, feat)
                masks = [row_mask(block, feat) for block in blocks]
            else:
                blocks = (((0, cells), (0, cells)),)
                masks = [col_mask(cells, feat, ctx[table])]

            @pl.loop(0, HEADS)
            def _(head):
                done = 0
                at_q, at_k, at_v = lanes(head, hd), lanes(HEADS + head, hd), lanes(2 * HEADS + head, hd)
                for ((q0, q1), (k0, k1)), mask in zip(blocks, masks):
                    q = qkv_v[site, q0:q1, at_q]
                    k = qkv_v[site, k0:k1, at_k]
                    v = qkv_v[site, k0:k1, at_v]
                    do = do_v[q0:q1, at_q]
                    p = probs(q, k, mask, scale)
                    dp = mm_nt(do, v)
                    ds = p * (dp - jnp.sum(p * dp, axis=-1, keepdims=True)) * scale
                    dqkv_v[site, q0:q1, at_q] = mm(ds, k)
                    for at, term in ((at_k, mm_tn(ds, q)), (at_v, mm_tn(p, do))):
                        if done > k0:
                            dqkv_v[site, k0:done, at] += term[: done - k0]
                            dqkv_v[site, done:k1, at] = term[done - k0 :]
                        else:
                            dqkv_v[site, k0:k1, at] = term
                    done = k1

            outs.append(start(dqkv_v.at[site], dqkvs.at[table, site], sem_out.at[7 + site]))
            if site == 1:
                c_win.wait()

            @pl.loop(0, width // tile)
            def _(j):
                at = lanes(j, tile)
                do_v[:, at] = mm_nt(dqkv_v[site], win_v[site, at, :])

        dh, a, dg_row = norm_back(h_v[0], gains[0:1, :], do_v[...])
        do_v[...] = dh_v[0] + dh
        a_v[0] = a
        dgain[0:1, :] = dg_row
        outs.append(start(a_v.at[0], as_.at[table, 0], sem_out.at[9]))
        outs.append(start(do_v, dx_hbm, sem_out.at[10]))
        for copy in outs:
            copy.wait()


SMEM = pl.BlockSpec(memory_space=pltpu.SMEM)
VMEM = pl.BlockSpec(memory_space=pltpu.VMEM)
ANY = pl.BlockSpec(memory_space=pl.ANY)


def f32(*shape):
    return jax.ShapeDtypeStruct(shape, jnp.float32)


def forward(rows, feat, tables, ctl, ctx, x, params, saved):
    gains, win, wout, wup, wdown = params
    cells, width = x.shape
    ff = wup.shape[1]
    first = saved is None
    operands = [ctl, ctx, x, gains, win, wout, wup, wdown]
    specs = [SMEM, SMEM, ANY, VMEM, ANY, ANY, ANY, ANY]
    aliases = {}
    if not first:
        aliases = {len(operands) + i: i + 1 for i in range(4)}
        operands += list(saved)
        specs += [ANY] * 4
    outs = pl.pallas_call(
        functools.partial(fwd_kernel, rows, feat, first),
        out_shape=(
            f32(cells, width),
            f32(tables, 3, cells, width),
            f32(tables, 2, cells, 3 * width),
            f32(tables, 2, cells, width),
            f32(tables, cells, ff),
        ),
        in_specs=specs,
        out_specs=[ANY] * 5,
        input_output_aliases=aliases,
        scratch_shapes=[
            pltpu.VMEM(win.shape, jnp.float32),
            pltpu.VMEM(wout.shape, jnp.float32),
            pltpu.VMEM(wup.shape, jnp.float32),
            pltpu.VMEM(wdown.shape, jnp.float32),
            pltpu.VMEM((3, cells, width), jnp.float32),
            pltpu.VMEM((2, cells, 3 * width), jnp.float32),
            pltpu.VMEM((2, cells, width), jnp.float32),
            pltpu.VMEM((cells, ff), jnp.float32),
            pltpu.VMEM((cells, ff), jnp.float32),
            pltpu.VMEM((cells, width), jnp.float32),
            pltpu.VMEM((cells, width), jnp.float32),
            pltpu.SemaphoreType.DMA((7,)),
            pltpu.SemaphoreType.DMA((9,)),
        ],
        compiler_params=pltpu.CompilerParams(vmem_limit_bytes=VMEM_LIMIT),
        name="layer_forward",
    )(*operands)
    return outs[0], outs[1:]


def backward(rows, feat, tables, ctl, ctx, dy_a, dy_b, params, saved, kept):
    gains, win, wout, wup, wdown = params
    cells, width = dy_a.shape
    ff = wup.shape[1]
    first = kept is None
    hs, qkvs, _, zs = saved
    operands = [ctl, ctx, dy_a, dy_b, gains, win, wout, wup, wdown, hs, qkvs, zs]
    specs = [SMEM, SMEM, ANY, ANY, VMEM, ANY, ANY, ANY, ANY, ANY, ANY, ANY]
    aliases = {}
    if not first:
        aliases = {len(operands) + i: i + 2 for i in range(5)}
        operands += list(kept)
        specs += [ANY] * 5
    outs = pl.pallas_call(
        functools.partial(bwd_kernel, rows, feat, first),
        out_shape=(
            f32(cells, width),
            f32(3, width),
            f32(tables, 3, cells, width),
            f32(tables, 2, cells, 3 * width),
            f32(tables, 3, cells, width),
            f32(tables, cells, ff),
            f32(tables, cells, ff),
        ),
        in_specs=specs,
        out_specs=[ANY, VMEM] + [ANY] * 5,
        input_output_aliases=aliases,
        scratch_shapes=[
            pltpu.VMEM(win.shape, jnp.float32),
            pltpu.VMEM(wout.shape, jnp.float32),
            pltpu.VMEM(wup.shape, jnp.float32),
            pltpu.VMEM(wdown.shape, jnp.float32),
            pltpu.VMEM((3, cells, width), jnp.float32),
            pltpu.VMEM((2, cells, 3 * width), jnp.float32),
            pltpu.VMEM((cells, ff), jnp.float32),
            pltpu.VMEM((3, cells, width), jnp.float32),
            pltpu.VMEM((2, cells, 3 * width), jnp.float32),
            pltpu.VMEM((3, cells, width), jnp.float32),
            pltpu.VMEM((cells, ff), jnp.float32),
            pltpu.VMEM((cells, width), jnp.float32),
            pltpu.SemaphoreType.DMA((8,)),
            pltpu.SemaphoreType.DMA((11,)),
        ],
        compiler_params=pltpu.CompilerParams(vmem_limit_bytes=VMEM_LIMIT),
        name="layer_backward",
    )(*operands)
    return outs[0], outs[1], outs[2:]


def local(
    cells,
    missing_mask,
    missing_embed,
    context_rows,
    norm_gains,
    attn_in,
    attn_out,
    mlp_up,
    mlp_down,
    cotangent,
):
    section = lax.axis_index("section")
    tables, rows, feat, width = cells.shape
    count = rows * feat
    params = (norm_gains[0], attn_in[0], attn_out[0], mlp_up[0], mlp_down[0])
    masked = (missing_mask == 1)[..., None]
    filled = jnp.where(masked, missing_embed, cells).reshape(tables, count, width)
    cot = cotangent.reshape(tables, count, width)
    is_first = section == 0

    def ctl(at_first, at_last):
        return jnp.where(is_first, jnp.array(at_first, jnp.int32), jnp.array(at_last, jnp.int32))

    fwd = functools.partial(forward, rows, feat, tables)
    bwd = functools.partial(backward, rows, feat, tables)
    idle = (0, 0, 0)
    fwd_pairs, bwd_pairs = [(0, 1)], [(1, 0)]

    y0, saved = fwd(ctl((1, 0, 0), idle), context_rows, filled[0], params, None)
    r0 = lax.ppermute(y0, "section", fwd_pairs)
    y1, saved = fwd(ctl((1, 1, 0), idle), context_rows, filled[1], params, saved)
    r1 = lax.ppermute(y1, "section", fwd_pairs)
    y2, saved = fwd(ctl(idle, (1, 0, 0)), context_rows, r0, params, saved)
    d0, dg0, kept = bwd(ctl(idle, (1, 0, 0)), context_rows, cot[0], cot[0], params, saved, None)
    e0 = lax.ppermute(d0, "section", bwd_pairs)
    y3, saved = fwd(ctl(idle, (1, 1, 0)), context_rows, r1, params, saved)
    d1, dg1, kept = bwd(ctl((1, 0, 1), (1, 1, 0)), context_rows, cot[1], e0, params, saved, kept)
    e1 = lax.ppermute(d1, "section", bwd_pairs)
    d2, dg2, kept = bwd(ctl((1, 1, 0), idle), context_rows, e1, e1, params, saved, kept)

    layer_out = jnp.where(is_first, jnp.stack([y0, y1]), jnp.stack([y2, y3]))
    d_inputs = jnp.where(is_first, jnp.stack([d1, d2]), jnp.stack([d0, d1]))
    d_gain = jnp.where(is_first, dg1 + dg2, dg0 + dg1)
    as_, dqkvs, dhs, gs, dzs = kept
    os = saved[2]

    def summed(a, b, spec):
        return jnp.einsum(spec, a, b, precision=PREC, preferred_element_type=jnp.float32)

    d_up = summed(as_[:, 2], dzs, "tck,tcn->kn")
    d_down = summed(gs, dhs[:, 2], "tck,tcn->kn")
    d_out = jnp.stack([summed(os[:, s], dhs[:, s], "tck,tcn->kn") for s in range(2)])
    d_in = jnp.stack([summed(as_[:, s], dqkvs[:, s], "tck,tcn->kn") for s in range(2)])

    d_inputs = d_inputs.reshape(cells.shape)
    missing = jnp.where(is_first, jnp.sum(jnp.where(masked, d_inputs, 0.0), axis=(0, 1, 2)), 0.0)
    input_grad = jnp.where(is_first & masked, 0.0, d_inputs)
    up_all, down_all = lax.psum((d_up, d_down), "dp")
    in_all, out_all, gain_all = lax.psum((d_in, d_out, d_gain), "dp")
    missing_all = lax.psum(missing, ("section", "dp"))
    return (
        layer_out.reshape(cells.shape)[None],
        input_grad[None],
        gain_all[None],
        in_all[None],
        out_all[None],
        up_all[None],
        down_all[None],
        missing_all,
    )


def solution(mesh):
    in_specs = (
        P("dp", None, None, None),
        P("dp", None, None),
        P(),
        P("dp"),
        P("section", None, None),
        P("section", None, None, None),
        P("section", None, None, None),
        P("section", None, None),
        P("section", None, None),
        P("dp", None, None, None),
    )
    out_specs = (
        P("section", "dp", None, None, None),
        P("section", "dp", None, None, None),
        P("section", None, None),
        P("section", None, None, None),
        P("section", None, None, None),
        P("section", None, None),
        P("section", None, None),
        P(),
    )
    return jax.shard_map(local, mesh=mesh, in_specs=in_specs, out_specs=out_specs, check_vma=False)
```

```python
import functools
from types import SimpleNamespace

import jax
import jax.numpy as jnp
from jax import lax
from jax.experimental import pallas as pl
from jax.experimental.pallas import tpu as pltpu
from jax.sharding import PartitionSpec as P

HEADS = 4
EPSILON = 1e-05
NEG = -1e30
INV_SQRT2 = 0.7071067811865476
INV_SQRT2PI = 0.3989422804014327
VMEM_LIMIT = 62 * 1024 * 1024
TILE = 512
F32, BF16 = jnp.float32, jnp.bfloat16


def dot(a, b, contract=((1,), (0,))):
    return lax.dot_general(a, b, (contract, ((), ())), preferred_element_type=F32)


def split(v):
    hi = v.astype(BF16)
    return hi, (v - hi.astype(F32)).astype(BF16)


def put(ref, index, v):
    hi, lo = split(v)
    ref[(0, *index)] = hi
    ref[(1, *index)] = lo


def parts(ref, *index):
    return ref[(0, *index)], ref[(1, *index)]


def wide(a, b, ca, cb):
    (ah, al), (bh, bl) = a, b
    return dot(jnp.concatenate([ah, ah, al], ca), jnp.concatenate([bh, bl, bh], cb), ((ca,), (cb,)))


def side(a, b):
    (ah, al), (bh, bl) = a, b
    width = bh.shape[1]
    both = dot(ah, jnp.concatenate([bh, bl], 1))
    return both[:, :width] + both[:, width:] + dot(al, bh)


def normalized(h):
    centred = h - jnp.mean(h, axis=-1, keepdims=True)
    rstd = lax.rsqrt(jnp.mean(centred * centred, axis=-1, keepdims=True) + EPSILON)
    return centred * rstd, rstd


def norm_back(n, rstd, gain, da):
    dn = da * gain
    return rstd * (dn - jnp.mean(dn, axis=-1, keepdims=True) - n * jnp.mean(dn * n, axis=-1, keepdims=True))


def cell_ids(start, count, rows, along):
    shape = (count, 1) if along == 0 else (1, count)
    at = lax.broadcasted_iota(jnp.int32, shape, along) + start
    feat = lax.shift_right_logical(at * ((1 << 20) // rows + 1), 20)
    return at - feat * rows, feat


def up16(n):
    return (n + 15) // 16 * 16


def col_blocks(rows, feat):
    cells = up16(rows * feat)
    half = up16((feat + 1) // 2 * rows)
    first_keys = min(cells, up16((((half - 1) // rows) + 1) * rows))
    second_keys = ((half // rows) * rows) // 16 * 16
    return (((0, half), (0, first_keys)), ((half, cells), (second_keys, cells)))


def lanes(j, width):
    return pl.ds(pl.multiple_of(j * width, width), width)


def start(src, dst, sem):
    copy = pltpu.make_async_copy(src, dst, sem)
    copy.start()
    return copy


def attention_biases(rows, feat, context, col_refs, row_ref, keys_along):
    for ((q0, q1), (k0, k1)), ref in zip(col_blocks(rows, feat), col_refs):
        _, q_feat = cell_ids(q0, q1 - q0, rows, 1 - keys_along)
        k_row, k_feat = cell_ids(k0, k1 - k0, rows, keys_along)
        ref[...] = jnp.where((q_feat == k_feat) & (k_row < context), 0.0, NEG)
    cells = up16(rows * feat)
    q_row, _ = cell_ids(0, cells, rows, 1 - keys_along)
    k_row, k_feat = cell_ids(0, cells, rows, keys_along)
    row_ref[...] = jnp.where((q_row == k_row) & (k_feat < feat), 0.0, NEG)


def phi_of(z):
    return 0.5 * (1.0 + lax.erf(z * INV_SQRT2))


SMEM, VMEM, ANY = pltpu.SMEM, pltpu.VMEM, pl.ANY


def call(name, body, ins, outs, carried, scratch):
    held = {k: v for k, v in carried.items() if not isinstance(v, jax.ShapeDtypeStruct)}
    names = [*ins, *("_" + k for k in held), *outs, *carried, *scratch]

    def kernel(*refs):
        body(SimpleNamespace(**dict(zip(names, refs))))

    first_carried = len(outs)
    order = list(carried)
    results = pl.pallas_call(
        kernel,
        out_shape=[t for t, _ in outs.values()] + [jax.ShapeDtypeStruct(v.shape, v.dtype) for v in carried.values()],
        in_specs=[pl.BlockSpec(memory_space=s) for _, s in ins.values()] + [pl.BlockSpec(memory_space=ANY)] * len(held),
        out_specs=[pl.BlockSpec(memory_space=s) for _, s in outs.values()]
        + [pl.BlockSpec(memory_space=ANY)] * len(carried),
        input_output_aliases={len(ins) + i: first_carried + order.index(k) for i, k in enumerate(held)},
        scratch_shapes=list(scratch.values()),
        compiler_params=pltpu.CompilerParams(vmem_limit_bytes=VMEM_LIMIT),
        name=name,
    )(*(a for a, _ in ins.values()), *held.values())
    return SimpleNamespace(**dict(zip([*outs, *carried], results)))


def f32(*shape):
    return jax.ShapeDtypeStruct(shape, F32)


def b16(*shape):
    return jax.ShapeDtypeStruct(shape, BF16)


def dma(n):
    return pltpu.SemaphoreType.DMA((n,))


class Layer:
    def __init__(self, tables, rows, feat, width, ff):
        self.tables, self.rows, self.feat, self.width, self.ff = tables, rows, feat, width, ff
        self.cells = up16(rows * feat)
        self.hd = width // HEADS
        self.scale = self.hd ** (-0.5)

    def bias_scratch(self, keys_along):
        def shape(q, k):
            return (k, q) if keys_along == 0 else (q, k)

        out = {}
        for name, ((q0, q1), (k0, k1)) in zip(("bias_a", "bias_b"), col_blocks(self.rows, self.feat)):
            out[name] = VMEM(shape(q1 - q0, k1 - k0), F32)
        out["bias_row"] = VMEM((self.cells, self.cells), F32)
        return out

    def sites(self, r, site):
        if site == 1:
            return list(zip(col_blocks(self.rows, self.feat), (r.bias_a, r.bias_b)))
        return [(((0, self.cells), (0, self.cells)), r.bias_row)]

    def forward(self, kind, ctl, ctx, x, extra, gains, weights, saved):
        t, c, w, ff = self.tables, self.cells, self.width, self.ff
        splitting = weights is None
        ins = {"ctl": (ctl, SMEM), "ctx": (ctx, SMEM), "x": (x, ANY), "gains": (gains, VMEM)}
        if kind == "cells":
            ins |= {"mask": (extra.mask, VMEM), "embed": (extra.embed, VMEM)}
        names = ("win", "wout", "wup", "wdown")
        raw = extra.raw
        shapes = [(2, *a.shape) for a in raw]
        for n, a in zip(names, raw if splitting else weights):
            ins[n] = (a, ANY)
        outs = {"y": (f32(self.rows * self.feat, w), ANY)}
        if splitting:
            outs |= {n + "_out": (b16(*s), ANY) for n, s in zip(names, shapes)}
        if saved is None:
            saved = {
                "out": f32(t, self.rows * self.feat, w),
                "hs": f32(t, 3, c, w),
                "qkvs": b16(t, 2, 2, c, 3 * w),
                "os": b16(t, 2, 2, c, w),
                "zs": f32(t, c, ff),
            }
        scratch = {n + "_v": VMEM(s, BF16) for n, s in zip(names, shapes)}
        scratch |= {
            "h_v": VMEM((3, c, w), F32),
            "qkv_v": VMEM((2, 2, c, 3 * w), BF16),
            "o_v": VMEM((2, 2, c, w), BF16),
            "z_v": VMEM((c, ff), F32),
            "g_v": VMEM((2, c, ff), BF16),
            "a_v": VMEM((2, c, w), BF16),
            "y_v": VMEM((c, w), F32),
            "sem_in": dma(5),
            "sem_out": dma(14),
        } | self.bias_scratch(1)
        if splitting:
            scratch |= {n + "_raw": VMEM(a.shape, F32) for n, a in zip(names, raw)}

        def body(r):
            vs = [getattr(r, n + "_v") for n in names]
            kept = []
            if splitting:
                raws = [getattr(r, n + "_raw") for n in names]
                loads = [start(getattr(r, n), v, r.sem_in.at[1 + i]) for i, (n, v) in enumerate(zip(names, raws))]
                for i, n in enumerate(names):
                    loads[i].wait()
                    split_weights(raws[i], vs[i])
                    kept.append(start(vs[i], getattr(r, n + "_out"), r.sem_out.at[10 + i]))

            @pl.when(r.ctl[0] == 1)
            def _():
                if splitting:
                    waits = [lambda: None] * 4
                else:
                    waits = [start(getattr(r, n), v, r.sem_in.at[1 + i]).wait for i, (n, v) in enumerate(zip(names, vs))]
                self.forward_body(r, kind, waits)

            for copy in kept:
                copy.wait()

        res = call("layer_forward", body, ins, outs, saved, scratch)
        if splitting:
            weights = [getattr(res, n + "_out") for n in names]
        return res.y, weights, {k: getattr(res, k) for k in saved}

    def forward_body(self, r, kind, waits):
        rows, feat, c, w, ff, hd = self.rows, self.feat, self.cells, self.width, self.ff, self.hd
        table = r.ctl[1]
        stores = []

        def keep(src, dst):
            stores.append(start(src, dst, r.sem_out.at[len(stores)]))

        real = rows * feat
        x = r.x if kind == "flat" else r.x.at[table]
        load_x = start(x, r.h_v.at[0, 0:real], r.sem_in.at[0])
        attention_biases(rows, feat, r.ctx[table], (r.bias_a, r.bias_b), r.bias_row, 1)
        r.h_v[0, real:, :] = jnp.zeros((c - real, w), F32)
        load_x.wait()
        if kind != "flat":
            r.h_v[0] = jnp.where(r.mask[table] == 1.0, r.embed[...], r.h_v[0])
        keep(r.h_v.at[0], r.hs.at[table, 0])
        for site in range(2):
            put(r.a_v, (), normalized(r.h_v[site])[0] * r.gains[site : site + 1, :])
            if site == 0:
                waits[0]()

            @pl.loop(0, 3 * w // TILE)
            def _(j):
                at = lanes(j, TILE)
                out = wide(parts(r.a_v), parts(r.win_v, site, slice(None), at), 1, 0)
                put(r.qkv_v, (site, slice(None), at), out)

            keep(r.qkv_v.at[:, site], r.qkvs.at[table, :, site])

            @pl.loop(0, HEADS)
            def _(head):
                for ((q0, q1), (k0, k1)), bias in self.sites(r, site):
                    q = parts(r.qkv_v, site, slice(q0, q1), lanes(head, hd))
                    k = parts(r.qkv_v, site, slice(k0, k1), lanes(HEADS + head, hd))
                    v = parts(r.qkv_v, site, slice(k0, k1), lanes(2 * HEADS + head, hd))
                    s = wide(q, k, 1, 1) * self.scale + bias[...]
                    e = jnp.exp(s - jnp.max(s, axis=-1, keepdims=True))
                    p = e * (1.0 / jnp.sum(e, axis=-1, keepdims=True))
                    put(r.o_v, (site, slice(q0, q1), lanes(head, hd)), side(split(p), v))

            keep(r.o_v.at[:, site], r.os.at[table, :, site])
            if site == 0:
                waits[1]()
            r.h_v[site + 1] = r.h_v[site] + wide(parts(r.o_v, site), parts(r.wout_v, site), 1, 0)
            keep(r.h_v.at[site + 1], r.hs.at[table, site + 1])
        put(r.a_v, (), normalized(r.h_v[2])[0] * r.gains[2:3, :])
        waits[2]()

        @pl.loop(0, ff // TILE)
        def _(j):
            at = lanes(j, TILE)
            z = wide(parts(r.a_v), parts(r.wup_v, slice(None), at), 1, 0)
            r.z_v[:, at] = z
            put(r.g_v, (slice(None), at), z * phi_of(z))

        keep(r.z_v, r.zs.at[table])
        waits[3]()
        r.y_v[...] = r.h_v[2]

        @pl.loop(0, ff // TILE)
        def _(j):
            at = lanes(j, TILE)
            r.y_v[...] += wide(parts(r.g_v, slice(None), at), parts(r.wdown_v, at), 1, 0)

        keep(r.y_v.at[0:real], r.y)
        keep(r.y_v.at[0:real], r.out.at[table])
        for copy in stores:
            copy.wait()

    def mlp_back(self, ctl, cot, dy, gains, weights, saved, kept):
        t, c, w, ff = self.tables, self.cells, self.width, self.ff
        rows, feat = self.rows, self.feat
        ins = {"ctl": (ctl, SMEM), "gains": (gains, VMEM), "wup": (weights[2], ANY), "wdown": (weights[3], ANY)}
        ins |= {"hs": (saved["hs"], ANY), "zs": (saved["zs"], ANY), "dy": (dy, ANY)}
        if cot is not None:
            ins["cot"] = (cot, ANY)
        if kept is None:
            kept = {
                "dys": b16(t, 2, c, w),
                "gs": b16(t, 2, c, ff),
                "dzs": b16(t, 2, c, ff),
                "a2s": b16(t, 2, c, w),
            }
        outs = {"dw": (f32(c, w), ANY), "dgain": (f32(1, w), VMEM)}
        scratch = {
            "wup_v": VMEM(weights[2].shape, BF16),
            "wdown_v": VMEM(weights[3].shape, BF16),
            "w_v": VMEM((c, w), F32),
            "dy_v": VMEM((c, w), F32),
            "da_v": VMEM((c, w), F32),
            "z_v": VMEM((c, ff), F32),
            "dys_v": VMEM((2, c, w), BF16),
            "g_v": VMEM((2, c, ff), BF16),
            "dz_v": VMEM((2, c, ff), BF16),
            "a_v": VMEM((2, c, w), BF16),
            "sem_in": dma(5),
            "sem_out": dma(5),
        }

        def body(r):
            @pl.when(r.ctl[0] == 1)
            def _():
                table, real = r.ctl[1], rows * feat
                r.dy_v[real:, :] = jnp.zeros((c - real, w), F32)
                c_down = start(r.wdown, r.wdown_v, r.sem_in.at[1])
                c_z = start(r.zs.at[table], r.z_v, r.sem_in.at[2])
                c_up = start(r.wup, r.wup_v, r.sem_in.at[3])
                c_w = start(r.hs.at[table, 2], r.w_v, r.sem_in.at[4])
                if cot is not None:

                    @pl.when(r.ctl[2] == 0)
                    def _():
                        start(r.cot.at[table], r.dy_v.at[0:real], r.sem_in.at[0]).wait()

                @pl.when(r.ctl[2] == 1)
                def _():
                    start(r.dy, r.dy_v.at[0:real], r.sem_in.at[0]).wait()

                put(r.dys_v, (), r.dy_v[...])
                stores = [start(r.dys_v, r.dys.at[table], r.sem_out.at[0])]
                c_down.wait()
                c_z.wait()

                @pl.loop(0, ff // TILE)
                def _(j):
                    at = lanes(j, TILE)
                    dg = wide(parts(r.dys_v), parts(r.wdown_v, at), 1, 1)
                    z = r.z_v[:, at]
                    phi = phi_of(z)
                    put(r.g_v, (slice(None), at), z * phi)
                    put(r.dz_v, (slice(None), at), dg * (phi + z * (INV_SQRT2PI * jnp.exp(-0.5 * z * z))))

                stores.append(start(r.g_v, r.gs.at[table], r.sem_out.at[1]))
                stores.append(start(r.dz_v, r.dzs.at[table], r.sem_out.at[2]))
                c_up.wait()
                r.da_v[...] = jnp.zeros((c, w), F32)

                @pl.loop(0, ff // TILE)
                def _(j):
                    at = lanes(j, TILE)
                    r.da_v[...] += wide(parts(r.dz_v, slice(None), at), parts(r.wup_v, slice(None), at), 1, 1)

                c_w.wait()
                gain = r.gains[2:3, :]
                n, rstd = normalized(r.w_v[...])
                put(r.a_v, (), n * gain)
                stores.append(start(r.a_v, r.a2s.at[table], r.sem_out.at[3]))
                da = r.da_v[...]
                r.dgain[...] = jnp.sum(da * n, axis=0, keepdims=True)
                r.dy_v[...] += norm_back(n, rstd, gain, da)
                stores.append(start(r.dy_v, r.dw, r.sem_out.at[4]))
                for copy in stores:
                    copy.wait()

        res = call("mlp_backward", body, ins, outs, kept, scratch)
        return res.dw, res.dgain, {k: getattr(res, k) for k in kept}

    def attn_back(self, ctl, ctx, dw, mask, gains, weights, saved, kept):
        t, c, w = self.tables, self.cells, self.width
        rows, feat, hd = self.rows, self.feat, self.hd
        ins = {"ctl": (ctl, SMEM), "ctx": (ctx, SMEM), "dw": (dw, ANY), "mask": (mask, VMEM), "gains": (gains, VMEM)}
        ins |= {"win": (weights[0], ANY), "wout": (weights[1], ANY), "hs": (saved["hs"], ANY), "qkvs": (saved["qkvs"], ANY)}
        if kept is None:
            kept = {
                "din": f32(t, rows * feat, w),
                "as_": b16(t, 2, 2, c, w),
                "dqkvs": b16(t, 2, 2, c, 3 * w),
                "dhs": b16(t, 2, 2, c, w),
            }
        outs = {"dx": (f32(rows * feat, w), ANY), "small": (f32(3, w), VMEM)}
        scratch = {
            "win_v": VMEM(weights[0].shape, BF16),
            "wout_v": VMEM(weights[1].shape, BF16),
            "h_v": VMEM((2, c, w), F32),
            "dh_v": VMEM((c, w), F32),
            "da_v": VMEM((c, w), F32),
            "qkv_v": VMEM((2, 2, c, 3 * w), BF16),
            "dqkv_v": VMEM((2, 2, c, 3 * w), BF16),
            "dqkv_f": VMEM((c, 3 * w), F32),
            "do_v": VMEM((2, c, w), BF16),
            "dhs_v": VMEM((2, 2, c, w), BF16),
            "a_v": VMEM((2, 2, c, w), BF16),
            "sem_in": dma(5),
            "sem_out": dma(8),
        } | self.bias_scratch(0)

        def body(r):
            @pl.when(r.ctl[0] == 1)
            def _():
                table, real = r.ctl[1], rows * feat
                c_dw = start(r.dw, r.dh_v, r.sem_in.at[0])
                c_wout = start(r.wout, r.wout_v, r.sem_in.at[1])
                c_qkv = start(r.qkvs.at[table], r.qkv_v, r.sem_in.at[2])
                c_win = start(r.win, r.win_v, r.sem_in.at[3])
                c_h = start(r.hs.at[table, 0:2], r.h_v, r.sem_in.at[4])
                stores = []

                def keep(src, dst):
                    stores.append(start(src, dst, r.sem_out.at[len(stores)]))

                attention_biases(rows, feat, r.ctx[table], (r.bias_a, r.bias_b), r.bias_row, 0)
                c_dw.wait()
                for site in (1, 0):
                    put(r.dhs_v, (site,), r.dh_v[...])
                    keep(r.dhs_v.at[:, site], r.dhs.at[table, :, site])
                    if site == 1:
                        c_wout.wait()
                    put(r.do_v, (), wide(parts(r.dhs_v, site), parts(r.wout_v, site), 1, 1))
                    if site == 1:
                        c_qkv.wait()

                    @pl.loop(0, HEADS)
                    def _(head):
                        done = 0
                        at_q, at_k, at_v = lanes(head, hd), lanes(HEADS + head, hd), lanes(2 * HEADS + head, hd)
                        for ((q0, q1), (k0, k1)), bias in self.sites(r, site):
                            q = parts(r.qkv_v, site, slice(q0, q1), at_q)
                            k = parts(r.qkv_v, site, slice(k0, k1), at_k)
                            v = parts(r.qkv_v, site, slice(k0, k1), at_v)
                            do = parts(r.do_v, slice(q0, q1), at_q)
                            s = wide(k, q, 1, 1) * self.scale + bias[...]
                            e = jnp.exp(s - jnp.max(s, axis=0, keepdims=True))
                            p = e * (1.0 / jnp.sum(e, axis=0, keepdims=True))
                            dp = wide(v, do, 1, 1)
                            ds = split(p * (dp - jnp.sum(p * dp, axis=0, keepdims=True)) * self.scale)
                            r.dqkv_f[q0:q1, at_q] = wide(tuple(x.T for x in k), ds, 1, 0).T
                            for at, term in ((at_k, side(ds, q)), (at_v, side(split(p), do))):
                                if done > k0:
                                    r.dqkv_f[k0:done, at] += term[: done - k0]
                                    r.dqkv_f[done:k1, at] = term[done - k0 :]
                                else:
                                    r.dqkv_f[k0:k1, at] = term
                            done = k1

                    if site == 1:
                        c_win.wait()
                    r.da_v[...] = jnp.zeros((c, w), F32)

                    @pl.loop(0, 3 * w // TILE)
                    def _(j):
                        at = lanes(j, TILE)
                        d = split(r.dqkv_f[:, at])
                        r.dqkv_v[0, site, :, at] = d[0]
                        r.dqkv_v[1, site, :, at] = d[1]
                        r.da_v[...] += wide(d, parts(r.win_v, site, slice(None), at), 1, 1)

                    keep(r.dqkv_v.at[:, site], r.dqkvs.at[table, :, site])
                    if site == 1:
                        c_h.wait()
                    gain = r.gains[site : site + 1, :]
                    n, rstd = normalized(r.h_v[site])
                    put(r.a_v, (site,), n * gain)
                    keep(r.a_v.at[:, site], r.as_.at[table, :, site])
                    da = r.da_v[...]
                    r.small[site : site + 1, :] = jnp.sum(da * n, axis=0, keepdims=True)
                    r.dh_v[...] += norm_back(n, rstd, gain, da)
                keep(r.dh_v.at[0:real], r.dx)
                missing = r.mask[table] == 1.0
                r.small[2:3, :] = jnp.sum(jnp.where(missing, r.dh_v[...], 0.0), axis=0, keepdims=True)
                r.da_v[...] = jnp.where(missing, 0.0, r.dh_v[...])
                keep(r.da_v.at[0:real], r.din.at[table])
                for copy in stores:
                    copy.wait()

        res = call("attention_backward", body, ins, outs, kept, scratch)
        return res.dx, res.small, {k: getattr(res, k) for k in kept}


def split_weights(raw, v):
    step = 64
    lead = raw.shape[:-2]
    for at in [(s,) for s in range(lead[0])] if lead else [()]:

        @pl.loop(0, raw.shape[-2] // step)
        def _(j):
            block = pl.ds(pl.multiple_of(j * step, step), step)
            put(v, (*at, block), raw[(*at, block)])


def weight_grad(a, b, site=None):
    t, c = a.shape[0], a.shape[-2]
    k, n = a.shape[-1], b.shape[-1]
    sites = 1 if a.ndim == 4 else a.shape[2]
    lead = () if a.ndim == 4 else (1,)
    tile = 256

    def kernel(a_ref, b_ref, out_ref):
        mid = (0,) * len(lead)

        def ends(ref, at):
            return [(ref[(i, 0, *mid, slice(None), at)], ref[(i, 1, *mid, slice(None), at)]) for i in range(t)]

        left = ends(a_ref, slice(None))

        @pl.loop(0, n // TILE)
        def _(j):
            at = lanes(j, TILE)
            total = None
            for (ah, al), (bh, bl) in zip(left, ends(b_ref, at)):
                term = dot(jnp.concatenate([ah, ah, al], 0), jnp.concatenate([bh, bl, bh], 0), ((0,), (0,)))
                total = term if total is None else total + term
            out_ref[(*mid, slice(None), at)] = total

    def spec(block, index):
        return pl.BlockSpec(block, index)

    if lead:
        a_spec = spec((t, 2, 1, c, tile), lambda s, i: (0, 0, s, 0, i))
        b_spec = spec((t, 2, 1, c, n), lambda s, i: (0, 0, s, 0, 0))
        o_spec = spec((1, tile, n), lambda s, i: (s, i, 0))
        shape = f32(sites, k, n)
    else:
        a_spec = spec((t, 2, c, tile), lambda s, i: (0, 0, 0, i))
        b_spec = spec((t, 2, c, n), lambda s, i: (0, 0, 0, 0))
        o_spec = spec((tile, n), lambda s, i: (i, 0))
        shape = f32(k, n)
    return pl.pallas_call(
        kernel,
        grid=(sites, k // tile),
        in_specs=[a_spec, b_spec],
        out_specs=o_spec,
        out_shape=shape,
        compiler_params=pltpu.CompilerParams(vmem_limit_bytes=VMEM_LIMIT),
        cost_estimate=pl.CostEstimate(flops=6 * sites * t * c * k * n, bytes_accessed=4 * sites * (t * c * (k + n) + k * n), transcendentals=0),
        name="weight_gradient",
    )(a, b)


def local(
    cells,
    missing_mask,
    missing_embed,
    context_rows,
    norm_gains,
    attn_in,
    attn_out,
    mlp_up,
    mlp_down,
    cotangent,
):
    section = lax.axis_index("section")
    tables, rows, feat, width = cells.shape
    layer = Layer(tables, rows, feat, width, mlp_up.shape[2])
    gains = norm_gains[0]
    is_first = section == 0

    def flat(tables_of_cells):
        return jnp.swapaxes(tables_of_cells, 1, 2).reshape(tables, rows * feat, -1)

    def unflat(cells_of_tables):
        return jnp.swapaxes(cells_of_tables.reshape(tables, feat, rows, width), 1, 2)

    cells, cotangent = flat(cells), flat(cotangent)
    flat_mask = flat(missing_mask == 1)
    flat_mask = jnp.pad(flat_mask, ((0, 0), (0, layer.cells - rows * feat), (0, 0)))
    mask = flat_mask.astype(F32)
    mask_here = jnp.where(is_first, mask, 0.0)

    def ctl(at_first, at_last):
        return jnp.where(is_first, jnp.array(at_first, jnp.int32), jnp.array(at_last, jnp.int32))

    idle = (0, 0, 0)
    fwd_pairs, bwd_pairs = [(0, 1)], [(1, 0)]
    extra = SimpleNamespace(mask=mask, embed=missing_embed[None], raw=(attn_in[0], attn_out[0], mlp_up[0], mlp_down[0]))

    def forward(kind, control, x, weights, saved):
        return layer.forward(kind, control, context_rows, x, extra, gains, weights, saved)

    def mlp_back(control, cot, dy, kept):
        return layer.mlp_back(control, cot, dy, gains, weights, saved, kept)

    def attn_back(control, dw, kept):
        return layer.attn_back(control, context_rows, dw, mask_here, gains, weights, saved, kept)

    y0, weights, saved = forward("cells", ctl((1, 0, 0), idle), cells, None, None)
    r0 = lax.ppermute(y0, "section", fwd_pairs)
    y1, _, saved = forward("cells", ctl((1, 1, 0), idle), cells, weights, saved)
    r1 = lax.ppermute(y1, "section", fwd_pairs)
    _, _, saved = forward("flat", ctl(idle, (1, 0, 0)), r0, weights, saved)
    dw0, dg0, kept_m = mlp_back(ctl(idle, (1, 0, 0)), cotangent, r0, None)
    d0, small0, kept_a = attn_back(ctl(idle, (1, 0, 0)), dw0, None)
    e0 = lax.ppermute(d0, "section", bwd_pairs)
    _, _, saved = forward("flat", ctl(idle, (1, 1, 0)), r1, weights, saved)
    dw1, dg1, kept_m = mlp_back(ctl((1, 0, 1), (1, 1, 0)), cotangent, e0, kept_m)
    d1, small1, kept_a = attn_back(ctl((1, 0, 0), (1, 1, 0)), dw1, kept_a)
    e1 = lax.ppermute(d1, "section", bwd_pairs)
    dw2, dg2, kept_m = mlp_back(ctl((1, 1, 1), idle), None, e1, kept_m)
    d_up = weight_grad(kept_m["a2s"], kept_m["dzs"])
    d_down = weight_grad(kept_m["gs"], kept_m["dys"])
    up_all, down_all = lax.psum((d_up, d_down), "dp")
    _, small2, kept_a = attn_back(ctl((1, 1, 0), idle), dw2, kept_a)
    d_in = weight_grad(kept_a["as_"], kept_a["dqkvs"])
    d_out = weight_grad(saved["os"], kept_a["dhs"])

    def row(first_a, first_b, last_a, last_b):
        return jnp.where(is_first, first_a + first_b, last_a + last_b)

    d_small = jnp.concatenate(
        [
            row(small1[0:2], small2[0:2], small0[0:2], small1[0:2]),
            row(dg1, dg2, dg0, dg1),
            jnp.where(is_first, small1[2:3] + small2[2:3], 0.0),
            jnp.zeros((4, width), F32),
        ],
        0,
    )
    d_rest = jnp.concatenate([d_out.reshape(2 * width, width), d_small], 0)
    (d_in, d_rest), up_all, down_all = lax.optimization_barrier(((d_in, d_rest), up_all, down_all))
    in_all, rest_all = lax.psum((d_in, d_rest), "dp")
    out_all = rest_all[: 2 * width].reshape(2, width, width)
    gain_all = rest_all[2 * width : 2 * width + 3]
    missing = rest_all[2 * width + 3]
    missing_all = jnp.where(is_first, missing, lax.ppermute(missing, "section", fwd_pairs))
    return (
        unflat(saved["out"])[None],
        unflat(kept_a["din"])[None],
        gain_all[None],
        in_all[None],
        out_all[None],
        up_all[None],
        down_all[None],
        missing_all,
    )


def solution(mesh):
    in_specs = (
        P("dp", None, None, None),
        P("dp", None, None),
        P(),
        P("dp"),
        P("section", None, None),
        P("section", None, None, None),
        P("section", None, None, None),
        P("section", None, None),
        P("section", None, None),
        P("dp", None, None, None),
    )
    out_specs = (
        P("section", "dp", None, None, None),
        P("section", "dp", None, None, None),
        P("section", None, None),
        P("section", None, None, None),
        P("section", None, None, None),
        P("section", None, None),
        P("section", None, None),
        P(),
    )
    return jax.shard_map(local, mesh=mesh, in_specs=in_specs, out_specs=out_specs, check_vma=False)
```

```python
import functools
from types import SimpleNamespace

import jax
import jax.numpy as jnp
from jax import lax
from jax.experimental import pallas as pl
from jax.experimental.pallas import tpu as pltpu
from jax.sharding import PartitionSpec as P

HEADS = 4
EPSILON = 1e-05
NEG = -1e30
INV_SQRT2 = 0.7071067811865476
INV_SQRT2PI = 0.3989422804014327
VMEM_LIMIT = 62 * 1024 * 1024
TILE = 512
F32, BF16 = jnp.float32, jnp.bfloat16


def dot(a, b, contract=((1,), (0,))):
    return lax.dot_general(a, b, (contract, ((), ())), preferred_element_type=F32)


def split(v):
    hi = v.astype(BF16)
    return hi, (v - hi.astype(F32)).astype(BF16)


def put(ref, index, v):
    hi, lo = split(v)
    ref[(0, *index)] = hi
    ref[(1, *index)] = lo


def parts(ref, *index):
    return ref[(0, *index)], ref[(1, *index)]


def wide(a, b, ca, cb):
    (ah, al), (bh, bl) = a, b
    return dot(jnp.concatenate([ah, ah, al], ca), jnp.concatenate([bh, bl, bh], cb), ((ca,), (cb,)))


def side(a, b):
    (ah, al), (bh, bl) = a, b
    width = bh.shape[1]
    both = dot(ah, jnp.concatenate([bh, bl], 1))
    return both[:, :width] + both[:, width:] + dot(al, bh)


def normalized(h):
    centred = h - jnp.mean(h, axis=-1, keepdims=True)
    rstd = lax.rsqrt(jnp.mean(centred * centred, axis=-1, keepdims=True) + EPSILON)
    return centred * rstd, rstd


def norm_back(n, rstd, gain, da):
    dn = da * gain
    return rstd * (dn - jnp.mean(dn, axis=-1, keepdims=True) - n * jnp.mean(dn * n, axis=-1, keepdims=True))


def cell_ids(start, count, rows, along):
    shape = (count, 1) if along == 0 else (1, count)
    at = lax.broadcasted_iota(jnp.int32, shape, along) + start
    feat = lax.shift_right_logical(at * ((1 << 20) // rows + 1), 20)
    return at - feat * rows, feat


def up16(n):
    return (n + 15) // 16 * 16


def col_blocks(rows, feat):
    cells = up16(rows * feat)
    half = up16((feat + 1) // 2 * rows)
    first_keys = min(cells, up16((((half - 1) // rows) + 1) * rows))
    second_keys = ((half // rows) * rows) // 16 * 16
    return (((0, half), (0, first_keys)), ((half, cells), (second_keys, cells)))


def lanes(j, width):
    return pl.ds(pl.multiple_of(j * width, width), width)


def start(src, dst, sem):
    copy = pltpu.make_async_copy(src, dst, sem)
    copy.start()
    return copy


def attention_biases(rows, feat, context, col_refs, row_ref, keys_along):
    for ((q0, q1), (k0, k1)), ref in zip(col_blocks(rows, feat), col_refs):
        _, q_feat = cell_ids(q0, q1 - q0, rows, 1 - keys_along)
        k_row, k_feat = cell_ids(k0, k1 - k0, rows, keys_along)
        ref[...] = jnp.where((q_feat == k_feat) & (k_row < context), 0.0, NEG)
    cells = up16(rows * feat)
    q_row, _ = cell_ids(0, cells, rows, 1 - keys_along)
    k_row, k_feat = cell_ids(0, cells, rows, keys_along)
    row_ref[...] = jnp.where((q_row == k_row) & (k_feat < feat), 0.0, NEG)


def phi_of(z):
    return 0.5 * (1.0 + lax.erf(z * INV_SQRT2))


SMEM, VMEM, ANY = pltpu.SMEM, pltpu.VMEM, pl.ANY


def call(name, body, ins, outs, carried, scratch):
    held = {k: v for k, v in carried.items() if not isinstance(v, jax.ShapeDtypeStruct)}
    names = [*ins, *("_" + k for k in held), *outs, *carried, *scratch]

    def kernel(*refs):
        body(SimpleNamespace(**dict(zip(names, refs))))

    first_carried = len(outs)
    order = list(carried)
    results = pl.pallas_call(
        kernel,
        out_shape=[t for t, _ in outs.values()] + [jax.ShapeDtypeStruct(v.shape, v.dtype) for v in carried.values()],
        in_specs=[pl.BlockSpec(memory_space=s) for _, s in ins.values()] + [pl.BlockSpec(memory_space=ANY)] * len(held),
        out_specs=[pl.BlockSpec(memory_space=s) for _, s in outs.values()]
        + [pl.BlockSpec(memory_space=ANY)] * len(carried),
        input_output_aliases={len(ins) + i: first_carried + order.index(k) for i, k in enumerate(held)},
        scratch_shapes=list(scratch.values()),
        compiler_params=pltpu.CompilerParams(vmem_limit_bytes=VMEM_LIMIT),
        name=name,
    )(*(a for a, _ in ins.values()), *held.values())
    return SimpleNamespace(**dict(zip([*outs, *carried], results)))


def f32(*shape):
    return jax.ShapeDtypeStruct(shape, F32)


def b16(*shape):
    return jax.ShapeDtypeStruct(shape, BF16)


def dma(n):
    return pltpu.SemaphoreType.DMA((n,))


class Layer:
    def __init__(self, tables, rows, feat, width, ff):
        self.tables, self.rows, self.feat, self.width, self.ff = tables, rows, feat, width, ff
        self.cells = up16(rows * feat)
        self.hd = width // HEADS
        self.scale = self.hd ** (-0.5)

    def bias_scratch(self, keys_along):
        def shape(q, k):
            return (k, q) if keys_along == 0 else (q, k)

        out = {}
        for name, ((q0, q1), (k0, k1)) in zip(("bias_a", "bias_b"), col_blocks(self.rows, self.feat)):
            out[name] = VMEM(shape(q1 - q0, k1 - k0), F32)
        out["bias_row"] = VMEM((self.cells, self.cells), F32)
        return out

    def sites(self, r, site):
        if site == 1:
            return list(zip(col_blocks(self.rows, self.feat), (r.bias_a, r.bias_b)))
        return [(((0, self.cells), (0, self.cells)), r.bias_row)]

    def forward(self, kind, ctl, ctx, x, extra, gains, weights, saved):
        t, c, w, ff = self.tables, self.cells, self.width, self.ff
        splitting = weights is None
        ins = {"ctl": (ctl, SMEM), "ctx": (ctx, SMEM), "x": (x, ANY), "gains": (gains, VMEM)}
        if kind == "cells":
            ins |= {"mask": (extra.mask, VMEM), "embed": (extra.embed, VMEM)}
        names = ("win", "wout", "wup", "wdown")
        raw = extra.raw
        shapes = [(2, *a.shape) for a in raw]
        for n, a in zip(names, raw if splitting else weights):
            ins[n] = (a, ANY)
        outs = {"y": (f32(self.rows * self.feat, w), ANY)}
        if splitting:
            outs |= {n + "_out": (b16(*s), ANY) for n, s in zip(names, shapes)}
        if saved is None:
            saved = {
                "out": f32(t, self.rows * self.feat, w),
                "hs": f32(t, 3, c, w),
                "qkvs": b16(t, 2, 2, c, 3 * w),
                "os": b16(t, 2, 2, c, w),
                "zs": f32(t, c, ff),
            }
        scratch = {n + "_v": VMEM(s, BF16) for n, s in zip(names, shapes)}
        scratch |= {
            "h_v": VMEM((3, c, w), F32),
            "qkv_v": VMEM((2, 2, c, 3 * w), BF16),
            "o_v": VMEM((2, 2, c, w), BF16),
            "z_v": VMEM((c, ff), F32),
            "g_v": VMEM((2, c, ff), BF16),
            "a_v": VMEM((2, c, w), BF16),
            "y_v": VMEM((c, w), F32),
            "sem_in": dma(5),
            "sem_out": dma(14),
        } | self.bias_scratch(1)
        if splitting:
            scratch |= {n + "_raw": VMEM(a.shape, F32) for n, a in zip(names, raw)}

        def body(r):
            vs = [getattr(r, n + "_v") for n in names]
            kept = []
            if splitting:
                raws = [getattr(r, n + "_raw") for n in names]
                loads = [start(getattr(r, n), v, r.sem_in.at[1 + i]) for i, (n, v) in enumerate(zip(names, raws))]
                for i, n in enumerate(names):
                    loads[i].wait()
                    split_weights(raws[i], vs[i])
                    kept.append(start(vs[i], getattr(r, n + "_out"), r.sem_out.at[10 + i]))

            @pl.when(r.ctl[0] == 1)
            def _():
                if splitting:
                    waits = [lambda: None] * 4
                else:
                    waits = [start(getattr(r, n), v, r.sem_in.at[1 + i]).wait for i, (n, v) in enumerate(zip(names, vs))]
                self.forward_body(r, kind, waits)

            for copy in kept:
                copy.wait()

        res = call("layer_forward", body, ins, outs, saved, scratch)
        if splitting:
            weights = [getattr(res, n + "_out") for n in names]
        return res.y, weights, {k: getattr(res, k) for k in saved}

    def forward_body(self, r, kind, waits):
        rows, feat, c, w, ff, hd = self.rows, self.feat, self.cells, self.width, self.ff, self.hd
        table = r.ctl[1]
        stores = []

        def keep(src, dst):
            stores.append(start(src, dst, r.sem_out.at[len(stores)]))

        real = rows * feat
        x = r.x if kind == "flat" else r.x.at[table]
        load_x = start(x, r.h_v.at[0, 0:real], r.sem_in.at[0])
        attention_biases(rows, feat, r.ctx[table], (r.bias_a, r.bias_b), r.bias_row, 1)
        r.h_v[0, real:, :] = jnp.zeros((c - real, w), F32)
        load_x.wait()
        if kind != "flat":
            r.h_v[0] = jnp.where(r.mask[table] == 1.0, r.embed[...], r.h_v[0])
        keep(r.h_v.at[0], r.hs.at[table, 0])
        for site in range(2):
            put(r.a_v, (), normalized(r.h_v[site])[0] * r.gains[site : site + 1, :])
            if site == 0:
                waits[0]()

            @pl.loop(0, 3 * w // TILE)
            def _(j):
                at = lanes(j, TILE)
                out = wide(parts(r.a_v), parts(r.win_v, site, slice(None), at), 1, 0)
                put(r.qkv_v, (site, slice(None), at), out)

            keep(r.qkv_v.at[:, site], r.qkvs.at[table, :, site])

            @pl.loop(0, HEADS)
            def _(head):
                for ((q0, q1), (k0, k1)), bias in self.sites(r, site):
                    q = parts(r.qkv_v, site, slice(q0, q1), lanes(head, hd))
                    k = parts(r.qkv_v, site, slice(k0, k1), lanes(HEADS + head, hd))
                    v = parts(r.qkv_v, site, slice(k0, k1), lanes(2 * HEADS + head, hd))
                    s = wide(q, k, 1, 1) * self.scale + bias[...]
                    e = jnp.exp(s - jnp.max(s, axis=-1, keepdims=True))
                    p = e * (1.0 / jnp.sum(e, axis=-1, keepdims=True))
                    put(r.o_v, (site, slice(q0, q1), lanes(head, hd)), side(split(p), v))

            keep(r.o_v.at[:, site], r.os.at[table, :, site])
            if site == 0:
                waits[1]()
            r.h_v[site + 1] = r.h_v[site] + wide(parts(r.o_v, site), parts(r.wout_v, site), 1, 0)
            keep(r.h_v.at[site + 1], r.hs.at[table, site + 1])
        put(r.a_v, (), normalized(r.h_v[2])[0] * r.gains[2:3, :])
        waits[2]()

        @pl.loop(0, ff // TILE)
        def _(j):
            at = lanes(j, TILE)
            z = wide(parts(r.a_v), parts(r.wup_v, slice(None), at), 1, 0)
            r.z_v[:, at] = z
            put(r.g_v, (slice(None), at), z * phi_of(z))

        keep(r.z_v, r.zs.at[table])
        waits[3]()
        r.y_v[...] = r.h_v[2]

        @pl.loop(0, ff // TILE)
        def _(j):
            at = lanes(j, TILE)
            r.y_v[...] += wide(parts(r.g_v, slice(None), at), parts(r.wdown_v, at), 1, 0)

        keep(r.y_v.at[0:real], r.y)
        keep(r.y_v.at[0:real], r.out.at[table])
        for copy in stores:
            copy.wait()

    def mlp_back(self, ctl, cot, dy, gains, weights, saved, kept):
        t, c, w, ff = self.tables, self.cells, self.width, self.ff
        rows, feat = self.rows, self.feat
        ins = {"ctl": (ctl, SMEM), "gains": (gains, VMEM), "wup": (weights[2], ANY), "wdown": (weights[3], ANY)}
        ins |= {"hs": (saved["hs"], ANY), "zs": (saved["zs"], ANY), "dy": (dy, ANY)}
        if cot is not None:
            ins["cot"] = (cot, ANY)
        if kept is None:
            kept = {
                "dys": b16(t, 2, c, w),
                "gs": b16(t, 2, c, ff),
                "dzs": b16(t, 2, c, ff),
                "a2s": b16(t, 2, c, w),
            }
        outs = {"dw": (f32(c, w), ANY), "dgain": (f32(1, w), VMEM)}
        scratch = {
            "wup_v": VMEM(weights[2].shape, BF16),
            "wdown_v": VMEM(weights[3].shape, BF16),
            "w_v": VMEM((c, w), F32),
            "dy_v": VMEM((c, w), F32),
            "da_v": VMEM((c, w), F32),
            "z_v": VMEM((c, ff), F32),
            "dys_v": VMEM((2, c, w), BF16),
            "g_v": VMEM((2, c, ff), BF16),
            "dz_v": VMEM((2, c, ff), BF16),
            "a_v": VMEM((2, c, w), BF16),
            "sem_in": dma(5),
            "sem_out": dma(5),
        }

        def body(r):
            @pl.when(r.ctl[0] == 1)
            def _():
                table, real = r.ctl[1], rows * feat
                r.dy_v[real:, :] = jnp.zeros((c - real, w), F32)
                c_down = start(r.wdown, r.wdown_v, r.sem_in.at[1])
                c_z = start(r.zs.at[table], r.z_v, r.sem_in.at[2])
                c_up = start(r.wup, r.wup_v, r.sem_in.at[3])
                c_w = start(r.hs.at[table, 2], r.w_v, r.sem_in.at[4])
                if cot is not None:

                    @pl.when(r.ctl[2] == 0)
                    def _():
                        start(r.cot.at[table], r.dy_v.at[0:real], r.sem_in.at[0]).wait()

                @pl.when(r.ctl[2] == 1)
                def _():
                    start(r.dy, r.dy_v.at[0:real], r.sem_in.at[0]).wait()

                put(r.dys_v, (), r.dy_v[...])
                stores = [start(r.dys_v, r.dys.at[table], r.sem_out.at[0])]
                c_down.wait()
                c_z.wait()

                @pl.loop(0, ff // TILE)
                def _(j):
                    at = lanes(j, TILE)
                    dg = wide(parts(r.dys_v), parts(r.wdown_v, at), 1, 1)
                    z = r.z_v[:, at]
                    phi = phi_of(z)
                    put(r.g_v, (slice(None), at), z * phi)
                    put(r.dz_v, (slice(None), at), dg * (phi + z * (INV_SQRT2PI * jnp.exp(-0.5 * z * z))))

                stores.append(start(r.g_v, r.gs.at[table], r.sem_out.at[1]))
                stores.append(start(r.dz_v, r.dzs.at[table], r.sem_out.at[2]))
                c_up.wait()
                r.da_v[...] = jnp.zeros((c, w), F32)

                @pl.loop(0, ff // TILE)
                def _(j):
                    at = lanes(j, TILE)
                    r.da_v[...] += wide(parts(r.dz_v, slice(None), at), parts(r.wup_v, slice(None), at), 1, 1)

                c_w.wait()
                gain = r.gains[2:3, :]
                n, rstd = normalized(r.w_v[...])
                put(r.a_v, (), n * gain)
                stores.append(start(r.a_v, r.a2s.at[table], r.sem_out.at[3]))
                da = r.da_v[...]
                r.dgain[...] = jnp.sum(da * n, axis=0, keepdims=True)
                r.dy_v[...] += norm_back(n, rstd, gain, da)
                stores.append(start(r.dy_v, r.dw, r.sem_out.at[4]))
                for copy in stores:
                    copy.wait()

        res = call("mlp_backward", body, ins, outs, kept, scratch)
        return res.dw, res.dgain, {k: getattr(res, k) for k in kept}

    def attn_back(self, ctl, ctx, dw, mask, gains, weights, saved, kept):
        t, c, w = self.tables, self.cells, self.width
        rows, feat, hd = self.rows, self.feat, self.hd
        ins = {"ctl": (ctl, SMEM), "ctx": (ctx, SMEM), "dw": (dw, ANY), "mask": (mask, VMEM), "gains": (gains, VMEM)}
        ins |= {"win": (weights[0], ANY), "wout": (weights[1], ANY), "hs": (saved["hs"], ANY), "qkvs": (saved["qkvs"], ANY)}
        if kept is None:
            kept = {
                "din": f32(t, rows * feat, w),
                "as_": b16(t, 2, 2, c, w),
                "dqkvs": b16(t, 2, 2, c, 3 * w),
                "dhs": b16(t, 2, 2, c, w),
            }
        outs = {"dx": (f32(rows * feat, w), ANY), "small": (f32(3, w), VMEM)}
        scratch = {
            "win_v": VMEM(weights[0].shape, BF16),
            "wout_v": VMEM(weights[1].shape, BF16),
            "h_v": VMEM((2, c, w), F32),
            "dh_v": VMEM((c, w), F32),
            "da_v": VMEM((c, w), F32),
            "qkv_v": VMEM((2, 2, c, 3 * w), BF16),
            "dqkv_v": VMEM((2, 2, c, 3 * w), BF16),
            "dqkv_f": VMEM((c, 3 * w), F32),
            "do_v": VMEM((2, c, w), BF16),
            "dhs_v": VMEM((2, 2, c, w), BF16),
            "a_v": VMEM((2, 2, c, w), BF16),
            "sem_in": dma(5),
            "sem_out": dma(8),
        } | self.bias_scratch(0)

        def body(r):
            @pl.when(r.ctl[0] == 1)
            def _():
                table, real = r.ctl[1], rows * feat
                c_dw = start(r.dw, r.dh_v, r.sem_in.at[0])
                c_wout = start(r.wout, r.wout_v, r.sem_in.at[1])
                c_qkv = start(r.qkvs.at[table], r.qkv_v, r.sem_in.at[2])
                c_win = start(r.win, r.win_v, r.sem_in.at[3])
                c_h = start(r.hs.at[table, 0:2], r.h_v, r.sem_in.at[4])
                stores = []

                def keep(src, dst):
                    stores.append(start(src, dst, r.sem_out.at[len(stores)]))

                attention_biases(rows, feat, r.ctx[table], (r.bias_a, r.bias_b), r.bias_row, 0)
                c_dw.wait()
                for site in (1, 0):
                    put(r.dhs_v, (site,), r.dh_v[...])
                    keep(r.dhs_v.at[:, site], r.dhs.at[table, :, site])
                    if site == 1:
                        c_wout.wait()
                    put(r.do_v, (), wide(parts(r.dhs_v, site), parts(r.wout_v, site), 1, 1))
                    if site == 1:
                        c_qkv.wait()

                    @pl.loop(0, HEADS)
                    def _(head):
                        done = 0
                        at_q, at_k, at_v = lanes(head, hd), lanes(HEADS + head, hd), lanes(2 * HEADS + head, hd)
                        for ((q0, q1), (k0, k1)), bias in self.sites(r, site):
                            q = parts(r.qkv_v, site, slice(q0, q1), at_q)
                            k = parts(r.qkv_v, site, slice(k0, k1), at_k)
                            v = parts(r.qkv_v, site, slice(k0, k1), at_v)
                            do = parts(r.do_v, slice(q0, q1), at_q)
                            s = wide(k, q, 1, 1) * self.scale + bias[...]
                            e = jnp.exp(s - jnp.max(s, axis=0, keepdims=True))
                            p = e * (1.0 / jnp.sum(e, axis=0, keepdims=True))
                            dp = wide(v, do, 1, 1)
                            ds = split(p * (dp - jnp.sum(p * dp, axis=0, keepdims=True)) * self.scale)
                            r.dqkv_f[q0:q1, at_q] = wide(tuple(x.T for x in k), ds, 1, 0).T
                            for at, term in ((at_k, side(ds, q)), (at_v, side(split(p), do))):
                                if done > k0:
                                    r.dqkv_f[k0:done, at] += term[: done - k0]
                                    r.dqkv_f[done:k1, at] = term[done - k0 :]
                                else:
                                    r.dqkv_f[k0:k1, at] = term
                            done = k1

                    if site == 1:
                        c_win.wait()
                    r.da_v[...] = jnp.zeros((c, w), F32)

                    @pl.loop(0, 3 * w // TILE)
                    def _(j):
                        at = lanes(j, TILE)
                        d = split(r.dqkv_f[:, at])
                        r.dqkv_v[0, site, :, at] = d[0]
                        r.dqkv_v[1, site, :, at] = d[1]
                        r.da_v[...] += wide(d, parts(r.win_v, site, slice(None), at), 1, 1)

                    keep(r.dqkv_v.at[:, site], r.dqkvs.at[table, :, site])
                    if site == 1:
                        c_h.wait()
                    gain = r.gains[site : site + 1, :]
                    n, rstd = normalized(r.h_v[site])
                    put(r.a_v, (site,), n * gain)
                    keep(r.a_v.at[:, site], r.as_.at[table, :, site])
                    da = r.da_v[...]
                    r.small[site : site + 1, :] = jnp.sum(da * n, axis=0, keepdims=True)
                    r.dh_v[...] += norm_back(n, rstd, gain, da)
                keep(r.dh_v.at[0:real], r.dx)
                missing = r.mask[table] == 1.0
                r.small[2:3, :] = jnp.sum(jnp.where(missing, r.dh_v[...], 0.0), axis=0, keepdims=True)
                r.da_v[...] = jnp.where(missing, 0.0, r.dh_v[...])
                keep(r.da_v.at[0:real], r.din.at[table])
                for copy in stores:
                    copy.wait()

        res = call("attention_backward", body, ins, outs, kept, scratch)
        return res.dx, res.small, {k: getattr(res, k) for k in kept}


def split_weights(raw, v):
    step = 64
    lead = raw.shape[:-2]
    for at in [(s,) for s in range(lead[0])] if lead else [()]:

        @pl.loop(0, raw.shape[-2] // step)
        def _(j):
            block = pl.ds(pl.multiple_of(j * step, step), step)
            put(v, (*at, block), raw[(*at, block)])


class GradSum:
    BLOCK = 256
    SLACK = 2
    RING = 8

    def __init__(self, count, tables, cells, width, ff):
        self.count, self.tables, self.cells, self.width = count, tables, cells, width
        self.rest = count // 4
        shapes = [("gs", "dys", None, "down", ff, width), ("a2s", "dzs", None, "up", width, ff)]
        for site in (1, 0):
            shapes.append(("as_", "dqkvs", site, "win", width, 3 * width))
            shapes.append(("os", "dhs", site, "wout", width, width))
        self.groups, at = [], 0
        for left, right, site, out, k, n in shapes:
            blocks = (k // self.BLOCK) * (n // TILE)
            self.groups.append((at, at + blocks, left, right, site, out, n // TILE))
            at += blocks
        self.blocks = at
        self.per_chunk = max(1, 4 * self.rest * 8 // self.BLOCK)
        self.chunks = self.blocks // self.per_chunk
        self.rows = self.per_chunk * self.BLOCK

    def select(self, q, action):
        for group in self.groups:
            first, stop, *_, across = group

            @pl.when((q >= first) & (q < stop))
            def _():
                action(group, (q - first) // across, (q - first) % across)

    def load(self, r, q):
        slot = q % 2

        def action(group, i, j):
            _, _, left, right, site, _, _ = group
            mid = () if site is None else (site,)
            a, b = getattr(r, left), getattr(r, right)
            for t in range(self.tables):
                for part in range(2):
                    sem = 2 * t + part
                    at = (t, part, *mid, slice(None))
                    start(a.at[(*at, lanes(i, self.BLOCK))], r.a_v.at[slot, t, part], r.a_sem.at[slot, sem])
                    start(b.at[(*at, lanes(j, TILE))], r.b_v.at[slot, t, part], r.b_sem.at[slot, sem])

        self.select(q, action)

    def wait_load(self, r, slot):
        for t in range(self.tables):
            for part in range(2):
                sem = 2 * t + part
                a, b = r.a_v.at[slot, t, part], r.b_v.at[slot, t, part]
                pltpu.make_async_copy(a, a, r.a_sem.at[slot, sem]).wait()
                pltpu.make_async_copy(b, b, r.b_sem.at[slot, sem]).wait()

    def product(self, r, q):
        slot = q % 2
        self.wait_load(r, slot)

        @pl.when(q + 1 < self.blocks)
        def _():
            self.load(r, q + 1)

        left, right = [], []
        for t in range(self.tables):
            (ah, al), (bh, bl) = parts(r.a_v.at[slot, t]), parts(r.b_v.at[slot, t])
            left += [ah, ah, al]
            right += [bh, bl, bh]
        rows = pl.ds(pl.multiple_of(q % self.per_chunk * self.BLOCK, self.BLOCK), self.BLOCK)
        r.sums[q // self.per_chunk % self.RING, rows] = dot(jnp.concatenate(left, 0), jnp.concatenate(right, 0), ((0,), (0,)))

    def store(self, r, q):
        def action(group, i, j):
            _, _, _, _, site, out, _ = group
            dst = getattr(r, out)
            rows = pl.ds(pl.multiple_of(i * self.BLOCK, self.BLOCK), self.BLOCK)
            dst = dst.at[rows, lanes(j, TILE)] if site is None else dst.at[site, rows, lanes(j, TILE)]
            u = q % self.per_chunk
            at = pl.ds(pl.multiple_of(u * self.BLOCK, self.BLOCK), self.BLOCK)
            start(r.full.at[q // self.per_chunk, at], dst, r.store_sem.at[q // self.per_chunk % 2, u])

        self.select(q, action)

    def wait_store(self, r, c):
        for u in range(self.per_chunk):
            block = r.full.at[c, u * self.BLOCK : (u + 1) * self.BLOCK]
            pltpu.make_async_copy(block, block, r.store_sem.at[c % 2, u]).wait()

    def kernel(self, r):
        count, rest, rows = self.count, self.rest, self.rows
        half, quarter, piece = rows // 2, rows // 4, rows // 4 // rest
        me, section = lax.axis_index("dp"), lax.axis_index("section")
        core, pair, place = me % 2, me // 2 % 2, me // 4
        sibling, neighbour = me + 1 - 2 * core, me + 2 - 4 * pair

        def peer(j):
            return lax.rem(place + j, rest) * 4 + me % 4

        def span(at, size):
            return pl.ds(pl.multiple_of(at, size), size)

        mine = core * half
        own = mine + pair * quarter
        other = mine + (1 - pair) * quarter

        def remote(src, dst, send, recv, device):
            return pltpu.make_async_remote_copy(
                src_ref=src, dst_ref=dst, send_sem=send, recv_sem=recv, device_id=device, device_id_type=pl.DeviceIdType.MESH
            )

        barrier = pltpu.get_barrier_semaphore()
        pl.semaphore_signal(barrier, inc=1, device_id={"section": 1 - section}, device_id_type=pl.DeviceIdType.MESH)
        for device in (sibling, neighbour):
            pl.semaphore_signal(barrier, inc=1, device_id={"dp": device}, device_id_type=pl.DeviceIdType.MESH)

        @pl.loop(1, rest)
        def _(j):
            pl.semaphore_signal(barrier, inc=1, device_id={"dp": peer(j)}, device_id_type=pl.DeviceIdType.MESH)

        self.load(r, 0)
        pl.semaphore_wait(barrier, rest + 2)

        def halve(c):
            src = r.sums.at[c % self.RING, span((1 - core) * half, half)]
            return remote(src, r.got_half.at[c], r.send.at[0, c % self.RING], r.recv.at[0, c], {"dp": sibling})

        def quarter_copy(c):
            src = r.sums.at[c % self.RING, span(other, quarter)]
            return remote(src, r.got_quarter.at[c], r.send.at[1, c % self.RING], r.recv.at[1, c], {"dp": neighbour})

        def scatter(c, j):
            src = r.sums.at[c % self.RING, span(own + lax.rem(place + j, rest) * piece, piece)]
            dst = r.got_piece.at[c, j - 1]
            return remote(src, dst, r.send_rest.at[0, c % self.RING, j - 1], r.recv_rest.at[0, c, j - 1], {"dp": peer(j)})

        def gather(c, j):
            at = r.full.at[c, span(own + place * piece, piece)]
            return remote(at, at, r.send_rest.at[1, c % self.RING, j - 1], r.recv_rest.at[1, c, j - 1], {"dp": peer(j)})

        def gather_quarter(c):
            at = r.full.at[c, span(own, quarter)]
            return remote(at, at, r.send.at[2, c % self.RING], r.recv.at[2, c], {"dp": neighbour})

        def gather_half(c):
            at = r.full.at[c, span(mine, half)]
            return remote(at, at, r.send.at[3, c % self.RING], r.recv.at[3, c], {"dp": sibling})

        def each(action):
            pl.loop(1, rest)(action)

        def after_halve(c):
            halve(c).wait()
            r.sums[c % self.RING, span(mine, half)] += r.got_half[c]
            quarter_copy(c).start()

        def after_quarter(c):
            quarter_copy(c).wait()
            r.sums[c % self.RING, span(own, quarter)] += r.got_quarter[c]
            each(lambda j: scatter(c, j).start())

        def after_scatter(c):
            each(lambda j: scatter(c, j).wait())
            total = r.sums[c % self.RING, span(own + place * piece, piece)]
            for j in range(rest - 1):
                total += r.got_piece[c, j]
            r.full[c, span(own + place * piece, piece)] = total
            each(lambda j: gather(c, j).start())

        def after_gather(c):
            each(lambda j: gather(c, j).wait())
            gather_quarter(c).start()

        def after_gather_quarter(c):
            gather_quarter(c).wait()
            gather_half(c).start()

        def after_gather_half(c):
            gather_half(c).wait()

            @pl.when(c >= 2)
            def _():
                self.wait_store(r, c - 2)

            @pl.loop(0, self.per_chunk)
            def _(u):
                self.store(r, c * self.per_chunk + u)

        stages = [after_halve, after_quarter, after_scatter, after_gather, after_gather_quarter, after_gather_half]

        def small_copy(k, device):
            return remote(r.small_v.at[k], r.got_small.at[k], r.small_send.at[k], r.small_recv.at[k], device)

        def small_rest(j):
            dst = r.got_small.at[2 + j]
            return remote(r.small_v.at[3], dst, r.small_send.at[2 + j], r.small_recv.at[2 + j], {"dp": peer(j)})

        def small_step(step):
            @pl.when(step == 0)
            def _():
                r.small_v[0] = r.small[...]
                small_copy(0, {"section": 1 - section}).start()

            @pl.when(step == 2)
            def _():
                small_copy(0, {"section": 1 - section}).wait()
                row = lax.broadcasted_iota(jnp.int32, (8, self.width), 0)
                r.small_v[1] = r.small_v[0] + jnp.where(row == 3, r.got_small[0], 0.0)
                small_copy(1, {"dp": sibling}).start()

            @pl.when(step == 4)
            def _():
                small_copy(1, {"dp": sibling}).wait()
                r.small_v[2] = r.small_v[1] + r.got_small[1]
                small_copy(2, {"dp": neighbour}).start()

            @pl.when(step == 6)
            def _():
                small_copy(2, {"dp": neighbour}).wait()
                r.small_v[3] = r.small_v[2] + r.got_small[2]
                each(lambda j: small_rest(j).start())

            @pl.when(step == 8)
            def _():
                each(lambda j: small_rest(j).wait())
                total = r.small_v[3]
                for j in range(1, rest):
                    total += r.got_small[2 + j]
                r.small_out[...] = total

        @pl.loop(0, self.chunks + self.SLACK * len(stages))
        def _(step):
            for k in reversed(range(len(stages))):
                c = step - self.SLACK * (k + 1)

                @pl.when((c >= 0) & (c < self.chunks))
                def _():
                    stages[k](c)

            small_step(step)

            @pl.when(step < self.chunks)
            def _():
                @pl.loop(0, self.per_chunk)
                def _(u):
                    self.product(r, step * self.per_chunk + u)

                halve(step).start()

        for c in range(max(0, self.chunks - 2), self.chunks):
            self.wait_store(r, c)

    def __call__(self, operands, small):
        t, cells, width = self.tables, self.cells, self.width
        names = list(operands)
        rest, chunks, rows = self.rest, self.chunks, self.rows
        piece = rows // 4 // rest
        ff = operands["gs"].shape[-1]
        outs = {
            "win": f32(2, width, 3 * width),
            "wout": f32(2, width, width),
            "up": f32(width, ff),
            "down": f32(ff, width),
            "small_out": f32(8, width),
        }
        scratch = {
            "sums": VMEM((self.RING, rows, TILE), F32),
            "full": VMEM((chunks, rows, TILE), F32),
            "got_half": VMEM((chunks, rows // 2, TILE), F32),
            "got_quarter": VMEM((chunks, rows // 4, TILE), F32),
            "got_piece": VMEM((chunks, rest - 1, piece, TILE), F32),
            "a_v": VMEM((2, t, 2, cells, self.BLOCK), BF16),
            "b_v": VMEM((2, t, 2, cells, TILE), BF16),
            "small_v": VMEM((4, 8, width), F32),
            "got_small": VMEM((2 + rest, 8, width), F32),
            "a_sem": pltpu.SemaphoreType.DMA((2, 2 * t)),
            "b_sem": pltpu.SemaphoreType.DMA((2, 2 * t)),
            "store_sem": pltpu.SemaphoreType.DMA((2, self.per_chunk)),
            "send": pltpu.SemaphoreType.DMA((4, self.RING)),
            "recv": pltpu.SemaphoreType.DMA((4, chunks)),
            "send_rest": pltpu.SemaphoreType.DMA((2, self.RING, rest - 1)),
            "recv_rest": pltpu.SemaphoreType.DMA((2, chunks, rest - 1)),
            "small_send": pltpu.SemaphoreType.DMA((2 + rest,)),
            "small_recv": pltpu.SemaphoreType.DMA((2 + rest,)),
        }
        refs = [*names, "small", *outs, *scratch]

        def body(*args):
            self.kernel(SimpleNamespace(**dict(zip(refs, args))))

        results = pl.pallas_call(
            body,
            out_shape=list(outs.values()),
            in_specs=[pl.BlockSpec(memory_space=ANY)] * len(names) + [pl.BlockSpec(memory_space=VMEM)],
            out_specs=[pl.BlockSpec(memory_space=ANY)] * 4 + [pl.BlockSpec(memory_space=VMEM)],
            scratch_shapes=list(scratch.values()),
            compiler_params=pltpu.CompilerParams(vmem_limit_bytes=VMEM_LIMIT, collective_id=0, has_side_effects=True),
            name="weight_gradient_sum",
        )(*operands.values(), small)
        return SimpleNamespace(**dict(zip(outs, results)))


def local(
    cells,
    missing_mask,
    missing_embed,
    context_rows,
    norm_gains,
    attn_in,
    attn_out,
    mlp_up,
    mlp_down,
    cotangent,
):
    section = lax.axis_index("section")
    tables, rows, feat, width = cells.shape
    layer = Layer(tables, rows, feat, width, mlp_up.shape[2])
    gains = norm_gains[0]
    is_first = section == 0

    def flat(tables_of_cells):
        return jnp.swapaxes(tables_of_cells, 1, 2).reshape(tables, rows * feat, -1)

    def unflat(cells_of_tables):
        return jnp.swapaxes(cells_of_tables.reshape(tables, feat, rows, width), 1, 2)

    cells, cotangent = flat(cells), flat(cotangent)
    flat_mask = flat(missing_mask == 1)
    flat_mask = jnp.pad(flat_mask, ((0, 0), (0, layer.cells - rows * feat), (0, 0)))
    mask = flat_mask.astype(F32)
    mask_here = jnp.where(is_first, mask, 0.0)

    def ctl(at_first, at_last):
        return jnp.where(is_first, jnp.array(at_first, jnp.int32), jnp.array(at_last, jnp.int32))

    idle = (0, 0, 0)
    fwd_pairs, bwd_pairs = [(0, 1)], [(1, 0)]
    extra = SimpleNamespace(mask=mask, embed=missing_embed[None], raw=(attn_in[0], attn_out[0], mlp_up[0], mlp_down[0]))

    def forward(kind, control, x, weights, saved):
        return layer.forward(kind, control, context_rows, x, extra, gains, weights, saved)

    def mlp_back(control, cot, dy, kept):
        return layer.mlp_back(control, cot, dy, gains, weights, saved, kept)

    def attn_back(control, dw, kept):
        return layer.attn_back(control, context_rows, dw, mask_here, gains, weights, saved, kept)

    y0, weights, saved = forward("cells", ctl((1, 0, 0), idle), cells, None, None)
    r0 = lax.ppermute(y0, "section", fwd_pairs)
    y1, _, saved = forward("cells", ctl((1, 1, 0), idle), cells, weights, saved)
    r1 = lax.ppermute(y1, "section", fwd_pairs)
    _, _, saved = forward("flat", ctl(idle, (1, 0, 0)), r0, weights, saved)
    dw0, dg0, kept_m = mlp_back(ctl(idle, (1, 0, 0)), cotangent, r0, None)
    d0, small0, kept_a = attn_back(ctl(idle, (1, 0, 0)), dw0, None)
    e0 = lax.ppermute(d0, "section", bwd_pairs)
    _, _, saved = forward("flat", ctl(idle, (1, 1, 0)), r1, weights, saved)
    dw1, dg1, kept_m = mlp_back(ctl((1, 0, 1), (1, 1, 0)), cotangent, e0, kept_m)
    d1, small1, kept_a = attn_back(ctl((1, 0, 0), (1, 1, 0)), dw1, kept_a)
    e1 = lax.ppermute(d1, "section", bwd_pairs)
    dw2, dg2, kept_m = mlp_back(ctl((1, 1, 1), idle), None, e1, kept_m)
    _, small2, kept_a = attn_back(ctl((1, 1, 0), idle), dw2, kept_a)
    def row(first_a, first_b, last_a, last_b):
        return jnp.where(is_first, first_a + first_b, last_a + last_b)

    d_small = jnp.concatenate(
        [
            row(small1[0:2], small2[0:2], small0[0:2], small1[0:2]),
            row(dg1, dg2, dg0, dg1),
            jnp.where(is_first, small1[2:3] + small2[2:3], 0.0),
            jnp.zeros((4, width), F32),
        ],
        0,
    )
    operands = kept_m | kept_a | {"os": saved["os"]}
    input_grads = operands.pop("din")
    sums = GradSum(lax.axis_size("dp"), tables, layer.cells, width, mlp_up.shape[2])(operands, d_small)
    return (
        unflat(saved["out"])[None],
        unflat(input_grads)[None],
        sums.small_out[0:3][None],
        sums.win[None],
        sums.wout[None],
        sums.up[None],
        sums.down[None],
        sums.small_out[3],
    )


def solution(mesh):
    in_specs = (
        P("dp", None, None, None),
        P("dp", None, None),
        P(),
        P("dp"),
        P("section", None, None),
        P("section", None, None, None),
        P("section", None, None, None),
        P("section", None, None),
        P("section", None, None),
        P("dp", None, None, None),
    )
    out_specs = (
        P("section", "dp", None, None, None),
        P("section", "dp", None, None, None),
        P("section", None, None),
        P("section", None, None, None),
        P("section", None, None, None),
        P("section", None, None),
        P("section", None, None),
        P(),
    )
    return jax.shard_map(local, mesh=mesh, in_specs=in_specs, out_specs=out_specs, check_vma=False)
```

```python
import functools
from types import SimpleNamespace

import jax
import jax.numpy as jnp
from jax import lax
from jax.experimental import pallas as pl
from jax.experimental.pallas import tpu as pltpu
from jax.sharding import PartitionSpec as P

HEADS = 4
EPSILON = 1e-05
NEG = -1e30
INV_SQRT2PI = 0.3989422804014327
ERFC_P = 0.33
ERFC_C = (0.1863578482, 0.1829552331, 0.2012284886, 0.0472047191, 0.4085317677, -0.3511862269, 0.4602596132, -0.1353514118)
VMEM_LIMIT = 62 * 1024 * 1024
TILE = 512
F32, BF16 = jnp.float32, jnp.bfloat16


def dot(a, b, contract=((1,), (0,))):
    return lax.dot_general(a, b, (contract, ((), ())), preferred_element_type=F32)


def split(v):
    hi = v.astype(BF16)
    return hi, (v - hi.astype(F32)).astype(BF16)


def put(ref, index, v):
    hi, lo = split(v)
    ref[(0, *index)] = hi
    ref[(1, *index)] = lo


def parts(ref, *index):
    return ref[(0, *index)], ref[(1, *index)]


def wide(a, b, ca, cb):
    (ah, al), (bh, bl) = a, b
    return dot(jnp.concatenate([ah, ah, al], ca), jnp.concatenate([bh, bl, bh], cb), ((ca,), (cb,)))


def side(a, b):
    (ah, al), (bh, bl) = a, b
    width = bh.shape[1]
    both = dot(ah, jnp.concatenate([bh, bl], 1))
    return both[:, :width] + both[:, width:] + dot(al, bh)


def normalized(h):
    centred = h - jnp.mean(h, axis=-1, keepdims=True)
    rstd = lax.rsqrt(jnp.mean(centred * centred, axis=-1, keepdims=True) + EPSILON)
    return centred * rstd, rstd


def norm_back(n, rstd, gain, da):
    dn = da * gain
    return rstd * (dn - jnp.mean(dn, axis=-1, keepdims=True) - n * jnp.mean(dn * n, axis=-1, keepdims=True))


def cell_ids(start, count, rows, along):
    shape = (count, 1) if along == 0 else (1, count)
    at = lax.broadcasted_iota(jnp.int32, shape, along) + start
    feat = lax.shift_right_logical(at * ((1 << 20) // rows + 1), 20)
    return at - feat * rows, feat


def up16(n):
    return (n + 15) // 16 * 16


def col_blocks(rows, feat):
    cells = up16(rows * feat)
    half = up16((feat + 1) // 2 * rows)
    first_keys = min(cells, up16((((half - 1) // rows) + 1) * rows))
    second_keys = ((half // rows) * rows) // 16 * 16
    return (((0, half), (0, first_keys)), ((half, cells), (second_keys, cells)))


def lanes(j, width):
    return pl.ds(pl.multiple_of(j * width, width), width)


def start(src, dst, sem):
    copy = pltpu.make_async_copy(src, dst, sem)
    copy.start()
    return copy


def col_biases(rows, feat, context, refs, keys_along):
    for ((q0, q1), (k0, k1)), ref in zip(col_blocks(rows, feat), refs):
        _, q_feat = cell_ids(q0, q1 - q0, rows, 1 - keys_along)
        k_row, k_feat = cell_ids(k0, k1 - k0, rows, keys_along)
        ref[...] = jnp.where((q_feat == k_feat) & (k_row < context), 0.0, NEG)


def row_bias(rows, feat, ref):
    cells = up16(rows * feat)
    q_row, q_feat = cell_ids(0, cells, rows, 0)
    k_row, k_feat = cell_ids(0, cells, rows, 1)
    ref[...] = jnp.where((q_row == k_row) & ((q_feat < feat) == (k_feat < feat)), 0.0, NEG)


def gelu_parts(z):
    size = jnp.abs(z)
    below = 1.0 + (ERFC_P * 0.7071067811865476) * size
    t = pl.reciprocal(below, approx=True)
    t = t * (2.0 - below * t)
    series = jnp.full_like(t, ERFC_C[-1])
    for c in ERFC_C[-2::-1]:
        series = series * t + c
    bell = jnp.exp(-0.5 * z * z)
    tail = 0.5 * (series * t) * bell
    phi = jnp.where(z >= 0.0, 1.0 - tail, tail)
    return z * phi, phi + z * (INV_SQRT2PI * bell)


SMEM, VMEM, ANY = pltpu.SMEM, pltpu.VMEM, pl.ANY


def f32(*shape):
    return jax.ShapeDtypeStruct(shape, F32)


def b16(*shape):
    return jax.ShapeDtypeStruct(shape, BF16)


def remote(src, dst, send, recv, device):
    return pltpu.make_async_remote_copy(
        src_ref=src, dst_ref=dst, send_sem=send, recv_sem=recv, device_id=device, device_id_type=pl.DeviceIdType.MESH
    )


def call(name, body, collective_id, ins, outs, scratch):
    names = [*ins, *outs, *scratch]

    def kernel(*refs):
        body(SimpleNamespace(**dict(zip(names, refs))))

    results = pl.pallas_call(
        kernel,
        out_shape=[t for t, _ in outs.values()],
        in_specs=[pl.BlockSpec(memory_space=s) for _, s in ins.values()],
        out_specs=[pl.BlockSpec(memory_space=s) for _, s in outs.values()],
        scratch_shapes=list(scratch.values()),
        compiler_params=pltpu.CompilerParams(
            vmem_limit_bytes=VMEM_LIMIT, collective_id=collective_id, has_side_effects=True
        ),
        name=name,
    )(*(a for a, _ in ins.values()))
    return dict(zip(outs, results))


class Layers:
    def __init__(self, tables, rows, feat, width, ff):
        self.tables, self.rows, self.feat, self.width, self.ff = tables, rows, feat, width, ff
        self.real, self.cells = rows * feat, up16(rows * feat)
        self.hd = width // HEADS
        self.scale = self.hd ** (-0.5)

    def sites(self, r, site):
        if site == 1:
            return list(zip(col_blocks(self.rows, self.feat), (r.bias_a, r.bias_b)))
        return [(((0, self.cells), (0, self.cells)), r.bias_row)]

    def __call__(self, cells, mask, embed, context, gains, weights, cotangent):
        t, c, w, ff, real = self.tables, self.cells, self.width, self.ff, self.real
        ins = {
            "cells": (cells, ANY),
            "mask": (mask, VMEM),
            "embed": (embed, VMEM),
            "ctx": (context, SMEM),
            "gains": (gains, VMEM),
            "cot": (cotangent, ANY),
        }
        names = ("win", "wout", "wup", "wdown")
        ins |= {n: (a, ANY) for n, a in zip(names, weights)}
        outs = {
            "out": f32(t, real, w),
            "din": f32(t, real, w),
            "hs": f32(t, 3, c, w),
            "qkvs": b16(t, 2, 2, c, 3 * w),
            "gps": f32(t, c, ff),
            "as_": b16(t, 2, 3, c, w),
            "os": b16(t, 2, 2, c, w),
            "gs": b16(t, 2, c, ff),
            "dys": b16(t, 2, c, w),
            "dzs": b16(t, 2, c, ff),
            "dhs": b16(t, 2, 2, c, w),
            "dqkvs": b16(t, 2, 2, c, 3 * w),
        }
        outs = {n: (s, ANY) for n, s in outs.items()} | {"small": (f32(8, w), VMEM)}
        scratch = {n + "_v": VMEM((2, *a.shape), BF16) for n, a in zip(names, weights)}
        scratch |= {
            "h_v": VMEM((3, c, w), F32),
            "qkv_v": VMEM((2, 2, c, 3 * w), BF16),
            "o_v": VMEM((2, 2, c, w), BF16),
            "gp_v": VMEM((c, ff), F32),
            "g_v": VMEM((2, c, ff), BF16),
            "a_v": VMEM((2, 3, c, w), BF16),
            "y_v": VMEM((t, c, w), F32),
            "dqkv_f": VMEM((c, 3 * w), F32),
            "dys_v": VMEM((2, c, w), BF16),
            "dy_v": VMEM((c, w), F32),
            "do_v": VMEM((2, c, w), BF16),
            "got": VMEM((t, real, w), F32),
            "bias_row": VMEM((c, c), F32),
            "raw_sem": pltpu.SemaphoreType.DMA((16,)),
            "in_sem": pltpu.SemaphoreType.DMA((4,)),
            "out_sem": pltpu.SemaphoreType.DMA((16,)),
            "send": pltpu.SemaphoreType.DMA((t, 2)),
            "recv": pltpu.SemaphoreType.DMA((t, 2)),
        }
        for name, ((q0, q1), (k0, k1)) in zip(("bias_a", "bias_b"), col_blocks(self.rows, self.feat)):
            assert (q0, q1) == (k0, k1)
            scratch[name] = VMEM((q1 - q0, q1 - q0), F32)
        return call("layers", self.kernel, 1, ins, outs, scratch)

    def split_weights(self, r):
        w, ff = self.width, self.ff
        half, wide_in = w // 2, 3 * w
        top, step = slice(0, half), 64
        rest = slice(half, w)
        pieces = []
        big, bigger = r.dqkv_f.at[top], r.gp_v.at[top]
        pieces.append((r.win.at[0, top], big, r.win_v, (0,), 0, slice(None)))
        pieces.append((r.win.at[0, rest], bigger.at[:, 0:wide_in], r.win_v, (0,), half, slice(None)))
        pieces.append((r.wout.at[0, top], r.h_v.at[0, top], r.wout_v, (0,), 0, slice(None)))
        pieces.append((r.wout.at[0, rest], r.h_v.at[1, top], r.wout_v, (0,), half, slice(None)))
        pieces.append((r.wout.at[1, top], r.h_v.at[2, top], r.wout_v, (1,), 0, slice(None)))
        pieces.append((r.wout.at[1, rest], r.y_v.at[0, top], r.wout_v, (1,), half, slice(None)))
        pieces.append((r.win.at[1, top], big, r.win_v, (1,), 0, slice(None)))
        pieces.append((r.win.at[1, rest], bigger.at[:, 0:wide_in], r.win_v, (1,), half, slice(None)))
        pieces.append((r.wup.at[rest, wide_in:ff], r.dy_v.at[top, 0 : ff - wide_in], r.wup_v, (), half, slice(wide_in, ff)))
        pieces.append((r.wup.at[top], bigger, r.wup_v, (), 0, slice(None)))
        pieces.append((r.wup.at[rest, 0:wide_in], big, r.wup_v, (), half, slice(0, wide_in)))
        rows = self.cells // step * step
        buffers = [r.h_v.at[0], r.h_v.at[1], r.h_v.at[2], r.y_v.at[0], r.y_v.at[1]]
        for i, at in enumerate(range(0, ff, rows)):
            size = min(rows, ff - at)
            pieces.append((r.wdown.at[at : at + size], buffers[i].at[0:size], r.wdown_v, (), at, slice(None)))
        users = [0, 1, 2, 3, 4, 5, 0, 1, 6, 1, 0, 2, 3, 4, 5, 7][: len(pieces)]
        copies = [pltpu.make_async_copy(p[0], p[1], r.raw_sem.at[i]) for i, p in enumerate(pieces)]
        first = {u: i for i, u in reversed(list(enumerate(users)))}
        for i in sorted(first.values()):
            copies[i].start()
        for i, (_, buffer, v, lead, at, columns) in enumerate(pieces):
            copies[i].wait()

            @pl.loop(0, buffer.shape[0] // step)
            def _(j):
                src = pl.ds(pl.multiple_of(j * step, step), step)
                dst = pl.ds(pl.multiple_of(at + j * step, step), step)
                put(v, (*lead, dst, columns), buffer[src])

            later = [k for k in range(i + 1, len(pieces)) if users[k] == users[i]]
            if later:
                copies[later[0]].start()

    def kernel(self, r):
        t, real, c = self.tables, self.real, self.cells
        section = lax.axis_index("section")
        other = {"section": 1 - section}
        barrier = pltpu.get_barrier_semaphore()
        pl.semaphore_signal(barrier, inc=1, device_id=other, device_id_type=pl.DeviceIdType.MESH)
        self.split_weights(r)
        row_bias(self.rows, self.feat, r.bias_row)
        r.small[...] = jnp.zeros_like(r.small)
        pl.semaphore_wait(barrier, 1)

        def relay(table, half):
            at = slice(half * self.width // 2, (half + 1) * self.width // 2)
            src, dst = r.y_v.at[table, 0:real, at], r.got.at[table, :, at]
            return remote(src, dst, r.send.at[table, half], r.recv.at[table, half], other)

        @pl.loop(0, 2 * t)
        def _(step):
            forward = (1 - section) * (1 - step // t) + section * (1 - step % 2)
            table = (1 - section) * (step % t) + section * (step // 2)

            @pl.when(forward == 1)
            def _():
                self.forward(r, table, section, relay)

            @pl.when(forward == 0)
            def _():
                self.backward(r, table, section, relay)

        @pl.when(section == 1)
        def _():
            for table in range(t):
                for half in range(2):
                    relay(table, half).wait_send()

    def forward(self, r, table, section, relay):
        c, w, ff, hd, real = self.cells, self.width, self.ff, self.hd, self.real
        stores = []

        def keep(src, dst):
            stores.append(start(src, dst, r.out_sem.at[len(stores)]))

        r.h_v[0, real:, :] = jnp.zeros((c - real, w), F32)
        col_biases(self.rows, self.feat, r.ctx[table], (r.bias_a, r.bias_b), 1)

        @pl.when(section == 0)
        def _():
            start(r.cells.at[table], r.h_v.at[0, 0:real], r.in_sem.at[0]).wait()
            r.h_v[0] = jnp.where(r.mask[table] == 1.0, r.embed[...], r.h_v[0])

        @pl.when(section == 1)
        def _():
            start(r.cot.at[table], r.dy_v.at[0:real], r.in_sem.at[1])
            for half in range(2):
                relay(table, half).wait_recv()
            r.h_v[0, 0:real] = r.got[table]

        keep(r.h_v.at[0], r.hs.at[table, 0])
        for site in range(2):
            put(r.a_v, (site,), normalized(r.h_v[site])[0] * r.gains[site : site + 1, :])
            keep(r.a_v.at[:, site], r.as_.at[table, :, site])
            for j in range(3 * w // TILE):
                at = slice(j * TILE, (j + 1) * TILE)
                out = wide(parts(r.a_v, site), parts(r.win_v, site, slice(None), at), 1, 0)
                put(r.qkv_v, (site, slice(None), at), out)
            keep(r.qkv_v.at[:, site], r.qkvs.at[table, :, site])

            @pl.loop(0, HEADS // 2)
            def _(two):
                for head in (2 * two, 2 * two + 1):
                    for ((q0, q1), (k0, k1)), bias in self.sites(r, site):
                        q = parts(r.qkv_v, site, slice(q0, q1), lanes(head, hd))
                        k = parts(r.qkv_v, site, slice(k0, k1), lanes(HEADS + head, hd))
                        v = parts(r.qkv_v, site, slice(k0, k1), lanes(2 * HEADS + head, hd))
                        s = wide(q, k, 1, 1) * self.scale + bias[...]
                        e = jnp.exp(s - jnp.max(s, axis=-1, keepdims=True))
                        p = e * (1.0 / jnp.sum(e, axis=-1, keepdims=True))
                        put(r.o_v, (site, slice(q0, q1), lanes(head, hd)), side(split(p), v))

            keep(r.o_v.at[:, site], r.os.at[table, :, site])
            r.h_v[site + 1] = r.h_v[site] + wide(parts(r.o_v, site), parts(r.wout_v, site), 1, 0)
            keep(r.h_v.at[site + 1], r.hs.at[table, site + 1])
        put(r.a_v, (2,), normalized(r.h_v[2])[0] * r.gains[2:3, :])
        keep(r.a_v.at[:, 2], r.as_.at[table, :, 2])

        def up(j):
            return wide(parts(r.a_v, 2), parts(r.wup_v, slice(None), slice(j * TILE, (j + 1) * TILE)), 1, 0)

        tiles = ff // TILE
        z = up(0)
        for j in range(tiles):
            at = slice(j * TILE, (j + 1) * TILE)
            following = up(j + 1) if j + 1 < tiles else None
            g, gp = gelu_parts(z)
            put(r.g_v, (slice(None), at), g)
            r.gp_v[:, at] = gp
            z = following
        keep(r.g_v, r.gs.at[table])
        keep(r.gp_v, r.gps.at[table])
        for half in range(2):
            at = slice(half * w // 2, (half + 1) * w // 2)
            r.y_v[table, :, at] = r.h_v[2, :, at] + wide(parts(r.g_v), parts(r.wdown_v, slice(None), at), 1, 0)

            @pl.when(section == 0)
            def _():
                relay(table, half).start()

        keep(r.y_v.at[table, 0:real], r.out.at[table])
        for copy in stores:
            copy.wait()

    def backward(self, r, table, section, relay):
        c, w, ff, hd, real = self.cells, self.width, self.ff, self.hd, self.real
        stores = []

        def keep(src, dst):
            stores.append(start(src, dst, r.out_sem.at[len(stores)]))

        col_biases(self.rows, self.feat, r.ctx[table], (r.bias_a, r.bias_b), 0)

        @pl.when(section == 0)
        def _():
            loads = [
                start(r.hs.at[table], r.h_v, r.in_sem.at[0]),
                start(r.qkvs.at[table], r.qkv_v, r.in_sem.at[1]),
                start(r.gps.at[table], r.gp_v, r.in_sem.at[2]),
            ]
            for half in range(2):
                relay(table, half).wait()
            r.dy_v[0:real] = r.got[table]
            for copy in loads:
                copy.wait()

        @pl.when(section == 1)
        def _():
            pltpu.make_async_copy(r.cot.at[table], r.dy_v.at[0:real], r.in_sem.at[1]).wait()

        r.dy_v[real:, :] = jnp.zeros((c - real, w), F32)
        put(r.dys_v, (), r.dy_v[...])
        keep(r.dys_v, r.dys.at[table])

        def down(j):
            return wide(parts(r.dys_v), parts(r.wdown_v, slice(j * TILE, (j + 1) * TILE)), 1, 1)

        tiles = ff // TILE
        dg = down(0)
        for j in range(tiles):
            at = slice(j * TILE, (j + 1) * TILE)
            following = down(j + 1) if j + 1 < tiles else None
            put(r.g_v, (slice(None), at), dg * r.gp_v[:, at])
            dg = following
        keep(r.g_v, r.dzs.at[table])
        da = wide(parts(r.g_v), parts(r.wup_v), 1, 1)

        def through_norm(site, da):
            n, rstd = normalized(r.h_v[site])
            r.small[site : site + 1, :] += jnp.sum(da * n, axis=0, keepdims=True)
            return norm_back(n, rstd, r.gains[site : site + 1, :], da)

        r.dy_v[...] += through_norm(2, da)
        for site in (1, 0):
            put(r.o_v, (site,), r.dy_v[...])
            keep(r.o_v.at[:, site], r.dhs.at[table, :, site])
            put(r.do_v, (), wide(parts(r.o_v, site), parts(r.wout_v, site), 1, 1))

            @pl.loop(0, HEADS // 2)
            def _(two):
                for head in (2 * two, 2 * two + 1):
                    at_q, at_k, at_v = lanes(head, hd), lanes(HEADS + head, hd), lanes(2 * HEADS + head, hd)
                    for ((q0, q1), (k0, k1)), bias in self.sites(r, site):
                        q = parts(r.qkv_v, site, slice(q0, q1), at_q)
                        k = parts(r.qkv_v, site, slice(k0, k1), at_k)
                        v = parts(r.qkv_v, site, slice(k0, k1), at_v)
                        do = parts(r.do_v, slice(q0, q1), at_q)
                        s = wide(k, q, 1, 1) * self.scale + bias[...]
                        e = jnp.exp(s - jnp.max(s, axis=0, keepdims=True))
                        p = e * (1.0 / jnp.sum(e, axis=0, keepdims=True))
                        dp = wide(v, do, 1, 1)
                        ds = split(p * (dp - jnp.sum(p * dp, axis=0, keepdims=True)) * self.scale)
                        r.dqkv_f[q0:q1, at_q] = wide(tuple(x.T for x in k), ds, 1, 0).T
                        r.dqkv_f[k0:k1, at_k] = side(ds, q)
                        r.dqkv_f[k0:k1, at_v] = side(split(p), do)

            for j in range(3 * w // TILE):
                at = slice(j * TILE, (j + 1) * TILE)
                put(r.qkv_v, (site, slice(None), at), r.dqkv_f[:, at])
            keep(r.qkv_v.at[:, site], r.dqkvs.at[table, :, site])
            da = wide(parts(r.qkv_v, site), parts(r.win_v, site), 1, 1)
            r.dy_v[...] += through_norm(site, da)

        @pl.when(section == 0)
        def _():
            missing = r.mask[table] == 1.0
            r.small[3:4, :] += jnp.sum(jnp.where(missing, r.dy_v[...], 0.0), axis=0, keepdims=True)
            r.y_v[table] = jnp.where(missing, 0.0, r.dy_v[...])

        @pl.when(section == 1)
        def _():
            r.y_v[table] = r.dy_v[...]
            for half in range(2):
                relay(table, half).start()

        keep(r.y_v.at[table, 0:real], r.din.at[table])
        for copy in stores:
            copy.wait()


class GradSum:
    BLOCK = 256
    SLACK = 2
    RING = 8

    def __init__(self, count, tables, cells, width, ff):
        self.count, self.tables, self.cells, self.width = count, tables, cells, width
        self.rest = count // 4
        shapes = [("gs", None, "dys", None, "down", None, ff, width), ("as_", 2, "dzs", None, "up", None, width, ff)]
        for site in (1, 0):
            shapes.append(("as_", site, "dqkvs", site, "win", site, width, 3 * width))
            shapes.append(("os", site, "dhs", site, "wout", site, width, width))
        self.groups, at = [], 0
        for *which, k, n in shapes:
            blocks = (k // self.BLOCK) * (n // TILE)
            self.groups.append((at, at + blocks, *which, n // TILE))
            at += blocks
        self.blocks = at
        self.per_chunk = max(1, 4 * self.rest * 8 // self.BLOCK)
        self.chunks = self.blocks // self.per_chunk
        self.rows = self.per_chunk * self.BLOCK

    def select(self, q, action):
        for group in self.groups:
            first, stop, *_, across = group

            @pl.when((q >= first) & (q < stop))
            def _():
                action(group, (q - first) // across, (q - first) % across)

    def load(self, r, q):
        slot = q % 2

        def action(group, i, j):
            _, _, left, left_site, right, right_site, *_ = group
            a, b = getattr(r, left), getattr(r, right)
            for t in range(self.tables):
                for part in range(2):
                    sem = 2 * t + part

                    def at(site):
                        return (t, part, slice(None)) if site is None else (t, part, site, slice(None))

                    start(a.at[(*at(left_site), lanes(i, self.BLOCK))], r.a_v.at[slot, t, part], r.a_sem.at[slot, sem])
                    start(b.at[(*at(right_site), lanes(j, TILE))], r.b_v.at[slot, t, part], r.b_sem.at[slot, sem])

        self.select(q, action)

    def wait_load(self, r, slot):
        for t in range(self.tables):
            for part in range(2):
                sem = 2 * t + part
                a, b = r.a_v.at[slot, t, part], r.b_v.at[slot, t, part]
                pltpu.make_async_copy(a, a, r.a_sem.at[slot, sem]).wait()
                pltpu.make_async_copy(b, b, r.b_sem.at[slot, sem]).wait()

    def product(self, r, q):
        slot = q % 2
        self.wait_load(r, slot)

        @pl.when(q + 1 < self.blocks)
        def _():
            self.load(r, q + 1)

        left, right = [], []
        for t in range(self.tables):
            (ah, al), (bh, bl) = parts(r.a_v.at[slot, t]), parts(r.b_v.at[slot, t])
            left += [ah, ah, al]
            right += [bh, bl, bh]
        rows = pl.ds(pl.multiple_of(q % self.per_chunk * self.BLOCK, self.BLOCK), self.BLOCK)
        r.sums[q // self.per_chunk % self.RING, rows] = dot(jnp.concatenate(left, 0), jnp.concatenate(right, 0), ((0,), (0,)))

    def store(self, r, q):
        def action(group, i, j):
            *_, out, site, _ = group
            dst = getattr(r, out)
            rows = pl.ds(pl.multiple_of(i * self.BLOCK, self.BLOCK), self.BLOCK)
            dst = dst.at[rows, lanes(j, TILE)] if site is None else dst.at[site, rows, lanes(j, TILE)]
            u = q % self.per_chunk
            at = pl.ds(pl.multiple_of(u * self.BLOCK, self.BLOCK), self.BLOCK)
            start(r.full.at[q // self.per_chunk, at], dst, r.store_sem.at[q // self.per_chunk % 2, u])

        self.select(q, action)

    def wait_store(self, r, c):
        for u in range(self.per_chunk):
            block = r.full.at[c, u * self.BLOCK : (u + 1) * self.BLOCK]
            pltpu.make_async_copy(block, block, r.store_sem.at[c % 2, u]).wait()

    def kernel(self, r):
        count, rest, rows = self.count, self.rest, self.rows
        half, quarter, piece = rows // 2, rows // 4, rows // 4 // rest
        me, section = lax.axis_index("dp"), lax.axis_index("section")
        core, pair, place = me % 2, me // 2 % 2, me // 4
        sibling, neighbour = me + 1 - 2 * core, me + 2 - 4 * pair

        def peer(j):
            return lax.rem(place + j, rest) * 4 + me % 4

        def span(at, size):
            return pl.ds(pl.multiple_of(at, size), size)

        mine = core * half
        own = mine + pair * quarter
        other = mine + (1 - pair) * quarter

        barrier = pltpu.get_barrier_semaphore()
        pl.semaphore_signal(barrier, inc=1, device_id={"section": 1 - section}, device_id_type=pl.DeviceIdType.MESH)
        for device in (sibling, neighbour):
            pl.semaphore_signal(barrier, inc=1, device_id={"dp": device}, device_id_type=pl.DeviceIdType.MESH)

        @pl.loop(1, rest)
        def _(j):
            pl.semaphore_signal(barrier, inc=1, device_id={"dp": peer(j)}, device_id_type=pl.DeviceIdType.MESH)

        self.load(r, 0)
        pl.semaphore_wait(barrier, rest + 2)

        def halve(c):
            src = r.sums.at[c % self.RING, span((1 - core) * half, half)]
            return remote(src, r.got_half.at[c], r.send.at[0, c % self.RING], r.recv.at[0, c], {"dp": sibling})

        def quarter_copy(c):
            src = r.sums.at[c % self.RING, span(other, quarter)]
            return remote(src, r.got_quarter.at[c], r.send.at[1, c % self.RING], r.recv.at[1, c], {"dp": neighbour})

        def scatter(c, j):
            src = r.sums.at[c % self.RING, span(own + lax.rem(place + j, rest) * piece, piece)]
            dst = r.got_piece.at[c, j - 1]
            return remote(src, dst, r.send_rest.at[0, c % self.RING, j - 1], r.recv_rest.at[0, c, j - 1], {"dp": peer(j)})

        def gather(c, j):
            at = r.full.at[c, span(own + place * piece, piece)]
            return remote(at, at, r.send_rest.at[1, c % self.RING, j - 1], r.recv_rest.at[1, c, j - 1], {"dp": peer(j)})

        def gather_quarter(c):
            at = r.full.at[c, span(own, quarter)]
            return remote(at, at, r.send.at[2, c % self.RING], r.recv.at[2, c], {"dp": neighbour})

        def gather_half(c):
            at = r.full.at[c, span(mine, half)]
            return remote(at, at, r.send.at[3, c % self.RING], r.recv.at[3, c], {"dp": sibling})

        def each(action):
            pl.loop(1, rest)(action)

        def after_halve(c):
            halve(c).wait()
            r.sums[c % self.RING, span(mine, half)] += r.got_half[c]
            quarter_copy(c).start()

        def after_quarter(c):
            quarter_copy(c).wait()
            r.sums[c % self.RING, span(own, quarter)] += r.got_quarter[c]
            each(lambda j: scatter(c, j).start())

        def after_scatter(c):
            each(lambda j: scatter(c, j).wait())
            total = r.sums[c % self.RING, span(own + place * piece, piece)]
            for j in range(rest - 1):
                total += r.got_piece[c, j]
            r.full[c, span(own + place * piece, piece)] = total
            each(lambda j: gather(c, j).start())

        def after_gather(c):
            each(lambda j: gather(c, j).wait())
            gather_quarter(c).start()

        def after_gather_quarter(c):
            gather_quarter(c).wait()
            gather_half(c).start()

        def after_gather_half(c):
            gather_half(c).wait()

            @pl.when(c >= 2)
            def _():
                self.wait_store(r, c - 2)

            @pl.loop(0, self.per_chunk)
            def _(u):
                self.store(r, c * self.per_chunk + u)

        stages = [after_halve, after_quarter, after_scatter, after_gather, after_gather_quarter, after_gather_half]

        def small_copy(k, device):
            return remote(r.small_v.at[k], r.got_small.at[k], r.small_send.at[k], r.small_recv.at[k], device)

        def small_rest(j):
            dst = r.got_small.at[2 + j]
            return remote(r.small_v.at[3], dst, r.small_send.at[2 + j], r.small_recv.at[2 + j], {"dp": peer(j)})

        def small_step(step):
            @pl.when(step == 0)
            def _():
                r.small_v[0] = r.small[...]
                small_copy(0, {"section": 1 - section}).start()

            @pl.when(step == 2)
            def _():
                small_copy(0, {"section": 1 - section}).wait()
                row = lax.broadcasted_iota(jnp.int32, (8, self.width), 0)
                r.small_v[1] = r.small_v[0] + jnp.where(row == 3, r.got_small[0], 0.0)
                small_copy(1, {"dp": sibling}).start()

            @pl.when(step == 4)
            def _():
                small_copy(1, {"dp": sibling}).wait()
                r.small_v[2] = r.small_v[1] + r.got_small[1]
                small_copy(2, {"dp": neighbour}).start()

            @pl.when(step == 6)
            def _():
                small_copy(2, {"dp": neighbour}).wait()
                r.small_v[3] = r.small_v[2] + r.got_small[2]
                each(lambda j: small_rest(j).start())

            @pl.when(step == 8)
            def _():
                each(lambda j: small_rest(j).wait())
                total = r.small_v[3]
                for j in range(1, rest):
                    total += r.got_small[2 + j]
                r.small_out[...] = total

        @pl.loop(0, self.chunks + self.SLACK * len(stages))
        def _(step):
            for k in reversed(range(len(stages))):
                c = step - self.SLACK * (k + 1)

                @pl.when((c >= 0) & (c < self.chunks))
                def _():
                    stages[k](c)

            small_step(step)

            @pl.when(step < self.chunks)
            def _():
                @pl.loop(0, self.per_chunk)
                def _(u):
                    self.product(r, step * self.per_chunk + u)

                halve(step).start()

        for c in range(max(0, self.chunks - 2), self.chunks):
            self.wait_store(r, c)

    def __call__(self, operands, small):
        t, cells, width = self.tables, self.cells, self.width
        rest, chunks, rows = self.rest, self.chunks, self.rows
        piece = rows // 4 // rest
        ff = operands["gs"].shape[-1]
        outs = {
            "win": f32(2, width, 3 * width),
            "wout": f32(2, width, width),
            "up": f32(width, ff),
            "down": f32(ff, width),
            "small_out": f32(8, width),
        }
        scratch = {
            "sums": VMEM((self.RING, rows, TILE), F32),
            "full": VMEM((chunks, rows, TILE), F32),
            "got_half": VMEM((chunks, rows // 2, TILE), F32),
            "got_quarter": VMEM((chunks, rows // 4, TILE), F32),
            "got_piece": VMEM((chunks, rest - 1, piece, TILE), F32),
            "a_v": VMEM((2, t, 2, cells, self.BLOCK), BF16),
            "b_v": VMEM((2, t, 2, cells, TILE), BF16),
            "small_v": VMEM((4, 8, width), F32),
            "got_small": VMEM((2 + rest, 8, width), F32),
            "a_sem": pltpu.SemaphoreType.DMA((2, 2 * t)),
            "b_sem": pltpu.SemaphoreType.DMA((2, 2 * t)),
            "store_sem": pltpu.SemaphoreType.DMA((2, self.per_chunk)),
            "send": pltpu.SemaphoreType.DMA((4, self.RING)),
            "recv": pltpu.SemaphoreType.DMA((4, chunks)),
            "send_rest": pltpu.SemaphoreType.DMA((2, self.RING, rest - 1)),
            "recv_rest": pltpu.SemaphoreType.DMA((2, chunks, rest - 1)),
            "small_send": pltpu.SemaphoreType.DMA((2 + rest,)),
            "small_recv": pltpu.SemaphoreType.DMA((2 + rest,)),
        }
        ins = {n: (a, ANY) for n, a in operands.items()} | {"small": (small, VMEM)}
        outs = {n: (s, VMEM if n == "small_out" else ANY) for n, s in outs.items()}
        return call("weight_gradient_sum", self.kernel, 0, ins, outs, scratch)


def local(
    cells,
    missing_mask,
    missing_embed,
    context_rows,
    norm_gains,
    attn_in,
    attn_out,
    mlp_up,
    mlp_down,
    cotangent,
):
    tables, rows, feat, width = cells.shape
    ff = mlp_up.shape[2]
    layers = Layers(tables, rows, feat, width, ff)

    def flat(tables_of_cells):
        return jnp.swapaxes(tables_of_cells, 1, 2).reshape(tables, rows * feat, -1)

    def unflat(cells_of_tables):
        return jnp.swapaxes(cells_of_tables.reshape(tables, feat, rows, width), 1, 2)[None]

    mask = jnp.pad(flat(missing_mask == 1).astype(F32), ((0, 0), (0, layers.cells - rows * feat), (0, 0)))
    weights = (attn_in[0], attn_out[0], mlp_up[0], mlp_down[0])
    done = layers(flat(cells), mask, missing_embed[None], context_rows, norm_gains[0], weights, flat(cotangent))
    operands = {n: done[n] for n in ("as_", "os", "gs", "dys", "dzs", "dhs", "dqkvs")}
    sums = GradSum(lax.axis_size("dp"), tables, layers.cells, width, ff)(operands, done["small"])
    return (
        unflat(done["out"]),
        unflat(done["din"]),
        sums["small_out"][0:3][None],
        sums["win"][None],
        sums["wout"][None],
        sums["up"][None],
        sums["down"][None],
        sums["small_out"][3],
    )


def solution(mesh):
    in_specs = (
        P("dp", None, None, None),
        P("dp", None, None),
        P(),
        P("dp"),
        P("section", None, None),
        P("section", None, None, None),
        P("section", None, None, None),
        P("section", None, None),
        P("section", None, None),
        P("dp", None, None, None),
    )
    out_specs = (
        P("section", "dp", None, None, None),
        P("section", "dp", None, None, None),
        P("section", None, None),
        P("section", None, None, None),
        P("section", None, None, None),
        P("section", None, None),
        P("section", None, None),
        P(),
    )
    return jax.shard_map(local, mesh=mesh, in_specs=in_specs, out_specs=out_specs, check_vma=False)
```

```python
import functools
from types import SimpleNamespace

import jax
import jax.numpy as jnp
from jax import lax
from jax.experimental import pallas as pl
from jax.experimental.pallas import tpu as pltpu
from jax.sharding import PartitionSpec as P

HEADS = 4
EPSILON = 1e-05
NEG = -1e30
INV_SQRT2PI = 0.3989422804014327
ERFC_P = 0.33
ERFC_C = (0.1863578482, 0.1829552331, 0.2012284886, 0.0472047191, 0.4085317677, -0.3511862269, 0.4602596132, -0.1353514118)
VMEM_LIMIT = 62 * 1024 * 1024
TILE = 512
F32, BF16 = jnp.float32, jnp.bfloat16


def dot(a, b, contract=((1,), (0,))):
    return lax.dot_general(a, b, (contract, ((), ())), preferred_element_type=F32)


def split(v):
    hi = v.astype(BF16)
    return hi, (v - hi.astype(F32)).astype(BF16)


def put(ref, index, v):
    hi, lo = split(v)
    ref[(0, *index)] = hi
    ref[(1, *index)] = lo


def parts(ref, *index):
    return ref[(0, *index)], ref[(1, *index)]


def wide(a, b, ca, cb):
    (ah, al), (bh, bl) = a, b
    return dot(jnp.concatenate([ah, ah, al], ca), jnp.concatenate([bh, bl, bh], cb), ((ca,), (cb,)))


def side(a, b):
    (ah, al), (bh, bl) = a, b
    width = bh.shape[1]
    both = dot(ah, jnp.concatenate([bh, bl], 1))
    return both[:, :width] + both[:, width:] + dot(al, bh)


def normalized(h):
    centred = h - jnp.mean(h, axis=-1, keepdims=True)
    rstd = lax.rsqrt(jnp.mean(centred * centred, axis=-1, keepdims=True) + EPSILON)
    return centred * rstd, rstd


def norm_back(n, rstd, gain, da):
    dn = da * gain
    return rstd * (dn - jnp.mean(dn, axis=-1, keepdims=True) - n * jnp.mean(dn * n, axis=-1, keepdims=True))


def cell_ids(start, count, rows, along):
    shape = (count, 1) if along == 0 else (1, count)
    at = lax.broadcasted_iota(jnp.int32, shape, along) + start
    feat = lax.shift_right_logical(at * ((1 << 20) // rows + 1), 20)
    return at - feat * rows, feat


def up16(n):
    return (n + 15) // 16 * 16


def col_blocks(rows, feat):
    cells = up16(rows * feat)
    half = up16((feat + 1) // 2 * rows)
    first_keys = min(cells, up16((((half - 1) // rows) + 1) * rows))
    second_keys = ((half // rows) * rows) // 16 * 16
    return (((0, half), (0, first_keys)), ((half, cells), (second_keys, cells)))


def lanes(j, width):
    return pl.ds(pl.multiple_of(j * width, width), width)


def start(src, dst, sem):
    copy = pltpu.make_async_copy(src, dst, sem)
    copy.start()
    return copy


def col_biases(rows, feat, context, refs, keys_along):
    for ((q0, q1), (k0, k1)), ref in zip(col_blocks(rows, feat), refs):
        _, q_feat = cell_ids(q0, q1 - q0, rows, 1 - keys_along)
        k_row, k_feat = cell_ids(k0, k1 - k0, rows, keys_along)
        ref[...] = jnp.where((q_feat == k_feat) & (k_row < context), 0.0, NEG)


def row_bias(rows, feat, ref):
    cells = up16(rows * feat)
    q_row, q_feat = cell_ids(0, cells, rows, 0)
    k_row, k_feat = cell_ids(0, cells, rows, 1)
    ref[...] = jnp.where((q_row == k_row) & ((q_feat < feat) == (k_feat < feat)), 0.0, NEG)


def gelu_parts(z):
    size = jnp.abs(z)
    below = 1.0 + (ERFC_P * 0.7071067811865476) * size
    t = pl.reciprocal(below, approx=True)
    t = t * (2.0 - below * t)
    series = jnp.full_like(t, ERFC_C[-1])
    for c in ERFC_C[-2::-1]:
        series = series * t + c
    bell = jnp.exp(-0.5 * z * z)
    tail = 0.5 * (series * t) * bell
    phi = jnp.where(z >= 0.0, 1.0 - tail, tail)
    return z * phi, phi + z * (INV_SQRT2PI * bell)


SMEM, VMEM, ANY = pltpu.SMEM, pltpu.VMEM, pl.ANY


def f32(*shape):
    return jax.ShapeDtypeStruct(shape, F32)


def b16(*shape):
    return jax.ShapeDtypeStruct(shape, BF16)


def dma(*shape):
    return pltpu.SemaphoreType.DMA(shape)


def remote(src, dst, send, recv, device):
    return pltpu.make_async_remote_copy(
        src_ref=src, dst_ref=dst, send_sem=send, recv_sem=recv, device_id=device, device_id_type=pl.DeviceIdType.MESH
    )


def call(name, body, collective_id, ins, outs, scratch):
    names = [*ins, *outs, *scratch]

    def kernel(*refs):
        body(SimpleNamespace(**dict(zip(names, refs))))

    results = pl.pallas_call(
        kernel,
        out_shape=[t for t, _ in outs.values()],
        in_specs=[pl.BlockSpec(memory_space=s) for _, s in ins.values()],
        out_specs=[pl.BlockSpec(memory_space=s) for _, s in outs.values()],
        scratch_shapes=list(scratch.values()),
        compiler_params=pltpu.CompilerParams(
            vmem_limit_bytes=VMEM_LIMIT, collective_id=collective_id, has_side_effects=True
        ),
        name=name,
    )(*(a for a, _ in ins.values()))
    return dict(zip(outs, results))


class Layers:
    def __init__(self, tables, rows, feat, width, ff):
        self.tables, self.rows, self.feat, self.width, self.ff = tables, rows, feat, width, ff
        self.real, self.cells = rows * feat, up16(rows * feat)
        self.hd = width // HEADS
        self.scale = self.hd ** (-0.5)

    def sites(self, r, site):
        if site == 1:
            return list(zip(col_blocks(self.rows, self.feat), (r.bias_a, r.bias_b)))
        return [(((0, self.cells), (0, self.cells)), r.bias_row)]

    def __call__(self, cells, mask, embed, context, gains, weights, cotangent):
        t, c, w, ff, real = self.tables, self.cells, self.width, self.ff, self.real
        ins = {
            "cells": (cells, ANY),
            "mask": (mask, VMEM),
            "embed": (embed, VMEM),
            "ctx": (context, SMEM),
            "gains": (gains, VMEM),
            "cot": (cotangent, ANY),
        }
        names = ("win", "wout", "wup", "wdown")
        ins |= {n: (a, ANY) for n, a in zip(names, weights)}
        outs = {
            "out": f32(t, real, w),
            "din": f32(t, real, w),
            "hs": f32(t, 3, c, w),
            "qkvs": b16(t, 2, 2, c, 3 * w),
            "gps": f32(t, c, ff),
            "as_": b16(t, 2, 3, c, w),
            "os": b16(t, 2, 2, c, w),
            "gs": b16(t, 2, c, ff),
            "dys": b16(t, 2, c, w),
            "dzs": b16(t, 2, c, ff),
            "dhs": b16(t, 2, 2, c, w),
            "dqkvs": b16(t, 2, 2, c, 3 * w),
        }
        outs = {n: (s, ANY) for n, s in outs.items()} | {"small": (f32(8, w), VMEM)}
        scratch = {n + "_v": VMEM((2, *a.shape), BF16) for n, a in zip(names, weights)}
        scratch |= {
            "h_v": VMEM((3, c, w), F32),
            "qkv_v": VMEM((2, 2, c, 3 * w), BF16),
            "o_v": VMEM((2, 2, c, w), BF16),
            "gp_v": VMEM((c, ff), F32),
            "g_v": VMEM((2, c, ff), BF16),
            "a_v": VMEM((2, 3, c, w), BF16),
            "y_v": VMEM((t, c, w), F32),
            "dqkv_f": VMEM((c, 3 * w), F32),
            "dys_v": VMEM((2, c, w), BF16),
            "dy_v": VMEM((c, w), F32),
            "do_v": VMEM((2, c, w), BF16),
            "got": VMEM((t, real, w), F32),
            "bias_row": VMEM((c, c), F32),
            "raw_sem": pltpu.SemaphoreType.DMA((16,)),
            "in_sem": pltpu.SemaphoreType.DMA((4,)),
            "out_sem": pltpu.SemaphoreType.DMA((16,)),
            "send": pltpu.SemaphoreType.DMA((t, 2)),
            "recv": pltpu.SemaphoreType.DMA((t, 2)),
        }
        for name, ((q0, q1), (k0, k1)) in zip(("bias_a", "bias_b"), col_blocks(self.rows, self.feat)):
            assert (q0, q1) == (k0, k1)
            scratch[name] = VMEM((q1 - q0, q1 - q0), F32)
        return call("layers", self.kernel, 1, ins, outs, scratch)

    def split_weights(self, r):
        w, ff = self.width, self.ff
        half, wide_in = w // 2, 3 * w
        top, step = slice(0, half), 64
        rest = slice(half, w)
        pieces = []
        big, bigger = r.dqkv_f.at[top], r.gp_v.at[top]
        pieces.append((r.win.at[0, top], big, r.win_v, (0,), 0, slice(None)))
        pieces.append((r.win.at[0, rest], bigger.at[:, 0:wide_in], r.win_v, (0,), half, slice(None)))
        pieces.append((r.wout.at[0, top], r.h_v.at[0, top], r.wout_v, (0,), 0, slice(None)))
        pieces.append((r.wout.at[0, rest], r.h_v.at[1, top], r.wout_v, (0,), half, slice(None)))
        pieces.append((r.wout.at[1, top], r.h_v.at[2, top], r.wout_v, (1,), 0, slice(None)))
        pieces.append((r.wout.at[1, rest], r.y_v.at[0, top], r.wout_v, (1,), half, slice(None)))
        pieces.append((r.win.at[1, top], big, r.win_v, (1,), 0, slice(None)))
        pieces.append((r.win.at[1, rest], bigger.at[:, 0:wide_in], r.win_v, (1,), half, slice(None)))
        pieces.append((r.wup.at[rest, wide_in:ff], r.dy_v.at[top, 0 : ff - wide_in], r.wup_v, (), half, slice(wide_in, ff)))
        pieces.append((r.wup.at[top], bigger, r.wup_v, (), 0, slice(None)))
        pieces.append((r.wup.at[rest, 0:wide_in], big, r.wup_v, (), half, slice(0, wide_in)))
        rows = self.cells // step * step
        buffers = [r.h_v.at[0], r.h_v.at[1], r.h_v.at[2], r.y_v.at[0], r.y_v.at[1]]
        for i, at in enumerate(range(0, ff, rows)):
            size = min(rows, ff - at)
            pieces.append((r.wdown.at[at : at + size], buffers[i].at[0:size], r.wdown_v, (), at, slice(None)))
        users = [0, 1, 2, 3, 4, 5, 0, 1, 6, 1, 0, 2, 3, 4, 5, 7][: len(pieces)]
        copies = [pltpu.make_async_copy(p[0], p[1], r.raw_sem.at[i]) for i, p in enumerate(pieces)]
        first = {u: i for i, u in reversed(list(enumerate(users)))}
        for i in sorted(first.values()):
            copies[i].start()
        for i, (_, buffer, v, lead, at, columns) in enumerate(pieces):
            copies[i].wait()

            @pl.loop(0, buffer.shape[0] // step)
            def _(j):
                src = pl.ds(pl.multiple_of(j * step, step), step)
                dst = pl.ds(pl.multiple_of(at + j * step, step), step)
                put(v, (*lead, dst, columns), buffer[src])

            later = [k for k in range(i + 1, len(pieces)) if users[k] == users[i]]
            if later:
                copies[later[0]].start()

    def kernel(self, r):
        t, real, c = self.tables, self.real, self.cells
        section = lax.axis_index("section")
        other = {"section": 1 - section}
        barrier = pltpu.get_barrier_semaphore()
        pl.semaphore_signal(barrier, inc=1, device_id=other, device_id_type=pl.DeviceIdType.MESH)
        self.split_weights(r)
        row_bias(self.rows, self.feat, r.bias_row)
        r.small[...] = jnp.zeros_like(r.small)
        pl.semaphore_wait(barrier, 1)

        def relay(table, half):
            at = slice(half * self.width // 2, (half + 1) * self.width // 2)
            src, dst = r.y_v.at[table, 0:real, at], r.got.at[table, :, at]
            return remote(src, dst, r.send.at[table, half], r.recv.at[table, half], other)

        @pl.loop(0, 2 * t)
        def _(step):
            forward = (1 - section) * (1 - step // t) + section * (1 - step % 2)
            table = (1 - section) * (step % t) + section * (step // 2)

            @pl.when(forward == 1)
            def _():
                self.forward(r, table, section, relay)

            @pl.when(forward == 0)
            def _():
                self.backward(r, table, section, relay)

        @pl.when(section == 1)
        def _():
            for table in range(t):
                for half in range(2):
                    relay(table, half).wait_send()

    def forward(self, r, table, section, relay):
        c, w, ff, hd, real = self.cells, self.width, self.ff, self.hd, self.real
        stores = []

        def keep(src, dst):
            stores.append(start(src, dst, r.out_sem.at[len(stores)]))

        r.h_v[0, real:, :] = jnp.zeros((c - real, w), F32)
        col_biases(self.rows, self.feat, r.ctx[table], (r.bias_a, r.bias_b), 1)

        @pl.when(section == 0)
        def _():
            start(r.cells.at[table], r.h_v.at[0, 0:real], r.in_sem.at[0]).wait()
            r.h_v[0] = jnp.where(r.mask[table] == 1.0, r.embed[...], r.h_v[0])

        @pl.when(section == 1)
        def _():
            start(r.cot.at[table], r.dy_v.at[0:real], r.in_sem.at[1])
            for half in range(2):
                relay(table, half).wait_recv()
            r.h_v[0, 0:real] = r.got[table]

        keep(r.h_v.at[0], r.hs.at[table, 0])
        for site in range(2):
            put(r.a_v, (site,), normalized(r.h_v[site])[0] * r.gains[site : site + 1, :])
            keep(r.a_v.at[:, site], r.as_.at[table, :, site])
            for j in range(3 * w // TILE):
                at = slice(j * TILE, (j + 1) * TILE)
                out = wide(parts(r.a_v, site), parts(r.win_v, site, slice(None), at), 1, 0)
                put(r.qkv_v, (site, slice(None), at), out)
            keep(r.qkv_v.at[:, site], r.qkvs.at[table, :, site])

            @pl.loop(0, HEADS // 2)
            def _(two):
                for head in (2 * two, 2 * two + 1):
                    for ((q0, q1), (k0, k1)), bias in self.sites(r, site):
                        q = parts(r.qkv_v, site, slice(q0, q1), lanes(head, hd))
                        k = parts(r.qkv_v, site, slice(k0, k1), lanes(HEADS + head, hd))
                        v = parts(r.qkv_v, site, slice(k0, k1), lanes(2 * HEADS + head, hd))
                        s = wide(q, k, 1, 1) * self.scale + bias[...]
                        e = jnp.exp(s - jnp.max(s, axis=-1, keepdims=True))
                        p = e * (1.0 / jnp.sum(e, axis=-1, keepdims=True))
                        put(r.o_v, (site, slice(q0, q1), lanes(head, hd)), side(split(p), v))

            keep(r.o_v.at[:, site], r.os.at[table, :, site])
            r.h_v[site + 1] = r.h_v[site] + wide(parts(r.o_v, site), parts(r.wout_v, site), 1, 0)
            keep(r.h_v.at[site + 1], r.hs.at[table, site + 1])
        put(r.a_v, (2,), normalized(r.h_v[2])[0] * r.gains[2:3, :])
        keep(r.a_v.at[:, 2], r.as_.at[table, :, 2])

        def up(j):
            return wide(parts(r.a_v, 2), parts(r.wup_v, slice(None), slice(j * TILE, (j + 1) * TILE)), 1, 0)

        tiles = ff // TILE
        z = up(0)
        for j in range(tiles):
            at = slice(j * TILE, (j + 1) * TILE)
            following = up(j + 1) if j + 1 < tiles else None
            g, gp = gelu_parts(z)
            put(r.g_v, (slice(None), at), g)
            r.gp_v[:, at] = gp
            z = following
        keep(r.g_v, r.gs.at[table])
        keep(r.gp_v, r.gps.at[table])
        for half in range(2):
            at = slice(half * w // 2, (half + 1) * w // 2)
            r.y_v[table, :, at] = r.h_v[2, :, at] + wide(parts(r.g_v), parts(r.wdown_v, slice(None), at), 1, 0)

            @pl.when(section == 0)
            def _():
                relay(table, half).start()

        keep(r.y_v.at[table, 0:real], r.out.at[table])
        for copy in stores:
            copy.wait()

    def backward(self, r, table, section, relay):
        c, w, ff, hd, real = self.cells, self.width, self.ff, self.hd, self.real
        stores = []

        def keep(src, dst):
            stores.append(start(src, dst, r.out_sem.at[len(stores)]))

        col_biases(self.rows, self.feat, r.ctx[table], (r.bias_a, r.bias_b), 0)

        @pl.when(section == 0)
        def _():
            loads = [
                start(r.hs.at[table], r.h_v, r.in_sem.at[0]),
                start(r.qkvs.at[table], r.qkv_v, r.in_sem.at[1]),
                start(r.gps.at[table], r.gp_v, r.in_sem.at[2]),
            ]
            for half in range(2):
                relay(table, half).wait()
            r.dy_v[0:real] = r.got[table]
            for copy in loads:
                copy.wait()

        @pl.when(section == 1)
        def _():
            pltpu.make_async_copy(r.cot.at[table], r.dy_v.at[0:real], r.in_sem.at[1]).wait()

        r.dy_v[real:, :] = jnp.zeros((c - real, w), F32)
        put(r.dys_v, (), r.dy_v[...])
        keep(r.dys_v, r.dys.at[table])

        def down(j):
            return wide(parts(r.dys_v), parts(r.wdown_v, slice(j * TILE, (j + 1) * TILE)), 1, 1)

        tiles = ff // TILE
        dg = down(0)
        for j in range(tiles):
            at = slice(j * TILE, (j + 1) * TILE)
            following = down(j + 1) if j + 1 < tiles else None
            put(r.g_v, (slice(None), at), dg * r.gp_v[:, at])
            dg = following
        keep(r.g_v, r.dzs.at[table])
        da = wide(parts(r.g_v), parts(r.wup_v), 1, 1)

        def through_norm(site, da):
            n, rstd = normalized(r.h_v[site])
            r.small[site : site + 1, :] += jnp.sum(da * n, axis=0, keepdims=True)
            return norm_back(n, rstd, r.gains[site : site + 1, :], da)

        r.dy_v[...] += through_norm(2, da)
        for site in (1, 0):
            put(r.o_v, (site,), r.dy_v[...])
            keep(r.o_v.at[:, site], r.dhs.at[table, :, site])
            put(r.do_v, (), wide(parts(r.o_v, site), parts(r.wout_v, site), 1, 1))

            @pl.loop(0, HEADS // 2)
            def _(two):
                for head in (2 * two, 2 * two + 1):
                    at_q, at_k, at_v = lanes(head, hd), lanes(HEADS + head, hd), lanes(2 * HEADS + head, hd)
                    for ((q0, q1), (k0, k1)), bias in self.sites(r, site):
                        q = parts(r.qkv_v, site, slice(q0, q1), at_q)
                        k = parts(r.qkv_v, site, slice(k0, k1), at_k)
                        v = parts(r.qkv_v, site, slice(k0, k1), at_v)
                        do = parts(r.do_v, slice(q0, q1), at_q)
                        s = wide(k, q, 1, 1) * self.scale + bias[...]
                        e = jnp.exp(s - jnp.max(s, axis=0, keepdims=True))
                        p = e * (1.0 / jnp.sum(e, axis=0, keepdims=True))
                        dp = wide(v, do, 1, 1)
                        ds = split(p * (dp - jnp.sum(p * dp, axis=0, keepdims=True)) * self.scale)
                        r.dqkv_f[q0:q1, at_q] = wide(tuple(x.T for x in k), ds, 1, 0).T
                        r.dqkv_f[k0:k1, at_k] = side(ds, q)
                        r.dqkv_f[k0:k1, at_v] = side(split(p), do)

            for j in range(3 * w // TILE):
                at = slice(j * TILE, (j + 1) * TILE)
                put(r.qkv_v, (site, slice(None), at), r.dqkv_f[:, at])
            keep(r.qkv_v.at[:, site], r.dqkvs.at[table, :, site])
            da = wide(parts(r.qkv_v, site), parts(r.win_v, site), 1, 1)
            r.dy_v[...] += through_norm(site, da)

        @pl.when(section == 0)
        def _():
            missing = r.mask[table] == 1.0
            r.small[3:4, :] += jnp.sum(jnp.where(missing, r.dy_v[...], 0.0), axis=0, keepdims=True)
            r.y_v[table] = jnp.where(missing, 0.0, r.dy_v[...])

        @pl.when(section == 1)
        def _():
            r.y_v[table] = r.dy_v[...]
            for half in range(2):
                relay(table, half).start()

        keep(r.y_v.at[table, 0:real], r.din.at[table])
        for copy in stores:
            copy.wait()


class GradSum:
    BLOCK = 256
    SLACK = 2

    def __init__(self, count, tables, cells, width, ff):
        self.count, self.tables, self.cells, self.width = count, tables, cells, width
        self.rest = count // 4
        shapes = [("gs", None, "dys", None, "down", None, ff, width), ("as_", 2, "dzs", None, "up", None, width, ff)]
        for site in (1, 0):
            shapes.append(("as_", site, "dqkvs", site, "win", site, width, 3 * width))
            shapes.append(("os", site, "dhs", site, "wout", site, width, width))
        self.groups, at = [], 0
        for *which, k, n in shapes:
            blocks = (k // self.BLOCK) * (n // TILE)
            self.groups.append((at, at + blocks, *which, n // TILE))
            at += blocks
        self.blocks = at
        self.per_chunk = max(1, 8 * self.rest * 8 // self.BLOCK)
        self.chunks = self.blocks // self.per_chunk
        self.rows = self.per_chunk * self.BLOCK
        self.ring = min(self.chunks, self.SLACK * (self.rest + 1) + 2)

    def select(self, q, action):
        for group in self.groups:
            first, stop, *_, across = group

            @pl.when((q >= first) & (q < stop))
            def _():
                action(group, (q - first) // across, (q - first) % across)

    def load(self, r, q):
        slot = q % 2

        def action(group, i, j):
            _, _, left, left_site, right, right_site, *_ = group
            a, b = getattr(r, left), getattr(r, right)
            for t in range(self.tables):
                for part in range(2):
                    sem = 2 * t + part

                    def at(site):
                        return (t, part, slice(None)) if site is None else (t, part, site, slice(None))

                    start(a.at[(*at(left_site), lanes(i, self.BLOCK))], r.a_v.at[slot, t, part], r.a_sem.at[slot, sem])
                    start(b.at[(*at(right_site), lanes(j, TILE))], r.b_v.at[slot, t, part], r.b_sem.at[slot, sem])

        self.select(q, action)

    def wait_load(self, r, slot):
        for t in range(self.tables):
            for part in range(2):
                sem = 2 * t + part
                a, b = r.a_v.at[slot, t, part], r.b_v.at[slot, t, part]
                pltpu.make_async_copy(a, a, r.a_sem.at[slot, sem]).wait()
                pltpu.make_async_copy(b, b, r.b_sem.at[slot, sem]).wait()

    def product(self, r, q):
        slot = q % 2
        self.wait_load(r, slot)

        @pl.when(q + 1 < self.blocks)
        def _():
            self.load(r, q + 1)

        left, right = [], []
        for t in range(self.tables):
            (ah, al), (bh, bl) = parts(r.a_v.at[slot, t]), parts(r.b_v.at[slot, t])
            left += [ah, ah, al]
            right += [bh, bl, bh]
        rows = pl.ds(pl.multiple_of(q % self.per_chunk * self.BLOCK, self.BLOCK), self.BLOCK)
        r.sums[q // self.per_chunk % self.ring, rows] = dot(jnp.concatenate(left, 0), jnp.concatenate(right, 0), ((0,), (0,)))

    def store(self, r, q):
        def action(group, i, j):
            *_, out, site, _ = group
            dst = getattr(r, out)
            rows = pl.ds(pl.multiple_of(i * self.BLOCK, self.BLOCK), self.BLOCK)
            dst = dst.at[rows, lanes(j, TILE)] if site is None else dst.at[site, rows, lanes(j, TILE)]
            u = q % self.per_chunk
            at = pl.ds(pl.multiple_of(u * self.BLOCK, self.BLOCK), self.BLOCK)
            start(r.full.at[q // self.per_chunk, at], dst, r.store_sem.at[q // self.per_chunk % 2, u])

        self.select(q, action)

    def wait_store(self, r, c):
        for u in range(self.per_chunk):
            block = r.full.at[c, u * self.BLOCK : (u + 1) * self.BLOCK]
            pltpu.make_async_copy(block, block, r.store_sem.at[c % 2, u]).wait()

    def kernel(self, r):
        rest, rows, ring = self.rest, self.rows, self.ring
        half = rows // 2
        part = half // 2
        sizes = (part // 2 // rest, part // rest)
        me, section = lax.axis_index("dp"), lax.axis_index("section")
        core, pair, place = me % 2, me // 2 % 2, me // 4
        sibling, neighbour = {"dp": me + 1 - 2 * core}, {"dp": me + 2 - 4 * pair}
        ways = ({"dp": me + 4}, {"dp": me - 4})

        def peer(j):
            return {"dp": lax.rem(place + j, rest) * 4 + me % 4}

        def span(at, size):
            return pl.ds(pl.multiple_of(at, size), size)

        mine = core * half
        own = mine + pair * (part // 2)
        other = mine + (1 - pair) * (part // 2)
        bases = (own, mine + part)

        barrier = pltpu.get_barrier_semaphore()

        def greet(device):
            pl.semaphore_signal(barrier, inc=1, device_id=device, device_id_type=pl.DeviceIdType.MESH)

        greet({"section": 1 - section})
        greet(sibling)
        greet(neighbour)

        @pl.loop(1, rest)
        def _(j):
            greet(peer(j))

        self.load(r, 0)
        pl.semaphore_wait(barrier, rest + 2)

        def halve(c):
            src = r.sums.at[c % ring, span((1 - core) * half, half)]
            return remote(src, r.got_half.at[c], r.send.at[0, c % ring], r.recv.at[0, c], sibling)

        def quarter(c):
            src = r.sums.at[c % ring, span(other, part // 2)]
            return remote(src, r.got_quarter.at[c], r.send.at[1, c % ring], r.recv.at[1, c], neighbour)

        def gather_quarter(c):
            at = r.full.at[c, span(own, part // 2)]
            return remote(at, at, r.send.at[2, c % ring], r.recv.at[2, c], neighbour)

        def gather_half(c):
            at = r.full.at[c, span(mine, half)]
            return remote(at, at, r.send.at[3, c % ring], r.recv.at[3, c], sibling)

        def piece(kind, b):
            return span(bases[kind] + b * sizes[kind], sizes[kind])

        def add_up(c):
            src = r.sums.at[c % ring, piece(1, place)]
            return remote(src, r.got_sum.at[c], r.send.at[4, c % ring], r.recv.at[4, c], neighbour)

        def line(kind, c, h, way, gather, b):
            if gather:
                src = dst = r.full.at[c, piece(kind, b)]
            else:
                src, dst = r.sums.at[c % ring, piece(kind, b)], r.got_line[kind].at[way, c, h]
            phase = 2 * way + int(gather)
            return remote(src, dst, r.send_line[kind].at[phase, c % ring, h], r.recv_line[kind].at[phase, c, h], ways[way])

        def hops(h, gather):
            if gather:
                right = ((place >= h) & (place < rest - 1), place - h, place >= h + 1, place - 1 - h)
                left = ((place + h < rest) & (place >= 1), place + h, place + 1 + h < rest, place + 1 + h)
            else:
                far = rest - 1 - h
                right = (place <= h, place + far, (place >= 1) & (place - 1 <= h), place - 1 + far)
                left = (rest - 1 - place <= h, place - far, (place <= rest - 2) & (rest - 2 - place <= h), place + 1 - far)
            return right, left

        def send_hop(kind, c, h, gather):
            for way, (sends, b, _, _) in enumerate(hops(h, gather)):

                @pl.when(sends)
                def _():
                    line(kind, c, h, way, gather, b).start()

        def end_hop(kind, c, h, gather):
            for way, (sends, b, receives, arriving) in enumerate(hops(h, gather)):

                @pl.when(sends)
                def _():
                    line(kind, c, h, way, gather, b).wait_send()

                @pl.when(receives)
                def _():
                    line(kind, c, h, way, gather, arriving).wait_recv()
                    if not gather:
                        r.sums[c % ring, piece(kind, arriving)] += r.got_line[kind][way, c, h]

        def hop(kind, c, h, gather, then):
            end_hop(kind, c, h, gather)

            @pl.when(h < rest - 2)
            def _():
                send_hop(kind, c, h + 1, gather)

            @pl.when(h == rest - 2)
            def _():
                then(c)

        def after_halve(c):
            halve(c).wait()
            r.sums[c % ring, span(mine, half)] += r.got_half[c]
            quarter(c).start()
            send_hop(1, c, 0, False)

        def after_quarter(c):
            quarter(c).wait()
            r.sums[c % ring, span(own, part // 2)] += r.got_quarter[c]
            send_hop(0, c, 0, False)

        def scattered(c):
            r.full[c, piece(0, place)] = r.sums[c % ring, piece(0, place)]
            send_hop(0, c, 0, True)

        def after_add_up(c):
            add_up(c).wait()
            r.full[c, piece(1, place)] = r.sums[c % ring, piece(1, place)] + r.got_sum[c]
            send_hop(1, c, 0, True)

        def after_gather_quarter(c):
            gather_quarter(c).wait()
            gather_half(c).start()

        def after_gather_half(c):
            gather_half(c).wait()

            @pl.when(c >= 2)
            def _():
                self.wait_store(r, c - 2)

            @pl.loop(0, self.per_chunk)
            def _(u):
                self.store(r, c * self.per_chunk + u)

        def small_copy(k, device):
            return remote(r.small_v.at[k], r.got_small.at[k], r.small_send.at[k], r.small_recv.at[k], device)

        def small_rest(j):
            dst = r.got_small.at[2 + j]
            return remote(r.small_v.at[3], dst, r.small_send.at[2 + j], r.small_recv.at[2 + j], peer(j))

        def small_step(step):
            @pl.when(step == 0)
            def _():
                r.small_v[0] = r.small[...]
                small_copy(0, {"section": 1 - section}).start()

            @pl.when(step == 2)
            def _():
                small_copy(0, {"section": 1 - section}).wait()
                row = lax.broadcasted_iota(jnp.int32, (8, self.width), 0)
                r.small_v[1] = r.small_v[0] + jnp.where(row == 3, r.got_small[0], 0.0)
                small_copy(1, sibling).start()

            @pl.when(step == 4)
            def _():
                small_copy(1, sibling).wait()
                r.small_v[2] = r.small_v[1] + r.got_small[1]
                small_copy(2, neighbour).start()

            @pl.when(step == 6)
            def _():
                small_copy(2, neighbour).wait()
                r.small_v[3] = r.small_v[2] + r.got_small[2]
                pl.loop(1, rest)(lambda j: small_rest(j).start())

            @pl.when(step == 8)
            def _():
                pl.loop(1, rest)(lambda j: small_rest(j).wait())
                total = r.small_v[3]
                for j in range(1, rest):
                    total += r.got_small[2 + j]
                r.small_out[...] = total

        last = 2 * rest + 2

        @pl.loop(0, self.chunks + self.SLACK * last)
        def _(step):
            def stage(time, action):
                c = step - self.SLACK * time

                @pl.when((c >= 0) & (c < self.chunks))
                def _():
                    action(c)

            stage(last, after_gather_half)
            stage(last - 1, after_gather_quarter)

            @pl.loop(0, rest - 1)
            def _(h):
                stage(rest + 2 + h, lambda c: hop(0, c, h, True, lambda c: gather_quarter(c).start()))
                stage(rest + 2 + h, lambda c: hop(1, c, h, True, lambda c: None))

            stage(rest + 1, after_add_up)

            @pl.loop(0, rest - 1)
            def _(h):
                stage(3 + h, lambda c: hop(0, c, h, False, scattered))
                stage(2 + h, lambda c: hop(1, c, h, False, lambda c: add_up(c).start()))

            stage(2, after_quarter)
            stage(1, after_halve)
            small_step(step)

            @pl.when(step < self.chunks)
            def _():
                @pl.loop(0, self.per_chunk)
                def _(u):
                    self.product(r, step * self.per_chunk + u)

                halve(step).start()

        for c in range(max(0, self.chunks - 2), self.chunks):
            self.wait_store(r, c)

    def __call__(self, operands, small):
        t, cells, width = self.tables, self.cells, self.width
        rest, chunks, rows, ring = self.rest, self.chunks, self.rows, self.ring
        part = rows // 4
        ff = operands["gs"].shape[-1]
        outs = {
            "win": f32(2, width, 3 * width),
            "wout": f32(2, width, width),
            "up": f32(width, ff),
            "down": f32(ff, width),
            "small_out": f32(8, width),
        }
        scratch = {
            "sums": VMEM((ring, rows, TILE), F32),
            "full": VMEM((chunks, rows, TILE), F32),
            "got_half": VMEM((chunks, rows // 2, TILE), F32),
            "got_quarter": VMEM((chunks, part // 2, TILE), F32),
            "got_sum": VMEM((chunks, part // rest, TILE), F32),
            "a_v": VMEM((2, t, 2, cells, self.BLOCK), BF16),
            "b_v": VMEM((2, t, 2, cells, TILE), BF16),
            "small_v": VMEM((4, 8, width), F32),
            "got_small": VMEM((2 + rest, 8, width), F32),
            "a_sem": dma(2, 2 * t),
            "b_sem": dma(2, 2 * t),
            "store_sem": dma(2, self.per_chunk),
            "send": dma(5, ring),
            "recv": dma(5, chunks),
            "small_send": dma(2 + rest),
            "small_recv": dma(2 + rest),
        }
        for kind, size in enumerate((part // 2 // rest, part // rest)):
            scratch[f"got_line{kind}"] = VMEM((2, chunks, rest - 1, size, TILE), F32)
            scratch[f"send_line{kind}"] = dma(4, ring, rest - 1)
            scratch[f"recv_line{kind}"] = dma(4, chunks, rest - 1)

        def body(r):
            for n in ("got_line", "send_line", "recv_line"):
                setattr(r, n, (getattr(r, n + "0"), getattr(r, n + "1")))
            self.kernel(r)

        ins = {n: (a, ANY) for n, a in operands.items()} | {"small": (small, VMEM)}
        outs = {n: (s, VMEM if n == "small_out" else ANY) for n, s in outs.items()}
        return call("weight_gradient_sum", body, 0, ins, outs, scratch)


def copied(arrays, small):
    cuts = []
    for i, a in enumerate(arrays):
        pieces = 4 if a.shape[0] % 32 == 0 else 2
        size = a.shape[0] // pieces
        cuts += [(i, slice(j * size, (j + 1) * size)) for j in range(pieces)]
    count = len(arrays)

    def kernel(*refs):
        srcs, small_ref = refs[:count], refs[count]
        dsts, gain_ref, missing_ref, sem = refs[count + 1 : -3], refs[-3], refs[-2], refs[-1]
        copies = [start(srcs[i].at[rows], dsts[i].at[rows], sem.at[n]) for n, (i, rows) in enumerate(cuts)]
        gain_ref[0] = small_ref[0:3, :]
        missing_ref[...] = small_ref[3:4, :]
        for copy in copies:
            copy.wait()

    width = small.shape[1]
    return pl.pallas_call(
        kernel,
        out_shape=[f32(*a.shape) for a in arrays] + [f32(1, 3, width), f32(1, width)],
        in_specs=[pl.BlockSpec(memory_space=ANY)] * count + [pl.BlockSpec(memory_space=VMEM)],
        out_specs=[pl.BlockSpec(memory_space=ANY)] * count + [pl.BlockSpec(memory_space=VMEM)] * 2,
        scratch_shapes=[dma(len(cuts))],
        compiler_params=pltpu.CompilerParams(vmem_limit_bytes=VMEM_LIMIT),
        name="results",
    )(*arrays, small)


def local(
    cells,
    missing_mask,
    missing_embed,
    context_rows,
    norm_gains,
    attn_in,
    attn_out,
    mlp_up,
    mlp_down,
    cotangent,
):
    tables, rows, feat, width = cells.shape
    ff = mlp_up.shape[2]
    layers = Layers(tables, rows, feat, width, ff)

    def flat(tables_of_cells):
        return jnp.swapaxes(tables_of_cells, 1, 2).reshape(tables, rows * feat, -1)

    def unflat(cells_of_tables):
        return jnp.swapaxes(cells_of_tables.reshape(tables, feat, rows, width), 1, 2)[None]

    mask = jnp.pad(flat(missing_mask == 1).astype(F32), ((0, 0), (0, layers.cells - rows * feat), (0, 0)))
    weights = (attn_in[0], attn_out[0], mlp_up[0], mlp_down[0])
    done = layers(flat(cells), mask, missing_embed[None], context_rows, norm_gains[0], weights, flat(cotangent))
    operands = {n: done[n] for n in ("as_", "os", "gs", "dys", "dzs", "dhs", "dqkvs")}
    sums = GradSum(lax.axis_size("dp"), tables, layers.cells, width, ff)(operands, done["small"])
    big = [sums["win"], sums["wout"], sums["up"], sums["down"], done["out"], done["din"]]
    big = [a.reshape(-1, a.shape[-1]) for a in big]
    win, wout, up, down, out, din, gain, missing = copied(big, sums["small_out"])
    return (
        unflat(out),
        unflat(din),
        gain,
        win.reshape(attn_in.shape),
        wout.reshape(attn_out.shape),
        up[None],
        down[None],
        missing[0],
    )


def solution(mesh):
    in_specs = (
        P("dp", None, None, None),
        P("dp", None, None),
        P(),
        P("dp"),
        P("section", None, None),
        P("section", None, None, None),
        P("section", None, None, None),
        P("section", None, None),
        P("section", None, None),
        P("dp", None, None, None),
    )
    out_specs = (
        P("section", "dp", None, None, None),
        P("section", "dp", None, None, None),
        P("section", None, None),
        P("section", None, None, None),
        P("section", None, None, None),
        P("section", None, None),
        P("section", None, None),
        P(),
    )
    return jax.shard_map(local, mesh=mesh, in_specs=in_specs, out_specs=out_specs, check_vma=False)
```

```python
import functools
from types import SimpleNamespace

import jax
import jax.numpy as jnp
from jax import lax
from jax.experimental import pallas as pl
from jax.experimental.pallas import tpu as pltpu
from jax.sharding import PartitionSpec as P

HEADS = 4
EPSILON = 1e-05
NEG = -1e30
INV_SQRT2PI = 0.3989422804014327
ERFC_P = 0.33
ERFC_C = (0.1863578482, 0.1829552331, 0.2012284886, 0.0472047191, 0.4085317677, -0.3511862269, 0.4602596132, -0.1353514118)
VMEM_LIMIT = 62 * 1024 * 1024
TILE = 512
F32, BF16 = jnp.float32, jnp.bfloat16


def dot(a, b, contract=((1,), (0,))):
    return lax.dot_general(a, b, (contract, ((), ())), preferred_element_type=F32)


def split(v):
    hi = v.astype(BF16)
    return hi, (v - hi.astype(F32)).astype(BF16)


def put(ref, index, v):
    hi, lo = split(v)
    ref[(0, *index)] = hi
    ref[(1, *index)] = lo


def parts(ref, *index):
    return ref[(0, *index)], ref[(1, *index)]


def wide(a, b, ca, cb):
    (ah, al), (bh, bl) = a, b
    return dot(jnp.concatenate([ah, ah, al], ca), jnp.concatenate([bh, bl, bh], cb), ((ca,), (cb,)))


def side(a, b):
    (ah, al), (bh, bl) = a, b
    width = bh.shape[1]
    both = dot(ah, jnp.concatenate([bh, bl], 1))
    return both[:, :width] + both[:, width:] + dot(al, bh)


def normalized(h):
    centred = h - jnp.mean(h, axis=-1, keepdims=True)
    rstd = lax.rsqrt(jnp.mean(centred * centred, axis=-1, keepdims=True) + EPSILON)
    return centred * rstd, rstd


def norm_back(n, rstd, gain, da):
    dn = da * gain
    return rstd * (dn - jnp.mean(dn, axis=-1, keepdims=True) - n * jnp.mean(dn * n, axis=-1, keepdims=True))


def cell_ids(start, count, rows, along):
    shape = (count, 1) if along == 0 else (1, count)
    at = lax.broadcasted_iota(jnp.int32, shape, along) + start
    feat = lax.shift_right_logical(at * ((1 << 20) // rows + 1), 20)
    return at - feat * rows, feat


def up16(n):
    return (n + 15) // 16 * 16


def col_blocks(rows, feat):
    cells = up16(rows * feat)
    half = up16((feat + 1) // 2 * rows)
    first_keys = min(cells, up16((((half - 1) // rows) + 1) * rows))
    second_keys = ((half // rows) * rows) // 16 * 16
    return (((0, half), (0, first_keys)), ((half, cells), (second_keys, cells)))


def lanes(j, width):
    return pl.ds(pl.multiple_of(j * width, width), width)


def start(src, dst, sem):
    copy = pltpu.make_async_copy(src, dst, sem)
    copy.start()
    return copy


def col_biases(rows, feat, context, refs, keys_along):
    for ((q0, q1), (k0, k1)), ref in zip(col_blocks(rows, feat), refs):
        _, q_feat = cell_ids(q0, q1 - q0, rows, 1 - keys_along)
        k_row, k_feat = cell_ids(k0, k1 - k0, rows, keys_along)
        ref[...] = jnp.where((q_feat == k_feat) & (k_row < context), 0.0, NEG)


def row_bias(rows, feat, ref):
    cells = up16(rows * feat)
    q_row, q_feat = cell_ids(0, cells, rows, 0)
    k_row, k_feat = cell_ids(0, cells, rows, 1)
    ref[...] = jnp.where((q_row == k_row) & ((q_feat < feat) == (k_feat < feat)), 0.0, NEG)


def gelu_parts(z):
    size = jnp.abs(z)
    below = 1.0 + (ERFC_P * 0.7071067811865476) * size
    t = pl.reciprocal(below, approx=True)
    t = t * (2.0 - below * t)
    series = jnp.full_like(t, ERFC_C[-1])
    for c in ERFC_C[-2::-1]:
        series = series * t + c
    bell = jnp.exp(-0.5 * z * z)
    tail = 0.5 * (series * t) * bell
    phi = jnp.where(z >= 0.0, 1.0 - tail, tail)
    return z * phi, phi + z * (INV_SQRT2PI * bell)


SMEM, VMEM, ANY = pltpu.SMEM, pltpu.VMEM, pl.ANY


def f32(*shape):
    return jax.ShapeDtypeStruct(shape, F32)


def b16(*shape):
    return jax.ShapeDtypeStruct(shape, BF16)


def dma(*shape):
    return pltpu.SemaphoreType.DMA(shape)


def remote(src, dst, send, recv, device):
    return pltpu.make_async_remote_copy(
        src_ref=src, dst_ref=dst, send_sem=send, recv_sem=recv, device_id=device, device_id_type=pl.DeviceIdType.MESH
    )


def call(name, body, collective_id, ins, outs, scratch):
    names = [*ins, *outs, *scratch]

    def kernel(*refs):
        body(SimpleNamespace(**dict(zip(names, refs))))

    results = pl.pallas_call(
        kernel,
        out_shape=[t for t, _ in outs.values()],
        in_specs=[pl.BlockSpec(memory_space=s) for _, s in ins.values()],
        out_specs=[pl.BlockSpec(memory_space=s) for _, s in outs.values()],
        scratch_shapes=list(scratch.values()),
        compiler_params=pltpu.CompilerParams(
            vmem_limit_bytes=VMEM_LIMIT, collective_id=collective_id, has_side_effects=True
        ),
        name=name,
    )(*(a for a, _ in ins.values()))
    return dict(zip(outs, results))


class Layers:
    def __init__(self, tables, rows, feat, width, ff):
        self.tables, self.rows, self.feat, self.width, self.ff = tables, rows, feat, width, ff
        self.real, self.cells = rows * feat, up16(rows * feat)
        self.hd = width // HEADS
        self.scale = self.hd ** (-0.5)

    def sites(self, r, site):
        if site == 1:
            return list(zip(col_blocks(self.rows, self.feat), (r.bias_a, r.bias_b)))
        return [(((0, self.cells), (0, self.cells)), r.bias_row)]

    def __call__(self, cells, mask, embed, context, gains, weights, cotangent):
        t, c, w, ff, real = self.tables, self.cells, self.width, self.ff, self.real
        ins = {
            "cells": (cells, ANY),
            "mask": (mask, VMEM),
            "embed": (embed, VMEM),
            "ctx": (context, SMEM),
            "gains": (gains, VMEM),
            "cot": (cotangent, ANY),
        }
        names = ("win", "wout", "wup", "wdown")
        ins |= {n: (a, ANY) for n, a in zip(names, weights)}
        outs = {
            "out": f32(t, real, w),
            "din": f32(t, real, w),
            "hs": f32(t, 3, c, w),
            "qkvs": b16(t, 2, 2, c, 3 * w),
            "gps": f32(t, c, ff),
            "as_": b16(t, 2, 3, c, w),
            "os": b16(t, 2, 2, c, w),
            "gs": b16(t, 2, c, ff),
            "dys": b16(t, 2, c, w),
            "dzs": b16(t, 2, c, ff),
            "dhs": b16(t, 2, 2, c, w),
            "dqkvs": b16(t, 2, 2, c, 3 * w),
        }
        outs = {n: (s, ANY) for n, s in outs.items()} | {"small": (f32(8, w), VMEM)}
        scratch = {n + "_v": VMEM((2, *a.shape), BF16) for n, a in zip(names, weights)}
        scratch |= {
            "h_v": VMEM((3, c, w), F32),
            "qkv_v": VMEM((2, 2, c, 3 * w), BF16),
            "o_v": VMEM((2, 2, c, w), BF16),
            "gp_v": VMEM((c, ff), F32),
            "g_v": VMEM((2, c, ff), BF16),
            "a_v": VMEM((2, 3, c, w), BF16),
            "y_v": VMEM((t, c, w), F32),
            "dqkv_f": VMEM((c, 3 * w), F32),
            "dys_v": VMEM((2, c, w), BF16),
            "dy_v": VMEM((c, w), F32),
            "do_v": VMEM((2, c, w), BF16),
            "got": VMEM((t, real, w), F32),
            "bias_row": VMEM((c, c), F32),
            "raw_sem": pltpu.SemaphoreType.DMA((16,)),
            "in_sem": pltpu.SemaphoreType.DMA((4,)),
            "out_sem": pltpu.SemaphoreType.DMA((16,)),
            "send": pltpu.SemaphoreType.DMA((t, 2)),
            "recv": pltpu.SemaphoreType.DMA((t, 2)),
        }
        for name, ((q0, q1), (k0, k1)) in zip(("bias_a", "bias_b"), col_blocks(self.rows, self.feat)):
            assert (q0, q1) == (k0, k1)
            scratch[name] = VMEM((q1 - q0, q1 - q0), F32)
        return call("layers", self.kernel, 1, ins, outs, scratch)

    def split_weights(self, r):
        w, ff = self.width, self.ff
        half, wide_in = w // 2, 3 * w
        top, step = slice(0, half), 64
        rest = slice(half, w)
        pieces = []
        big, bigger = r.dqkv_f.at[top], r.gp_v.at[top]
        pieces.append((r.win.at[0, top], big, r.win_v, (0,), 0, slice(None)))
        pieces.append((r.win.at[0, rest], bigger.at[:, 0:wide_in], r.win_v, (0,), half, slice(None)))
        pieces.append((r.wout.at[0, top], r.h_v.at[0, top], r.wout_v, (0,), 0, slice(None)))
        pieces.append((r.wout.at[0, rest], r.h_v.at[1, top], r.wout_v, (0,), half, slice(None)))
        pieces.append((r.wout.at[1, top], r.h_v.at[2, top], r.wout_v, (1,), 0, slice(None)))
        pieces.append((r.wout.at[1, rest], r.y_v.at[0, top], r.wout_v, (1,), half, slice(None)))
        pieces.append((r.win.at[1, top], big, r.win_v, (1,), 0, slice(None)))
        pieces.append((r.win.at[1, rest], bigger.at[:, 0:wide_in], r.win_v, (1,), half, slice(None)))
        pieces.append((r.wup.at[rest, wide_in:ff], r.dy_v.at[top, 0 : ff - wide_in], r.wup_v, (), half, slice(wide_in, ff)))
        pieces.append((r.wup.at[top], bigger, r.wup_v, (), 0, slice(None)))
        pieces.append((r.wup.at[rest, 0:wide_in], big, r.wup_v, (), half, slice(0, wide_in)))
        rows = self.cells // step * step
        buffers = [r.h_v.at[0], r.h_v.at[1], r.h_v.at[2], r.y_v.at[0], r.y_v.at[1]]
        for i, at in enumerate(range(0, ff, rows)):
            size = min(rows, ff - at)
            pieces.append((r.wdown.at[at : at + size], buffers[i].at[0:size], r.wdown_v, (), at, slice(None)))
        users = [0, 1, 2, 3, 4, 5, 0, 1, 6, 1, 0, 2, 3, 4, 5, 7][: len(pieces)]
        copies = [pltpu.make_async_copy(p[0], p[1], r.raw_sem.at[i]) for i, p in enumerate(pieces)]
        first = {u: i for i, u in reversed(list(enumerate(users)))}
        for i in sorted(first.values()):
            copies[i].start()
        for i, (_, buffer, v, lead, at, columns) in enumerate(pieces):
            copies[i].wait()

            @pl.loop(0, buffer.shape[0] // step)
            def _(j):
                src = pl.ds(pl.multiple_of(j * step, step), step)
                dst = pl.ds(pl.multiple_of(at + j * step, step), step)
                put(v, (*lead, dst, columns), buffer[src])

            later = [k for k in range(i + 1, len(pieces)) if users[k] == users[i]]
            if later:
                copies[later[0]].start()

    def kernel(self, r):
        t, real, c = self.tables, self.real, self.cells
        section = lax.axis_index("section")
        other = {"section": 1 - section}
        barrier = pltpu.get_barrier_semaphore()
        pl.semaphore_signal(barrier, inc=1, device_id=other, device_id_type=pl.DeviceIdType.MESH)
        self.split_weights(r)
        row_bias(self.rows, self.feat, r.bias_row)
        r.small[...] = jnp.zeros_like(r.small)
        pl.semaphore_wait(barrier, 1)

        def relay(table, half):
            at = slice(half * self.width // 2, (half + 1) * self.width // 2)
            src, dst = r.y_v.at[table, 0:real, at], r.got.at[table, :, at]
            return remote(src, dst, r.send.at[table, half], r.recv.at[table, half], other)

        @pl.loop(0, 2 * t)
        def _(step):
            forward = (1 - section) * (1 - step // t) + section * (1 - step % 2)
            table = (1 - section) * (step % t) + section * (step // 2)

            @pl.when(forward == 1)
            def _():
                self.forward(r, table, section, relay)

            @pl.when(forward == 0)
            def _():
                self.backward(r, table, section, relay)

        @pl.when(section == 1)
        def _():
            for table in range(t):
                for half in range(2):
                    relay(table, half).wait_send()

    def forward(self, r, table, section, relay):
        c, w, ff, hd, real = self.cells, self.width, self.ff, self.hd, self.real
        stores = []

        def keep(src, dst):
            stores.append(start(src, dst, r.out_sem.at[len(stores)]))

        r.h_v[0, real:, :] = jnp.zeros((c - real, w), F32)
        col_biases(self.rows, self.feat, r.ctx[table], (r.bias_a, r.bias_b), 1)

        @pl.when(section == 0)
        def _():
            start(r.cells.at[table], r.h_v.at[0, 0:real], r.in_sem.at[0]).wait()
            r.h_v[0] = jnp.where(r.mask[table] == 1.0, r.embed[...], r.h_v[0])

        @pl.when(section == 1)
        def _():
            start(r.cot.at[table], r.dy_v.at[0:real], r.in_sem.at[1])
            for half in range(2):
                relay(table, half).wait_recv()
            r.h_v[0, 0:real] = r.got[table]

        keep(r.h_v.at[0], r.hs.at[table, 0])
        for site in range(2):
            put(r.a_v, (site,), normalized(r.h_v[site])[0] * r.gains[site : site + 1, :])
            keep(r.a_v.at[:, site], r.as_.at[table, :, site])
            for j in range(3 * w // TILE):
                at = slice(j * TILE, (j + 1) * TILE)
                out = wide(parts(r.a_v, site), parts(r.win_v, site, slice(None), at), 1, 0)
                put(r.qkv_v, (site, slice(None), at), out)
            keep(r.qkv_v.at[:, site], r.qkvs.at[table, :, site])

            @pl.loop(0, HEADS // 2)
            def _(two):
                for head in (2 * two, 2 * two + 1):
                    for ((q0, q1), (k0, k1)), bias in self.sites(r, site):
                        q = parts(r.qkv_v, site, slice(q0, q1), lanes(head, hd))
                        k = parts(r.qkv_v, site, slice(k0, k1), lanes(HEADS + head, hd))
                        v = parts(r.qkv_v, site, slice(k0, k1), lanes(2 * HEADS + head, hd))
                        s = wide(q, k, 1, 1) * self.scale + bias[...]
                        e = jnp.exp(s - jnp.max(s, axis=-1, keepdims=True))
                        p = e * (1.0 / jnp.sum(e, axis=-1, keepdims=True))
                        put(r.o_v, (site, slice(q0, q1), lanes(head, hd)), side(split(p), v))

            keep(r.o_v.at[:, site], r.os.at[table, :, site])
            r.h_v[site + 1] = r.h_v[site] + wide(parts(r.o_v, site), parts(r.wout_v, site), 1, 0)
            keep(r.h_v.at[site + 1], r.hs.at[table, site + 1])
        put(r.a_v, (2,), normalized(r.h_v[2])[0] * r.gains[2:3, :])
        keep(r.a_v.at[:, 2], r.as_.at[table, :, 2])

        def up(j):
            return wide(parts(r.a_v, 2), parts(r.wup_v, slice(None), slice(j * TILE, (j + 1) * TILE)), 1, 0)

        tiles = ff // TILE
        z = up(0)
        for j in range(tiles):
            at = slice(j * TILE, (j + 1) * TILE)
            following = up(j + 1) if j + 1 < tiles else None
            g, gp = gelu_parts(z)
            put(r.g_v, (slice(None), at), g)
            r.gp_v[:, at] = gp
            z = following
        keep(r.g_v, r.gs.at[table])
        keep(r.gp_v, r.gps.at[table])
        for half in range(2):
            at = slice(half * w // 2, (half + 1) * w // 2)
            r.y_v[table, :, at] = r.h_v[2, :, at] + wide(parts(r.g_v), parts(r.wdown_v, slice(None), at), 1, 0)

            @pl.when(section == 0)
            def _():
                relay(table, half).start()

        keep(r.y_v.at[table, 0:real], r.out.at[table])
        for copy in stores:
            copy.wait()

    def backward(self, r, table, section, relay):
        c, w, ff, hd, real = self.cells, self.width, self.ff, self.hd, self.real
        stores = []

        def keep(src, dst):
            stores.append(start(src, dst, r.out_sem.at[len(stores)]))

        col_biases(self.rows, self.feat, r.ctx[table], (r.bias_a, r.bias_b), 0)

        @pl.when(section == 0)
        def _():
            loads = [
                start(r.hs.at[table], r.h_v, r.in_sem.at[0]),
                start(r.qkvs.at[table], r.qkv_v, r.in_sem.at[1]),
                start(r.gps.at[table], r.gp_v, r.in_sem.at[2]),
            ]
            for half in range(2):
                relay(table, half).wait()
            r.dy_v[0:real] = r.got[table]
            for copy in loads:
                copy.wait()

        @pl.when(section == 1)
        def _():
            pltpu.make_async_copy(r.cot.at[table], r.dy_v.at[0:real], r.in_sem.at[1]).wait()

        r.dy_v[real:, :] = jnp.zeros((c - real, w), F32)
        put(r.dys_v, (), r.dy_v[...])
        keep(r.dys_v, r.dys.at[table])

        def down(j):
            return wide(parts(r.dys_v), parts(r.wdown_v, slice(j * TILE, (j + 1) * TILE)), 1, 1)

        tiles = ff // TILE
        dg = down(0)
        for j in range(tiles):
            at = slice(j * TILE, (j + 1) * TILE)
            following = down(j + 1) if j + 1 < tiles else None
            put(r.g_v, (slice(None), at), dg * r.gp_v[:, at])
            dg = following
        keep(r.g_v, r.dzs.at[table])
        da = wide(parts(r.g_v), parts(r.wup_v), 1, 1)

        def through_norm(site, da):
            n, rstd = normalized(r.h_v[site])
            r.small[site : site + 1, :] += jnp.sum(da * n, axis=0, keepdims=True)
            return norm_back(n, rstd, r.gains[site : site + 1, :], da)

        r.dy_v[...] += through_norm(2, da)
        for site in (1, 0):
            put(r.o_v, (site,), r.dy_v[...])
            keep(r.o_v.at[:, site], r.dhs.at[table, :, site])
            put(r.do_v, (), wide(parts(r.o_v, site), parts(r.wout_v, site), 1, 1))

            @pl.loop(0, HEADS // 2)
            def _(two):
                for head in (2 * two, 2 * two + 1):
                    at_q, at_k, at_v = lanes(head, hd), lanes(HEADS + head, hd), lanes(2 * HEADS + head, hd)
                    for ((q0, q1), (k0, k1)), bias in self.sites(r, site):
                        q = parts(r.qkv_v, site, slice(q0, q1), at_q)
                        k = parts(r.qkv_v, site, slice(k0, k1), at_k)
                        v = parts(r.qkv_v, site, slice(k0, k1), at_v)
                        do = parts(r.do_v, slice(q0, q1), at_q)
                        s = wide(k, q, 1, 1) * self.scale + bias[...]
                        e = jnp.exp(s - jnp.max(s, axis=0, keepdims=True))
                        p = e * (1.0 / jnp.sum(e, axis=0, keepdims=True))
                        dp = wide(v, do, 1, 1)
                        ds = split(p * (dp - jnp.sum(p * dp, axis=0, keepdims=True)) * self.scale)
                        r.dqkv_f[q0:q1, at_q] = wide(tuple(x.T for x in k), ds, 1, 0).T
                        r.dqkv_f[k0:k1, at_k] = side(ds, q)
                        r.dqkv_f[k0:k1, at_v] = side(split(p), do)

            for j in range(3 * w // TILE):
                at = slice(j * TILE, (j + 1) * TILE)
                put(r.qkv_v, (site, slice(None), at), r.dqkv_f[:, at])
            keep(r.qkv_v.at[:, site], r.dqkvs.at[table, :, site])
            da = wide(parts(r.qkv_v, site), parts(r.win_v, site), 1, 1)
            r.dy_v[...] += through_norm(site, da)

        @pl.when(section == 0)
        def _():
            missing = r.mask[table] == 1.0
            r.small[3:4, :] += jnp.sum(jnp.where(missing, r.dy_v[...], 0.0), axis=0, keepdims=True)
            r.y_v[table] = jnp.where(missing, 0.0, r.dy_v[...])

        @pl.when(section == 1)
        def _():
            r.y_v[table] = r.dy_v[...]
            for half in range(2):
                relay(table, half).start()

        keep(r.y_v.at[table, 0:real], r.din.at[table])
        for copy in stores:
            copy.wait()


class GradSum:
    BLOCK = 256
    SLACK = 2

    def __init__(self, count, tables, cells, width, ff):
        self.count, self.tables, self.cells, self.width = count, tables, cells, width
        self.rest = count // 4
        shapes = [("gs", None, "dys", None, "down", None, ff, width), ("as_", 2, "dzs", None, "up", None, width, ff)]
        for site in (1, 0):
            shapes.append(("as_", site, "dqkvs", site, "win", site, width, 3 * width))
            shapes.append(("os", site, "dhs", site, "wout", site, width, width))
        self.groups, at = [], 0
        for *which, k, n in shapes:
            blocks = (k // self.BLOCK) * (n // TILE)
            self.groups.append((at, at + blocks, *which, n // TILE))
            at += blocks
        self.blocks = at
        self.per_chunk = max(1, 4 * self.rest * 8 // self.BLOCK)
        self.chunks = self.blocks // self.per_chunk
        self.rows = self.per_chunk * self.BLOCK
        self.ring = self.SLACK + 2

    def select(self, q, action):
        for group in self.groups:
            first, stop, *_, across = group

            @pl.when((q >= first) & (q < stop))
            def _():
                action(group, (q - first) // across, (q - first) % across)

    def load(self, r, q):
        slot = q % 2

        def action(group, i, j):
            _, _, left, left_site, right, right_site, *_ = group
            a, b = getattr(r, left), getattr(r, right)
            for t in range(self.tables):
                for part in range(2):
                    sem = 2 * t + part

                    def at(site):
                        return (t, part, slice(None)) if site is None else (t, part, site, slice(None))

                    start(a.at[(*at(left_site), lanes(i, self.BLOCK))], r.a_v.at[slot, t, part], r.a_sem.at[slot, sem])
                    start(b.at[(*at(right_site), lanes(j, TILE))], r.b_v.at[slot, t, part], r.b_sem.at[slot, sem])

        self.select(q, action)

    def wait_load(self, r, slot):
        for t in range(self.tables):
            for part in range(2):
                sem = 2 * t + part
                a, b = r.a_v.at[slot, t, part], r.b_v.at[slot, t, part]
                pltpu.make_async_copy(a, a, r.a_sem.at[slot, sem]).wait()
                pltpu.make_async_copy(b, b, r.b_sem.at[slot, sem]).wait()

    def product(self, r, q):
        slot = q % 2
        self.wait_load(r, slot)

        @pl.when(q + 1 < self.blocks)
        def _():
            self.load(r, q + 1)

        left, right = [], []
        for t in range(self.tables):
            (ah, al), (bh, bl) = parts(r.a_v.at[slot, t]), parts(r.b_v.at[slot, t])
            left += [ah, ah, al]
            right += [bh, bl, bh]
        rows = pl.ds(pl.multiple_of(q % self.per_chunk * self.BLOCK, self.BLOCK), self.BLOCK)
        r.products[q // self.per_chunk % self.ring, rows] = dot(jnp.concatenate(left, 0), jnp.concatenate(right, 0), ((0,), (0,)))

    def store(self, r, q):
        def action(group, i, j):
            *_, out, site, _ = group
            dst = getattr(r, out)
            rows = pl.ds(pl.multiple_of(i * self.BLOCK, self.BLOCK), self.BLOCK)
            dst = dst.at[rows, lanes(j, TILE)] if site is None else dst.at[site, rows, lanes(j, TILE)]
            u = q % self.per_chunk
            at = pl.ds(pl.multiple_of(u * self.BLOCK, self.BLOCK), self.BLOCK)
            start(r.full.at[q // self.per_chunk, at], dst, r.store_sem.at[q // self.per_chunk % 2, u])

        self.select(q, action)

    def wait_store(self, r, c):
        for u in range(self.per_chunk):
            block = r.full.at[c, u * self.BLOCK : (u + 1) * self.BLOCK]
            pltpu.make_async_copy(block, block, r.store_sem.at[c % 2, u]).wait()

    def kernel(self, r):
        rest, rows, ring = self.rest, self.rows, self.ring
        half = rows // 2
        quart = half // 2
        sizes = (quart // rest, half // rest)
        me, section = lax.axis_index("dp"), lax.axis_index("section")
        core, pair, place = me % 2, me // 2 % 2, me // 4
        sibling, neighbour = {"dp": me + 1 - 2 * core}, {"dp": me + 2 - 4 * pair}
        ways = ({"dp": me + 4}, {"dp": me - 4})

        def peer(j):
            return {"dp": lax.rem(place + j, rest) * 4 + me % 4}

        def span(at, size):
            return pl.ds(pl.multiple_of(at, size), size)

        mine = core * half
        own, other = pair * quart, (1 - pair) * quart
        bases = (own, 0)

        barrier = pltpu.get_barrier_semaphore()

        def greet(device):
            pl.semaphore_signal(barrier, inc=1, device_id=device, device_id_type=pl.DeviceIdType.MESH)

        greet({"section": 1 - section})
        greet(sibling)
        greet(neighbour)

        @pl.loop(1, rest)
        def _(j):
            greet(peer(j))

        self.load(r, 0)
        pl.semaphore_wait(barrier, rest + 2)

        def halve(c):
            src = r.products.at[c % ring, span((1 - core) * half, half)]
            return remote(src, r.sums.at[c], r.send.at[0, c % ring], r.recv.at[0, c], sibling)

        def gather_half(c):
            at = r.full.at[c, span(mine, half)]
            return remote(at, at, r.send.at[1, c % ring], r.recv.at[1, c], sibling)

        def quarter(c):
            dst = r.got_near.at[c]
            return remote(r.sums.at[c, span(other, quart)], dst, r.send.at[2, c % ring], r.recv.at[2, c], neighbour)

        def gather_quarter(c):
            at = r.full.at[c, span(mine + own, quart)]
            return remote(at, at, r.send.at[3, c % ring], r.recv.at[3, c], neighbour)

        def piece(kind, b):
            return span(bases[kind] + b * sizes[kind], sizes[kind])

        def full_piece(kind, b):
            return span(mine + bases[kind] + b * sizes[kind], sizes[kind])

        def add_up(c):
            dst = r.got_near.at[c, 0 : sizes[1]]
            return remote(r.sums.at[c, piece(1, place)], dst, r.send.at[2, c % ring], r.recv.at[2, c], neighbour)

        def line(kind, c, h, way, gather, b):
            if gather:
                src = dst = r.full.at[c, full_piece(kind, b)]
            else:
                src, dst = r.sums.at[c, piece(kind, b)], r.got_line.at[way, c, h, 0 : sizes[kind]]
            phase = 2 * way + int(gather)
            return remote(src, dst, r.send_line.at[phase, c % ring, h], r.recv_line.at[phase, c, h], ways[way])

        def hops(h, gather):
            if gather:
                right = ((place >= h) & (place < rest - 1), place - h, place >= h + 1, place - 1 - h)
                left = ((place + h < rest) & (place >= 1), place + h, place + 1 + h < rest, place + 1 + h)
            else:
                far = rest - 1 - h
                right = (place <= h, place + far, (place >= 1) & (place - 1 <= h), place - 1 + far)
                left = (rest - 1 - place <= h, place - far, (place <= rest - 2) & (rest - 2 - place <= h), place + 1 - far)
            return right, left

        def send_hop(kind, c, h, gather):
            for way, (sends, b, _, _) in enumerate(hops(h, gather)):

                @pl.when(sends)
                def _():
                    line(kind, c, h, way, gather, b).start()

        def end_hop(kind, c, h, gather):
            for way, (sends, b, receives, arriving) in enumerate(hops(h, gather)):

                @pl.when(sends)
                def _():
                    line(kind, c, h, way, gather, b).wait_send()

                @pl.when(receives)
                def _():
                    line(kind, c, h, way, gather, arriving).wait_recv()
                    if not gather:
                        r.sums[c, piece(kind, arriving)] += r.got_line[way, c, h, 0 : sizes[kind]]

        def hop(kind, c, h, gather, then):
            end_hop(kind, c, h, gather)

            @pl.when(h < rest - 2)
            def _():
                send_hop(kind, c, h + 1, gather)

            @pl.when(h == rest - 2)
            def _():
                then(c)

        def after_halve(c):
            halve(c).wait()
            r.sums[c] += r.products[c % ring, span(mine, half)]

            @pl.when(core == 0)
            def _():
                quarter(c).start()

            @pl.when(core == 1)
            def _():
                send_hop(1, c, 0, False)

        def after_quarter(c):
            quarter(c).wait()
            r.sums[c, span(own, quart)] += r.got_near[c]
            send_hop(0, c, 0, False)

        def scattered(c):
            r.full[c, full_piece(0, place)] = r.sums[c, piece(0, place)]
            send_hop(0, c, 0, True)

        def after_add_up(c):
            add_up(c).wait()
            r.full[c, full_piece(1, place)] = r.sums[c, piece(1, place)] + r.got_near[c, 0 : sizes[1]]
            send_hop(1, c, 0, True)

        def gathered(c):
            @pl.when(core == 0)
            def _():
                gather_quarter(c).wait()

            gather_half(c).start()

        def after_gather_half(c):
            gather_half(c).wait()

            @pl.when(c >= 2)
            def _():
                self.wait_store(r, c - 2)

            @pl.loop(0, self.per_chunk)
            def _(u):
                self.store(r, c * self.per_chunk + u)

        def small_copy(k, device):
            return remote(r.small_v.at[k], r.got_small.at[k], r.small_send.at[k], r.small_recv.at[k], device)

        def small_rest(j):
            dst = r.got_small.at[2 + j]
            return remote(r.small_v.at[3], dst, r.small_send.at[2 + j], r.small_recv.at[2 + j], peer(j))

        def small_step(step):
            @pl.when(step == 0)
            def _():
                r.small_v[0] = r.small[...]
                small_copy(0, {"section": 1 - section}).start()

            @pl.when(step == 2)
            def _():
                small_copy(0, {"section": 1 - section}).wait()
                row = lax.broadcasted_iota(jnp.int32, (8, self.width), 0)
                r.small_v[1] = r.small_v[0] + jnp.where(row == 3, r.got_small[0], 0.0)
                small_copy(1, sibling).start()

            @pl.when(step == 4)
            def _():
                small_copy(1, sibling).wait()
                r.small_v[2] = r.small_v[1] + r.got_small[1]
                small_copy(2, neighbour).start()

            @pl.when(step == 6)
            def _():
                small_copy(2, neighbour).wait()
                r.small_v[3] = r.small_v[2] + r.got_small[2]
                pl.loop(1, rest)(lambda j: small_rest(j).start())

            @pl.when(step == 8)
            def _():
                pl.loop(1, rest)(lambda j: small_rest(j).wait())
                total = r.small_v[3]
                for j in range(1, rest):
                    total += r.got_small[2 + j]
                r.small_out[...] = total

        last = 2 * rest + 2

        @pl.loop(0, self.chunks + self.SLACK * last)
        def _(step):
            def stage(time, action):
                c = step - self.SLACK * time

                @pl.when((c >= 0) & (c < self.chunks))
                def _():
                    action(c)

            stage(last, after_gather_half)
            stage(last - 1, gathered)

            @pl.when(core == 0)
            def _():
                @pl.loop(0, rest - 1)
                def _(h):
                    stage(rest + 2 + h, lambda c: hop(0, c, h, True, lambda c: gather_quarter(c).start()))

                @pl.loop(0, rest - 1)
                def _(h):
                    stage(3 + h, lambda c: hop(0, c, h, False, scattered))

                stage(2, after_quarter)

            @pl.when(core == 1)
            def _():
                @pl.loop(0, rest - 1)
                def _(h):
                    stage(rest + 2 + h, lambda c: hop(1, c, h, True, lambda c: None))

                stage(rest + 1, after_add_up)

                @pl.loop(0, rest - 1)
                def _(h):
                    stage(2 + h, lambda c: hop(1, c, h, False, lambda c: add_up(c).start()))

            stage(1, after_halve)
            small_step(step)

            @pl.when(step < self.chunks)
            def _():
                @pl.loop(0, self.per_chunk)
                def _(u):
                    self.product(r, step * self.per_chunk + u)

                halve(step).start()

        for c in range(max(0, self.chunks - 2), self.chunks):
            self.wait_store(r, c)

    def __call__(self, operands, small):
        t, cells, width = self.tables, self.cells, self.width
        rest, chunks, rows, ring = self.rest, self.chunks, self.rows, self.ring
        ff = operands["gs"].shape[-1]
        outs = {
            "win": f32(2, width, 3 * width),
            "wout": f32(2, width, width),
            "up": f32(width, ff),
            "down": f32(ff, width),
            "small_out": f32(8, width),
        }
        scratch = {
            "products": VMEM((ring, rows, TILE), F32),
            "sums": VMEM((chunks, rows // 2, TILE), F32),
            "full": VMEM((chunks, rows, TILE), F32),
            "got_near": VMEM((chunks, rows // 4, TILE), F32),
            "got_line": VMEM((2, chunks, rest - 1, rows // 2 // rest, TILE), F32),
            "a_v": VMEM((2, t, 2, cells, self.BLOCK), BF16),
            "b_v": VMEM((2, t, 2, cells, TILE), BF16),
            "small_v": VMEM((4, 8, width), F32),
            "got_small": VMEM((2 + rest, 8, width), F32),
            "a_sem": dma(2, 2 * t),
            "b_sem": dma(2, 2 * t),
            "store_sem": dma(2, self.per_chunk),
            "send": dma(4, ring),
            "recv": dma(4, chunks),
            "send_line": dma(4, ring, rest - 1),
            "recv_line": dma(4, chunks, rest - 1),
            "small_send": dma(2 + rest),
            "small_recv": dma(2 + rest),
        }
        ins = {n: (a, ANY) for n, a in operands.items()} | {"small": (small, VMEM)}
        outs = {n: (s, VMEM if n == "small_out" else ANY) for n, s in outs.items()}
        return call("weight_gradient_sum", self.kernel, 0, ins, outs, scratch)


def copied(arrays, small):
    cuts = []
    for i, a in enumerate(arrays):
        pieces = 4 if a.shape[0] % 32 == 0 else 2
        size = a.shape[0] // pieces
        cuts += [(i, slice(j * size, (j + 1) * size)) for j in range(pieces)]
    count = len(arrays)

    def kernel(*refs):
        srcs, small_ref = refs[:count], refs[count]
        dsts, gain_ref, missing_ref = refs[count + 1 : 2 * count + 1], refs[2 * count + 1], refs[2 * count + 2]
        buffers, sem = refs[2 * count + 3 : -1], refs[-1]
        loads = [start(srcs[i].at[rows], buffers[i].at[rows], sem.at[0, n]) for n, (i, rows) in enumerate(cuts)]
        gain_ref[0] = small_ref[0:3, :]
        missing_ref[...] = small_ref[3:4, :]
        stores = []
        for n, (i, rows) in enumerate(cuts):
            loads[n].wait()
            stores.append(start(buffers[i].at[rows], dsts[i].at[rows], sem.at[1, n]))
        for copy in stores:
            copy.wait()

    width = small.shape[1]
    return pl.pallas_call(
        kernel,
        out_shape=[f32(*a.shape) for a in arrays] + [f32(1, 3, width), f32(1, width)],
        in_specs=[pl.BlockSpec(memory_space=ANY)] * count + [pl.BlockSpec(memory_space=VMEM)],
        out_specs=[pl.BlockSpec(memory_space=ANY)] * count + [pl.BlockSpec(memory_space=VMEM)] * 2,
        scratch_shapes=[VMEM(a.shape, F32) for a in arrays] + [dma(2, len(cuts))],
        compiler_params=pltpu.CompilerParams(vmem_limit_bytes=VMEM_LIMIT),
        name="results",
    )(*arrays, small)


def local(
    cells,
    missing_mask,
    missing_embed,
    context_rows,
    norm_gains,
    attn_in,
    attn_out,
    mlp_up,
    mlp_down,
    cotangent,
):
    tables, rows, feat, width = cells.shape
    ff = mlp_up.shape[2]
    layers = Layers(tables, rows, feat, width, ff)

    def flat(tables_of_cells):
        return jnp.swapaxes(tables_of_cells, 1, 2).reshape(tables, rows * feat, -1)

    def unflat(cells_of_tables):
        return jnp.swapaxes(cells_of_tables.reshape(tables, feat, rows, width), 1, 2)[None]

    mask = jnp.pad(flat(missing_mask == 1).astype(F32), ((0, 0), (0, layers.cells - rows * feat), (0, 0)))
    weights = (attn_in[0], attn_out[0], mlp_up[0], mlp_down[0])
    done = layers(flat(cells), mask, missing_embed[None], context_rows, norm_gains[0], weights, flat(cotangent))
    operands = {n: done[n] for n in ("as_", "os", "gs", "dys", "dzs", "dhs", "dqkvs")}
    sums = GradSum(lax.axis_size("dp"), tables, layers.cells, width, ff)(operands, done["small"])
    big = [sums["win"], sums["wout"], sums["up"], sums["down"], done["out"], done["din"]]
    big = [a.reshape(-1, a.shape[-1]) for a in big]
    win, wout, up, down, out, din, gain, missing = copied(big, sums["small_out"])
    return (
        unflat(out),
        unflat(din),
        gain,
        win.reshape(attn_in.shape),
        wout.reshape(attn_out.shape),
        up[None],
        down[None],
        missing[0],
    )


def solution(mesh):
    in_specs = (
        P("dp", None, None, None),
        P("dp", None, None),
        P(),
        P("dp"),
        P("section", None, None),
        P("section", None, None, None),
        P("section", None, None, None),
        P("section", None, None),
        P("section", None, None),
        P("dp", None, None, None),
    )
    out_specs = (
        P("section", "dp", None, None, None),
        P("section", "dp", None, None, None),
        P("section", None, None),
        P("section", None, None, None),
        P("section", None, None, None),
        P("section", None, None),
        P("section", None, None),
        P(),
    )
    return jax.shard_map(local, mesh=mesh, in_specs=in_specs, out_specs=out_specs, check_vma=False)
```

```python
import functools
from types import SimpleNamespace

import jax
import jax.numpy as jnp
from jax import lax
from jax.experimental import pallas as pl
from jax.experimental.pallas import tpu as pltpu
from jax.sharding import PartitionSpec as P

HEADS = 4
EPSILON = 1e-05
NEG = -1e30
INV_SQRT2PI = 0.3989422804014327
LOG2E = 1.4426950408889634
LN2 = 0.6931471805599453
ERFC_P = 0.33
ERFC_C = (0.1863578482, 0.1829552331, 0.2012284886, 0.0472047191, 0.4085317677, -0.3511862269, 0.4602596132, -0.1353514118)
VMEM_LIMIT = 62 * 1024 * 1024
TILE = 512
F32, BF16 = jnp.float32, jnp.bfloat16


def dot(a, b, contract=((1,), (0,))):
    return lax.dot_general(a, b, (contract, ((), ())), preferred_element_type=F32)


def split(v):
    hi = v.astype(BF16)
    return hi, (v - hi.astype(F32)).astype(BF16)


def put(ref, index, v):
    hi, lo = split(v)
    ref[(0, *index)] = hi
    ref[(1, *index)] = lo


def parts(ref, *index):
    return ref[(0, *index)], ref[(1, *index)]


def wide(a, b, ca, cb):
    (ah, al), (bh, bl) = a, b
    return dot(jnp.concatenate([ah, ah, al], ca), jnp.concatenate([bh, bl, bh], cb), ((ca,), (cb,)))


def side(a, b):
    (ah, al), (bh, bl) = a, b
    width = bh.shape[1]
    both = dot(ah, jnp.concatenate([bh, bl], 1))
    return both[:, :width] + both[:, width:] + dot(al, bh)


def normalized(h):
    centred = h - jnp.mean(h, axis=-1, keepdims=True)
    rstd = lax.rsqrt(jnp.mean(centred * centred, axis=-1, keepdims=True) + EPSILON)
    return centred * rstd, rstd


def norm_back(n, rstd, gain, da):
    dn = da * gain
    return rstd * (dn - jnp.mean(dn, axis=-1, keepdims=True) - n * jnp.mean(dn * n, axis=-1, keepdims=True))


def cell_ids(start, count, rows, along):
    shape = (count, 1) if along == 0 else (1, count)
    at = lax.broadcasted_iota(jnp.int32, shape, along) + start
    feat = lax.shift_right_logical(at * ((1 << 20) // rows + 1), 20)
    return at - feat * rows, feat


def up16(n):
    return (n + 15) // 16 * 16


def col_blocks(rows, feat):
    cells = up16(rows * feat)
    half = up16((feat + 1) // 2 * rows)
    first_keys = min(cells, up16((((half - 1) // rows) + 1) * rows))
    second_keys = ((half // rows) * rows) // 16 * 16
    return (((0, half), (0, first_keys)), ((half, cells), (second_keys, cells)))


def staggered(units, *steps):
    state = [None] * len(units)
    for i in range(len(units) + 1):
        if i < len(units):
            state[i] = steps[0](*units[i])
        if i > 0:
            for step in steps[1:]:
                state[i - 1] = step(*units[i - 1], state[i - 1])


def lanes(j, width):
    return pl.ds(pl.multiple_of(j * width, width), width)


def start(src, dst, sem):
    copy = pltpu.make_async_copy(src, dst, sem)
    copy.start()
    return copy


def col_biases(rows, feat, context, refs, keys_along):
    for ((q0, q1), (k0, k1)), ref in zip(col_blocks(rows, feat), refs):
        _, q_feat = cell_ids(q0, q1 - q0, rows, 1 - keys_along)
        k_row, k_feat = cell_ids(k0, k1 - k0, rows, keys_along)
        ref[...] = jnp.where((q_feat == k_feat) & (k_row < context), 0.0, NEG)


def row_bias(rows, feat, ref):
    cells = up16(rows * feat)
    q_row, q_feat = cell_ids(0, cells, rows, 0)
    k_row, k_feat = cell_ids(0, cells, rows, 1)
    ref[...] = jnp.where((q_row == k_row) & ((q_feat < feat) == (k_feat < feat)), 0.0, NEG)


def gelu_parts(z):
    size = jnp.abs(z)
    below = 1.0 + (ERFC_P * 0.7071067811865476) * size
    t = pl.reciprocal(below, approx=True)
    t = t * (2.0 - below * t)
    series = jnp.full_like(t, ERFC_C[-1])
    for c in ERFC_C[-2::-1]:
        series = series * t + c
    bell = jnp.exp(-0.5 * z * z)
    tail = 0.5 * (series * t) * bell
    phi = jnp.where(z >= 0.0, 1.0 - tail, tail)
    return z * phi, phi + z * (INV_SQRT2PI * bell)


SMEM, VMEM, ANY = pltpu.SMEM, pltpu.VMEM, pl.ANY


def f32(*shape):
    return jax.ShapeDtypeStruct(shape, F32)


def b16(*shape):
    return jax.ShapeDtypeStruct(shape, BF16)


def dma(*shape):
    return pltpu.SemaphoreType.DMA(shape)


def remote(src, dst, send, recv, device):
    return pltpu.make_async_remote_copy(
        src_ref=src, dst_ref=dst, send_sem=send, recv_sem=recv, device_id=device, device_id_type=pl.DeviceIdType.MESH
    )


def call(name, body, collective_id, ins, outs, scratch):
    names = [*ins, *outs, *scratch]

    def kernel(*refs):
        body(SimpleNamespace(**dict(zip(names, refs))))

    results = pl.pallas_call(
        kernel,
        out_shape=[t for t, _ in outs.values()],
        in_specs=[pl.BlockSpec(memory_space=s) for _, s in ins.values()],
        out_specs=[pl.BlockSpec(memory_space=s) for _, s in outs.values()],
        scratch_shapes=list(scratch.values()),
        compiler_params=pltpu.CompilerParams(
            vmem_limit_bytes=VMEM_LIMIT, collective_id=collective_id, has_side_effects=True
        ),
        name=name,
    )(*(a for a, _ in ins.values()))
    return dict(zip(outs, results))


class Layers:
    def __init__(self, tables, rows, feat, width, ff):
        self.tables, self.rows, self.feat, self.width, self.ff = tables, rows, feat, width, ff
        self.real, self.cells = rows * feat, up16(rows * feat)
        self.hd = width // HEADS
        self.scale = self.hd ** (-0.5)

    def sites(self, r, site):
        if site == 1:
            return [(slice(*q), bias) for (q, _), bias in zip(col_blocks(self.rows, self.feat), (r.bias_a, r.bias_b))]
        return [(slice(0, self.cells), r.bias_row)]

    def __call__(self, cells, mask, embed, context, gains, weights, cotangent):
        t, c, w, ff, real = self.tables, self.cells, self.width, self.ff, self.real
        ins = {
            "cells": (cells, ANY),
            "mask": (mask, VMEM),
            "embed": (embed, VMEM),
            "ctx": (context, SMEM),
            "gains": (gains, VMEM),
            "cot": (cotangent, ANY),
        }
        names = ("win", "wout", "wup", "wdown")
        ins |= {n: (a, ANY) for n, a in zip(names, weights)}
        outs = {
            "out": f32(t, real, w),
            "din": f32(t, real, w),
            "hs": f32(t, 3, c, w),
            "qkvs": b16(t, 2, 2, c, 3 * w),
            "gps": f32(t, c, ff),
            "as_": b16(t, 2, 3, c, w),
            "os": b16(t, 2, 2, c, w),
            "gs": b16(t, 2, c, ff),
            "dys": b16(t, 2, c, w),
            "dzs": b16(t, 2, c, ff),
            "dhs": b16(t, 2, 2, c, w),
            "dqkvs": b16(t, 2, 2, c, 3 * w),
        }
        outs = {n: (s, ANY) for n, s in outs.items()} | {"small": (f32(8, w), VMEM)}
        scratch = {n + "_v": VMEM((2, *a.shape), BF16) for n, a in zip(names, weights)}
        scratch |= {
            "h_v": VMEM((3, c, w), F32),
            "qkv_v": VMEM((2, 2, c, 3 * w), BF16),
            "o_v": VMEM((2, 2, c, w), BF16),
            "gp_v": VMEM((c, ff), F32),
            "g_v": VMEM((2, c, ff), BF16),
            "a_v": VMEM((2, 3, c, w), BF16),
            "y_v": VMEM((t, c, w), F32),
            "dqkv_f": VMEM((c, 3 * w), F32),
            "dys_v": VMEM((2, c, w), BF16),
            "dy_v": VMEM((c, w), F32),
            "do_v": VMEM((2, c, w), BF16),
            "got": VMEM((t, real, w), F32),
            "bias_row": VMEM((c, c), F32),
            "stat_v": VMEM((c, 128), F32),
            "lse_v": VMEM((t, 2 * HEADS, c), F32),
            "raw_sem": pltpu.SemaphoreType.DMA((16,)),
            "in_sem": pltpu.SemaphoreType.DMA((4,)),
            "out_sem": pltpu.SemaphoreType.DMA((16,)),
            "send": pltpu.SemaphoreType.DMA((t, 2)),
            "recv": pltpu.SemaphoreType.DMA((t, 2)),
        }
        for name, ((q0, q1), (k0, k1)) in zip(("bias_a", "bias_b"), col_blocks(self.rows, self.feat)):
            assert (q0, q1) == (k0, k1)
            scratch[name] = VMEM((q1 - q0, q1 - q0), F32)
        return call("layers", self.kernel, 1, ins, outs, scratch)

    def split_weights(self, r):
        w, ff = self.width, self.ff
        half, wide_in = w // 2, 3 * w
        top, step = slice(0, half), 64
        rest = slice(half, w)
        pieces = []
        big, bigger = r.dqkv_f.at[top], r.gp_v.at[top]
        pieces.append((r.win.at[0, top], big, r.win_v, (0,), 0, slice(None)))
        pieces.append((r.win.at[0, rest], bigger.at[:, 0:wide_in], r.win_v, (0,), half, slice(None)))
        pieces.append((r.wout.at[0, top], r.h_v.at[0, top], r.wout_v, (0,), 0, slice(None)))
        pieces.append((r.wout.at[0, rest], r.h_v.at[1, top], r.wout_v, (0,), half, slice(None)))
        pieces.append((r.wout.at[1, top], r.h_v.at[2, top], r.wout_v, (1,), 0, slice(None)))
        pieces.append((r.wout.at[1, rest], r.y_v.at[0, top], r.wout_v, (1,), half, slice(None)))
        pieces.append((r.win.at[1, top], big, r.win_v, (1,), 0, slice(None)))
        pieces.append((r.win.at[1, rest], bigger.at[:, 0:wide_in], r.win_v, (1,), half, slice(None)))
        pieces.append((r.wup.at[rest, wide_in:ff], r.dy_v.at[top, 0 : ff - wide_in], r.wup_v, (), half, slice(wide_in, ff)))
        pieces.append((r.wup.at[top], bigger, r.wup_v, (), 0, slice(None)))
        pieces.append((r.wup.at[rest, 0:wide_in], big, r.wup_v, (), half, slice(0, wide_in)))
        rows = self.cells // step * step
        buffers = [r.h_v.at[0], r.h_v.at[1], r.h_v.at[2], r.y_v.at[0], r.y_v.at[1]]
        for i, at in enumerate(range(0, ff, rows)):
            size = min(rows, ff - at)
            pieces.append((r.wdown.at[at : at + size], buffers[i].at[0:size], r.wdown_v, (), at, slice(None)))
        users = [0, 1, 2, 3, 4, 5, 0, 1, 6, 1, 0, 2, 3, 4, 5, 7][: len(pieces)]
        copies = [pltpu.make_async_copy(p[0], p[1], r.raw_sem.at[i]) for i, p in enumerate(pieces)]
        first = {u: i for i, u in reversed(list(enumerate(users)))}
        for i in sorted(first.values()):
            copies[i].start()
        for i, (_, buffer, v, lead, at, columns) in enumerate(pieces):
            copies[i].wait()

            @pl.loop(0, buffer.shape[0] // step)
            def _(j):
                src = pl.ds(pl.multiple_of(j * step, step), step)
                dst = pl.ds(pl.multiple_of(at + j * step, step), step)
                put(v, (*lead, dst, columns), buffer[src])

            later = [k for k in range(i + 1, len(pieces)) if users[k] == users[i]]
            if later:
                copies[later[0]].start()

    def kernel(self, r):
        t, real, c = self.tables, self.real, self.cells
        section = lax.axis_index("section")
        other = {"section": 1 - section}
        barrier = pltpu.get_barrier_semaphore()
        pl.semaphore_signal(barrier, inc=1, device_id=other, device_id_type=pl.DeviceIdType.MESH)
        self.split_weights(r)
        row_bias(self.rows, self.feat, r.bias_row)
        r.small[...] = jnp.zeros_like(r.small)
        pl.semaphore_wait(barrier, 1)

        def relay(table, half):
            at = slice(half * self.width // 2, (half + 1) * self.width // 2)
            src, dst = r.y_v.at[table, 0:real, at], r.got.at[table, :, at]
            return remote(src, dst, r.send.at[table, half], r.recv.at[table, half], other)

        @pl.loop(0, 2 * t)
        def _(step):
            forward = (1 - section) * (1 - step // t) + section * (1 - step % 2)
            table = (1 - section) * (step % t) + section * (step // 2)

            @pl.when(forward == 1)
            def _():
                self.forward(r, table, section, relay)

            @pl.when(forward == 0)
            def _():
                self.backward(r, table, section, relay)

        @pl.when(section == 1)
        def _():
            for table in range(t):
                for half in range(2):
                    relay(table, half).wait_send()

    def forward(self, r, table, section, relay):
        c, w, ff, hd, real = self.cells, self.width, self.ff, self.hd, self.real
        stores = []

        def keep(src, dst):
            stores.append(start(src, dst, r.out_sem.at[len(stores)]))

        r.h_v[0, real:, :] = jnp.zeros((c - real, w), F32)
        col_biases(self.rows, self.feat, r.ctx[table], (r.bias_a, r.bias_b), 1)

        @pl.when(section == 0)
        def _():
            start(r.cells.at[table], r.h_v.at[0, 0:real], r.in_sem.at[0]).wait()
            r.h_v[0] = jnp.where(r.mask[table] == 1.0, r.embed[...], r.h_v[0])

        @pl.when(section == 1)
        def _():
            start(r.cot.at[table], r.dy_v.at[0:real], r.in_sem.at[1])
            for half in range(2):
                relay(table, half).wait_recv()
            r.h_v[0, 0:real] = r.got[table]

        keep(r.h_v.at[0], r.hs.at[table, 0])
        for site in range(2):
            put(r.a_v, (site,), normalized(r.h_v[site])[0] * r.gains[site : site + 1, :])
            keep(r.a_v.at[:, site], r.as_.at[table, :, site])

            def project(j):
                at = slice(j * TILE, (j + 1) * TILE)
                return wide(parts(r.a_v, site), parts(r.win_v, site, slice(None), at), 1, 0)

            def keep_projected(j, out):
                if j < w // TILE:
                    out = out * (self.scale * LOG2E)
                put(r.qkv_v, (site, slice(None), slice(j * TILE, (j + 1) * TILE)), out)

            staggered([(j,) for j in range(3 * w // TILE)], project, keep_projected)
            keep(r.qkv_v.at[:, site], r.qkvs.at[table, :, site])

            def scores(head, span, bias):
                q = parts(r.qkv_v, site, span, lanes(head, hd))
                k = parts(r.qkv_v, site, span, lanes(HEADS + head, hd))
                return wide(q, k, 1, 1)

            def softmax(head, span, bias, s):
                s = s + bias[...]
                top = jnp.max(s, axis=-1, keepdims=True)
                e = jnp.exp2(s - top)
                total = jnp.sum(e, axis=-1, keepdims=True)
                column = lax.broadcasted_iota(jnp.int32, (1, r.stat_v.shape[1]), 1) == site * HEADS + head
                r.stat_v[span, :] = jnp.where(column, top + jnp.log2(total), r.stat_v[span, :])
                return split(e), 1.0 / total

            def blend(head, span, bias, state):
                e, inverse = state
                v = parts(r.qkv_v, site, span, lanes(2 * HEADS + head, hd))
                put(r.o_v, (site, span, lanes(head, hd)), side(e, v) * inverse)

            @pl.loop(0, HEADS // 2)
            def _(two):
                units = [(head, *unit) for head in (2 * two, 2 * two + 1) for unit in self.sites(r, site)]
                staggered(units, scores, softmax, blend)

            keep(r.o_v.at[:, site], r.os.at[table, :, site])
            r.h_v[site + 1] = r.h_v[site] + wide(parts(r.o_v, site), parts(r.wout_v, site), 1, 0)
            keep(r.h_v.at[site + 1], r.hs.at[table, site + 1])
        r.lse_v[table] = r.stat_v[...].T[0 : 2 * HEADS]
        put(r.a_v, (2,), normalized(r.h_v[2])[0] * r.gains[2:3, :])
        keep(r.a_v.at[:, 2], r.as_.at[table, :, 2])

        def up(j):
            return wide(parts(r.a_v, 2), parts(r.wup_v, slice(None), slice(j * TILE, (j + 1) * TILE)), 1, 0)

        tiles = ff // TILE
        z = up(0)
        for j in range(tiles):
            at = slice(j * TILE, (j + 1) * TILE)
            following = up(j + 1) if j + 1 < tiles else None
            g, gp = gelu_parts(z)
            put(r.g_v, (slice(None), at), g)
            r.gp_v[:, at] = gp
            z = following
        keep(r.g_v, r.gs.at[table])
        keep(r.gp_v, r.gps.at[table])
        for half in range(2):
            at = slice(half * w // 2, (half + 1) * w // 2)
            r.y_v[table, :, at] = r.h_v[2, :, at] + wide(parts(r.g_v), parts(r.wdown_v, slice(None), at), 1, 0)

            @pl.when(section == 0)
            def _():
                relay(table, half).start()

        keep(r.y_v.at[table, 0:real], r.out.at[table])
        for copy in stores:
            copy.wait()

    def backward(self, r, table, section, relay):
        c, w, ff, hd, real = self.cells, self.width, self.ff, self.hd, self.real
        stores = []

        def keep(src, dst):
            stores.append(start(src, dst, r.out_sem.at[len(stores)]))

        col_biases(self.rows, self.feat, r.ctx[table], (r.bias_a, r.bias_b), 0)

        @pl.when(section == 0)
        def _():
            loads = [
                start(r.hs.at[table], r.h_v, r.in_sem.at[0]),
                start(r.qkvs.at[table], r.qkv_v, r.in_sem.at[1]),
                start(r.gps.at[table], r.gp_v, r.in_sem.at[2]),
            ]
            for half in range(2):
                relay(table, half).wait()
            r.dy_v[0:real] = r.got[table]
            for copy in loads:
                copy.wait()

        @pl.when(section == 1)
        def _():
            pltpu.make_async_copy(r.cot.at[table], r.dy_v.at[0:real], r.in_sem.at[1]).wait()

        r.dy_v[real:, :] = jnp.zeros((c - real, w), F32)
        put(r.dys_v, (), r.dy_v[...])
        keep(r.dys_v, r.dys.at[table])

        def down(j):
            return wide(parts(r.dys_v), parts(r.wdown_v, slice(j * TILE, (j + 1) * TILE)), 1, 1)

        tiles = ff // TILE
        dg = down(0)
        for j in range(tiles):
            at = slice(j * TILE, (j + 1) * TILE)
            following = down(j + 1) if j + 1 < tiles else None
            put(r.g_v, (slice(None), at), dg * r.gp_v[:, at])
            dg = following
        keep(r.g_v, r.dzs.at[table])
        da = wide(parts(r.g_v), parts(r.wup_v), 1, 1)

        def through_norm(site, da):
            n, rstd = normalized(r.h_v[site])
            r.small[site : site + 1, :] += jnp.sum(da * n, axis=0, keepdims=True)
            return norm_back(n, rstd, r.gains[site : site + 1, :], da)

        r.dy_v[...] += through_norm(2, da)
        for site in (1, 0):
            put(r.o_v, (site,), r.dy_v[...])
            keep(r.o_v.at[:, site], r.dhs.at[table, :, site])
            put(r.do_v, (), wide(parts(r.o_v, site), parts(r.wout_v, site), 1, 1))

            def part_of(which, head, span):
                return parts(r.qkv_v, site, span, lanes(which * HEADS + head, hd))

            def products(head, span, bias):
                do = parts(r.do_v, span, lanes(head, hd))
                s = wide(part_of(1, head, span), part_of(0, head, span), 1, 1)
                return s, wide(part_of(2, head, span), do, 1, 1)

            def gradients(head, span, bias, state):
                s, dp = state
                p = jnp.exp2(s + bias[...] - r.lse_v[table, pl.ds(site * HEADS + head, 1), span])
                ds = p * (dp - jnp.sum(p * dp, axis=0, keepdims=True))
                return split(p), split(ds)

            def back(head, span, bias, state):
                p, ds = state
                k = part_of(1, head, span)
                r.dqkv_f[span, lanes(head, hd)] = (wide(tuple(x.T for x in k), ds, 1, 0) * self.scale).T
                r.dqkv_f[span, lanes(HEADS + head, hd)] = side(ds, part_of(0, head, span)) * LN2
                r.dqkv_f[span, lanes(2 * HEADS + head, hd)] = side(p, parts(r.do_v, span, lanes(head, hd)))

            @pl.loop(0, HEADS // 2)
            def _(two):
                units = [(head, *unit) for head in (2 * two, 2 * two + 1) for unit in self.sites(r, site)]
                staggered(units, products, gradients, back)

            for j in range(3 * w // TILE):
                at = slice(j * TILE, (j + 1) * TILE)
                put(r.qkv_v, (site, slice(None), at), r.dqkv_f[:, at])
            keep(r.qkv_v.at[:, site], r.dqkvs.at[table, :, site])
            da = wide(parts(r.qkv_v, site), parts(r.win_v, site), 1, 1)
            r.dy_v[...] += through_norm(site, da)

        @pl.when(section == 0)
        def _():
            missing = r.mask[table] == 1.0
            r.small[3:4, :] += jnp.sum(jnp.where(missing, r.dy_v[...], 0.0), axis=0, keepdims=True)
            r.y_v[table] = jnp.where(missing, 0.0, r.dy_v[...])

        @pl.when(section == 1)
        def _():
            r.y_v[table] = r.dy_v[...]
            for half in range(2):
                relay(table, half).start()

        keep(r.y_v.at[table, 0:real], r.din.at[table])
        for copy in stores:
            copy.wait()


class GradSum:
    BLOCK = 256
    SLACK = 2

    def __init__(self, count, tables, cells, width, ff):
        self.count, self.tables, self.cells, self.width = count, tables, cells, width
        self.rest = count // 4
        shapes = [("gs", None, "dys", None, "down", None, ff, width), ("as_", 2, "dzs", None, "up", None, width, ff)]
        for site in (1, 0):
            shapes.append(("as_", site, "dqkvs", site, "win", site, width, 3 * width))
            shapes.append(("os", site, "dhs", site, "wout", site, width, width))
        self.groups, at = [], 0
        for *which, k, n in shapes:
            blocks = (k // self.BLOCK) * (n // TILE)
            self.groups.append((at, at + blocks, *which, n // TILE))
            at += blocks
        self.blocks = at
        self.per_chunk = max(1, 4 * self.rest * 8 // self.BLOCK)
        self.chunks = self.blocks // self.per_chunk
        self.rows = self.per_chunk * self.BLOCK
        self.ring = self.SLACK + 2

    def select(self, q, action):
        for group in self.groups:
            first, stop, *_, across = group

            @pl.when((q >= first) & (q < stop))
            def _():
                action(group, (q - first) // across, (q - first) % across)

    def load(self, r, q):
        slot = q % 2

        def action(group, i, j):
            _, _, left, left_site, right, right_site, *_ = group
            a, b = getattr(r, left), getattr(r, right)
            for t in range(self.tables):
                for part in range(2):
                    sem = 2 * t + part

                    def at(site):
                        return (t, part, slice(None)) if site is None else (t, part, site, slice(None))

                    start(a.at[(*at(left_site), lanes(i, self.BLOCK))], r.a_v.at[slot, t, part], r.a_sem.at[slot, sem])
                    start(b.at[(*at(right_site), lanes(j, TILE))], r.b_v.at[slot, t, part], r.b_sem.at[slot, sem])

        self.select(q, action)

    def wait_load(self, r, slot):
        for t in range(self.tables):
            for part in range(2):
                sem = 2 * t + part
                a, b = r.a_v.at[slot, t, part], r.b_v.at[slot, t, part]
                pltpu.make_async_copy(a, a, r.a_sem.at[slot, sem]).wait()
                pltpu.make_async_copy(b, b, r.b_sem.at[slot, sem]).wait()

    def product(self, r, q):
        slot = q % 2
        self.wait_load(r, slot)

        @pl.when(q + 1 < self.blocks)
        def _():
            self.load(r, q + 1)

        left, right = [], []
        for t in range(self.tables):
            (ah, al), (bh, bl) = parts(r.a_v.at[slot, t]), parts(r.b_v.at[slot, t])
            left += [ah, ah, al]
            right += [bh, bl, bh]
        rows = pl.ds(pl.multiple_of(q % self.per_chunk * self.BLOCK, self.BLOCK), self.BLOCK)
        r.products[q // self.per_chunk % self.ring, rows] = dot(jnp.concatenate(left, 0), jnp.concatenate(right, 0), ((0,), (0,)))

    def store(self, r, q):
        def action(group, i, j):
            *_, out, site, _ = group
            dst = getattr(r, out)
            rows = pl.ds(pl.multiple_of(i * self.BLOCK, self.BLOCK), self.BLOCK)
            dst = dst.at[rows, lanes(j, TILE)] if site is None else dst.at[site, rows, lanes(j, TILE)]
            u = q % self.per_chunk
            at = pl.ds(pl.multiple_of(u * self.BLOCK, self.BLOCK), self.BLOCK)
            start(r.full.at[q // self.per_chunk, at], dst, r.store_sem.at[q // self.per_chunk % 2, u])

        self.select(q, action)

    def wait_store(self, r, c):
        for u in range(self.per_chunk):
            block = r.full.at[c, u * self.BLOCK : (u + 1) * self.BLOCK]
            pltpu.make_async_copy(block, block, r.store_sem.at[c % 2, u]).wait()

    def kernel(self, r):
        rest, rows, ring = self.rest, self.rows, self.ring
        half = rows // 2
        quart = half // 2
        sizes = (quart // rest, half // rest)
        me = lax.axis_index("dp")
        core, pair, place = me % 2, me // 2 % 2, me // 4
        sibling, neighbour = {"dp": me + 1 - 2 * core}, {"dp": me + 2 - 4 * pair}
        ways = ({"dp": me + 4}, {"dp": me - 4})

        def peer(j):
            return {"dp": lax.rem(place + j, rest) * 4 + me % 4}

        def span(at, size):
            return pl.ds(pl.multiple_of(at, size), size)

        mine = core * half
        own, other = pair * quart, (1 - pair) * quart
        bases = (own, 0)

        barrier = pltpu.get_barrier_semaphore()

        def greet(device):
            pl.semaphore_signal(barrier, inc=1, device_id=device, device_id_type=pl.DeviceIdType.MESH)

        greet(sibling)
        greet(neighbour)

        @pl.loop(1, rest)
        def _(j):
            greet(peer(j))

        self.load(r, 0)
        pl.semaphore_wait(barrier, rest + 1)

        def halve(c):
            src = r.products.at[c % ring, span((1 - core) * half, half)]
            return remote(src, r.sums.at[c], r.send.at[0, c % ring], r.recv.at[0, c], sibling)

        def gather_half(c):
            at = r.full.at[c, span(mine, half)]
            return remote(at, at, r.send.at[1, c % ring], r.recv.at[1, c], sibling)

        def quarter(c):
            dst = r.got_near.at[c]
            return remote(r.sums.at[c, span(other, quart)], dst, r.send.at[2, c % ring], r.recv.at[2, c], neighbour)

        def gather_quarter(c):
            at = r.full.at[c, span(mine + own, quart)]
            return remote(at, at, r.send.at[3, c % ring], r.recv.at[3, c], neighbour)

        def piece(kind, b):
            return span(bases[kind] + b * sizes[kind], sizes[kind])

        def full_piece(kind, b):
            return span(mine + bases[kind] + b * sizes[kind], sizes[kind])

        def add_up(c):
            dst = r.got_near.at[c, 0 : sizes[1]]
            return remote(r.sums.at[c, piece(1, place)], dst, r.send.at[2, c % ring], r.recv.at[2, c], neighbour)

        def line(kind, c, h, way, gather, b):
            if gather:
                src = dst = r.full.at[c, full_piece(kind, b)]
            else:
                src, dst = r.sums.at[c, piece(kind, b)], r.got_line.at[way, c, h, 0 : sizes[kind]]
            phase = 2 * way + int(gather)
            return remote(src, dst, r.send_line.at[phase, c % ring, h], r.recv_line.at[phase, c, h], ways[way])

        def hops(h, gather):
            if gather:
                right = ((place >= h) & (place < rest - 1), place - h, place >= h + 1, place - 1 - h)
                left = ((place + h < rest) & (place >= 1), place + h, place + 1 + h < rest, place + 1 + h)
            else:
                far = rest - 1 - h
                right = (place <= h, place + far, (place >= 1) & (place - 1 <= h), place - 1 + far)
                left = (rest - 1 - place <= h, place - far, (place <= rest - 2) & (rest - 2 - place <= h), place + 1 - far)
            return right, left

        def send_hop(kind, c, h, gather):
            for way, (sends, b, _, _) in enumerate(hops(h, gather)):

                @pl.when(sends)
                def _():
                    line(kind, c, h, way, gather, b).start()

        def end_hop(kind, c, h, gather):
            for way, (sends, b, receives, arriving) in enumerate(hops(h, gather)):

                @pl.when(sends)
                def _():
                    line(kind, c, h, way, gather, b).wait_send()

                @pl.when(receives)
                def _():
                    line(kind, c, h, way, gather, arriving).wait_recv()
                    if not gather:
                        r.sums[c, piece(kind, arriving)] += r.got_line[way, c, h, 0 : sizes[kind]]

        def hop(kind, c, h, gather, then):
            end_hop(kind, c, h, gather)

            @pl.when(h < rest - 2)
            def _():
                send_hop(kind, c, h + 1, gather)

            @pl.when(h == rest - 2)
            def _():
                then(c)

        def after_halve(c):
            halve(c).wait()
            r.sums[c] += r.products[c % ring, span(mine, half)]

            @pl.when(core == 0)
            def _():
                quarter(c).start()

            @pl.when(core == 1)
            def _():
                send_hop(1, c, 0, False)

        def after_quarter(c):
            quarter(c).wait()
            r.sums[c, span(own, quart)] += r.got_near[c]
            send_hop(0, c, 0, False)

        def scattered(c):
            r.full[c, full_piece(0, place)] = r.sums[c, piece(0, place)]
            send_hop(0, c, 0, True)

        def after_add_up(c):
            add_up(c).wait()
            r.full[c, full_piece(1, place)] = r.sums[c, piece(1, place)] + r.got_near[c, 0 : sizes[1]]
            send_hop(1, c, 0, True)

        def gathered(c):
            @pl.when(core == 0)
            def _():
                gather_quarter(c).wait()

            gather_half(c).start()

        def after_gather_half(c):
            gather_half(c).wait()

            @pl.when(c >= 2)
            def _():
                self.wait_store(r, c - 2)

            @pl.loop(0, self.per_chunk)
            def _(u):
                self.store(r, c * self.per_chunk + u)

        def small_copy(k, device):
            return remote(r.small_v.at[k], r.got_small.at[k], r.small_send.at[k], r.small_recv.at[k], device)

        def small_rest(j):
            dst = r.got_small.at[2 + j]
            return remote(r.small_v.at[3], dst, r.small_send.at[2 + j], r.small_recv.at[2 + j], peer(j))

        def small_step(step):
            @pl.when(step == 2)
            def _():
                r.small_v[1] = r.small[...]
                small_copy(1, sibling).start()

            @pl.when(step == 4)
            def _():
                small_copy(1, sibling).wait()
                r.small_v[2] = r.small_v[1] + r.got_small[1]
                small_copy(2, neighbour).start()

            @pl.when(step == 6)
            def _():
                small_copy(2, neighbour).wait()
                r.small_v[3] = r.small_v[2] + r.got_small[2]
                pl.loop(1, rest)(lambda j: small_rest(j).start())

            @pl.when(step == 8)
            def _():
                pl.loop(1, rest)(lambda j: small_rest(j).wait())
                total = r.small_v[3]
                for j in range(1, rest):
                    total += r.got_small[2 + j]
                r.small_out[...] = total

        last = 2 * rest + 2

        @pl.loop(0, self.chunks + self.SLACK * last)
        def _(step):
            def stage(time, action):
                c = step - self.SLACK * time

                @pl.when((c >= 0) & (c < self.chunks))
                def _():
                    action(c)

            stage(last, after_gather_half)
            stage(last - 1, gathered)

            @pl.when(core == 0)
            def _():
                @pl.loop(0, rest - 1)
                def _(h):
                    stage(rest + 2 + h, lambda c: hop(0, c, h, True, lambda c: gather_quarter(c).start()))

                @pl.loop(0, rest - 1)
                def _(h):
                    stage(3 + h, lambda c: hop(0, c, h, False, scattered))

                stage(2, after_quarter)

            @pl.when(core == 1)
            def _():
                @pl.loop(0, rest - 1)
                def _(h):
                    stage(rest + 2 + h, lambda c: hop(1, c, h, True, lambda c: None))

                stage(rest + 1, after_add_up)

                @pl.loop(0, rest - 1)
                def _(h):
                    stage(2 + h, lambda c: hop(1, c, h, False, lambda c: add_up(c).start()))

            stage(1, after_halve)
            small_step(step)

            @pl.when(step < self.chunks)
            def _():
                @pl.loop(0, self.per_chunk)
                def _(u):
                    self.product(r, step * self.per_chunk + u)

                halve(step).start()

        for c in range(max(0, self.chunks - 2), self.chunks):
            self.wait_store(r, c)

    def __call__(self, operands, small):
        t, cells, width = self.tables, self.cells, self.width
        rest, chunks, rows, ring = self.rest, self.chunks, self.rows, self.ring
        ff = operands["gs"].shape[-1]
        outs = {
            "win": f32(2, width, 3 * width),
            "wout": f32(2, width, width),
            "up": f32(width, ff),
            "down": f32(ff, width),
            "small_out": f32(8, width),
        }
        scratch = {
            "products": VMEM((ring, rows, TILE), F32),
            "sums": VMEM((chunks, rows // 2, TILE), F32),
            "full": VMEM((chunks, rows, TILE), F32),
            "got_near": VMEM((chunks, rows // 4, TILE), F32),
            "got_line": VMEM((2, chunks, rest - 1, rows // 2 // rest, TILE), F32),
            "a_v": VMEM((2, t, 2, cells, self.BLOCK), BF16),
            "b_v": VMEM((2, t, 2, cells, TILE), BF16),
            "small_v": VMEM((4, 8, width), F32),
            "got_small": VMEM((2 + rest, 8, width), F32),
            "a_sem": dma(2, 2 * t),
            "b_sem": dma(2, 2 * t),
            "store_sem": dma(2, self.per_chunk),
            "send": dma(4, ring),
            "recv": dma(4, chunks),
            "send_line": dma(4, ring, rest - 1),
            "recv_line": dma(4, chunks, rest - 1),
            "small_send": dma(2 + rest),
            "small_recv": dma(2 + rest),
        }
        ins = {n: (a, ANY) for n, a in operands.items()} | {"small": (small, VMEM)}
        outs = {n: (s, VMEM if n == "small_out" else ANY) for n, s in outs.items()}
        return call("weight_gradient_sum", self.kernel, 0, ins, outs, scratch)


def copied(arrays, small):
    cuts = []
    for i, a in enumerate(arrays):
        pieces = 4 if a.shape[0] % 32 == 0 else 2
        size = a.shape[0] // pieces
        cuts += [(i, slice(j * size, (j + 1) * size)) for j in range(pieces)]
    count = len(arrays)

    def kernel(*refs):
        srcs, small_ref = refs[:count], refs[count]
        dsts, gain_ref = refs[count + 1 : 2 * count + 1], refs[2 * count + 1]
        buffers, sem = refs[2 * count + 2 : -1], refs[-1]
        loads = [start(srcs[i].at[rows], buffers[i].at[rows], sem.at[0, n]) for n, (i, rows) in enumerate(cuts)]
        gain_ref[0] = small_ref[0:3, :]
        stores = []
        for n, (i, rows) in enumerate(cuts):
            loads[n].wait()
            stores.append(start(buffers[i].at[rows], dsts[i].at[rows], sem.at[1, n]))
        for copy in stores:
            copy.wait()

    width = small.shape[1]
    return pl.pallas_call(
        kernel,
        out_shape=[f32(*a.shape) for a in arrays] + [f32(1, 3, width)],
        in_specs=[pl.BlockSpec(memory_space=ANY)] * count + [pl.BlockSpec(memory_space=VMEM)],
        out_specs=[pl.BlockSpec(memory_space=ANY)] * count + [pl.BlockSpec(memory_space=VMEM)],
        scratch_shapes=[VMEM(a.shape, F32) for a in arrays] + [dma(2, len(cuts))],
        compiler_params=pltpu.CompilerParams(vmem_limit_bytes=VMEM_LIMIT),
        name="results",
    )(*arrays, small)


def local(
    cells,
    missing_mask,
    missing_embed,
    context_rows,
    norm_gains,
    attn_in,
    attn_out,
    mlp_up,
    mlp_down,
    cotangent,
):
    tables, rows, feat, width = cells.shape
    ff = mlp_up.shape[2]
    layers = Layers(tables, rows, feat, width, ff)

    def flat(tables_of_cells):
        return jnp.swapaxes(tables_of_cells, 1, 2).reshape(tables, rows * feat, -1)

    def unflat(cells_of_tables):
        return jnp.swapaxes(cells_of_tables.reshape(tables, feat, rows, width), 1, 2)[None]

    mask = jnp.pad(flat(missing_mask == 1).astype(F32), ((0, 0), (0, layers.cells - rows * feat), (0, 0)))
    weights = (attn_in[0], attn_out[0], mlp_up[0], mlp_down[0])
    done = layers(flat(cells), mask, missing_embed[None], context_rows, norm_gains[0], weights, flat(cotangent))
    operands = {n: done[n] for n in ("as_", "os", "gs", "dys", "dzs", "dhs", "dqkvs")}
    sums = GradSum(lax.axis_size("dp"), tables, layers.cells, width, ff)(operands, done["small"])
    big = [sums["win"], sums["wout"], sums["up"], sums["down"], done["out"], done["din"]]
    big = [a.reshape(-1, a.shape[-1]) for a in big]
    missing = sums["small_out"][3]
    from_first = lax.ppermute(missing, "section", [(0, 1)])
    win, wout, up, down, out, din, gain = copied(big, sums["small_out"])
    return (
        unflat(out),
        unflat(din),
        gain,
        win.reshape(attn_in.shape),
        wout.reshape(attn_out.shape),
        up[None],
        down[None],
        jnp.where(lax.axis_index("section") == 0, missing, from_first),
    )


def solution(mesh):
    in_specs = (
        P("dp", None, None, None),
        P("dp", None, None),
        P(),
        P("dp"),
        P("section", None, None),
        P("section", None, None, None),
        P("section", None, None, None),
        P("section", None, None),
        P("section", None, None),
        P("dp", None, None, None),
    )
    out_specs = (
        P("section", "dp", None, None, None),
        P("section", "dp", None, None, None),
        P("section", None, None),
        P("section", None, None, None),
        P("section", None, None, None),
        P("section", None, None),
        P("section", None, None),
        P(),
    )
    return jax.shard_map(local, mesh=mesh, in_specs=in_specs, out_specs=out_specs, check_vma=False)
```

```python
import functools
from types import SimpleNamespace

import jax
import jax.numpy as jnp
from jax import lax
from jax.experimental import pallas as pl
from jax.experimental.pallas import tpu as pltpu
from jax.sharding import PartitionSpec as P

HEADS = 4
EPSILON = 1e-05
NEG = -1e30
INV_SQRT2PI = 0.3989422804014327
LOG2E = 1.4426950408889634
LN2 = 0.6931471805599453
ERFC_P = 0.33
ERFC_C = (0.1863578482, 0.1829552331, 0.2012284886, 0.0472047191, 0.4085317677, -0.3511862269, 0.4602596132, -0.1353514118)
VMEM_LIMIT = 62 * 1024 * 1024
SUM_VMEM_LIMIT = 44 * 1024 * 1024
TILE = 512
F32, BF16 = jnp.float32, jnp.bfloat16


def dot(a, b, contract=((1,), (0,))):
    return lax.dot_general(a, b, (contract, ((), ())), preferred_element_type=F32)


def split(v):
    hi = v.astype(BF16)
    return hi, (v - hi.astype(F32)).astype(BF16)


def put(ref, index, v):
    hi, lo = split(v)
    ref[(0, *index)] = hi
    ref[(1, *index)] = lo


def parts(ref, *index):
    return ref[(0, *index)], ref[(1, *index)]


def wide(a, b, ca, cb):
    (ah, al), (bh, bl) = a, b
    return dot(jnp.concatenate([ah, ah, al], ca), jnp.concatenate([bh, bl, bh], cb), ((ca,), (cb,)))


def side(a, b):
    (ah, al), (bh, bl) = a, b
    width = bh.shape[1]
    both = dot(ah, jnp.concatenate([bh, bl], 1))
    return both[:, :width] + both[:, width:] + dot(al, bh)


def normalized(h):
    centred = h - jnp.mean(h, axis=-1, keepdims=True)
    rstd = lax.rsqrt(jnp.mean(centred * centred, axis=-1, keepdims=True) + EPSILON)
    return centred * rstd, rstd


def norm_back(n, rstd, gain, da):
    dn = da * gain
    return rstd * (dn - jnp.mean(dn, axis=-1, keepdims=True) - n * jnp.mean(dn * n, axis=-1, keepdims=True))


def cell_ids(start, count, rows, along):
    shape = (count, 1) if along == 0 else (1, count)
    at = lax.broadcasted_iota(jnp.int32, shape, along) + start
    feat = lax.shift_right_logical(at * ((1 << 20) // rows + 1), 20)
    return at - feat * rows, feat


def up16(n):
    return (n + 15) // 16 * 16


def col_blocks(rows, feat):
    cells = up16(rows * feat)
    half = up16((feat + 1) // 2 * rows)
    first_keys = min(cells, up16((((half - 1) // rows) + 1) * rows))
    second_keys = ((half // rows) * rows) // 16 * 16
    return (((0, half), (0, first_keys)), ((half, cells), (second_keys, cells)))


def when(cond):
    if isinstance(cond, bool):
        return (lambda action: action()) if cond else (lambda action: None)
    return pl.when(cond)


def over(count, action):
    if count <= 4:
        for i in range(count):
            action(i)
    else:
        pl.loop(0, count)(action)


def staggered(units, *steps):
    state = [None] * len(units)
    for i in range(len(units) + 1):
        if i < len(units):
            state[i] = steps[0](*units[i])
        if i > 0:
            for step in steps[1:]:
                state[i - 1] = step(*units[i - 1], state[i - 1])


def lanes(j, width):
    return pl.ds(pl.multiple_of(j * width, width), width)


def start(src, dst, sem):
    copy = pltpu.make_async_copy(src, dst, sem)
    copy.start()
    return copy


def col_biases(rows, feat, context, refs, keys_along):
    for ((q0, q1), (k0, k1)), ref in zip(col_blocks(rows, feat), refs):
        _, q_feat = cell_ids(q0, q1 - q0, rows, 1 - keys_along)
        k_row, k_feat = cell_ids(k0, k1 - k0, rows, keys_along)
        ref[...] = jnp.where((q_feat == k_feat) & (k_row < context), 0.0, NEG)


def row_bias(rows, feat, ref):
    cells = up16(rows * feat)
    q_row, q_feat = cell_ids(0, cells, rows, 0)
    k_row, k_feat = cell_ids(0, cells, rows, 1)
    ref[...] = jnp.where((q_row == k_row) & ((q_feat < feat) == (k_feat < feat)), 0.0, NEG)


def gelu_parts(z):
    size = jnp.abs(z)
    below = 1.0 + (ERFC_P * 0.7071067811865476) * size
    t = pl.reciprocal(below, approx=True)
    t = t * (2.0 - below * t)
    series = jnp.full_like(t, ERFC_C[-1])
    for c in ERFC_C[-2::-1]:
        series = series * t + c
    bell = jnp.exp(-0.5 * z * z)
    tail = 0.5 * (series * t) * bell
    phi = jnp.where(z >= 0.0, 1.0 - tail, tail)
    return z * phi, phi + z * (INV_SQRT2PI * bell)


SMEM, VMEM, ANY = pltpu.SMEM, pltpu.VMEM, pl.ANY


def f32(*shape):
    return jax.ShapeDtypeStruct(shape, F32)


def b16(*shape):
    return jax.ShapeDtypeStruct(shape, BF16)


def dma(*shape):
    return pltpu.SemaphoreType.DMA(shape)


def remote(src, dst, send, recv, device):
    return pltpu.make_async_remote_copy(
        src_ref=src, dst_ref=dst, send_sem=send, recv_sem=recv, device_id=device, device_id_type=pl.DeviceIdType.MESH
    )


def call(name, body, collective_id, ins, outs, scratch, limit):
    names = [*ins, *outs, *scratch]

    def kernel(*refs):
        body(SimpleNamespace(**dict(zip(names, refs))))

    results = pl.pallas_call(
        kernel,
        out_shape=[t for t, _ in outs.values()],
        in_specs=[pl.BlockSpec(memory_space=s) for _, s in ins.values()],
        out_specs=[pl.BlockSpec(memory_space=s) for _, s in outs.values()],
        scratch_shapes=list(scratch.values()),
        compiler_params=pltpu.CompilerParams(
            vmem_limit_bytes=limit, collective_id=collective_id, has_side_effects=collective_id is not None
        ),
        name=name,
    )(*(a for a, _ in ins.values()))
    return dict(zip(outs, results))


class Layers:
    def __init__(self, tables, rows, feat, width, ff):
        self.tables, self.rows, self.feat, self.width, self.ff = tables, rows, feat, width, ff
        self.real, self.cells = rows * feat, up16(rows * feat)
        self.hd = width // HEADS
        self.scale = self.hd ** (-0.5)

    def sites(self, r, site):
        if site == 1:
            return [(slice(*q), bias) for (q, _), bias in zip(col_blocks(self.rows, self.feat), (r.bias_a, r.bias_b))]
        return [(slice(0, self.cells), r.bias_row)]

    def __call__(self, cells, mask, embed, context, gains, weights, cotangent):
        t, c, w, ff, real = self.tables, self.cells, self.width, self.ff, self.real
        ins = {
            "cells": (cells, ANY),
            "mask": (mask, VMEM),
            "embed": (embed, VMEM),
            "ctx": (context, SMEM),
            "gains": (gains, VMEM),
            "cot": (cotangent, ANY),
        }
        names = ("win", "wout", "wup", "wdown")
        ins |= {n: (a, ANY) for n, a in zip(names, weights)}
        outs = {
            "out": f32(t, real, w),
            "din": f32(t, real, w),
            "hs": f32(t, 3, c, w),
            "qkvs": b16(t, 2, 2, c, 3 * w),
            "gps": f32(t, c, ff),
            "as_": b16(t, 2, 3, c, w),
            "os": b16(t, 2, 2, c, w),
            "gs": b16(t, 2, c, ff),
            "dys": b16(t, 2, c, w),
            "dzs": b16(t, 2, c, ff),
            "dhs": b16(t, 2, 2, c, w),
            "dqkvs": b16(t, 2, 2, c, 3 * w),
        }
        outs = {n: (s, ANY) for n, s in outs.items()} | {"small": (f32(8, w), VMEM)}
        scratch = {n + "_v": VMEM((2, *a.shape), BF16) for n, a in zip(names, weights)}
        scratch |= {
            "h_v": VMEM((3, c, w), F32),
            "qkv_v": VMEM((2, 2, c, 3 * w), BF16),
            "o_v": VMEM((2, 2, c, w), BF16),
            "gp_v": VMEM((c, ff), F32),
            "g_v": VMEM((2, c, ff), BF16),
            "a_v": VMEM((2, 3, c, w), BF16),
            "y_v": VMEM((t, c, w), F32),
            "dqkv_f": VMEM((c, 3 * w), F32),
            "dys_v": VMEM((2, c, w), BF16),
            "dy_v": VMEM((c, w), F32),
            "do_v": VMEM((2, c, w), BF16),
            "got": VMEM((t, real, w), F32),
            "bias_row": VMEM((c, c), F32),
            "stat_v": VMEM((c, 128), F32),
            "lse_v": VMEM((t, 2 * HEADS, c), F32),
            "raw_sem": pltpu.SemaphoreType.DMA((16,)),
            "in_sem": pltpu.SemaphoreType.DMA((4,)),
            "out_sem": pltpu.SemaphoreType.DMA((16,)),
            "send": pltpu.SemaphoreType.DMA((t, 2)),
            "recv": pltpu.SemaphoreType.DMA((t, 2)),
        }
        for name, ((q0, q1), (k0, k1)) in zip(("bias_a", "bias_b"), col_blocks(self.rows, self.feat)):
            assert (q0, q1) == (k0, k1)
            scratch[name] = VMEM((q1 - q0, q1 - q0), F32)
        return call("layers", self.kernel, 1, ins, outs, scratch, VMEM_LIMIT)

    def split_weights(self, r):
        w, ff = self.width, self.ff
        half, wide_in = w // 2, 3 * w
        top, step = slice(0, half), 64
        rest = slice(half, w)
        pieces = []
        big, bigger = r.dqkv_f.at[top], r.gp_v.at[top]
        pieces.append((r.win.at[0, top], big, r.win_v, (0,), 0, slice(None)))
        pieces.append((r.win.at[0, rest], bigger.at[:, 0:wide_in], r.win_v, (0,), half, slice(None)))
        pieces.append((r.wout.at[0, top], r.h_v.at[0, top], r.wout_v, (0,), 0, slice(None)))
        pieces.append((r.wout.at[0, rest], r.h_v.at[1, top], r.wout_v, (0,), half, slice(None)))
        pieces.append((r.wout.at[1, top], r.h_v.at[2, top], r.wout_v, (1,), 0, slice(None)))
        pieces.append((r.wout.at[1, rest], r.y_v.at[0, top], r.wout_v, (1,), half, slice(None)))
        pieces.append((r.win.at[1, top], big, r.win_v, (1,), 0, slice(None)))
        pieces.append((r.win.at[1, rest], bigger.at[:, 0:wide_in], r.win_v, (1,), half, slice(None)))
        pieces.append((r.wup.at[rest, wide_in:ff], r.dy_v.at[top, 0 : ff - wide_in], r.wup_v, (), half, slice(wide_in, ff)))
        pieces.append((r.wup.at[top], bigger, r.wup_v, (), 0, slice(None)))
        pieces.append((r.wup.at[rest, 0:wide_in], big, r.wup_v, (), half, slice(0, wide_in)))
        rows = self.cells // step * step
        buffers = [r.h_v.at[0], r.h_v.at[1], r.h_v.at[2], r.y_v.at[0], r.y_v.at[1]]
        for i, at in enumerate(range(0, ff, rows)):
            size = min(rows, ff - at)
            pieces.append((r.wdown.at[at : at + size], buffers[i].at[0:size], r.wdown_v, (), at, slice(None)))
        users = [0, 1, 2, 3, 4, 5, 0, 1, 6, 1, 0, 2, 3, 4, 5, 7][: len(pieces)]
        copies = [pltpu.make_async_copy(p[0], p[1], r.raw_sem.at[i]) for i, p in enumerate(pieces)]
        first = {u: i for i, u in reversed(list(enumerate(users)))}
        for i in sorted(first.values()):
            copies[i].start()
        for i, (_, buffer, v, lead, at, columns) in enumerate(pieces):
            copies[i].wait()

            @pl.loop(0, buffer.shape[0] // step)
            def _(j):
                src = pl.ds(pl.multiple_of(j * step, step), step)
                dst = pl.ds(pl.multiple_of(at + j * step, step), step)
                put(v, (*lead, dst, columns), buffer[src])

            later = [k for k in range(i + 1, len(pieces)) if users[k] == users[i]]
            if later:
                copies[later[0]].start()

    def kernel(self, r):
        t, real, c = self.tables, self.real, self.cells
        section = lax.axis_index("section")
        other = {"section": 1 - section}
        barrier = pltpu.get_barrier_semaphore()
        pl.semaphore_signal(barrier, inc=1, device_id=other, device_id_type=pl.DeviceIdType.MESH)
        self.split_weights(r)
        row_bias(self.rows, self.feat, r.bias_row)
        r.small[...] = jnp.zeros_like(r.small)
        pl.semaphore_wait(barrier, 1)

        def relay(table, half):
            at = slice(half * self.width // 2, (half + 1) * self.width // 2)
            src, dst = r.y_v.at[table, 0:real, at], r.got.at[table, :, at]
            return remote(src, dst, r.send.at[table, half], r.recv.at[table, half], other)

        @pl.loop(0, 2 * t)
        def _(step):
            forward = (1 - section) * (1 - step // t) + section * (1 - step % 2)
            table = (1 - section) * (step % t) + section * (step // 2)

            @pl.when(forward == 1)
            def _():
                self.forward(r, table, section, relay)

            @pl.when(forward == 0)
            def _():
                self.backward(r, table, section, relay)

        @pl.when(section == 1)
        def _():
            for table in range(t):
                for half in range(2):
                    relay(table, half).wait_send()

    def forward(self, r, table, section, relay):
        c, w, ff, hd, real = self.cells, self.width, self.ff, self.hd, self.real
        stores = []

        def keep(src, dst):
            stores.append(start(src, dst, r.out_sem.at[len(stores)]))

        r.h_v[0, real:, :] = jnp.zeros((c - real, w), F32)
        col_biases(self.rows, self.feat, r.ctx[table], (r.bias_a, r.bias_b), 1)

        @pl.when(section == 0)
        def _():
            start(r.cells.at[table], r.h_v.at[0, 0:real], r.in_sem.at[0]).wait()
            r.h_v[0] = jnp.where(r.mask[table] == 1.0, r.embed[...], r.h_v[0])

        @pl.when(section == 1)
        def _():
            start(r.cot.at[table], r.dy_v.at[0:real], r.in_sem.at[1])
            for half in range(2):
                relay(table, half).wait_recv()
            r.h_v[0, 0:real] = r.got[table]

        keep(r.h_v.at[0], r.hs.at[table, 0])
        for site in range(2):
            put(r.a_v, (site,), normalized(r.h_v[site])[0] * r.gains[site : site + 1, :])
            keep(r.a_v.at[:, site], r.as_.at[table, :, site])

            def project(j):
                at = slice(j * TILE, (j + 1) * TILE)
                return wide(parts(r.a_v, site), parts(r.win_v, site, slice(None), at), 1, 0)

            def keep_projected(j, out):
                if j < w // TILE:
                    out = out * (self.scale * LOG2E)
                put(r.qkv_v, (site, slice(None), slice(j * TILE, (j + 1) * TILE)), out)

            staggered([(j,) for j in range(3 * w // TILE)], project, keep_projected)
            keep(r.qkv_v.at[:, site], r.qkvs.at[table, :, site])

            def scores(head, span, bias):
                q = parts(r.qkv_v, site, span, lanes(head, hd))
                k = parts(r.qkv_v, site, span, lanes(HEADS + head, hd))
                return wide(q, k, 1, 1)

            def softmax(head, span, bias, s):
                s = s + bias[...]
                top = jnp.max(s, axis=-1, keepdims=True)
                e = jnp.exp2(s - top)
                total = jnp.sum(e, axis=-1, keepdims=True)
                column = lax.broadcasted_iota(jnp.int32, (1, r.stat_v.shape[1]), 1) == site * HEADS + head
                r.stat_v[span, :] = jnp.where(column, top + jnp.log2(total), r.stat_v[span, :])
                return split(e), 1.0 / total

            def blend(head, span, bias, state):
                e, inverse = state
                v = parts(r.qkv_v, site, span, lanes(2 * HEADS + head, hd))
                put(r.o_v, (site, span, lanes(head, hd)), side(e, v) * inverse)

            @pl.loop(0, HEADS // 2)
            def _(two):
                units = [(head, *unit) for head in (2 * two, 2 * two + 1) for unit in self.sites(r, site)]
                staggered(units, scores, softmax, blend)

            keep(r.o_v.at[:, site], r.os.at[table, :, site])
            r.h_v[site + 1] = r.h_v[site] + wide(parts(r.o_v, site), parts(r.wout_v, site), 1, 0)
            keep(r.h_v.at[site + 1], r.hs.at[table, site + 1])
        r.lse_v[table] = r.stat_v[...].T[0 : 2 * HEADS]
        put(r.a_v, (2,), normalized(r.h_v[2])[0] * r.gains[2:3, :])
        keep(r.a_v.at[:, 2], r.as_.at[table, :, 2])

        def up(j):
            return wide(parts(r.a_v, 2), parts(r.wup_v, slice(None), slice(j * TILE, (j + 1) * TILE)), 1, 0)

        tiles = ff // TILE
        z = up(0)
        for j in range(tiles):
            at = slice(j * TILE, (j + 1) * TILE)
            following = up(j + 1) if j + 1 < tiles else None
            g, gp = gelu_parts(z)
            put(r.g_v, (slice(None), at), g)
            r.gp_v[:, at] = gp
            z = following
        keep(r.g_v, r.gs.at[table])
        keep(r.gp_v, r.gps.at[table])
        for half in range(2):
            at = slice(half * w // 2, (half + 1) * w // 2)
            r.y_v[table, :, at] = r.h_v[2, :, at] + wide(parts(r.g_v), parts(r.wdown_v, slice(None), at), 1, 0)

            @pl.when(section == 0)
            def _():
                relay(table, half).start()

        keep(r.y_v.at[table, 0:real], r.out.at[table])
        for copy in stores:
            copy.wait()

    def backward(self, r, table, section, relay):
        c, w, ff, hd, real = self.cells, self.width, self.ff, self.hd, self.real
        stores = []

        def keep(src, dst):
            stores.append(start(src, dst, r.out_sem.at[len(stores)]))

        col_biases(self.rows, self.feat, r.ctx[table], (r.bias_a, r.bias_b), 0)

        @pl.when(section == 0)
        def _():
            loads = [
                start(r.hs.at[table], r.h_v, r.in_sem.at[0]),
                start(r.qkvs.at[table], r.qkv_v, r.in_sem.at[1]),
                start(r.gps.at[table], r.gp_v, r.in_sem.at[2]),
            ]
            for half in range(2):
                relay(table, half).wait()
            r.dy_v[0:real] = r.got[table]
            for copy in loads:
                copy.wait()

        @pl.when(section == 1)
        def _():
            pltpu.make_async_copy(r.cot.at[table], r.dy_v.at[0:real], r.in_sem.at[1]).wait()

        r.dy_v[real:, :] = jnp.zeros((c - real, w), F32)
        put(r.dys_v, (), r.dy_v[...])
        keep(r.dys_v, r.dys.at[table])

        def down(j):
            return wide(parts(r.dys_v), parts(r.wdown_v, slice(j * TILE, (j + 1) * TILE)), 1, 1)

        tiles = ff // TILE
        dg = down(0)
        for j in range(tiles):
            at = slice(j * TILE, (j + 1) * TILE)
            following = down(j + 1) if j + 1 < tiles else None
            put(r.g_v, (slice(None), at), dg * r.gp_v[:, at])
            dg = following
        keep(r.g_v, r.dzs.at[table])
        da = wide(parts(r.g_v), parts(r.wup_v), 1, 1)

        def through_norm(site, da):
            n, rstd = normalized(r.h_v[site])
            r.small[site : site + 1, :] += jnp.sum(da * n, axis=0, keepdims=True)
            return norm_back(n, rstd, r.gains[site : site + 1, :], da)

        r.dy_v[...] += through_norm(2, da)
        for site in (1, 0):
            put(r.o_v, (site,), r.dy_v[...])
            keep(r.o_v.at[:, site], r.dhs.at[table, :, site])
            put(r.do_v, (), wide(parts(r.o_v, site), parts(r.wout_v, site), 1, 1))

            def part_of(which, head, span):
                return parts(r.qkv_v, site, span, lanes(which * HEADS + head, hd))

            def products(head, span, bias):
                do = parts(r.do_v, span, lanes(head, hd))
                s = wide(part_of(1, head, span), part_of(0, head, span), 1, 1)
                return s, wide(part_of(2, head, span), do, 1, 1)

            def gradients(head, span, bias, state):
                s, dp = state
                p = jnp.exp2(s + bias[...] - r.lse_v[table, pl.ds(site * HEADS + head, 1), span])
                ds = p * (dp - jnp.sum(p * dp, axis=0, keepdims=True))
                return split(p), split(ds)

            def back(head, span, bias, state):
                p, ds = state
                k = part_of(1, head, span)
                r.dqkv_f[span, lanes(head, hd)] = (wide(tuple(x.T for x in k), ds, 1, 0) * self.scale).T
                r.dqkv_f[span, lanes(HEADS + head, hd)] = side(ds, part_of(0, head, span)) * LN2
                r.dqkv_f[span, lanes(2 * HEADS + head, hd)] = side(p, parts(r.do_v, span, lanes(head, hd)))

            @pl.loop(0, HEADS // 2)
            def _(two):
                units = [(head, *unit) for head in (2 * two, 2 * two + 1) for unit in self.sites(r, site)]
                staggered(units, products, gradients, back)

            for j in range(3 * w // TILE):
                at = slice(j * TILE, (j + 1) * TILE)
                put(r.qkv_v, (site, slice(None), at), r.dqkv_f[:, at])
            keep(r.qkv_v.at[:, site], r.dqkvs.at[table, :, site])
            da = wide(parts(r.qkv_v, site), parts(r.win_v, site), 1, 1)
            r.dy_v[...] += through_norm(site, da)

        @pl.when(section == 0)
        def _():
            missing = r.mask[table] == 1.0
            r.small[3:4, :] += jnp.sum(jnp.where(missing, r.dy_v[...], 0.0), axis=0, keepdims=True)
            r.y_v[table] = jnp.where(missing, 0.0, r.dy_v[...])

        @pl.when(section == 1)
        def _():
            r.y_v[table] = r.dy_v[...]
            for half in range(2):
                relay(table, half).start()

        keep(r.y_v.at[table, 0:real], r.din.at[table])
        for copy in stores:
            copy.wait()


class GradSum:
    ROWS, COLS = 512, 256
    SLACK = 2

    def __init__(self, count, tables, cells, width, ff):
        self.count, self.tables, self.cells, self.width = count, tables, cells, width
        self.rest = count // 4
        shapes = [("gs", None, "dys", None, "down", None, ff, width), ("as_", 2, "dzs", None, "up", None, width, ff)]
        for site in (1, 0):
            shapes.append(("as_", site, "dqkvs", site, "win", site, width, 3 * width))
            shapes.append(("os", site, "dhs", site, "wout", site, width, width))
        self.groups, at = [], 0
        for *which, k, n in shapes:
            blocks = (k // self.ROWS) * (n // self.COLS)
            self.groups.append((at, at + blocks, *which, n // self.COLS))
            at += blocks
        self.blocks = at
        self.per_chunk = max(1, 4 * self.rest * 8 // self.ROWS)
        self.chunks = self.blocks // self.per_chunk
        self.rows = self.per_chunk * self.ROWS
        self.ring = self.SLACK + 2
        self.depth = (cells + 127) // 128 * 128

    def select(self, q, action):
        for group in self.groups:
            first, stop, *_, across = group

            @pl.when((q >= first) & (q < stop))
            def _():
                action(group, (q - first) // across, (q - first) % across)

    def starts_row(self, q):
        found = False
        for first, stop, *_, across in self.groups:
            found = found | ((q >= first) & (q < stop) & ((q - first) % across == 0))
        return found

    def load(self, r, q):
        slot = q % 2

        def action(group, i, j):
            _, _, left, left_site, right, right_site, *_ = group
            a, b = getattr(r, left), getattr(r, right)

            def at(t, part, site):
                return (t, part, slice(None)) if site is None else (t, part, site, slice(None))

            for t in range(self.tables):
                rows = slice(t * self.depth, t * self.depth + self.cells)
                for part in range(2):
                    sem = 2 * t + part
                    start(b.at[(*at(t, part, right_site), lanes(j, self.COLS))], r.b_v.at[slot, part, rows], r.b_sem.at[slot, sem])

                    @pl.when(j == 0)
                    def _():
                        start(a.at[(*at(t, part, left_site), lanes(i, self.ROWS))], r.a_v.at[part, rows], r.a_sem.at[sem])

        self.select(q, action)

    def each_operand(self):
        return [(2 * t + part, part, slice(t * self.depth, t * self.depth + self.cells)) for t in range(self.tables) for part in range(2)]

    def product(self, r, q):
        slot = q % 2

        @pl.when(self.starts_row(q))
        def _():
            for sem, part, rows in self.each_operand():
                a = r.a_v.at[part, rows]
                pltpu.make_async_copy(a, a, r.a_sem.at[sem]).wait()
            for part in range(2):
                r.left_v[part] = r.a_v[part].T

        for sem, part, rows in self.each_operand():
            b = r.b_v.at[slot, part, rows]
            pltpu.make_async_copy(b, b, r.b_sem.at[slot, sem]).wait()

        @pl.when(q + 1 < self.blocks)
        def _():
            self.load(r, q + 1)

        rows = pl.ds(pl.multiple_of(q % self.per_chunk * self.ROWS, self.ROWS), self.ROWS)
        r.products[q // self.per_chunk % self.ring, rows] = side(parts(r.left_v), parts(r.b_v.at[slot]))

    def kernel(self, r):
        rest, rows, ring = self.rest, self.rows, self.ring
        half = rows // 2
        quart = half // 2
        sizes = (quart // rest, half // rest)
        me = lax.axis_index("dp")
        core, pair, place = me % 2, me // 2 % 2, me // 4
        sibling, neighbour = {"dp": me + 1 - 2 * core}, {"dp": me + 2 - 4 * pair}
        ways = ({"dp": me + 4}, {"dp": me - 4})

        def peer(j):
            return {"dp": lax.rem(place + j, rest) * 4 + me % 4}

        def span(at, size):
            return pl.ds(pl.multiple_of(at, size), size)

        mine = core * half
        own, other = pair * quart, (1 - pair) * quart
        bases = (own, 0)

        barrier = pltpu.get_barrier_semaphore()

        def greet(device):
            pl.semaphore_signal(barrier, inc=1, device_id=device, device_id_type=pl.DeviceIdType.MESH)

        greet(sibling)
        greet(neighbour)

        @pl.loop(1, rest)
        def _(j):
            greet(peer(j))

        for t in range(self.tables):
            pad = slice(t * self.depth + self.cells, (t + 1) * self.depth)
            for part in range(2):
                r.a_v[part, pad] = jnp.zeros_like(r.a_v[part, pad])
                for slot in range(2):
                    r.b_v[slot, part, pad] = jnp.zeros_like(r.b_v[slot, part, pad])
        self.load(r, 0)
        pl.semaphore_wait(barrier, rest + 1)

        def halve(c):
            src = r.products.at[c % ring, span((1 - core) * half, half)]
            return remote(src, r.sums.at[c], r.send.at[0, c % ring], r.recv.at[0, c], sibling)

        def gather_half(c):
            at = r.full.at[c, span(mine, half)]
            return remote(at, at, r.send.at[1, c % ring], r.recv.at[1, c], sibling)

        def quarter(c):
            dst = r.got_near.at[c]
            return remote(r.sums.at[c, span(other, quart)], dst, r.send.at[2, c % ring], r.recv.at[2, c], neighbour)

        def gather_quarter(c):
            at = r.full.at[c, span(mine + own, quart)]
            return remote(at, at, r.send.at[3, c % ring], r.recv.at[3, c], neighbour)

        def piece(kind, b):
            return span(bases[kind] + b * sizes[kind], sizes[kind])

        def full_piece(kind, b):
            return span(mine + bases[kind] + b * sizes[kind], sizes[kind])

        def add_up(c):
            dst = r.got_near.at[c, 0 : sizes[1]]
            return remote(r.sums.at[c, piece(1, place)], dst, r.send.at[2, c % ring], r.recv.at[2, c], neighbour)

        def line(kind, c, h, way, gather, b):
            if gather:
                src = dst = r.full.at[c, full_piece(kind, b)]
            else:
                src, dst = r.sums.at[c, piece(kind, b)], r.got_line.at[way, c, h, 0 : sizes[kind]]
            phase = 2 * way + int(gather)
            return remote(src, dst, r.send_line.at[phase, c % ring, h], r.recv_line.at[phase, c, h], ways[way])

        def hops(h, gather):
            if gather:
                right = ((place >= h) & (place < rest - 1), place - h, place >= h + 1, place - 1 - h)
                left = ((place + h < rest) & (place >= 1), place + h, place + 1 + h < rest, place + 1 + h)
            else:
                far = rest - 1 - h
                right = (place <= h, place + far, (place >= 1) & (place - 1 <= h), place - 1 + far)
                left = (rest - 1 - place <= h, place - far, (place <= rest - 2) & (rest - 2 - place <= h), place + 1 - far)
            return right, left

        def send_hop(kind, c, h, gather):
            for way, (sends, b, _, _) in enumerate(hops(h, gather)):

                @pl.when(sends)
                def _():
                    line(kind, c, h, way, gather, b).start()

        def end_hop(kind, c, h, gather):
            for way, (sends, b, receives, arriving) in enumerate(hops(h, gather)):

                @pl.when(sends)
                def _():
                    line(kind, c, h, way, gather, b).wait_send()

                @pl.when(receives)
                def _():
                    line(kind, c, h, way, gather, arriving).wait_recv()
                    if not gather:
                        r.sums[c, piece(kind, arriving)] += r.got_line[way, c, h, 0 : sizes[kind]]

        def hop(kind, c, h, gather, then):
            end_hop(kind, c, h, gather)

            @when(h < rest - 2)
            def _():
                send_hop(kind, c, h + 1, gather)

            @when(h == rest - 2)
            def _():
                then(c)

        def after_halve(c):
            halve(c).wait()
            r.sums[c] += r.products[c % ring, span(mine, half)]

            @pl.when(core == 0)
            def _():
                quarter(c).start()

            @pl.when(core == 1)
            def _():
                send_hop(1, c, 0, False)

        def after_quarter(c):
            quarter(c).wait()
            r.sums[c, span(own, quart)] += r.got_near[c]
            send_hop(0, c, 0, False)

        def scattered(c):
            r.full[c, full_piece(0, place)] = r.sums[c, piece(0, place)]
            send_hop(0, c, 0, True)

        def after_add_up(c):
            add_up(c).wait()
            r.full[c, full_piece(1, place)] = r.sums[c, piece(1, place)] + r.got_near[c, 0 : sizes[1]]
            send_hop(1, c, 0, True)

        def gathered(c):
            @pl.when(core == 0)
            def _():
                gather_quarter(c).wait()

            gather_half(c).start()

        def after_gather_half(c):
            gather_half(c).wait()

        def small_copy(k, device):
            return remote(r.small_v.at[k], r.got_small.at[k], r.small_send.at[k], r.small_recv.at[k], device)

        def small_rest(j):
            dst = r.got_small.at[2 + j]
            return remote(r.small_v.at[3], dst, r.small_send.at[2 + j], r.small_recv.at[2 + j], peer(j))

        def small_step(step):
            @pl.when(step == 2)
            def _():
                r.small_v[1] = r.small[...]
                small_copy(1, sibling).start()

            @pl.when(step == 4)
            def _():
                small_copy(1, sibling).wait()
                r.small_v[2] = r.small_v[1] + r.got_small[1]
                small_copy(2, neighbour).start()

            @pl.when(step == 6)
            def _():
                small_copy(2, neighbour).wait()
                r.small_v[3] = r.small_v[2] + r.got_small[2]
                pl.loop(1, rest)(lambda j: small_rest(j).start())

            @pl.when(step == 8)
            def _():
                pl.loop(1, rest)(lambda j: small_rest(j).wait())
                total = r.small_v[3]
                for j in range(1, rest):
                    total += r.got_small[2 + j]
                r.small_out[...] = total

        last = 2 * rest + 2

        @pl.loop(0, self.chunks + self.SLACK * last)
        def _(step):
            def stage(time, action):
                c = step - self.SLACK * time

                @pl.when((c >= 0) & (c < self.chunks))
                def _():
                    action(c)

            stage(last, after_gather_half)
            stage(last - 1, gathered)

            @pl.when(core == 0)
            def _():
                over(rest - 1, lambda h: stage(rest + 2 + h, lambda c: hop(0, c, h, True, lambda c: gather_quarter(c).start())))

                over(rest - 1, lambda h: stage(3 + h, lambda c: hop(0, c, h, False, scattered)))

                stage(2, after_quarter)

            @pl.when(core == 1)
            def _():
                over(rest - 1, lambda h: stage(rest + 2 + h, lambda c: hop(1, c, h, True, lambda c: None)))

                stage(rest + 1, after_add_up)

                over(rest - 1, lambda h: stage(2 + h, lambda c: hop(1, c, h, False, lambda c: add_up(c).start())))

            stage(1, after_halve)
            small_step(step)

            @pl.when(step < self.chunks)
            def _():
                @pl.loop(0, self.per_chunk)
                def _(u):
                    self.product(r, step * self.per_chunk + u)

                halve(step).start()

    def __call__(self, operands, small):
        t, width, deep = self.tables, self.width, self.tables * self.depth
        rest, chunks, rows, ring, cols = self.rest, self.chunks, self.rows, self.ring, self.COLS
        outs = {"full": VMEM((chunks, rows, cols), F32), "small_out": f32(8, width)}
        scratch = {
            "products": VMEM((ring, rows, cols), F32),
            "sums": VMEM((chunks, rows // 2, cols), F32),
            "got_near": VMEM((chunks, rows // 4, cols), F32),
            "got_line": VMEM((2, chunks, rest - 1, rows // 2 // rest, cols), F32),
            "a_v": VMEM((2, deep, self.ROWS), BF16),
            "left_v": VMEM((2, self.ROWS, deep), BF16),
            "b_v": VMEM((2, 2, deep, cols), BF16),
            "small_v": VMEM((4, 8, width), F32),
            "got_small": VMEM((2 + rest, 8, width), F32),
            "a_sem": dma(2 * t),
            "b_sem": dma(2, 2 * t),
            "send": dma(4, ring),
            "recv": dma(4, chunks),
            "send_line": dma(4, ring, rest - 1),
            "recv_line": dma(4, chunks, rest - 1),
            "small_send": dma(2 + rest),
            "small_recv": dma(2 + rest),
        }
        ins = {n: (a, ANY) for n, a in operands.items()} | {"small": (small, VMEM)}
        outs = {n: (s, VMEM) for n, s in outs.items()}
        return call("weight_gradient_sum", self.kernel, 0, ins, outs, scratch, SUM_VMEM_LIMIT)

    def results(self, sums, small, tables, ff):
        width = self.width
        sums = pltpu.with_memory_space_constraint(sums, pltpu.VMEM)
        ins = {"full": (sums, VMEM), "small": (small, VMEM)} | {f"table{i}": (a, ANY) for i, a in enumerate(tables)}
        outs = {
            "win": f32(2, width, 3 * width),
            "wout": f32(2, width, width),
            "up": f32(width, ff),
            "down": f32(ff, width),
        } | {f"out{i}": f32(*a.shape) for i, a in enumerate(tables)}
        outs = {n: (s, ANY) for n, s in outs.items()} | {"gain": (f32(1, 3, width), VMEM)}
        scratch = {f"table_v{i}": VMEM(a.shape, F32) for i, a in enumerate(tables)}
        scratch |= {"sem": dma(self.blocks), "in_sem": dma(len(tables)), "out_sem": dma(len(tables))}

        def body(r):
            buffers = [getattr(r, f"table_v{i}") for i in range(len(tables))]
            loads = [start(getattr(r, f"table{i}"), v, r.in_sem.at[i]) for i, v in enumerate(buffers)]
            stores = []
            for first, stop, *_, out, site, across in self.groups:
                dst = getattr(r, out) if site is None else getattr(r, out).at[site]
                for q in range(first, stop):
                    i, j = (q - first) // across, (q - first) % across
                    u = q % self.per_chunk
                    src = r.full.at[q // self.per_chunk, u * self.ROWS : (u + 1) * self.ROWS]
                    at = (slice(i * self.ROWS, (i + 1) * self.ROWS), slice(j * self.COLS, (j + 1) * self.COLS))
                    stores.append(start(src, dst.at[at], r.sem.at[q]))
            r.gain[0] = r.small[0:3, :]
            for i, v in enumerate(buffers):
                loads[i].wait()
                stores.append(start(v, getattr(r, f"out{i}"), r.out_sem.at[i]))
            for copy in stores:
                copy.wait()

        return call("results", body, None, ins, outs, scratch, SUM_VMEM_LIMIT)


def local(
    cells,
    missing_mask,
    missing_embed,
    context_rows,
    norm_gains,
    attn_in,
    attn_out,
    mlp_up,
    mlp_down,
    cotangent,
):
    tables, rows, feat, width = cells.shape
    ff = mlp_up.shape[2]
    layers = Layers(tables, rows, feat, width, ff)

    def flat(tables_of_cells):
        return jnp.swapaxes(tables_of_cells, 1, 2).reshape(tables, rows * feat, -1)

    def unflat(cells_of_tables):
        return jnp.swapaxes(cells_of_tables.reshape(tables, feat, rows, width), 1, 2)[None]

    mask = jnp.pad(flat(missing_mask == 1).astype(F32), ((0, 0), (0, layers.cells - rows * feat), (0, 0)))
    weights = (attn_in[0], attn_out[0], mlp_up[0], mlp_down[0])
    done = layers(flat(cells), mask, missing_embed[None], context_rows, norm_gains[0], weights, flat(cotangent))
    operands = {n: done[n] for n in ("as_", "os", "gs", "dys", "dzs", "dhs", "dqkvs")}
    grad_sum = GradSum(lax.axis_size("dp"), tables, layers.cells, width, ff)
    sums = grad_sum(operands, done["small"])
    missing = sums["small_out"][3]
    from_first = lax.ppermute(missing, "section", [(0, 1)])
    got = grad_sum.results(sums["full"], sums["small_out"], (done["out"], done["din"]), ff)
    return (
        unflat(got["out0"]),
        unflat(got["out1"]),
        got["gain"],
        got["win"][None],
        got["wout"][None],
        got["up"][None],
        got["down"][None],
        jnp.where(lax.axis_index("section") == 0, missing, from_first),
    )


def solution(mesh):
    in_specs = (
        P("dp", None, None, None),
        P("dp", None, None),
        P(),
        P("dp"),
        P("section", None, None),
        P("section", None, None, None),
        P("section", None, None, None),
        P("section", None, None),
        P("section", None, None),
        P("dp", None, None, None),
    )
    out_specs = (
        P("section", "dp", None, None, None),
        P("section", "dp", None, None, None),
        P("section", None, None),
        P("section", None, None, None),
        P("section", None, None, None),
        P("section", None, None),
        P("section", None, None),
        P(),
    )
    return jax.shard_map(local, mesh=mesh, in_specs=in_specs, out_specs=out_specs, check_vma=False)
```

```python
import functools
from types import SimpleNamespace

import jax
import jax.numpy as jnp
from jax import lax
from jax.experimental import pallas as pl
from jax.experimental.pallas import tpu as pltpu
from jax.sharding import PartitionSpec as P

HEADS = 4
EPSILON = 1e-05
NEG = -1e30
INV_SQRT2PI = 0.3989422804014327
LOG2E = 1.4426950408889634
LN2 = 0.6931471805599453
ERFC_P = 0.33
ERFC_C = (0.1863578482, 0.1829552331, 0.2012284886, 0.0472047191, 0.4085317677, -0.3511862269, 0.4602596132, -0.1353514118)
VMEM_LIMIT = 62 * 1024 * 1024
SUM_VMEM_LIMIT = 44 * 1024 * 1024
TILE = 512
F32, BF16 = jnp.float32, jnp.bfloat16


def dot(a, b, contract=((1,), (0,))):
    return lax.dot_general(a, b, (contract, ((), ())), preferred_element_type=F32)


def split(v):
    hi = v.astype(BF16)
    return hi, (v - hi.astype(F32)).astype(BF16)


def put(ref, index, v):
    hi, lo = split(v)
    ref[(0, *index)] = hi
    ref[(1, *index)] = lo


def parts(ref, *index):
    return ref[(0, *index)], ref[(1, *index)]


def wide(a, b, ca, cb):
    (ah, al), (bh, bl) = a, b
    return dot(jnp.concatenate([ah, ah, al], ca), jnp.concatenate([bh, bl, bh], cb), ((ca,), (cb,)))


def side(a, b):
    (ah, al), (bh, bl) = a, b
    width = bh.shape[1]
    both = dot(ah, jnp.concatenate([bh, bl], 1))
    return both[:, :width] + both[:, width:] + dot(al, bh)


def normalized(h):
    centred = h - jnp.mean(h, axis=-1, keepdims=True)
    rstd = lax.rsqrt(jnp.mean(centred * centred, axis=-1, keepdims=True) + EPSILON)
    return centred * rstd, rstd


def norm_back(n, rstd, gain, da):
    dn = da * gain
    return rstd * (dn - jnp.mean(dn, axis=-1, keepdims=True) - n * jnp.mean(dn * n, axis=-1, keepdims=True))


def cell_ids(start, count, inner, along):
    shape = (count, 1) if along == 0 else (1, count)
    at = lax.broadcasted_iota(jnp.int32, shape, along) + start
    outer = lax.shift_right_logical(at * ((1 << 20) // inner + 1), 20)
    return outer, at - outer * inner


def up16(n):
    return (n + 15) // 16 * 16


def blocks(outer, inner):
    cells = up16(outer * inner)
    half = up16((outer + 1) // 2 * inner)
    first_keys = min(cells, up16((((half - 1) // inner) + 1) * inner))
    second_keys = ((half // inner) * inner) // 16 * 16
    return ((slice(0, half), slice(0, first_keys)), (slice(half, cells), slice(second_keys, cells)))


def when(cond):
    if isinstance(cond, bool):
        return (lambda action: action()) if cond else (lambda action: None)
    return pl.when(cond)


def over(count, action):
    if count <= 4:
        for i in range(count):
            action(i)
    else:
        pl.loop(0, count)(action)


def staggered(units, *steps):
    state = [None] * len(units)
    for i in range(len(units) + 1):
        if i < len(units):
            state[i] = steps[0](*units[i])
        if i > 0:
            for step in steps[1:]:
                state[i - 1] = step(*units[i - 1], state[i - 1])


def lanes(j, width):
    return pl.ds(pl.multiple_of(j * width, width), width)


def start(src, dst, sem):
    copy = pltpu.make_async_copy(src, dst, sem)
    copy.start()
    return copy


def fill_biases(outer, inner, limit, refs, keys_along):
    for (queries, keys), ref in zip(blocks(outer, inner), refs):
        q_outer, _ = cell_ids(queries.start, queries.stop - queries.start, inner, 1 - keys_along)
        k_outer, k_inner = cell_ids(keys.start, keys.stop - keys.start, inner, keys_along)
        ref[...] = jnp.where((q_outer == k_outer) & (k_inner < limit), 0.0, NEG)


def gelu_parts(z):
    size = jnp.abs(z)
    below = 1.0 + (ERFC_P * 0.7071067811865476) * size
    t = pl.reciprocal(below, approx=True)
    t = t * (2.0 - below * t)
    series = jnp.full_like(t, ERFC_C[-1])
    for c in ERFC_C[-2::-1]:
        series = series * t + c
    bell = jnp.exp(-0.5 * z * z)
    tail = 0.5 * (series * t) * bell
    phi = jnp.where(z >= 0.0, 1.0 - tail, tail)
    return z * phi, phi + z * (INV_SQRT2PI * bell)


SMEM, VMEM, ANY = pltpu.SMEM, pltpu.VMEM, pl.ANY


def f32(*shape):
    return jax.ShapeDtypeStruct(shape, F32)


def b16(*shape):
    return jax.ShapeDtypeStruct(shape, BF16)


def dma(*shape):
    return pltpu.SemaphoreType.DMA(shape)


def remote(src, dst, send, recv, device):
    return pltpu.make_async_remote_copy(
        src_ref=src, dst_ref=dst, send_sem=send, recv_sem=recv, device_id=device, device_id_type=pl.DeviceIdType.MESH
    )


def call(name, body, collective_id, ins, outs, scratch, limit):
    names = [*ins, *outs, *scratch]

    def kernel(*refs):
        body(SimpleNamespace(**dict(zip(names, refs))))

    results = pl.pallas_call(
        kernel,
        out_shape=[t for t, _ in outs.values()],
        in_specs=[pl.BlockSpec(memory_space=s) for _, s in ins.values()],
        out_specs=[pl.BlockSpec(memory_space=s) for _, s in outs.values()],
        scratch_shapes=list(scratch.values()),
        compiler_params=pltpu.CompilerParams(
            vmem_limit_bytes=limit, collective_id=collective_id, has_side_effects=collective_id is not None
        ),
        name=name,
    )(*(a for a, _ in ins.values()))
    return dict(zip(outs, results))


class Layers:
    def __init__(self, tables, rows, feat, width, ff):
        self.tables, self.rows, self.feat, self.width, self.ff = tables, rows, feat, width, ff
        self.real, self.cells = rows * feat, up16(rows * feat)
        self.hd = width // HEADS
        self.scale = self.hd ** (-0.5)

    def sites(self, r, site, keys_along):
        if site == 1:
            ranges, biases = blocks(self.feat, self.rows), r.col_bias
        else:
            ranges, biases = blocks(self.rows, self.feat), r.row_bias
        return [(*unit, bias) for unit, bias in zip(ranges, biases[keys_along])]

    def set_out(self, r, src, count):
        for k in range(self.width // 128):
            r.perm_v[k, 0:count] = src[0:count, k * 128 : (k + 1) * 128]

    def by_rows(self, r, dst):
        for row in range(self.rows):
            for k in range(self.width // 128):
                at = (slice(row * self.feat, (row + 1) * self.feat), slice(k * 128, (k + 1) * 128))
                dst[at] = r.perm_v[k, pl.ds(row, self.feat, stride=self.rows), :]

    def by_features(self, r, dst):
        for feat in range(self.feat):
            for k in range(self.width // 128):
                at = (slice(feat * self.rows, (feat + 1) * self.rows), slice(k * 128, (k + 1) * 128))
                dst[at] = r.perm_v[k, pl.ds(feat, self.rows, stride=self.feat), :]

    def __call__(self, cells, mask, embed, context, gains, weights, cotangent):
        t, c, w, ff, real = self.tables, self.cells, self.width, self.ff, self.real
        rows, feat = self.rows, self.feat
        ins = {
            "cells": (cells, ANY),
            "mask": (mask, VMEM),
            "embed": (embed, VMEM),
            "ctx": (context, SMEM),
            "gains": (gains, VMEM),
            "cot": (cotangent, ANY),
        }
        names = ("win", "wout", "wup", "wdown")
        ins |= {n: (a, ANY) for n, a in zip(names, weights)}
        outs = {
            "out": f32(t, real, w),
            "din": f32(t, real, w),
            "hs": f32(t, 3, c, w),
            "qkvs": b16(t, 2, 2, c, 3 * w),
            "gps": f32(t, c, ff),
            "as_": b16(t, 2, 3, c, w),
            "os": b16(t, 2, 2, c, w),
            "gs": b16(t, 2, c, ff),
            "dys": b16(t, 2, c, w),
            "dzs": b16(t, 2, c, ff),
            "dhs": b16(t, 2, 2, c, w),
            "dqkvs": b16(t, 2, 2, c, 3 * w),
        }
        outs = {n: (s, ANY) for n, s in outs.items()} | {"small": (f32(8, w), VMEM)}
        scratch = {n + "_v": VMEM((2, *a.shape), BF16) for n, a in zip(names, weights)}
        scratch |= {
            "h_v": VMEM((3, c, w), F32),
            "qkv_v": VMEM((2, 2, c, 3 * w), BF16),
            "o_v": VMEM((2, 2, c, w), BF16),
            "gp_v": VMEM((c, ff), F32),
            "g_v": VMEM((2, c, ff), BF16),
            "a_v": VMEM((2, 3, c, w), BF16),
            "y_v": VMEM((t, c, w), F32),
            "dqkv_f": VMEM((c, 3 * w), F32),
            "perm_v": VMEM((w // 128, c, 128), F32),
            "dys_v": VMEM((2, c, w), BF16),
            "dy_v": VMEM((c, w), F32),
            "do_v": VMEM((2, c, w), BF16),
            "got": VMEM((t, real, w), F32),
            "stat_v": VMEM((c, 128), F32),
            "lse_v": VMEM((t, 2 * HEADS, c), F32),
            "raw_sem": pltpu.SemaphoreType.DMA((16,)),
            "in_sem": pltpu.SemaphoreType.DMA((4,)),
            "out_sem": pltpu.SemaphoreType.DMA((16,)),
            "send": pltpu.SemaphoreType.DMA((t, 2)),
            "recv": pltpu.SemaphoreType.DMA((t, 2)),
        }
        for name, ranges in (("col_bias", blocks(feat, rows)), ("row_bias", blocks(rows, feat))):
            for i, (queries, keys) in enumerate(ranges):
                shape = (queries.stop - queries.start, keys.stop - keys.start)
                scratch[f"{name}0{i}"] = VMEM(shape[::-1], F32)
                scratch[f"{name}1{i}"] = VMEM(shape, F32)

        def body(r):
            for n in ("col_bias", "row_bias"):
                setattr(r, n, [[getattr(r, f"{n}{along}{i}") for i in range(2)] for along in range(2)])
            self.kernel(r)

        return call("layers", body, 1, ins, outs, scratch, VMEM_LIMIT)

    def split_weights(self, r):
        w, ff = self.width, self.ff
        half, wide_in = w // 2, 3 * w
        top, step = slice(0, half), 64
        rest = slice(half, w)
        pieces = []
        big, bigger = r.dqkv_f.at[top], r.gp_v.at[top]
        pieces.append((r.win.at[0, top], big, r.win_v, (0,), 0, slice(None)))
        pieces.append((r.win.at[0, rest], bigger.at[:, 0:wide_in], r.win_v, (0,), half, slice(None)))
        pieces.append((r.wout.at[0, top], r.h_v.at[0, top], r.wout_v, (0,), 0, slice(None)))
        pieces.append((r.wout.at[0, rest], r.h_v.at[1, top], r.wout_v, (0,), half, slice(None)))
        pieces.append((r.wout.at[1, top], r.h_v.at[2, top], r.wout_v, (1,), 0, slice(None)))
        pieces.append((r.wout.at[1, rest], r.y_v.at[0, top], r.wout_v, (1,), half, slice(None)))
        pieces.append((r.win.at[1, top], big, r.win_v, (1,), 0, slice(None)))
        pieces.append((r.win.at[1, rest], bigger.at[:, 0:wide_in], r.win_v, (1,), half, slice(None)))
        pieces.append((r.wup.at[rest, wide_in:ff], r.dy_v.at[top, 0 : ff - wide_in], r.wup_v, (), half, slice(wide_in, ff)))
        pieces.append((r.wup.at[top], bigger, r.wup_v, (), 0, slice(None)))
        pieces.append((r.wup.at[rest, 0:wide_in], big, r.wup_v, (), half, slice(0, wide_in)))
        rows = self.cells // step * step
        buffers = [r.h_v.at[0], r.h_v.at[1], r.h_v.at[2], r.y_v.at[0], r.y_v.at[1]]
        for i, at in enumerate(range(0, ff, rows)):
            size = min(rows, ff - at)
            pieces.append((r.wdown.at[at : at + size], buffers[i].at[0:size], r.wdown_v, (), at, slice(None)))
        users = [0, 1, 2, 3, 4, 5, 0, 1, 6, 1, 0, 2, 3, 4, 5, 7][: len(pieces)]
        copies = [pltpu.make_async_copy(p[0], p[1], r.raw_sem.at[i]) for i, p in enumerate(pieces)]
        first = {u: i for i, u in reversed(list(enumerate(users)))}
        for i in sorted(first.values()):
            copies[i].start()
        for i, (_, buffer, v, lead, at, columns) in enumerate(pieces):
            copies[i].wait()

            @pl.loop(0, buffer.shape[0] // step)
            def _(j):
                src = pl.ds(pl.multiple_of(j * step, step), step)
                dst = pl.ds(pl.multiple_of(at + j * step, step), step)
                put(v, (*lead, dst, columns), buffer[src])

            later = [k for k in range(i + 1, len(pieces)) if users[k] == users[i]]
            if later:
                copies[later[0]].start()

    def kernel(self, r):
        t, real, c = self.tables, self.real, self.cells
        section = lax.axis_index("section")
        other = {"section": 1 - section}
        barrier = pltpu.get_barrier_semaphore()
        pl.semaphore_signal(barrier, inc=1, device_id=other, device_id_type=pl.DeviceIdType.MESH)
        self.split_weights(r)
        for along in range(2):
            fill_biases(self.rows, self.feat, self.feat, r.row_bias[along], along)
        r.small[...] = jnp.zeros_like(r.small)
        pl.semaphore_wait(barrier, 1)

        def relay(table, half):
            at = slice(half * self.width // 2, (half + 1) * self.width // 2)
            src, dst = r.y_v.at[table, 0:real, at], r.got.at[table, :, at]
            return remote(src, dst, r.send.at[table, half], r.recv.at[table, half], other)

        @pl.loop(0, 2 * t)
        def _(step):
            forward = (1 - section) * (1 - step // t) + section * (1 - step % 2)
            table = (1 - section) * (step % t) + section * (step // 2)

            @pl.when(forward == 1)
            def _():
                self.forward(r, table, section, relay)

            @pl.when(forward == 0)
            def _():
                self.backward(r, table, section, relay)

        @pl.when(section == 1)
        def _():
            for table in range(t):
                for half in range(2):
                    relay(table, half).wait_send()

    def forward(self, r, table, section, relay):
        c, w, ff, hd, real = self.cells, self.width, self.ff, self.hd, self.real
        stores, held = [], []

        def keep(src, dst, to_reload=False):
            copy = pltpu.make_async_copy(src, dst, r.out_sem.at[len(stores) + len(held)])
            if to_reload:
                held.append(copy)
                pl.when(section == 0)(copy.start)
            else:
                stores.append(copy)
                copy.start()

        for level in range(2):
            r.h_v[level, real:, :] = jnp.zeros((c - real, w), F32)
        fill_biases(self.feat, self.rows, r.ctx[table], r.col_bias[1], 1)

        @pl.when(section == 0)
        def _():
            start(r.cells.at[table], r.dy_v.at[0:real], r.in_sem.at[0]).wait()
            r.dy_v[0:real] = jnp.where(r.mask[table, 0:real] == 1.0, r.embed[...], r.dy_v[0:real])
            self.set_out(r, r.dy_v, real)

        @pl.when(section == 1)
        def _():
            start(r.cot.at[table], r.dy_v.at[0:real], r.in_sem.at[1])
            for half in range(2):
                relay(table, half).wait_recv()
            self.set_out(r, r.got.at[table], real)

        self.by_rows(r, r.h_v.at[0])
        keep(r.h_v.at[0], r.hs.at[table, 0], True)
        for site in range(2):
            put(r.a_v, (site,), normalized(r.h_v[site])[0] * r.gains[site : site + 1, :])
            keep(r.a_v.at[:, site], r.as_.at[table, :, site])

            def project(j):
                at = slice(j * TILE, (j + 1) * TILE)
                return wide(parts(r.a_v, site), parts(r.win_v, site, slice(None), at), 1, 0)

            def keep_projected(j, out):
                if j < w // TILE:
                    out = out * (self.scale * LOG2E)
                put(r.qkv_v, (site, slice(None), slice(j * TILE, (j + 1) * TILE)), out)

            staggered([(j,) for j in range(3 * w // TILE)], project, keep_projected)
            keep(r.qkv_v.at[:, site], r.qkvs.at[table, :, site], True)

            def scores(head, queries, keys, bias):
                q = parts(r.qkv_v, site, queries, lanes(head, hd))
                k = parts(r.qkv_v, site, keys, lanes(HEADS + head, hd))
                return wide(q, k, 1, 1)

            def softmax(head, queries, keys, bias, s):
                s = s + bias[...]
                top = jnp.max(s, axis=-1, keepdims=True)
                e = jnp.exp2(s - top)
                total = jnp.sum(e, axis=-1, keepdims=True)
                column = lax.broadcasted_iota(jnp.int32, (1, r.stat_v.shape[1]), 1) == site * HEADS + head
                r.stat_v[queries, :] = jnp.where(column, top + jnp.log2(total), r.stat_v[queries, :])
                return split(e), 1.0 / total

            def blend(head, queries, keys, bias, state):
                e, inverse = state
                v = parts(r.qkv_v, site, keys, lanes(2 * HEADS + head, hd))
                put(r.o_v, (site, queries, lanes(head, hd)), side(e, v) * inverse)

            @pl.loop(0, HEADS // 2)
            def _(two):
                units = [(head, *unit) for head in (2 * two, 2 * two + 1) for unit in self.sites(r, site, 1)]
                staggered(units, scores, softmax, blend)

            keep(r.o_v.at[:, site], r.os.at[table, :, site])
            after = r.h_v[site] + wide(parts(r.o_v, site), parts(r.wout_v, site), 1, 0)
            if site == 0:
                self.set_out(r, after, c)
                self.by_features(r, r.h_v.at[1])
            else:
                r.h_v[2] = after
            keep(r.h_v.at[site + 1], r.hs.at[table, site + 1], True)
        r.lse_v[table] = r.stat_v[...].T[0 : 2 * HEADS]
        put(r.a_v, (2,), normalized(r.h_v[2])[0] * r.gains[2:3, :])
        keep(r.a_v.at[:, 2], r.as_.at[table, :, 2])

        def up(j):
            return wide(parts(r.a_v, 2), parts(r.wup_v, slice(None), slice(j * TILE, (j + 1) * TILE)), 1, 0)

        tiles = ff // TILE
        z = up(0)
        for j in range(tiles):
            at = slice(j * TILE, (j + 1) * TILE)
            following = up(j + 1) if j + 1 < tiles else None
            g, gp = gelu_parts(z)
            put(r.g_v, (slice(None), at), g)
            r.gp_v[:, at] = gp
            z = following
        keep(r.g_v, r.gs.at[table])
        keep(r.gp_v, r.gps.at[table], True)
        for half in range(2):
            at = slice(half * w // 2, (half + 1) * w // 2)
            r.y_v[table, :, at] = r.h_v[2, :, at] + wide(parts(r.g_v), parts(r.wdown_v, slice(None), at), 1, 0)

            @pl.when(section == 0)
            def _():
                relay(table, half).start()

        keep(r.y_v.at[table, 0:real], r.out.at[table])
        for copy in stores:
            copy.wait()

        @pl.when(section == 0)
        def _():
            for copy in held:
                copy.wait()

    def backward(self, r, table, section, relay):
        c, w, ff, hd, real = self.cells, self.width, self.ff, self.hd, self.real
        stores = []

        def keep(src, dst):
            stores.append(start(src, dst, r.out_sem.at[len(stores)]))

        fill_biases(self.feat, self.rows, r.ctx[table], r.col_bias[0], 0)

        @pl.when(section == 0)
        def _():
            loads = [
                start(r.hs.at[table], r.h_v, r.in_sem.at[0]),
                start(r.qkvs.at[table], r.qkv_v, r.in_sem.at[1]),
                start(r.gps.at[table], r.gp_v, r.in_sem.at[2]),
            ]
            for half in range(2):
                relay(table, half).wait()
            r.dy_v[0:real] = r.got[table]
            for copy in loads:
                copy.wait()

        @pl.when(section == 1)
        def _():
            pltpu.make_async_copy(r.cot.at[table], r.dy_v.at[0:real], r.in_sem.at[1]).wait()

        r.dy_v[real:, :] = jnp.zeros((c - real, w), F32)
        put(r.dys_v, (), r.dy_v[...])
        keep(r.dys_v, r.dys.at[table])

        def down(j):
            return wide(parts(r.dys_v), parts(r.wdown_v, slice(j * TILE, (j + 1) * TILE)), 1, 1)

        tiles = ff // TILE
        dg = down(0)
        for j in range(tiles):
            at = slice(j * TILE, (j + 1) * TILE)
            following = down(j + 1) if j + 1 < tiles else None
            put(r.g_v, (slice(None), at), dg * r.gp_v[:, at])
            dg = following
        keep(r.g_v, r.dzs.at[table])
        da = wide(parts(r.g_v), parts(r.wup_v), 1, 1)

        def through_norm(site, da):
            n, rstd = normalized(r.h_v[site])
            r.small[site : site + 1, :] += jnp.sum(da * n, axis=0, keepdims=True)
            return norm_back(n, rstd, r.gains[site : site + 1, :], da)

        r.dy_v[...] += through_norm(2, da)
        for site in (1, 0):
            if site == 0:
                self.set_out(r, r.dy_v, real)
                self.by_rows(r, r.dy_v)
            put(r.o_v, (site,), r.dy_v[...])
            keep(r.o_v.at[:, site], r.dhs.at[table, :, site])
            put(r.do_v, (), wide(parts(r.o_v, site), parts(r.wout_v, site), 1, 1))

            def part_of(which, head, span):
                return parts(r.qkv_v, site, span, lanes(which * HEADS + head, hd))

            def products(head, queries, keys, bias):
                do = parts(r.do_v, queries, lanes(head, hd))
                s = wide(part_of(1, head, keys), part_of(0, head, queries), 1, 1)
                return s, wide(part_of(2, head, keys), do, 1, 1)

            def gradients(head, queries, keys, bias, state):
                s, dp = state
                p = jnp.exp2(s + bias[...] - r.lse_v[table, pl.ds(site * HEADS + head, 1), queries])
                ds = p * (dp - jnp.sum(p * dp, axis=0, keepdims=True))
                return split(p), split(ds)

            def back(head, queries, keys, bias, state):
                p, ds = state
                k = part_of(1, head, keys)
                r.dqkv_f[queries, lanes(head, hd)] = (wide(tuple(x.T for x in k), ds, 1, 0) * self.scale).T
                dk = side(ds, part_of(0, head, queries)) * LN2
                dv = side(p, parts(r.do_v, queries, lanes(head, hd)))
                for which, term in ((1, dk), (2, dv)):
                    at = lanes(which * HEADS + head, hd)
                    if keys.start == 0:
                        r.dqkv_f[keys, at] = term
                    else:
                        known = overlap - keys.start
                        if known:
                            r.dqkv_f[keys.start : overlap, at] += term[:known]
                        r.dqkv_f[overlap : keys.stop, at] = term[known:]

            overlap = self.sites(r, site, 0)[0][1].stop

            @pl.loop(0, HEADS // 2)
            def _(two):
                units = [(head, *unit) for head in (2 * two, 2 * two + 1) for unit in self.sites(r, site, 0)]
                staggered(units, products, gradients, back)

            for j in range(3 * w // TILE):
                at = slice(j * TILE, (j + 1) * TILE)
                put(r.qkv_v, (site, slice(None), at), r.dqkv_f[:, at])
            keep(r.qkv_v.at[:, site], r.dqkvs.at[table, :, site])
            da = wide(parts(r.qkv_v, site), parts(r.win_v, site), 1, 1)
            r.dy_v[...] += through_norm(site, da)

        self.set_out(r, r.dy_v, real)
        self.by_features(r, r.dy_v)

        @pl.when(section == 0)
        def _():
            missing = r.mask[table] == 1.0
            r.small[3:4, :] += jnp.sum(jnp.where(missing, r.dy_v[...], 0.0), axis=0, keepdims=True)
            r.y_v[table] = jnp.where(missing, 0.0, r.dy_v[...])

        @pl.when(section == 1)
        def _():
            r.y_v[table] = r.dy_v[...]
            for half in range(2):
                relay(table, half).start()

        keep(r.y_v.at[table, 0:real], r.din.at[table])
        for copy in stores:
            copy.wait()


class GradSum:
    ROWS, COLS = 512, 256
    SLACK = 2

    def __init__(self, count, tables, cells, width, ff):
        self.count, self.tables, self.cells, self.width = count, tables, cells, width
        self.rest = count // 4
        shapes = [("gs", None, "dys", None, "down", None, ff, width), ("as_", 2, "dzs", None, "up", None, width, ff)]
        for site in (1, 0):
            shapes.append(("as_", site, "dqkvs", site, "win", site, width, 3 * width))
            shapes.append(("os", site, "dhs", site, "wout", site, width, width))
        self.groups, at = [], 0
        for *which, k, n in shapes:
            blocks = (k // self.ROWS) * (n // self.COLS)
            self.groups.append((at, at + blocks, *which, n // self.COLS))
            at += blocks
        self.blocks = at
        self.per_chunk = max(2, 4 * self.rest * 8 // self.ROWS)
        self.chunks = self.blocks // self.per_chunk
        self.rows = self.per_chunk * self.ROWS
        self.ring = self.SLACK + 2
        self.depth = (cells + 127) // 128 * 128

    def select(self, q, action):
        for group in self.groups:
            first, stop, *_, across = group

            @pl.when((q >= first) & (q < stop))
            def _():
                action(group, (q - first) // across, (q - first) % across)

    def starts_row(self, q):
        found = False
        for first, stop, *_, across in self.groups:
            found = found | ((q >= first) & (q < stop) & ((q - first) % across == 0))
        return found

    def load(self, r, q):
        slot = q % 2

        def action(group, i, j):
            _, _, left, left_site, right, right_site, *_ = group
            a, b = getattr(r, left), getattr(r, right)

            def at(t, part, site):
                return (t, part, slice(None)) if site is None else (t, part, site, slice(None))

            for t in range(self.tables):
                rows = slice(t * self.depth, t * self.depth + self.cells)
                for part in range(2):
                    sem = 2 * t + part
                    start(b.at[(*at(t, part, right_site), lanes(j, self.COLS))], r.b_v.at[slot, part, rows], r.b_sem.at[slot, sem])

                    @pl.when(j == 0)
                    def _():
                        start(a.at[(*at(t, part, left_site), lanes(i, self.ROWS))], r.a_v.at[part, rows], r.a_sem.at[sem])

        self.select(q, action)

    def each_operand(self):
        return [(2 * t + part, part, slice(t * self.depth, t * self.depth + self.cells)) for t in range(self.tables) for part in range(2)]

    def product(self, r, q):
        slot = q % 2

        @pl.when(self.starts_row(q))
        def _():
            for sem, part, rows in self.each_operand():
                a = r.a_v.at[part, rows]
                pltpu.make_async_copy(a, a, r.a_sem.at[sem]).wait()
            for part in range(2):
                r.left_v[part] = r.a_v[part].T

        for sem, part, rows in self.each_operand():
            b = r.b_v.at[slot, part, rows]
            pltpu.make_async_copy(b, b, r.b_sem.at[slot, sem]).wait()

        @pl.when(q + 1 < self.blocks)
        def _():
            self.load(r, q + 1)

        rows = pl.ds(pl.multiple_of(q % self.per_chunk * self.ROWS, self.ROWS), self.ROWS)
        r.products[q // self.per_chunk % self.ring, rows] = side(parts(r.left_v), parts(r.b_v.at[slot]))

    def kernel(self, r):
        rest, rows, ring = self.rest, self.rows, self.ring
        half = rows // 2
        quart = half // 2
        sizes = (quart // rest, half // rest)
        me, section = lax.axis_index("dp"), lax.axis_index("section")
        core, pair, place = me % 2, me // 2 % 2, me // 4
        sibling, neighbour = {"dp": me + 1 - 2 * core}, {"dp": me + 2 - 4 * pair}
        ways = ({"dp": me + 4}, {"dp": me - 4})

        def peer(j):
            return {"dp": lax.rem(place + j, rest) * 4 + me % 4}

        def span(at, size):
            return pl.ds(pl.multiple_of(at, size), size)

        mine = core * half
        own, other = pair * quart, (1 - pair) * quart
        bases = (own, 0)

        barrier = pltpu.get_barrier_semaphore()

        def greet(device):
            pl.semaphore_signal(barrier, inc=1, device_id=device, device_id_type=pl.DeviceIdType.MESH)

        greet(sibling)
        greet(neighbour)

        @pl.loop(1, rest)
        def _(j):
            greet(peer(j))

        for t in range(self.tables):
            pad = slice(t * self.depth + self.cells, (t + 1) * self.depth)
            for part in range(2):
                r.a_v[part, pad] = jnp.zeros_like(r.a_v[part, pad])
                for slot in range(2):
                    r.b_v[slot, part, pad] = jnp.zeros_like(r.b_v[slot, part, pad])
        self.load(r, 0)

        @pl.when(section == 1)
        def _():
            greet({"section": 0})

        pl.semaphore_wait(barrier, rest + 2 - section)

        def halve(c):
            src = r.products.at[c % ring, span((1 - core) * half, half)]
            return remote(src, r.sums.at[c], r.send.at[0, c % ring], r.recv.at[0, c], sibling)

        def gather_half(c):
            at = r.full.at[c, span(mine, half)]
            return remote(at, at, r.send.at[1, c % ring], r.recv.at[1, c], sibling)

        def quarter(c):
            dst = r.got_near.at[c]
            return remote(r.sums.at[c, span(other, quart)], dst, r.send.at[2, c % ring], r.recv.at[2, c], neighbour)

        def gather_quarter(c):
            at = r.full.at[c, span(mine + own, quart)]
            return remote(at, at, r.send.at[3, c % ring], r.recv.at[3, c], neighbour)

        def piece(kind, b):
            return span(bases[kind] + b * sizes[kind], sizes[kind])

        def full_piece(kind, b):
            return span(mine + bases[kind] + b * sizes[kind], sizes[kind])

        def add_up(c):
            dst = r.got_near.at[c, 0 : sizes[1]]
            return remote(r.sums.at[c, piece(1, place)], dst, r.send.at[2, c % ring], r.recv.at[2, c], neighbour)

        def line(kind, c, h, way, gather, b):
            if gather:
                src = dst = r.full.at[c, full_piece(kind, b)]
            else:
                src, dst = r.sums.at[c, piece(kind, b)], r.got_line.at[way, c, h, 0 : sizes[kind]]
            phase = 2 * way + int(gather)
            return remote(src, dst, r.send_line.at[phase, c % ring, h], r.recv_line.at[phase, c, h], ways[way])

        def hops(h, gather):
            if gather:
                right = ((place >= h) & (place < rest - 1), place - h, place >= h + 1, place - 1 - h)
                left = ((place + h < rest) & (place >= 1), place + h, place + 1 + h < rest, place + 1 + h)
            else:
                far = rest - 1 - h
                right = (place <= h, place + far, (place >= 1) & (place - 1 <= h), place - 1 + far)
                left = (rest - 1 - place <= h, place - far, (place <= rest - 2) & (rest - 2 - place <= h), place + 1 - far)
            return right, left

        def send_hop(kind, c, h, gather):
            for way, (sends, b, _, _) in enumerate(hops(h, gather)):

                @pl.when(sends)
                def _():
                    line(kind, c, h, way, gather, b).start()

        def end_hop(kind, c, h, gather):
            for way, (sends, b, receives, arriving) in enumerate(hops(h, gather)):

                @pl.when(sends)
                def _():
                    line(kind, c, h, way, gather, b).wait_send()

                @pl.when(receives)
                def _():
                    line(kind, c, h, way, gather, arriving).wait_recv()
                    if not gather:
                        r.sums[c, piece(kind, arriving)] += r.got_line[way, c, h, 0 : sizes[kind]]

        def hop(kind, c, h, gather, then):
            end_hop(kind, c, h, gather)

            @when(h < rest - 2)
            def _():
                send_hop(kind, c, h + 1, gather)

            @when(h == rest - 2)
            def _():
                then(c)

        def after_halve(c):
            halve(c).wait()
            r.sums[c] += r.products[c % ring, span(mine, half)]

            @pl.when(core == 0)
            def _():
                quarter(c).start()

            @pl.when(core == 1)
            def _():
                send_hop(1, c, 0, False)

        def after_quarter(c):
            quarter(c).wait()
            r.sums[c, span(own, quart)] += r.got_near[c]
            send_hop(0, c, 0, False)

        def scattered(c):
            r.full[c, full_piece(0, place)] = r.sums[c, piece(0, place)]
            send_hop(0, c, 0, True)

        def after_add_up(c):
            add_up(c).wait()
            r.full[c, full_piece(1, place)] = r.sums[c, piece(1, place)] + r.got_near[c, 0 : sizes[1]]
            send_hop(1, c, 0, True)

        def gathered(c):
            @pl.when(core == 0)
            def _():
                gather_quarter(c).wait()

            gather_half(c).start()

        def after_gather_half(c):
            gather_half(c).wait()

        def small_copy(k, device):
            return remote(r.small_v.at[k], r.got_small.at[k], r.small_send.at[k], r.small_recv.at[k], device)

        def small_rest(j):
            dst = r.got_small.at[2 + j]
            return remote(r.small_v.at[3], dst, r.small_send.at[2 + j], r.small_recv.at[2 + j], peer(j))

        def small_step(step):
            @pl.when(step == 2)
            def _():
                r.small_v[1] = r.small[...]
                small_copy(1, sibling).start()

            @pl.when(step == 4)
            def _():
                small_copy(1, sibling).wait()
                r.small_v[2] = r.small_v[1] + r.got_small[1]
                small_copy(2, neighbour).start()

            @pl.when(step == 6)
            def _():
                small_copy(2, neighbour).wait()
                r.small_v[3] = r.small_v[2] + r.got_small[2]
                pl.loop(1, rest)(lambda j: small_rest(j).start())

            @pl.when(step == 8)
            def _():
                pl.loop(1, rest)(lambda j: small_rest(j).wait())
                total = r.small_v[3]
                for j in range(1, rest):
                    total += r.got_small[2 + j]
                r.small_v[0] = total

                @pl.when(section == 0)
                def _():
                    small_copy(0, {"section": 1}).start()

        last = 2 * rest + 2

        @pl.loop(0, self.chunks + self.SLACK * last)
        def _(step):
            def stage(time, action):
                c = step - self.SLACK * time

                @pl.when((c >= 0) & (c < self.chunks))
                def _():
                    action(c)

            stage(last, after_gather_half)
            stage(last - 1, gathered)

            @pl.when(core == 0)
            def _():
                over(rest - 1, lambda h: stage(rest + 2 + h, lambda c: hop(0, c, h, True, lambda c: gather_quarter(c).start())))

                over(rest - 1, lambda h: stage(3 + h, lambda c: hop(0, c, h, False, scattered)))

                stage(2, after_quarter)

            @pl.when(core == 1)
            def _():
                over(rest - 1, lambda h: stage(rest + 2 + h, lambda c: hop(1, c, h, True, lambda c: None)))

                stage(rest + 1, after_add_up)

                over(rest - 1, lambda h: stage(2 + h, lambda c: hop(1, c, h, False, lambda c: add_up(c).start())))

            stage(1, after_halve)
            small_step(step)

            @pl.when(step < self.chunks)
            def _():
                @pl.loop(0, self.per_chunk)
                def _(u):
                    self.product(r, step * self.per_chunk + u)

                halve(step).start()

        r.small_out[...] = r.small_v[0]

        @pl.when(section == 0)
        def _():
            small_copy(0, {"section": 1}).wait_send()

        @pl.when(section == 1)
        def _():
            small_copy(0, {"section": 1}).wait_recv()
            r.small_out[3:4] = r.got_small[0, 3:4]

    def __call__(self, operands, small):
        t, width, deep = self.tables, self.width, self.tables * self.depth
        rest, chunks, rows, ring, cols = self.rest, self.chunks, self.rows, self.ring, self.COLS
        outs = {"full": VMEM((chunks, rows, cols), F32), "small_out": f32(8, width)}
        scratch = {
            "products": VMEM((ring, rows, cols), F32),
            "sums": VMEM((chunks, rows // 2, cols), F32),
            "got_near": VMEM((chunks, rows // 4, cols), F32),
            "got_line": VMEM((2, chunks, rest - 1, rows // 2 // rest, cols), F32),
            "a_v": VMEM((2, deep, self.ROWS), BF16),
            "left_v": VMEM((2, self.ROWS, deep), BF16),
            "b_v": VMEM((2, 2, deep, cols), BF16),
            "small_v": VMEM((4, 8, width), F32),
            "got_small": VMEM((2 + rest, 8, width), F32),
            "a_sem": dma(2 * t),
            "b_sem": dma(2, 2 * t),
            "send": dma(4, ring),
            "recv": dma(4, chunks),
            "send_line": dma(4, ring, rest - 1),
            "recv_line": dma(4, chunks, rest - 1),
            "small_send": dma(2 + rest),
            "small_recv": dma(2 + rest),
        }
        ins = {n: (a, ANY) for n, a in operands.items()} | {"small": (small, VMEM)}
        outs = {n: (s, VMEM) for n, s in outs.items()}
        return call("weight_gradient_sum", self.kernel, 0, ins, outs, scratch, SUM_VMEM_LIMIT)

    def results(self, sums, small, tables, ff):
        width = self.width
        sums = pltpu.with_memory_space_constraint(sums, pltpu.VMEM)
        ins = {"full": (sums, VMEM), "small": (small, VMEM)} | {f"table{i}": (a, ANY) for i, a in enumerate(tables)}
        outs = {
            "win": f32(2, width, 3 * width),
            "wout": f32(2, width, width),
            "up": f32(width, ff),
            "down": f32(ff, width),
        } | {f"out{i}": f32(*a.shape) for i, a in enumerate(tables)}
        outs = {n: (s, ANY) for n, s in outs.items()}
        outs |= {"gain": (f32(1, 3, width), VMEM), "missing": (f32(1, width), VMEM)}
        scratch = {f"table_v{i}": VMEM(a.shape, F32) for i, a in enumerate(tables)}
        scratch |= {"sem": dma(self.blocks), "in_sem": dma(len(tables)), "out_sem": dma(len(tables))}

        def body(r):
            buffers = [getattr(r, f"table_v{i}") for i in range(len(tables))]
            loads = [start(getattr(r, f"table{i}"), v, r.in_sem.at[i]) for i, v in enumerate(buffers)]
            stores = []
            for first, stop, *_, out, site, across in self.groups:
                dst = getattr(r, out) if site is None else getattr(r, out).at[site]
                for q in range(first, stop):
                    i, j = (q - first) // across, (q - first) % across
                    u = q % self.per_chunk
                    src = r.full.at[q // self.per_chunk, u * self.ROWS : (u + 1) * self.ROWS]
                    at = (slice(i * self.ROWS, (i + 1) * self.ROWS), slice(j * self.COLS, (j + 1) * self.COLS))
                    stores.append(start(src, dst.at[at], r.sem.at[q]))
            r.gain[0] = r.small[0:3, :]
            r.missing[...] = r.small[3:4, :]
            for i, v in enumerate(buffers):
                loads[i].wait()
                stores.append(start(v, getattr(r, f"out{i}"), r.out_sem.at[i]))
            for copy in stores:
                copy.wait()

        return call("results", body, None, ins, outs, scratch, SUM_VMEM_LIMIT)


def local(
    cells,
    missing_mask,
    missing_embed,
    context_rows,
    norm_gains,
    attn_in,
    attn_out,
    mlp_up,
    mlp_down,
    cotangent,
):
    tables, rows, feat, width = cells.shape
    ff = mlp_up.shape[2]
    layers = Layers(tables, rows, feat, width, ff)

    def flat(tables_of_cells):
        return jnp.swapaxes(tables_of_cells, 1, 2).reshape(tables, rows * feat, -1)

    def unflat(cells_of_tables):
        return jnp.swapaxes(cells_of_tables.reshape(tables, feat, rows, width), 1, 2)[None]

    mask = jnp.pad(flat(missing_mask == 1).astype(F32), ((0, 0), (0, layers.cells - rows * feat), (0, 0)))
    weights = (attn_in[0], attn_out[0], mlp_up[0], mlp_down[0])
    done = layers(flat(cells), mask, missing_embed[None], context_rows, norm_gains[0], weights, flat(cotangent))
    operands = {n: done[n] for n in ("as_", "os", "gs", "dys", "dzs", "dhs", "dqkvs")}
    grad_sum = GradSum(lax.axis_size("dp"), tables, layers.cells, width, ff)
    sums = grad_sum(operands, done["small"])
    got = grad_sum.results(sums["full"], sums["small_out"], (done["out"], done["din"]), ff)
    return (
        unflat(got["out0"]),
        unflat(got["out1"]),
        got["gain"],
        got["win"][None],
        got["wout"][None],
        got["up"][None],
        got["down"][None],
        got["missing"][0],
    )


def solution(mesh):
    in_specs = (
        P("dp", None, None, None),
        P("dp", None, None),
        P(),
        P("dp"),
        P("section", None, None),
        P("section", None, None, None),
        P("section", None, None, None),
        P("section", None, None),
        P("section", None, None),
        P("dp", None, None, None),
    )
    out_specs = (
        P("section", "dp", None, None, None),
        P("section", "dp", None, None, None),
        P("section", None, None),
        P("section", None, None, None),
        P("section", None, None, None),
        P("section", None, None),
        P("section", None, None),
        P(),
    )
    return jax.shard_map(local, mesh=mesh, in_specs=in_specs, out_specs=out_specs, check_vma=False)
```

```python
import functools
from types import SimpleNamespace

import jax
import jax.numpy as jnp
from jax import lax
from jax.experimental import pallas as pl
from jax.experimental.pallas import tpu as pltpu
from jax.sharding import PartitionSpec as P

HEADS = 4
EPSILON = 1e-05
NEG = -1e30
INV_SQRT2PI = 0.3989422804014327
LOG2E = 1.4426950408889634
LN2 = 0.6931471805599453
ERFC_P = 0.33
ERFC_C = (0.1863578482, 0.1829552331, 0.2012284886, 0.0472047191, 0.4085317677, -0.3511862269, 0.4602596132, -0.1353514118)
VMEM_LIMIT = 62 * 1024 * 1024
SUM_VMEM_LIMIT = 44 * 1024 * 1024
TILE = 512
F32, BF16 = jnp.float32, jnp.bfloat16


def dot(a, b, contract=((1,), (0,))):
    return lax.dot_general(a, b, (contract, ((), ())), preferred_element_type=F32)


def split(v):
    hi = v.astype(BF16)
    return hi, (v - hi.astype(F32)).astype(BF16)


def put(ref, index, v):
    hi, lo = split(v)
    ref[(0, *index)] = hi
    ref[(1, *index)] = lo


def parts(ref, *index):
    return ref[(0, *index)], ref[(1, *index)]


def wide(a, b, ca, cb):
    (ah, al), (bh, bl) = a, b
    return dot(jnp.concatenate([ah, ah, al], ca), jnp.concatenate([bh, bl, bh], cb), ((ca,), (cb,)))


def side(a, b):
    (ah, al), (bh, bl) = a, b
    width = bh.shape[1]
    both = dot(ah, jnp.concatenate([bh, bl], 1))
    return both[:, :width] + both[:, width:] + dot(al, bh)


def normalized(h):
    centred = h - jnp.mean(h, axis=-1, keepdims=True)
    rstd = lax.rsqrt(jnp.mean(centred * centred, axis=-1, keepdims=True) + EPSILON)
    return centred * rstd, rstd


def norm_back(n, rstd, gain, da):
    dn = da * gain
    return rstd * (dn - jnp.mean(dn, axis=-1, keepdims=True) - n * jnp.mean(dn * n, axis=-1, keepdims=True))


def cell_ids(start, count, inner, along):
    shape = (count, 1) if along == 0 else (1, count)
    at = lax.broadcasted_iota(jnp.int32, shape, along) + start
    outer = lax.shift_right_logical(at * ((1 << 20) // inner + 1), 20)
    return outer, at - outer * inner


def up16(n):
    return (n + 15) // 16 * 16


def blocks(outer, inner):
    cells = up16(outer * inner)
    half = up16((outer + 1) // 2 * inner)
    first_keys = min(cells, up16((((half - 1) // inner) + 1) * inner))
    second_keys = ((half // inner) * inner) // 16 * 16
    return ((slice(0, half), slice(0, first_keys)), (slice(half, cells), slice(second_keys, cells)))


def when(cond):
    if isinstance(cond, bool):
        return (lambda action: action()) if cond else (lambda action: None)
    return pl.when(cond)


def over(count, action):
    if count <= 4:
        for i in range(count):
            action(i)
    else:
        pl.loop(0, count)(action)


def staggered(units, *steps):
    state = [None] * len(units)
    for i in range(len(units) + 1):
        if i < len(units):
            state[i] = steps[0](*units[i])
        if i > 0:
            for step in steps[1:]:
                state[i - 1] = step(*units[i - 1], state[i - 1])


def lanes(j, width):
    return pl.ds(pl.multiple_of(j * width, width), width)


def start(src, dst, sem):
    copy = pltpu.make_async_copy(src, dst, sem)
    copy.start()
    return copy


def fill_biases(outer, inner, limit, refs, keys_along):
    for (queries, keys), ref in zip(blocks(outer, inner), refs):
        q_outer, _ = cell_ids(queries.start, queries.stop - queries.start, inner, 1 - keys_along)
        k_outer, k_inner = cell_ids(keys.start, keys.stop - keys.start, inner, keys_along)
        ref[...] = jnp.where((q_outer == k_outer) & (k_inner < limit), 0.0, NEG)


def gelu_parts(z):
    size = jnp.abs(z)
    below = 1.0 + (ERFC_P * 0.7071067811865476) * size
    t = pl.reciprocal(below, approx=True)
    t = t * (2.0 - below * t)
    series = jnp.full_like(t, ERFC_C[-1])
    for c in ERFC_C[-2::-1]:
        series = series * t + c
    bell = jnp.exp(-0.5 * z * z)
    tail = 0.5 * (series * t) * bell
    phi = jnp.where(z >= 0.0, 1.0 - tail, tail)
    return z * phi, phi + z * (INV_SQRT2PI * bell)


SMEM, VMEM, ANY = pltpu.SMEM, pltpu.VMEM, pl.ANY


def f32(*shape):
    return jax.ShapeDtypeStruct(shape, F32)


def b16(*shape):
    return jax.ShapeDtypeStruct(shape, BF16)


def dma(*shape):
    return pltpu.SemaphoreType.DMA(shape)


def remote(src, dst, send, recv, device):
    return pltpu.make_async_remote_copy(
        src_ref=src, dst_ref=dst, send_sem=send, recv_sem=recv, device_id=device, device_id_type=pl.DeviceIdType.MESH
    )


def call(name, body, collective_id, ins, outs, scratch, limit):
    names = [*ins, *outs, *scratch]

    def kernel(*refs):
        body(SimpleNamespace(**dict(zip(names, refs))))

    results = pl.pallas_call(
        kernel,
        out_shape=[t for t, _ in outs.values()],
        in_specs=[pl.BlockSpec(memory_space=s) for _, s in ins.values()],
        out_specs=[pl.BlockSpec(memory_space=s) for _, s in outs.values()],
        scratch_shapes=list(scratch.values()),
        compiler_params=pltpu.CompilerParams(
            vmem_limit_bytes=limit, collective_id=collective_id, has_side_effects=collective_id is not None
        ),
        name=name,
    )(*(a for a, _ in ins.values()))
    return dict(zip(outs, results))


class Layers:
    SPLIT_ROWS = 64

    def __init__(self, tables, rows, feat, width, ff):
        self.tables, self.rows, self.feat, self.width, self.ff = tables, rows, feat, width, ff
        self.real, self.cells = rows * feat, up16(rows * feat)
        self.hd = width // HEADS
        self.scale = self.hd ** (-0.5)

    def sites(self, r, site, keys_along):
        if site == 1:
            ranges, biases = blocks(self.feat, self.rows), r.col_bias
        else:
            ranges, biases = blocks(self.rows, self.feat), r.row_bias
        return [(*unit, bias) for unit, bias in zip(ranges, biases[keys_along])]

    def set_out(self, r, src, count):
        for k in range(self.width // 128):
            r.perm_v[k, 0:count] = src[0:count, k * 128 : (k + 1) * 128]

    def by_rows(self, r, dst):
        for row in range(self.rows):
            for k in range(self.width // 128):
                at = (slice(row * self.feat, (row + 1) * self.feat), slice(k * 128, (k + 1) * 128))
                dst[at] = r.perm_v[k, pl.ds(row, self.feat, stride=self.rows), :]

    def by_features(self, r, dst):
        for feat in range(self.feat):
            for k in range(self.width // 128):
                at = (slice(feat * self.rows, (feat + 1) * self.rows), slice(k * 128, (k + 1) * 128))
                dst[at] = r.perm_v[k, pl.ds(feat, self.rows, stride=self.feat), :]

    def __call__(self, cells, mask, embed, context, gains, weights, cotangent):
        t, c, w, ff, real = self.tables, self.cells, self.width, self.ff, self.real
        rows, feat = self.rows, self.feat
        ins = {
            "cells": (cells, ANY),
            "mask": (mask, VMEM),
            "embed": (embed, VMEM),
            "ctx": (context, SMEM),
            "gains": (gains, VMEM),
            "cot": (cotangent, ANY),
        }
        names = ("win", "wout", "wup", "wdown")
        ins |= {n: (a, ANY) for n, a in zip(names, weights)}
        outs = {
            "out": f32(t, real, w),
            "din": f32(t, real, w),
            "hs": f32(t, 3, c, w),
            "qkvs": b16(t, 2, 2, c, 3 * w),
            "gps": f32(t, c, ff),
            "as_": b16(t, 2, 3, c, w),
            "os": b16(t, 2, 2, c, w),
            "gs": b16(t, 2, c, ff),
            "dys": b16(t, 2, c, w),
            "dzs": b16(t, 2, c, ff),
            "dhs": b16(t, 2, 2, c, w),
            "dqkvs": b16(t, 2, 2, c, 3 * w),
        }
        outs = {n: (s, ANY) for n, s in outs.items()} | {"small": (f32(8, w), VMEM)}
        scratch = {n + "_v": VMEM((2, *a.shape), BF16) for n, a in zip(names, weights)}
        scratch |= {
            "h_v": VMEM((3, c, w), F32),
            "qkv_v": VMEM((2, 2, c, 3 * w), BF16),
            "o_v": VMEM((2, 2, c, w), BF16),
            "gp_v": VMEM((c, ff), F32),
            "g_v": VMEM((2, c, ff), BF16),
            "a_v": VMEM((2, 3, c, w), BF16),
            "y_v": VMEM((t, c, w), F32),
            "dqkv_f": VMEM((c, 3 * w), F32),
            "perm_v": VMEM((w // 128, c, 128), F32),
            "dys_v": VMEM((2, c, w), BF16),
            "dy_v": VMEM((c, w), F32),
            "do_v": VMEM((2, c, w), BF16),
            "got": VMEM((t, real, w), F32),
            "stat_v": VMEM((c, 128), F32),
            "lse_v": VMEM((t, 2 * HEADS, c), F32),
            "spare_v": VMEM((w // 2, w), F32),
            "raw_sem": pltpu.SemaphoreType.DMA((20,)),
            "in_sem": pltpu.SemaphoreType.DMA((4,)),
            "out_sem": pltpu.SemaphoreType.DMA((16,)),
            "send": pltpu.SemaphoreType.DMA((t, 2)),
            "recv": pltpu.SemaphoreType.DMA((t, 2)),
        }
        for name, ranges in (("col_bias", blocks(feat, rows)), ("row_bias", blocks(rows, feat))):
            for i, (queries, keys) in enumerate(ranges):
                shape = (queries.stop - queries.start, keys.stop - keys.start)
                scratch[f"{name}0{i}"] = VMEM(shape[::-1], F32)
                scratch[f"{name}1{i}"] = VMEM(shape, F32)

        def body(r):
            for n in ("col_bias", "row_bias"):
                setattr(r, n, [[getattr(r, f"{n}{along}{i}") for i in range(2)] for along in range(2)])
            self.kernel(r)

        return call("layers", body, 1, ins, outs, scratch, VMEM_LIMIT)

    def raw_pieces(self, r):
        w, ff = self.width, self.ff
        half, wide_in, step = w // 2, 3 * w, self.SPLIT_ROWS
        top, rest, whole = slice(0, half), slice(half, w), slice(None)
        big, bigger = r.dqkv_f.at[top], r.gp_v.at[top]
        pieces = [
            (r.win.at[0, top], big, r.win_v, (0,), 0, whole, 0),
            (r.win.at[0, rest], bigger.at[:, 0:wide_in], r.win_v, (0,), half, whole, 1),
            (r.wout.at[0, top], r.h_v.at[0, top], r.wout_v, (0,), 0, whole, 2),
            (r.wout.at[0, rest], r.h_v.at[1, top], r.wout_v, (0,), half, whole, 3),
            (r.win.at[1, top], big, r.win_v, (1,), 0, whole, 0),
            (r.win.at[1, rest], bigger.at[:, 0:wide_in], r.win_v, (1,), half, whole, 1),
            (r.wout.at[1, top], r.h_v.at[2, top], r.wout_v, (1,), 0, whole, 4),
            (r.wout.at[1, rest], r.spare_v, r.wout_v, (1,), half, whole, 5),
        ]
        self.attention_pieces = len(pieces)
        pieces.append((r.wup.at[top], bigger, r.wup_v, (), 0, whole, 1))
        pieces.append((r.wup.at[rest, 0:wide_in], big, r.wup_v, (), half, slice(0, wide_in), 0))
        pieces.append((r.wup.at[rest, wide_in:ff], r.spare_v, r.wup_v, (), half, slice(wide_in, ff), 5))
        high = self.cells // step * step
        buffers = [r.y_v.at[0, 0:high], r.y_v.at[1, 0:high]]
        low = slice(half, half + (self.cells - half) // step * step)
        for k in range(3):
            buffers.append(r.dqkv_f.at[low, k * w : (k + 1) * w])
        for k in range(ff // w):
            buffers.append(r.gp_v.at[low, k * w : (k + 1) * w])
        at = 0
        for i, buffer in enumerate(buffers):
            size = min(buffer.shape[0], ff - at)
            if size:
                pieces.append((r.wdown.at[at : at + size], buffer.at[0:size], r.wdown_v, (), at, whole, 6 + i))
            at += size
        assert at == ff
        return pieces

    def raw_copy(self, r, i):
        src, buffer = self.raw_pieces(r)[i][:2]
        return pltpu.make_async_copy(src, buffer, r.raw_sem.at[i])

    def split_piece(self, r, i):
        pieces = self.raw_pieces(r)
        _, buffer, v, lead, at, columns, user = pieces[i]
        step = self.SPLIT_ROWS
        self.raw_copy(r, i).wait()

        @pl.loop(0, buffer.shape[0] // step)
        def _(j):
            src = pl.ds(pl.multiple_of(j * step, step), step)
            dst = pl.ds(pl.multiple_of(at + j * step, step), step)
            put(v, (*lead, dst, columns), buffer[src])

        later = [k for k in range(i + 1, len(pieces)) if pieces[k][-1] == user]
        if later:
            self.raw_copy(r, later[0]).start()

    def start_raw(self, r):
        seen = set()
        for i, piece in enumerate(self.raw_pieces(r)):
            if piece[-1] not in seen:
                self.raw_copy(r, i).start()
            seen.add(piece[-1])

    def split_attention(self, r):
        for i in range(self.attention_pieces):
            self.split_piece(r, i)

    def split_mlp(self, r):
        for i in range(self.attention_pieces, len(self.raw_pieces(r))):
            self.split_piece(r, i)

    def kernel(self, r):
        t, real, c = self.tables, self.real, self.cells
        section = lax.axis_index("section")
        other = {"section": 1 - section}
        barrier = pltpu.get_barrier_semaphore()
        pl.semaphore_signal(barrier, inc=1, device_id=other, device_id_type=pl.DeviceIdType.MESH)
        self.start_raw(r)

        @pl.when(section == 0)
        def _():
            start(r.cells.at[0], r.dy_v.at[0:real], r.in_sem.at[0])

        self.split_attention(r)

        @pl.when(section == 1)
        def _():
            self.split_mlp(r)

        for along in range(2):
            fill_biases(self.rows, self.feat, self.feat, r.row_bias[along], along)
        r.small[...] = jnp.zeros_like(r.small)
        pl.semaphore_wait(barrier, 1)

        def relay(table, half):
            at = slice(half * self.width // 2, (half + 1) * self.width // 2)
            src, dst = r.y_v.at[table, 0:real, at], r.got.at[table, :, at]
            return remote(src, dst, r.send.at[table, half], r.recv.at[table, half], other)

        @pl.loop(0, 2 * t)
        def _(step):
            forward = (1 - section) * (1 - step // t) + section * (1 - step % 2)
            table = (1 - section) * (step % t) + section * (step // 2)

            @pl.when(forward == 1)
            def _():
                self.forward(r, table, section, relay, step)

            @pl.when(forward == 0)
            def _():
                self.backward(r, table, section, relay)

        @pl.when(section == 1)
        def _():
            for table in range(t):
                for half in range(2):
                    relay(table, half).wait_send()

    def forward(self, r, table, section, relay, step):
        c, w, ff, hd, real = self.cells, self.width, self.ff, self.hd, self.real
        stores, held = [], []

        def keep(src, dst, to_reload=False):
            copy = pltpu.make_async_copy(src, dst, r.out_sem.at[len(stores) + len(held)])
            if to_reload:
                held.append(copy)
                pl.when(section == 0)(copy.start)
            else:
                stores.append(copy)
                copy.start()

        for level in range(2):
            r.h_v[level, real:, :] = jnp.zeros((c - real, w), F32)
        fill_biases(self.feat, self.rows, r.ctx[table], r.col_bias[1], 1)

        @pl.when(section == 0)
        def _():
            load = pltpu.make_async_copy(r.cells.at[table], r.dy_v.at[0:real], r.in_sem.at[0])
            pl.when(step > 0)(load.start)
            load.wait()
            r.dy_v[0:real] = jnp.where(r.mask[table, 0:real] == 1.0, r.embed[...], r.dy_v[0:real])
            self.set_out(r, r.dy_v, real)

        @pl.when(section == 1)
        def _():
            start(r.cot.at[table], r.dy_v.at[0:real], r.in_sem.at[1])
            for half in range(2):
                relay(table, half).wait_recv()
            self.set_out(r, r.got.at[table], real)

        self.by_rows(r, r.h_v.at[0])
        keep(r.h_v.at[0], r.hs.at[table, 0], True)
        for site in range(2):
            put(r.a_v, (site,), normalized(r.h_v[site])[0] * r.gains[site : site + 1, :])
            keep(r.a_v.at[:, site], r.as_.at[table, :, site])

            def project(j):
                at = slice(j * TILE, (j + 1) * TILE)
                return wide(parts(r.a_v, site), parts(r.win_v, site, slice(None), at), 1, 0)

            def keep_projected(j, out):
                if j < w // TILE:
                    out = out * (self.scale * LOG2E)
                put(r.qkv_v, (site, slice(None), slice(j * TILE, (j + 1) * TILE)), out)

            staggered([(j,) for j in range(3 * w // TILE)], project, keep_projected)
            keep(r.qkv_v.at[:, site], r.qkvs.at[table, :, site], True)

            def scores(head, queries, keys, bias):
                q = parts(r.qkv_v, site, queries, lanes(head, hd))
                k = parts(r.qkv_v, site, keys, lanes(HEADS + head, hd))
                return wide(q, k, 1, 1)

            def softmax(head, queries, keys, bias, s):
                s = s + bias[...]
                top = jnp.max(s, axis=-1, keepdims=True)
                e = jnp.exp2(s - top)
                total = jnp.sum(e, axis=-1, keepdims=True)
                column = lax.broadcasted_iota(jnp.int32, (1, r.stat_v.shape[1]), 1) == site * HEADS + head
                r.stat_v[queries, :] = jnp.where(column, top + jnp.log2(total), r.stat_v[queries, :])
                return split(e), 1.0 / total

            def blend(head, queries, keys, bias, state):
                e, inverse = state
                v = parts(r.qkv_v, site, keys, lanes(2 * HEADS + head, hd))
                put(r.o_v, (site, queries, lanes(head, hd)), side(e, v) * inverse)

            @pl.loop(0, HEADS // 2)
            def _(two):
                units = [(head, *unit) for head in (2 * two, 2 * two + 1) for unit in self.sites(r, site, 1)]
                staggered(units, scores, softmax, blend)

            keep(r.o_v.at[:, site], r.os.at[table, :, site])
            after = r.h_v[site] + wide(parts(r.o_v, site), parts(r.wout_v, site), 1, 0)
            if site == 0:
                self.set_out(r, after, c)
                self.by_features(r, r.h_v.at[1])
            else:
                r.h_v[2] = after
            keep(r.h_v.at[site + 1], r.hs.at[table, site + 1], True)
        r.lse_v[table] = r.stat_v[...].T[0 : 2 * HEADS]
        put(r.a_v, (2,), normalized(r.h_v[2])[0] * r.gains[2:3, :])
        keep(r.a_v.at[:, 2], r.as_.at[table, :, 2])

        @pl.when((section == 0) & (step == 0))
        def _():
            self.split_mlp(r)

        def up(j):
            return wide(parts(r.a_v, 2), parts(r.wup_v, slice(None), slice(j * TILE, (j + 1) * TILE)), 1, 0)

        tiles = ff // TILE
        z = up(0)
        for j in range(tiles):
            at = slice(j * TILE, (j + 1) * TILE)
            following = up(j + 1) if j + 1 < tiles else None
            g, gp = gelu_parts(z)
            put(r.g_v, (slice(None), at), g)
            r.gp_v[:, at] = gp
            z = following
        keep(r.g_v, r.gs.at[table])
        keep(r.gp_v, r.gps.at[table], True)
        for half in range(2):
            at = slice(half * w // 2, (half + 1) * w // 2)
            r.y_v[table, :, at] = r.h_v[2, :, at] + wide(parts(r.g_v), parts(r.wdown_v, slice(None), at), 1, 0)

            @pl.when(section == 0)
            def _():
                relay(table, half).start()

        keep(r.y_v.at[table, 0:real], r.out.at[table])
        for copy in stores:
            copy.wait()

        @pl.when(section == 0)
        def _():
            for copy in held:
                copy.wait()

    def backward(self, r, table, section, relay):
        c, w, ff, hd, real = self.cells, self.width, self.ff, self.hd, self.real
        stores = []

        def keep(src, dst):
            stores.append(start(src, dst, r.out_sem.at[len(stores)]))

        fill_biases(self.feat, self.rows, r.ctx[table], r.col_bias[0], 0)

        @pl.when(section == 0)
        def _():
            loads = [
                start(r.hs.at[table], r.h_v, r.in_sem.at[0]),
                start(r.qkvs.at[table], r.qkv_v, r.in_sem.at[1]),
                start(r.gps.at[table], r.gp_v, r.in_sem.at[2]),
            ]
            for half in range(2):
                relay(table, half).wait()
            r.dy_v[0:real] = r.got[table]
            for copy in loads:
                copy.wait()

        @pl.when(section == 1)
        def _():
            pltpu.make_async_copy(r.cot.at[table], r.dy_v.at[0:real], r.in_sem.at[1]).wait()

        r.dy_v[real:, :] = jnp.zeros((c - real, w), F32)
        put(r.dys_v, (), r.dy_v[...])
        keep(r.dys_v, r.dys.at[table])

        def down(j):
            return wide(parts(r.dys_v), parts(r.wdown_v, slice(j * TILE, (j + 1) * TILE)), 1, 1)

        tiles = ff // TILE
        dg = down(0)
        for j in range(tiles):
            at = slice(j * TILE, (j + 1) * TILE)
            following = down(j + 1) if j + 1 < tiles else None
            put(r.g_v, (slice(None), at), dg * r.gp_v[:, at])
            dg = following
        keep(r.g_v, r.dzs.at[table])
        da = wide(parts(r.g_v), parts(r.wup_v), 1, 1)

        def through_norm(site, da):
            n, rstd = normalized(r.h_v[site])
            r.small[site : site + 1, :] += jnp.sum(da * n, axis=0, keepdims=True)
            return norm_back(n, rstd, r.gains[site : site + 1, :], da)

        r.dy_v[...] += through_norm(2, da)
        for site in (1, 0):
            if site == 0:
                self.set_out(r, r.dy_v, real)
                self.by_rows(r, r.dy_v)
            put(r.o_v, (site,), r.dy_v[...])
            keep(r.o_v.at[:, site], r.dhs.at[table, :, site])
            put(r.do_v, (), wide(parts(r.o_v, site), parts(r.wout_v, site), 1, 1))

            def part_of(which, head, span):
                return parts(r.qkv_v, site, span, lanes(which * HEADS + head, hd))

            def products(head, queries, keys, bias):
                do = parts(r.do_v, queries, lanes(head, hd))
                s = wide(part_of(1, head, keys), part_of(0, head, queries), 1, 1)
                return s, wide(part_of(2, head, keys), do, 1, 1)

            def gradients(head, queries, keys, bias, state):
                s, dp = state
                p = jnp.exp2(s + bias[...] - r.lse_v[table, pl.ds(site * HEADS + head, 1), queries])
                ds = p * (dp - jnp.sum(p * dp, axis=0, keepdims=True))
                return split(p), split(ds)

            def back(head, queries, keys, bias, state):
                p, ds = state
                k = part_of(1, head, keys)
                r.dqkv_f[queries, lanes(head, hd)] = (wide(tuple(x.T for x in k), ds, 1, 0) * self.scale).T
                dk = side(ds, part_of(0, head, queries)) * LN2
                dv = side(p, parts(r.do_v, queries, lanes(head, hd)))
                for which, term in ((1, dk), (2, dv)):
                    at = lanes(which * HEADS + head, hd)
                    if keys.start == 0:
                        r.dqkv_f[keys, at] = term
                    else:
                        known = overlap - keys.start
                        if known:
                            r.dqkv_f[keys.start : overlap, at] += term[:known]
                        r.dqkv_f[overlap : keys.stop, at] = term[known:]

            overlap = self.sites(r, site, 0)[0][1].stop

            @pl.loop(0, HEADS // 2)
            def _(two):
                units = [(head, *unit) for head in (2 * two, 2 * two + 1) for unit in self.sites(r, site, 0)]
                staggered(units, products, gradients, back)

            for j in range(3 * w // TILE):
                at = slice(j * TILE, (j + 1) * TILE)
                put(r.qkv_v, (site, slice(None), at), r.dqkv_f[:, at])
            keep(r.qkv_v.at[:, site], r.dqkvs.at[table, :, site])
            da = wide(parts(r.qkv_v, site), parts(r.win_v, site), 1, 1)
            r.dy_v[...] += through_norm(site, da)

        self.set_out(r, r.dy_v, real)
        self.by_features(r, r.dy_v)

        @pl.when(section == 0)
        def _():
            missing = r.mask[table] == 1.0
            r.small[3:4, :] += jnp.sum(jnp.where(missing, r.dy_v[...], 0.0), axis=0, keepdims=True)
            r.y_v[table] = jnp.where(missing, 0.0, r.dy_v[...])

        @pl.when(section == 1)
        def _():
            r.y_v[table] = r.dy_v[...]
            for half in range(2):
                relay(table, half).start()

        keep(r.y_v.at[table, 0:real], r.din.at[table])
        for copy in stores:
            copy.wait()


class GradSum:
    ROWS, COLS = 512, 256
    SLACK = 2

    def __init__(self, count, tables, cells, width, ff):
        self.count, self.tables, self.cells, self.width = count, tables, cells, width
        self.rest = count // 4
        shapes = [("gs", None, "dys", None, "down", None, ff, width), ("as_", 2, "dzs", None, "up", None, width, ff)]
        for site in (1, 0):
            shapes.append(("as_", site, "dqkvs", site, "win", site, width, 3 * width))
            shapes.append(("os", site, "dhs", site, "wout", site, width, width))
        self.groups, at = [], 0
        for *which, k, n in shapes:
            blocks = (k // self.ROWS) * (n // self.COLS)
            self.groups.append((at, at + blocks, *which, n // self.COLS))
            at += blocks
        self.blocks = at
        self.per_chunk = 1
        self.chunks = self.blocks // self.per_chunk
        self.hops = self.rest // 2 - 1
        self.sends = self.SLACK * (self.hops + 1) + 2
        self.rows = self.per_chunk * self.ROWS
        self.ring = self.SLACK + 2
        self.depth = (cells + 127) // 128 * 128

    def select(self, q, action):
        for group in self.groups:
            first, stop, *_, across = group

            @pl.when((q >= first) & (q < stop))
            def _():
                action(group, (q - first) // across, (q - first) % across)

    def starts_row(self, q):
        found = False
        for first, stop, *_, across in self.groups:
            found = found | ((q >= first) & (q < stop) & ((q - first) % across == 0))
        return found

    def load(self, r, q):
        slot = q % 2

        def action(group, i, j):
            _, _, left, left_site, right, right_site, *_ = group
            a, b = getattr(r, left), getattr(r, right)

            def at(t, part, site):
                return (t, part, slice(None)) if site is None else (t, part, site, slice(None))

            for t in range(self.tables):
                rows = slice(t * self.depth, t * self.depth + self.cells)
                for part in range(2):
                    sem = 2 * t + part
                    start(b.at[(*at(t, part, right_site), lanes(j, self.COLS))], r.b_v.at[slot, part, rows], r.b_sem.at[slot, sem])

                    @pl.when(j == 0)
                    def _():
                        start(a.at[(*at(t, part, left_site), lanes(i, self.ROWS))], r.a_v.at[part, rows], r.a_sem.at[sem])

        self.select(q, action)

    def each_operand(self):
        return [(2 * t + part, part, slice(t * self.depth, t * self.depth + self.cells)) for t in range(self.tables) for part in range(2)]

    def product(self, r, q):
        slot = q % 2

        @pl.when(self.starts_row(q))
        def _():
            for sem, part, rows in self.each_operand():
                a = r.a_v.at[part, rows]
                pltpu.make_async_copy(a, a, r.a_sem.at[sem]).wait()
            for part in range(2):
                r.left_v[part] = r.a_v[part].T

        for sem, part, rows in self.each_operand():
            b = r.b_v.at[slot, part, rows]
            pltpu.make_async_copy(b, b, r.b_sem.at[slot, sem]).wait()

        @pl.when(q + 1 < self.blocks)
        def _():
            self.load(r, q + 1)

        rows = pl.ds(pl.multiple_of(q % self.per_chunk * self.ROWS, self.ROWS), self.ROWS)
        r.products[q // self.per_chunk % self.ring, rows] = side(parts(r.left_v), parts(r.b_v.at[slot]))

    def kernel(self, r):
        rest, rows, ring = self.rest, self.rows, self.ring
        half = rows // 2
        quart = half // 2
        me, section = lax.axis_index("dp"), lax.axis_index("section")
        core, pair, place = me % 2, me // 2 % 2, me // 4
        sibling, neighbour = {"dp": me + 1 - 2 * core}, {"dp": me + 2 - 4 * pair}
        far = place // (rest // 2)
        along = (1 - far) * place + far * (rest - 1 - place)
        inward, outward = {"dp": me + 4 - 8 * far}, {"dp": me - 4 + 8 * far}
        hops = self.hops

        def peer(j):
            return {"dp": lax.rem(place + j, rest) * 4 + me % 4}

        def span(at, size):
            return pl.ds(pl.multiple_of(at, size), size)

        mine = core * half
        own, other = pair * quart, (1 - pair) * quart
        keeps, gives = far * quart, (1 - far) * quart

        barrier = pltpu.get_barrier_semaphore()

        def greet(device):
            pl.semaphore_signal(barrier, inc=1, device_id=device, device_id_type=pl.DeviceIdType.MESH)

        greet(sibling)
        greet(neighbour)

        @pl.loop(1, rest)
        def _(j):
            greet(peer(j))

        for t in range(self.tables):
            pad = slice(t * self.depth + self.cells, (t + 1) * self.depth)
            for part in range(2):
                r.a_v[part, pad] = jnp.zeros_like(r.a_v[part, pad])
                for slot in range(2):
                    r.b_v[slot, part, pad] = jnp.zeros_like(r.b_v[slot, part, pad])
        self.load(r, 0)

        @pl.when(section == 1)
        def _():
            greet({"section": 0})

        pl.semaphore_wait(barrier, rest + 2 - section)

        def copy(which, c, src, dst, device):
            return remote(src, dst, r.send.at[which, c % self.sends], r.recv.at[which, c], device)

        def halve(c):
            return copy(0, c, r.products.at[c % ring, span((1 - core) * half, half)], r.sums.at[c], sibling)

        def gather_half(c):
            at = r.full.at[c, span(mine, half)]
            return copy(1, c, at, at, sibling)

        def quarter(c):
            return copy(2, c, r.sums.at[c, span(other, quart)], r.got_near.at[c], neighbour)

        def gather_quarter(c):
            at = r.full.at[c, span(mine + own, quart)]
            return copy(3, c, at, at, neighbour)

        def add_up(c):
            return copy(2, c, r.sums.at[c, span(keeps, quart)], r.got_near.at[c], neighbour)

        def come(kind, c):
            if kind == 0:
                return copy(4, c, r.sums.at[c, span(own, quart)], r.got_in.at[c, 0:quart], inward)
            return copy(4, c, r.sums.at[c], r.got_in.at[c], inward)

        def meet(kind, c):
            at = span(own if kind == 0 else gives, quart)
            return copy(5, c, r.sums.at[c, at], r.got_mid.at[c], inward)

        def give_back(c):
            at = r.full.at[c, span(mine + keeps, quart)]
            return copy(6, c, at, at, inward)

        def leave(kind, c):
            at = r.full.at[c, span(mine + own, quart) if kind == 0 else span(mine, half)]
            return copy(7, c, at, at, outward)

        def reduced(kind, c, h, at_end):
            @pl.when((along == h) & (h < hops))
            def _():
                come(kind, c).start()

            @pl.when((along == h) & (h == hops))
            def _():
                at_end(c)

        def come_hop(kind, c, h):
            @pl.when(along == h)
            def _():
                come(kind, c).wait_send()

            @pl.when(along == h + 1)
            def _():
                come(kind, c).wait_recv()
                if kind == 0:
                    r.sums[c, span(own, quart)] += r.got_in[c, 0:quart]
                else:
                    r.sums[c] += r.got_in[c]

            reduced(kind, c, h + 1, lambda c: meet(kind, c).start())

        def pass_out(kind, c, h):
            @pl.when((along == h) & (h > 0))
            def _():
                leave(kind, c).start()

            if kind == 0:

                @pl.when(along == h)
                def _():
                    gather_quarter(c).start()

        def leave_hop(kind, c, g):
            h = hops - g

            @pl.when(along == h)
            def _():
                leave(kind, c).wait_send()

            @pl.when(along == h - 1)
            def _():
                leave(kind, c).wait_recv()

            pass_out(kind, c, h - 1)

        def after_halve(c):
            halve(c).wait()
            r.sums[c] += r.products[c % ring, span(mine, half)]

            @pl.when(core == 0)
            def _():
                quarter(c).start()

            @pl.when(core == 1)
            def _():
                reduced(1, c, 0, lambda c: meet(1, c).start())

        def after_quarter(c):
            quarter(c).wait()
            r.sums[c, span(own, quart)] += r.got_near[c]
            reduced(0, c, 0, lambda c: meet(0, c).start())

        def after_meet(kind, c):
            @pl.when(along == hops)
            def _():
                meet(kind, c).wait()
                if kind == 0:
                    r.full[c, span(mine + own, quart)] = r.sums[c, span(own, quart)] + r.got_mid[c]
                else:
                    r.sums[c, span(keeps, quart)] += r.got_mid[c]
                    add_up(c).start()

            if kind == 0:
                pass_out(0, c, hops)

        def after_add_up(c):
            @pl.when(along == hops)
            def _():
                add_up(c).wait()
                r.full[c, span(mine + keeps, quart)] = r.sums[c, span(keeps, quart)] + r.got_near[c]
                give_back(c).start()

        def after_give_back(c):
            @pl.when(along == hops)
            def _():
                give_back(c).wait()

            pass_out(1, c, hops)

        def gathered(c):
            @pl.when(core == 0)
            def _():
                gather_quarter(c).wait()

            gather_half(c).start()

        def after_gather_half(c):
            gather_half(c).wait()

        def small_copy(k, device):
            return remote(r.small_v.at[k], r.got_small.at[k], r.small_send.at[k], r.small_recv.at[k], device)

        def small_rest(j):
            dst = r.got_small.at[2 + j]
            return remote(r.small_v.at[3], dst, r.small_send.at[2 + j], r.small_recv.at[2 + j], peer(j))

        def small_step(step):
            @pl.when(step == 2)
            def _():
                r.small_v[1] = r.small[...]
                small_copy(1, sibling).start()

            @pl.when(step == 4)
            def _():
                small_copy(1, sibling).wait()
                r.small_v[2] = r.small_v[1] + r.got_small[1]
                small_copy(2, neighbour).start()

            @pl.when(step == 6)
            def _():
                small_copy(2, neighbour).wait()
                r.small_v[3] = r.small_v[2] + r.got_small[2]
                pl.loop(1, rest)(lambda j: small_rest(j).start())

            @pl.when(step == 8)
            def _():
                pl.loop(1, rest)(lambda j: small_rest(j).wait())
                total = r.small_v[3]
                for j in range(1, rest):
                    total += r.got_small[2 + j]
                r.small_v[0] = total

                @pl.when(section == 0)
                def _():
                    small_copy(0, {"section": 1}).start()

        last = 2 * hops + 5

        @pl.loop(0, self.chunks + self.SLACK * last)
        def _(step):
            def stage(time, action):
                c = step - self.SLACK * time

                @pl.when((c >= 0) & (c < self.chunks))
                def _():
                    action(c)

            stage(last, after_gather_half)

            @pl.when(core == 0)
            def _():
                over(hops, lambda g: stage(hops + 4 + g, lambda c: leave_hop(0, c, g)))
                stage(hops + 3, lambda c: after_meet(0, c))
                over(hops, lambda h: stage(3 + h, lambda c: come_hop(0, c, h)))
                stage(2, after_quarter)

            @pl.when(core == 1)
            def _():
                over(hops, lambda g: stage(hops + 5 + g, lambda c: leave_hop(1, c, g)))
                stage(hops + 4, after_give_back)
                stage(hops + 3, after_add_up)
                stage(hops + 2, lambda c: after_meet(1, c))
                over(hops, lambda h: stage(2 + h, lambda c: come_hop(1, c, h)))

            stage(last - 1, gathered)
            stage(1, after_halve)
            small_step(step)

            @pl.when(step < self.chunks)
            def _():
                @pl.loop(0, self.per_chunk)
                def _(u):
                    self.product(r, step * self.per_chunk + u)

                halve(step).start()

        r.small_out[...] = r.small_v[0]

        @pl.when(section == 0)
        def _():
            small_copy(0, {"section": 1}).wait_send()

        @pl.when(section == 1)
        def _():
            small_copy(0, {"section": 1}).wait_recv()
            r.small_out[3:4] = r.got_small[0, 3:4]

    def __call__(self, operands, small):
        t, width, deep = self.tables, self.width, self.tables * self.depth
        rest, chunks, rows, ring, cols = self.rest, self.chunks, self.rows, self.ring, self.COLS
        outs = {"full": VMEM((chunks, rows, cols), F32), "small_out": f32(8, width)}
        scratch = {
            "products": VMEM((ring, rows, cols), F32),
            "sums": VMEM((chunks, rows // 2, cols), F32),
            "got_near": VMEM((chunks, rows // 4, cols), F32),
            "got_mid": VMEM((chunks, rows // 4, cols), F32),
            "got_in": VMEM((chunks, rows // 2, cols), F32),
            "a_v": VMEM((2, deep, self.ROWS), BF16),
            "left_v": VMEM((2, self.ROWS, deep), BF16),
            "b_v": VMEM((2, 2, deep, cols), BF16),
            "small_v": VMEM((4, 8, width), F32),
            "got_small": VMEM((2 + rest, 8, width), F32),
            "a_sem": dma(2 * t),
            "b_sem": dma(2, 2 * t),
            "send": dma(8, self.sends),
            "recv": dma(8, chunks),
            "small_send": dma(2 + rest),
            "small_recv": dma(2 + rest),
        }
        ins = {n: (a, ANY) for n, a in operands.items()} | {"small": (small, VMEM)}
        outs = {n: (s, VMEM) for n, s in outs.items()}
        return call("weight_gradient_sum", self.kernel, 0, ins, outs, scratch, SUM_VMEM_LIMIT)

    def results(self, sums, small, tables, ff):
        width = self.width
        sums = pltpu.with_memory_space_constraint(sums, pltpu.VMEM)
        ins = {"full": (sums, VMEM), "small": (small, VMEM)} | {f"table{i}": (a, ANY) for i, a in enumerate(tables)}
        outs = {
            "win": f32(2, width, 3 * width),
            "wout": f32(2, width, width),
            "up": f32(width, ff),
            "down": f32(ff, width),
        } | {f"out{i}": f32(*a.shape) for i, a in enumerate(tables)}
        outs = {n: (s, ANY) for n, s in outs.items()}
        outs |= {"gain": (f32(1, 3, width), VMEM), "missing": (f32(1, width), VMEM)}
        scratch = {f"table_v{i}": VMEM(a.shape, F32) for i, a in enumerate(tables)}
        scratch |= {"sem": dma(self.blocks), "in_sem": dma(len(tables)), "out_sem": dma(len(tables))}

        def body(r):
            buffers = [getattr(r, f"table_v{i}") for i in range(len(tables))]
            loads = [start(getattr(r, f"table{i}"), v, r.in_sem.at[i]) for i, v in enumerate(buffers)]
            stores = []
            for first, stop, *_, out, site, across in self.groups:
                dst = getattr(r, out) if site is None else getattr(r, out).at[site]
                for q in range(first, stop):
                    i, j = (q - first) // across, (q - first) % across
                    u = q % self.per_chunk
                    src = r.full.at[q // self.per_chunk, u * self.ROWS : (u + 1) * self.ROWS]
                    at = (slice(i * self.ROWS, (i + 1) * self.ROWS), slice(j * self.COLS, (j + 1) * self.COLS))
                    stores.append(start(src, dst.at[at], r.sem.at[q]))
            r.gain[0] = r.small[0:3, :]
            r.missing[...] = r.small[3:4, :]
            for i, v in enumerate(buffers):
                loads[i].wait()
                stores.append(start(v, getattr(r, f"out{i}"), r.out_sem.at[i]))
            for copy in stores:
                copy.wait()

        return call("results", body, None, ins, outs, scratch, SUM_VMEM_LIMIT)


def local(
    cells,
    missing_mask,
    missing_embed,
    context_rows,
    norm_gains,
    attn_in,
    attn_out,
    mlp_up,
    mlp_down,
    cotangent,
):
    tables, rows, feat, width = cells.shape
    ff = mlp_up.shape[2]
    layers = Layers(tables, rows, feat, width, ff)

    def flat(tables_of_cells):
        return jnp.swapaxes(tables_of_cells, 1, 2).reshape(tables, rows * feat, -1)

    def unflat(cells_of_tables):
        return jnp.swapaxes(cells_of_tables.reshape(tables, feat, rows, width), 1, 2)[None]

    mask = jnp.pad(flat(missing_mask == 1).astype(F32), ((0, 0), (0, layers.cells - rows * feat), (0, 0)))
    weights = (attn_in[0], attn_out[0], mlp_up[0], mlp_down[0])
    done = layers(flat(cells), mask, missing_embed[None], context_rows, norm_gains[0], weights, flat(cotangent))
    operands = {n: done[n] for n in ("as_", "os", "gs", "dys", "dzs", "dhs", "dqkvs")}
    grad_sum = GradSum(lax.axis_size("dp"), tables, layers.cells, width, ff)
    sums = grad_sum(operands, done["small"])
    got = grad_sum.results(sums["full"], sums["small_out"], (done["out"], done["din"]), ff)
    return (
        unflat(got["out0"]),
        unflat(got["out1"]),
        got["gain"],
        got["win"][None],
        got["wout"][None],
        got["up"][None],
        got["down"][None],
        got["missing"][0],
    )


def solution(mesh):
    in_specs = (
        P("dp", None, None, None),
        P("dp", None, None),
        P(),
        P("dp"),
        P("section", None, None),
        P("section", None, None, None),
        P("section", None, None, None),
        P("section", None, None),
        P("section", None, None),
        P("dp", None, None, None),
    )
    out_specs = (
        P("section", "dp", None, None, None),
        P("section", "dp", None, None, None),
        P("section", None, None),
        P("section", None, None, None),
        P("section", None, None, None),
        P("section", None, None),
        P("section", None, None),
        P(),
    )
    return jax.shard_map(local, mesh=mesh, in_specs=in_specs, out_specs=out_specs, check_vma=False)
```

```python
import functools
from types import SimpleNamespace

import jax
import jax.numpy as jnp
from jax import lax
from jax.experimental import pallas as pl
from jax.experimental.pallas import tpu as pltpu
from jax.sharding import PartitionSpec as P

HEADS = 4
EPSILON = 1e-05
NEG = -1e30
INV_SQRT2PI = 0.3989422804014327
LOG2E = 1.4426950408889634
LN2 = 0.6931471805599453
ERFC_P = 0.33
ERFC_C = (0.1863578482, 0.1829552331, 0.2012284886, 0.0472047191, 0.4085317677, -0.3511862269, 0.4602596132, -0.1353514118)
VMEM_LIMIT = 62 * 1024 * 1024
SUM_VMEM_LIMIT = 44 * 1024 * 1024
TILE = 512
F32, BF16 = jnp.float32, jnp.bfloat16


def dot(a, b, contract=((1,), (0,))):
    return lax.dot_general(a, b, (contract, ((), ())), preferred_element_type=F32)


def split(v):
    hi = v.astype(BF16)
    return hi, (v - hi.astype(F32)).astype(BF16)


def put(ref, index, v):
    hi, lo = split(v)
    ref[(0, *index)] = hi
    ref[(1, *index)] = lo


def parts(ref, *index):
    return ref[(0, *index)], ref[(1, *index)]


def wide(a, b, ca, cb):
    (ah, al), (bh, bl) = a, b
    return dot(jnp.concatenate([ah, ah, al], ca), jnp.concatenate([bh, bl, bh], cb), ((ca,), (cb,)))


def side(a, b):
    (ah, al), (bh, bl) = a, b
    width = bh.shape[1]
    both = dot(ah, jnp.concatenate([bh, bl], 1))
    return both[:, :width] + both[:, width:] + dot(al, bh)


def normalized(h):
    centred = h - jnp.mean(h, axis=-1, keepdims=True)
    rstd = lax.rsqrt(jnp.mean(centred * centred, axis=-1, keepdims=True) + EPSILON)
    return centred * rstd, rstd


def norm_back(n, rstd, gain, da):
    dn = da * gain
    return rstd * (dn - jnp.mean(dn, axis=-1, keepdims=True) - n * jnp.mean(dn * n, axis=-1, keepdims=True))


def cell_ids(start, count, inner, along):
    shape = (count, 1) if along == 0 else (1, count)
    at = lax.broadcasted_iota(jnp.int32, shape, along) + start
    outer = lax.shift_right_logical(at * ((1 << 20) // inner + 1), 20)
    return outer, at - outer * inner


def up16(n):
    return (n + 15) // 16 * 16


def blocks(outer, inner):
    cells = up16(outer * inner)
    half = up16((outer + 1) // 2 * inner)
    first_keys = min(cells, up16((((half - 1) // inner) + 1) * inner))
    second_keys = ((half // inner) * inner) // 16 * 16
    return ((slice(0, half), slice(0, first_keys)), (slice(half, cells), slice(second_keys, cells)))


def when(cond):
    if isinstance(cond, bool):
        return (lambda action: action()) if cond else (lambda action: None)
    return pl.when(cond)


def over(count, action):
    if count <= 4:
        for i in range(count):
            action(i)
    else:
        pl.loop(0, count)(action)


def staggered(units, *steps):
    state = [None] * len(units)
    for i in range(len(units) + 1):
        if i < len(units):
            state[i] = steps[0](*units[i])
        if i > 0:
            for step in steps[1:]:
                state[i - 1] = step(*units[i - 1], state[i - 1])


def lanes(j, width):
    return pl.ds(pl.multiple_of(j * width, width), width)


def start(src, dst, sem):
    copy = pltpu.make_async_copy(src, dst, sem)
    copy.start()
    return copy


def fill_biases(outer, inner, limit, refs, keys_along):
    for (queries, keys), ref in zip(blocks(outer, inner), refs):
        q_outer, _ = cell_ids(queries.start, queries.stop - queries.start, inner, 1 - keys_along)
        k_outer, k_inner = cell_ids(keys.start, keys.stop - keys.start, inner, keys_along)
        ref[...] = jnp.where((q_outer == k_outer) & (k_inner < limit), 0.0, NEG)


def gelu_parts(z):
    size = jnp.abs(z)
    below = 1.0 + (ERFC_P * 0.7071067811865476) * size
    t = pl.reciprocal(below, approx=True)
    t = t * (2.0 - below * t)
    series = jnp.full_like(t, ERFC_C[-1])
    for c in ERFC_C[-2::-1]:
        series = series * t + c
    bell = jnp.exp(-0.5 * z * z)
    tail = 0.5 * (series * t) * bell
    phi = jnp.where(z >= 0.0, 1.0 - tail, tail)
    return z * phi, phi + z * (INV_SQRT2PI * bell)


SMEM, VMEM, ANY = pltpu.SMEM, pltpu.VMEM, pl.ANY


def f32(*shape):
    return jax.ShapeDtypeStruct(shape, F32)


def b16(*shape):
    return jax.ShapeDtypeStruct(shape, BF16)


def dma(*shape):
    return pltpu.SemaphoreType.DMA(shape)


def remote(src, dst, send, recv, device):
    return pltpu.make_async_remote_copy(
        src_ref=src, dst_ref=dst, send_sem=send, recv_sem=recv, device_id=device, device_id_type=pl.DeviceIdType.MESH
    )


def call(name, body, collective_id, ins, outs, scratch, limit):
    names = [*ins, *outs, *scratch]

    def kernel(*refs):
        body(SimpleNamespace(**dict(zip(names, refs))))

    results = pl.pallas_call(
        kernel,
        out_shape=[t for t, _ in outs.values()],
        in_specs=[pl.BlockSpec(memory_space=s) for _, s in ins.values()],
        out_specs=[pl.BlockSpec(memory_space=s) for _, s in outs.values()],
        scratch_shapes=list(scratch.values()),
        compiler_params=pltpu.CompilerParams(
            vmem_limit_bytes=limit, collective_id=collective_id, has_side_effects=collective_id is not None
        ),
        name=name,
    )(*(a for a, _ in ins.values()))
    return dict(zip(outs, results))


class Layers:
    SPLIT_ROWS = 64

    def __init__(self, tables, rows, feat, width, ff):
        self.tables, self.rows, self.feat, self.width, self.ff = tables, rows, feat, width, ff
        self.real, self.cells = rows * feat, up16(rows * feat)
        self.hd = width // HEADS
        self.scale = self.hd ** (-0.5)

    def sites(self, r, site, keys_along):
        if site == 1:
            ranges, biases = blocks(self.feat, self.rows), r.col_bias
        else:
            ranges, biases = blocks(self.rows, self.feat), r.row_bias
        return [(*unit, bias) for unit, bias in zip(ranges, biases[keys_along])]

    def set_out(self, r, src, count):
        for k in range(self.width // 128):
            r.perm_v[k, 0:count] = src[0:count, k * 128 : (k + 1) * 128]

    def by_rows(self, r, dst):
        for row in range(self.rows):
            for k in range(self.width // 128):
                at = (slice(row * self.feat, (row + 1) * self.feat), slice(k * 128, (k + 1) * 128))
                dst[at] = r.perm_v[k, pl.ds(row, self.feat, stride=self.rows), :]

    def by_features(self, r, dst):
        for feat in range(self.feat):
            for k in range(self.width // 128):
                at = (slice(feat * self.rows, (feat + 1) * self.rows), slice(k * 128, (k + 1) * 128))
                dst[at] = r.perm_v[k, pl.ds(feat, self.rows, stride=self.feat), :]

    def __call__(self, cells, mask, embed, context, gains, weights, cotangent):
        t, c, w, ff, real = self.tables, self.cells, self.width, self.ff, self.real
        rows, feat = self.rows, self.feat
        ins = {
            "cells": (cells, ANY),
            "mask": (mask, VMEM),
            "embed": (embed, VMEM),
            "ctx": (context, SMEM),
            "gains": (gains, VMEM),
            "cot": (cotangent, ANY),
        }
        names = ("win", "wout", "wup", "wdown")
        ins |= {n: (a, ANY) for n, a in zip(names, weights)}
        outs = {
            "out": f32(t, real, w),
            "din": f32(t, real, w),
            "ns": f32(t, 3, c, w),
            "qkvs": b16(t, 2, 2, c, 3 * w),
            "gps": f32(t, c, ff),
            "as_": b16(t, 2, 3, c, w),
            "os": b16(t, 2, 2, c, w),
            "gs": b16(t, 2, c, ff),
            "dys": b16(t, 2, c, w),
            "dzs": b16(t, 2, c, ff),
            "dhs": b16(t, 2, 2, c, w),
            "dqkvs": b16(t, 2, 2, c, 3 * w),
        }
        outs = {n: (s, ANY) for n, s in outs.items()} | {"small": (f32(8, w), VMEM)}
        scratch = {n + "_v": VMEM((2, *a.shape), BF16) for n, a in zip(names, weights)}
        scratch |= {
            "h_v": VMEM((2, c, w), F32),
            "n_v": VMEM((3, c, w), F32),
            "qkv_v": VMEM((2, 2, c, 3 * w), BF16),
            "o_v": VMEM((2, 2, c, w), BF16),
            "gp_v": VMEM((c, ff), F32),
            "g_v": VMEM((2, c, ff), BF16),
            "a_v": VMEM((2, 3, c, w), BF16),
            "y_v": VMEM((t, c, w), F32),
            "dqkv_f": VMEM((c, 3 * w), F32),
            "perm_v": VMEM((w // 128, c, 128), F32),
            "dys_v": VMEM((2, c, w), BF16),
            "dy_v": VMEM((c, w), F32),
            "do_v": VMEM((2, c, w), BF16),
            "got": VMEM((t, real, w), F32),
            "stat_v": VMEM((t, c, 128), F32),
            "lse_v": VMEM((t, 2 * HEADS, c), F32),
            "spare_v": VMEM((w // 2, w), F32),
            "raw_sem": pltpu.SemaphoreType.DMA((20,)),
            "in_sem": pltpu.SemaphoreType.DMA((4,)),
            "out_sem": pltpu.SemaphoreType.DMA((18,)),
            "send": pltpu.SemaphoreType.DMA((t, 2)),
            "recv": pltpu.SemaphoreType.DMA((t, 2)),
        }
        for name, ranges in (("col_bias", blocks(feat, rows)), ("row_bias", blocks(rows, feat))):
            for i, (queries, keys) in enumerate(ranges):
                shape = (queries.stop - queries.start, keys.stop - keys.start)
                scratch[f"{name}0{i}"] = VMEM(shape[::-1], F32)
                scratch[f"{name}1{i}"] = VMEM(shape, F32)

        def body(r):
            for n in ("col_bias", "row_bias"):
                setattr(r, n, [[getattr(r, f"{n}{along}{i}") for i in range(2)] for along in range(2)])
            self.kernel(r)

        return call("layers", body, 1, ins, outs, scratch, VMEM_LIMIT)

    def raw_pieces(self, r):
        w, ff = self.width, self.ff
        half, wide_in, step = w // 2, 3 * w, self.SPLIT_ROWS
        top, rest, whole = slice(0, half), slice(half, w), slice(None)
        big, bigger = r.dqkv_f.at[top], r.gp_v.at[top]
        pieces = [
            (r.win.at[0, top], big, r.win_v, (0,), 0, whole, 0),
            (r.win.at[0, rest], bigger.at[:, 0:wide_in], r.win_v, (0,), half, whole, 1),
            (r.wout.at[0, top], r.h_v.at[0, top], r.wout_v, (0,), 0, whole, 2),
            (r.wout.at[0, rest], r.h_v.at[1, top], r.wout_v, (0,), half, whole, 3),
            (r.win.at[1, top], big, r.win_v, (1,), 0, whole, 0),
            (r.win.at[1, rest], bigger.at[:, 0:wide_in], r.win_v, (1,), half, whole, 1),
            (r.wout.at[1, top], r.n_v.at[0, top], r.wout_v, (1,), 0, whole, 4),
            (r.wout.at[1, rest], r.spare_v, r.wout_v, (1,), half, whole, 5),
        ]
        self.attention_pieces = len(pieces)
        pieces.append((r.wup.at[top], bigger, r.wup_v, (), 0, whole, 1))
        pieces.append((r.wup.at[rest, 0:wide_in], big, r.wup_v, (), half, slice(0, wide_in), 0))
        pieces.append((r.wup.at[rest, wide_in:ff], r.spare_v, r.wup_v, (), half, slice(wide_in, ff), 5))
        high = self.cells // step * step
        buffers = [r.y_v.at[0, 0:high], r.y_v.at[1, 0:high]]
        low = slice(half, half + (self.cells - half) // step * step)
        for k in range(3):
            buffers.append(r.dqkv_f.at[low, k * w : (k + 1) * w])
        for k in range(ff // w):
            buffers.append(r.gp_v.at[low, k * w : (k + 1) * w])
        at = 0
        for i, buffer in enumerate(buffers):
            size = min(buffer.shape[0], ff - at)
            if size:
                pieces.append((r.wdown.at[at : at + size], buffer.at[0:size], r.wdown_v, (), at, whole, 6 + i))
            at += size
        assert at == ff
        return pieces

    def raw_copy(self, r, i):
        src, buffer = self.raw_pieces(r)[i][:2]
        return pltpu.make_async_copy(src, buffer, r.raw_sem.at[i])

    def split_piece(self, r, i):
        pieces = self.raw_pieces(r)
        _, buffer, v, lead, at, columns, user = pieces[i]
        step = self.SPLIT_ROWS
        self.raw_copy(r, i).wait()

        @pl.loop(0, buffer.shape[0] // step)
        def _(j):
            src = pl.ds(pl.multiple_of(j * step, step), step)
            dst = pl.ds(pl.multiple_of(at + j * step, step), step)
            put(v, (*lead, dst, columns), buffer[src])

        later = [k for k in range(i + 1, len(pieces)) if pieces[k][-1] == user]
        if later:
            self.raw_copy(r, later[0]).start()

    def start_raw(self, r):
        seen = set()
        for i, piece in enumerate(self.raw_pieces(r)):
            if piece[-1] not in seen:
                self.raw_copy(r, i).start()
            seen.add(piece[-1])

    def split_attention(self, r):
        for i in range(self.attention_pieces):
            self.split_piece(r, i)

    def split_mlp(self, r):
        for i in range(self.attention_pieces, len(self.raw_pieces(r))):
            self.split_piece(r, i)

    def kernel(self, r):
        t, real, c = self.tables, self.real, self.cells
        section = lax.axis_index("section")
        other = {"section": 1 - section}
        barrier = pltpu.get_barrier_semaphore()
        pl.semaphore_signal(barrier, inc=1, device_id=other, device_id_type=pl.DeviceIdType.MESH)
        self.start_raw(r)

        @pl.when(section == 0)
        def _():
            start(r.cells.at[0], r.dy_v.at[0:real], r.in_sem.at[0])

        self.split_attention(r)

        @pl.when(section == 1)
        def _():
            self.split_mlp(r)

        for along in range(2):
            fill_biases(self.rows, self.feat, self.feat, r.row_bias[along], along)
        r.small[...] = jnp.zeros_like(r.small)
        pl.semaphore_wait(barrier, 1)

        def relay(table, half):
            at = slice(half * self.width // 2, (half + 1) * self.width // 2)
            src, dst = r.y_v.at[table, 0:real, at], r.got.at[table, :, at]
            return remote(src, dst, r.send.at[table, half], r.recv.at[table, half], other)

        @pl.loop(0, 2 * t)
        def _(step):
            forward = (1 - section) * (1 - step // t) + section * (1 - step % 2)
            table = (1 - section) * (step % t) + section * (step // 2)

            @pl.when(forward == 1)
            def _():
                self.forward(r, table, section, relay, step)

            @pl.when(forward == 0)
            def _():
                self.backward(r, table, section, relay)

        @pl.when(section == 1)
        def _():
            for table in range(t):
                for half in range(2):
                    relay(table, half).wait_send()

    def forward(self, r, table, section, relay, step):
        c, w, ff, hd, real = self.cells, self.width, self.ff, self.hd, self.real
        stores, held = [], []

        def keep(src, dst, to_reload=False):
            copy = pltpu.make_async_copy(src, dst, r.out_sem.at[len(stores) + len(held)])
            if to_reload:
                held.append(copy)
                pl.when(section == 0)(copy.start)
            else:
                stores.append(copy)
                copy.start()

        for level in range(2):
            r.h_v[level, real:, :] = jnp.zeros((c - real, w), F32)

        def keep_column(k, at, value):
            column = lax.broadcasted_iota(jnp.int32, (1, r.stat_v.shape[2]), 1) == k
            r.stat_v[table, at, :] = jnp.where(column, value, r.stat_v[table, at, :])

        def norm(site):
            n, rstd = normalized(r.h_v[site % 2])
            r.n_v[site] = n
            keep(r.n_v.at[site], r.ns.at[table, site], True)
            keep_column(2 * HEADS + site, slice(None), rstd)
            put(r.a_v, (site,), n * r.gains[site : site + 1, :])
            keep(r.a_v.at[:, site], r.as_.at[table, :, site])

        fill_biases(self.feat, self.rows, r.ctx[table], r.col_bias[1], 1)

        @pl.when(section == 0)
        def _():
            load = pltpu.make_async_copy(r.cells.at[table], r.dy_v.at[0:real], r.in_sem.at[0])
            pl.when(step > 0)(load.start)
            load.wait()
            r.dy_v[0:real] = jnp.where(r.mask[table, 0:real] == 1.0, r.embed[...], r.dy_v[0:real])
            self.set_out(r, r.dy_v, real)

        @pl.when(section == 1)
        def _():
            start(r.cot.at[table], r.dy_v.at[0:real], r.in_sem.at[1])
            for half in range(2):
                relay(table, half).wait_recv()
            self.set_out(r, r.got.at[table], real)

        self.by_rows(r, r.h_v.at[0])
        for site in range(2):
            norm(site)

            def project(j):
                at = slice(j * TILE, (j + 1) * TILE)
                return wide(parts(r.a_v, site), parts(r.win_v, site, slice(None), at), 1, 0)

            def keep_projected(j, out):
                if j < w // TILE:
                    out = out * (self.scale * LOG2E)
                put(r.qkv_v, (site, slice(None), slice(j * TILE, (j + 1) * TILE)), out)

            staggered([(j,) for j in range(3 * w // TILE)], project, keep_projected)
            keep(r.qkv_v.at[:, site], r.qkvs.at[table, :, site], True)

            def scores(head, queries, keys, bias):
                q = parts(r.qkv_v, site, queries, lanes(head, hd))
                k = parts(r.qkv_v, site, keys, lanes(HEADS + head, hd))
                return wide(q, k, 1, 1)

            def softmax(head, queries, keys, bias, s):
                s = s + bias[...]
                top = jnp.max(s, axis=-1, keepdims=True)
                e = jnp.exp2(s - top)
                total = jnp.sum(e, axis=-1, keepdims=True)
                keep_column(site * HEADS + head, queries, top + jnp.log2(total))
                return split(e), 1.0 / total

            def blend(head, queries, keys, bias, state):
                e, inverse = state
                v = parts(r.qkv_v, site, keys, lanes(2 * HEADS + head, hd))
                put(r.o_v, (site, queries, lanes(head, hd)), side(e, v) * inverse)

            @pl.loop(0, HEADS // 2)
            def _(two):
                units = [(head, *unit) for head in (2 * two, 2 * two + 1) for unit in self.sites(r, site, 1)]
                staggered(units, scores, softmax, blend)

            keep(r.o_v.at[:, site], r.os.at[table, :, site])
            after = r.h_v[site] + wide(parts(r.o_v, site), parts(r.wout_v, site), 1, 0)
            if site == 0:
                self.set_out(r, after, c)
                self.by_features(r, r.h_v.at[1])
            else:
                r.h_v[0] = after
        r.lse_v[table] = r.stat_v[table].T[0 : 2 * HEADS]
        norm(2)

        @pl.when((section == 0) & (step == 0))
        def _():
            self.split_mlp(r)

        def up(j):
            return wide(parts(r.a_v, 2), parts(r.wup_v, slice(None), slice(j * TILE, (j + 1) * TILE)), 1, 0)

        tiles = ff // TILE
        z = up(0)
        for j in range(tiles):
            at = slice(j * TILE, (j + 1) * TILE)
            following = up(j + 1) if j + 1 < tiles else None
            g, gp = gelu_parts(z)
            put(r.g_v, (slice(None), at), g)
            r.gp_v[:, at] = gp
            z = following
        keep(r.g_v, r.gs.at[table])
        keep(r.gp_v, r.gps.at[table], True)
        for half in range(2):
            at = slice(half * w // 2, (half + 1) * w // 2)
            r.y_v[table, :, at] = r.h_v[0, :, at] + wide(parts(r.g_v), parts(r.wdown_v, slice(None), at), 1, 0)

            @pl.when(section == 0)
            def _():
                relay(table, half).start()

        keep(r.y_v.at[table, 0:real], r.out.at[table])
        for copy in stores:
            copy.wait()

        @pl.when(section == 0)
        def _():
            for copy in held:
                copy.wait()

    def backward(self, r, table, section, relay):
        c, w, ff, hd, real = self.cells, self.width, self.ff, self.hd, self.real
        stores = []

        def keep(src, dst):
            stores.append(start(src, dst, r.out_sem.at[len(stores)]))

        fill_biases(self.feat, self.rows, r.ctx[table], r.col_bias[0], 0)

        @pl.when(section == 0)
        def _():
            loads = [
                start(r.ns.at[table], r.n_v, r.in_sem.at[0]),
                start(r.qkvs.at[table], r.qkv_v, r.in_sem.at[1]),
                start(r.gps.at[table], r.gp_v, r.in_sem.at[2]),
            ]
            for half in range(2):
                relay(table, half).wait()
            r.dy_v[0:real] = r.got[table]
            for copy in loads:
                copy.wait()

        @pl.when(section == 1)
        def _():
            pltpu.make_async_copy(r.cot.at[table], r.dy_v.at[0:real], r.in_sem.at[1]).wait()

        r.dy_v[real:, :] = jnp.zeros((c - real, w), F32)
        put(r.dys_v, (), r.dy_v[...])
        keep(r.dys_v, r.dys.at[table])

        def down(j):
            return wide(parts(r.dys_v), parts(r.wdown_v, slice(j * TILE, (j + 1) * TILE)), 1, 1)

        tiles = ff // TILE
        dg = down(0)
        for j in range(tiles):
            at = slice(j * TILE, (j + 1) * TILE)
            following = down(j + 1) if j + 1 < tiles else None
            put(r.g_v, (slice(None), at), dg * r.gp_v[:, at])
            dg = following
        keep(r.g_v, r.dzs.at[table])
        da = wide(parts(r.g_v), parts(r.wup_v), 1, 1)

        def through_norm(site, da):
            n, k = r.n_v[site], 2 * HEADS + site
            rstd = r.stat_v[table, :, k : k + 1]
            r.small[site : site + 1, :] += jnp.sum(da * n, axis=0, keepdims=True)
            return norm_back(n, rstd, r.gains[site : site + 1, :], da)

        r.dy_v[...] += through_norm(2, da)
        for site in (1, 0):
            if site == 0:
                self.set_out(r, r.dy_v, real)
                self.by_rows(r, r.dy_v)
            put(r.o_v, (site,), r.dy_v[...])
            keep(r.o_v.at[:, site], r.dhs.at[table, :, site])
            put(r.do_v, (), wide(parts(r.o_v, site), parts(r.wout_v, site), 1, 1))

            def part_of(which, head, span):
                return parts(r.qkv_v, site, span, lanes(which * HEADS + head, hd))

            def products(head, queries, keys, bias):
                do = parts(r.do_v, queries, lanes(head, hd))
                s = wide(part_of(1, head, keys), part_of(0, head, queries), 1, 1)
                return s, wide(part_of(2, head, keys), do, 1, 1)

            def gradients(head, queries, keys, bias, state):
                s, dp = state
                p = jnp.exp2(s + bias[...] - r.lse_v[table, pl.ds(site * HEADS + head, 1), queries])
                ds = p * (dp - jnp.sum(p * dp, axis=0, keepdims=True))
                return split(p), split(ds)

            def back(head, queries, keys, bias, state):
                p, ds = state
                k = part_of(1, head, keys)
                r.dqkv_f[queries, lanes(head, hd)] = (wide(tuple(x.T for x in k), ds, 1, 0) * self.scale).T
                dk = side(ds, part_of(0, head, queries)) * LN2
                dv = side(p, parts(r.do_v, queries, lanes(head, hd)))
                for which, term in ((1, dk), (2, dv)):
                    at = lanes(which * HEADS + head, hd)
                    if keys.start == 0:
                        r.dqkv_f[keys, at] = term
                    else:
                        known = overlap - keys.start
                        if known:
                            r.dqkv_f[keys.start : overlap, at] += term[:known]
                        r.dqkv_f[overlap : keys.stop, at] = term[known:]

            overlap = self.sites(r, site, 0)[0][1].stop

            @pl.loop(0, HEADS // 2)
            def _(two):
                units = [(head, *unit) for head in (2 * two, 2 * two + 1) for unit in self.sites(r, site, 0)]
                staggered(units, products, gradients, back)

            for j in range(3 * w // TILE):
                at = slice(j * TILE, (j + 1) * TILE)
                put(r.qkv_v, (site, slice(None), at), r.dqkv_f[:, at])
            keep(r.qkv_v.at[:, site], r.dqkvs.at[table, :, site])
            da = wide(parts(r.qkv_v, site), parts(r.win_v, site), 1, 1)
            r.dy_v[...] += through_norm(site, da)

        self.set_out(r, r.dy_v, real)
        self.by_features(r, r.dy_v)

        @pl.when(section == 0)
        def _():
            missing = r.mask[table] == 1.0
            r.small[3:4, :] += jnp.sum(jnp.where(missing, r.dy_v[...], 0.0), axis=0, keepdims=True)
            r.y_v[table] = jnp.where(missing, 0.0, r.dy_v[...])

        @pl.when(section == 1)
        def _():
            r.y_v[table] = r.dy_v[...]
            for half in range(2):
                relay(table, half).start()

        keep(r.y_v.at[table, 0:real], r.din.at[table])
        for copy in stores:
            copy.wait()


class GradSum:
    ROWS, COLS = 512, 256
    PARTS = 2
    SLACK = 2

    def __init__(self, count, tables, cells, width, ff):
        self.count, self.tables, self.cells, self.width = count, tables, cells, width
        self.rest = count // 4
        shapes = [("gs", None, "dys", None, "down", None, ff, width), ("as_", 2, "dzs", None, "up", None, width, ff)]
        for site in (1, 0):
            shapes.append(("as_", site, "dqkvs", site, "win", site, width, 3 * width))
            shapes.append(("os", site, "dhs", site, "wout", site, width, width))
        self.groups, at = [], 0
        for *which, k, n in shapes:
            blocks = (k // self.ROWS) * (n // self.COLS)
            self.groups.append((at, at + blocks, *which, n // self.COLS))
            at += blocks
        self.blocks = at
        self.chunks = self.blocks * self.PARTS
        self.hops = self.rest // 2 - 1
        self.sends = self.SLACK * (self.hops + 1) + 2
        self.rows = self.ROWS // self.PARTS
        self.ring = self.SLACK // self.PARTS + 2
        self.depth = (cells + 127) // 128 * 128

    def select(self, q, action):
        for group in self.groups:
            first, stop, *_, across = group

            @pl.when((q >= first) & (q < stop))
            def _():
                action(group, (q - first) // across, (q - first) % across)

    def starts_row(self, q):
        found = False
        for first, stop, *_, across in self.groups:
            found = found | ((q >= first) & (q < stop) & ((q - first) % across == 0))
        return found

    def load(self, r, q):
        slot = q % 2

        def action(group, i, j):
            _, _, left, left_site, right, right_site, *_ = group
            a, b = getattr(r, left), getattr(r, right)

            def at(t, part, site):
                return (t, part, slice(None)) if site is None else (t, part, site, slice(None))

            for t in range(self.tables):
                rows = slice(t * self.depth, t * self.depth + self.cells)
                for part in range(2):
                    sem = 2 * t + part
                    start(b.at[(*at(t, part, right_site), lanes(j, self.COLS))], r.b_v.at[slot, part, rows], r.b_sem.at[slot, sem])

                    @pl.when(j == 0)
                    def _():
                        start(a.at[(*at(t, part, left_site), lanes(i, self.ROWS))], r.a_v.at[part, rows], r.a_sem.at[sem])

        self.select(q, action)

    def each_operand(self):
        return [(2 * t + part, part, slice(t * self.depth, t * self.depth + self.cells)) for t in range(self.tables) for part in range(2)]

    def product(self, r, q):
        slot = q % 2

        @pl.when(self.starts_row(q))
        def _():
            for sem, part, rows in self.each_operand():
                a = r.a_v.at[part, rows]
                pltpu.make_async_copy(a, a, r.a_sem.at[sem]).wait()
            for part in range(2):
                r.left_v[part] = r.a_v[part].T

        for sem, part, rows in self.each_operand():
            b = r.b_v.at[slot, part, rows]
            pltpu.make_async_copy(b, b, r.b_sem.at[slot, sem]).wait()

        @pl.when(q + 1 < self.blocks)
        def _():
            self.load(r, q + 1)

        r.products[q % self.ring] = side(parts(r.left_v), parts(r.b_v.at[slot]))

    def kernel(self, r):
        rest, rows, ring = self.rest, self.rows, self.ring
        half = rows // 2
        quart = half // 2
        me, section = lax.axis_index("dp"), lax.axis_index("section")
        core, pair, place = me % 2, me // 2 % 2, me // 4
        sibling, neighbour = {"dp": me + 1 - 2 * core}, {"dp": me + 2 - 4 * pair}
        far = place // (rest // 2)
        along = (1 - far) * place + far * (rest - 1 - place)
        inward, outward = {"dp": me + 4 - 8 * far}, {"dp": me - 4 + 8 * far}
        hops = self.hops

        def peer(j):
            return {"dp": lax.rem(place + j, rest) * 4 + me % 4}

        def span(at, size):
            return pl.ds(pl.multiple_of(at, size), size)

        mine = core * half
        own, other = pair * quart, (1 - pair) * quart
        keeps, gives = far * quart, (1 - far) * quart

        barrier = pltpu.get_barrier_semaphore()

        def greet(device):
            pl.semaphore_signal(barrier, inc=1, device_id=device, device_id_type=pl.DeviceIdType.MESH)

        greet(sibling)
        greet(neighbour)

        @pl.loop(1, rest)
        def _(j):
            greet(peer(j))

        for t in range(self.tables):
            pad = slice(t * self.depth + self.cells, (t + 1) * self.depth)
            for part in range(2):
                r.a_v[part, pad] = jnp.zeros_like(r.a_v[part, pad])
                for slot in range(2):
                    r.b_v[slot, part, pad] = jnp.zeros_like(r.b_v[slot, part, pad])
        self.load(r, 0)

        @pl.when(section == 1)
        def _():
            greet({"section": 0})

        pl.semaphore_wait(barrier, rest + 2 - section)

        def copy(which, c, src, dst, device):
            return remote(src, dst, r.send.at[which, c % self.sends], r.recv.at[which, c], device)

        def product_rows(c, which):
            return c // self.PARTS % ring, span(c % self.PARTS * rows + which * half, half)

        def halve(c):
            return copy(0, c, r.products.at[product_rows(c, 1 - core)], r.sums.at[c], sibling)

        def gather_half(c):
            at = r.full.at[c, span(mine, half)]
            return copy(1, c, at, at, sibling)

        def quarter(c):
            return copy(2, c, r.sums.at[c, span(other, quart)], r.got_near.at[c], neighbour)

        def gather_quarter(c):
            at = r.full.at[c, span(mine + own, quart)]
            return copy(3, c, at, at, neighbour)

        def add_up(c):
            return copy(2, c, r.sums.at[c, span(keeps, quart)], r.got_near.at[c], neighbour)

        def come(kind, c):
            if kind == 0:
                return copy(4, c, r.sums.at[c, span(own, quart)], r.got_in.at[c, 0:quart], inward)
            return copy(4, c, r.sums.at[c], r.got_in.at[c], inward)

        def meet(kind, c):
            at = span(own if kind == 0 else gives, quart)
            return copy(5, c, r.sums.at[c, at], r.got_mid.at[c], inward)

        def give_back(c):
            at = r.full.at[c, span(mine + keeps, quart)]
            return copy(6, c, at, at, inward)

        def leave(kind, c):
            at = r.full.at[c, span(mine + own, quart) if kind == 0 else span(mine, half)]
            return copy(7, c, at, at, outward)

        def reduced(kind, c, h, at_end):
            @pl.when((along == h) & (h < hops))
            def _():
                come(kind, c).start()

            @pl.when((along == h) & (h == hops))
            def _():
                at_end(c)

        def come_hop(kind, c, h):
            @pl.when(along == h)
            def _():
                come(kind, c).wait_send()

            @pl.when(along == h + 1)
            def _():
                come(kind, c).wait_recv()
                if kind == 0:
                    r.sums[c, span(own, quart)] += r.got_in[c, 0:quart]
                else:
                    r.sums[c] += r.got_in[c]

            reduced(kind, c, h + 1, lambda c: meet(kind, c).start())

        def pass_out(kind, c, h):
            @pl.when((along == h) & (h > 0))
            def _():
                leave(kind, c).start()

            if kind == 0:

                @pl.when(along == h)
                def _():
                    gather_quarter(c).start()

        def leave_hop(kind, c, g):
            h = hops - g

            @pl.when(along == h)
            def _():
                leave(kind, c).wait_send()

            @pl.when(along == h - 1)
            def _():
                leave(kind, c).wait_recv()

            pass_out(kind, c, h - 1)

        def after_halve(c):
            halve(c).wait()
            r.sums[c] += r.products[product_rows(c, core)]

            @pl.when(core == 0)
            def _():
                quarter(c).start()

            @pl.when(core == 1)
            def _():
                reduced(1, c, 0, lambda c: meet(1, c).start())

        def after_quarter(c):
            quarter(c).wait()
            r.sums[c, span(own, quart)] += r.got_near[c]
            reduced(0, c, 0, lambda c: meet(0, c).start())

        def after_meet(kind, c):
            @pl.when(along == hops)
            def _():
                meet(kind, c).wait()
                if kind == 0:
                    r.full[c, span(mine + own, quart)] = r.sums[c, span(own, quart)] + r.got_mid[c]
                else:
                    r.sums[c, span(keeps, quart)] += r.got_mid[c]
                    add_up(c).start()

            if kind == 0:
                pass_out(0, c, hops)

        def after_add_up(c):
            @pl.when(along == hops)
            def _():
                add_up(c).wait()
                r.full[c, span(mine + keeps, quart)] = r.sums[c, span(keeps, quart)] + r.got_near[c]
                give_back(c).start()

        def after_give_back(c):
            @pl.when(along == hops)
            def _():
                give_back(c).wait()

            pass_out(1, c, hops)

        def gathered(c):
            @pl.when(core == 0)
            def _():
                gather_quarter(c).wait()

            gather_half(c).start()

        def after_gather_half(c):
            gather_half(c).wait()

        def small_copy(k, device):
            return remote(r.small_v.at[k], r.got_small.at[k], r.small_send.at[k], r.small_recv.at[k], device)

        def small_rest(j):
            dst = r.got_small.at[2 + j]
            return remote(r.small_v.at[3], dst, r.small_send.at[2 + j], r.small_recv.at[2 + j], peer(j))

        def small_step(step):
            @pl.when(step == 2)
            def _():
                r.small_v[1] = r.small[...]
                small_copy(1, sibling).start()

            @pl.when(step == 4)
            def _():
                small_copy(1, sibling).wait()
                r.small_v[2] = r.small_v[1] + r.got_small[1]
                small_copy(2, neighbour).start()

            @pl.when(step == 6)
            def _():
                small_copy(2, neighbour).wait()
                r.small_v[3] = r.small_v[2] + r.got_small[2]
                pl.loop(1, rest)(lambda j: small_rest(j).start())

            @pl.when(step == 8)
            def _():
                pl.loop(1, rest)(lambda j: small_rest(j).wait())
                total = r.small_v[3]
                for j in range(1, rest):
                    total += r.got_small[2 + j]
                r.small_v[0] = total

                @pl.when(section == 0)
                def _():
                    small_copy(0, {"section": 1}).start()

        last = 2 * hops + 5

        def delay(time):
            return self.SLACK * time - (1 if time < last else 2)

        @pl.loop(0, self.chunks + delay(last))
        def _(step):
            def stage(time, action):
                c = step - (delay(time) if isinstance(time, int) else self.SLACK * time - 1)

                @pl.when((c >= 0) & (c < self.chunks))
                def _():
                    action(c)

            stage(last, after_gather_half)

            @pl.when(core == 0)
            def _():
                over(hops, lambda g: stage(hops + 4 + g, lambda c: leave_hop(0, c, g)))
                stage(hops + 3, lambda c: after_meet(0, c))
                over(hops, lambda h: stage(3 + h, lambda c: come_hop(0, c, h)))
                stage(2, after_quarter)

            @pl.when(core == 1)
            def _():
                over(hops, lambda g: stage(hops + 5 + g, lambda c: leave_hop(1, c, g)))
                stage(hops + 4, after_give_back)
                stage(hops + 3, after_add_up)
                stage(hops + 2, lambda c: after_meet(1, c))
                over(hops, lambda h: stage(2 + h, lambda c: come_hop(1, c, h)))

            stage(last - 1, gathered)
            stage(1, after_halve)
            small_step(step)

            @pl.when(step < self.chunks)
            def _():
                @pl.when(step % self.PARTS == 0)
                def _():
                    self.product(r, step // self.PARTS)

                halve(step).start()

        r.small_out[...] = r.small_v[0]

        @pl.when(section == 0)
        def _():
            small_copy(0, {"section": 1}).wait_send()

        @pl.when(section == 1)
        def _():
            small_copy(0, {"section": 1}).wait_recv()
            r.small_out[3:4] = r.got_small[0, 3:4]

    def __call__(self, operands, small):
        t, width, deep = self.tables, self.width, self.tables * self.depth
        rest, chunks, rows, ring, cols = self.rest, self.chunks, self.rows, self.ring, self.COLS
        outs = {"full": VMEM((chunks, rows, cols), F32), "small_out": f32(8, width)}
        scratch = {
            "products": VMEM((ring, self.ROWS, cols), F32),
            "sums": VMEM((chunks, rows // 2, cols), F32),
            "got_near": VMEM((chunks, rows // 4, cols), F32),
            "got_mid": VMEM((chunks, rows // 4, cols), F32),
            "got_in": VMEM((chunks, rows // 2, cols), F32),
            "a_v": VMEM((2, deep, self.ROWS), BF16),
            "left_v": VMEM((2, self.ROWS, deep), BF16),
            "b_v": VMEM((2, 2, deep, cols), BF16),
            "small_v": VMEM((4, 8, width), F32),
            "got_small": VMEM((2 + rest, 8, width), F32),
            "a_sem": dma(2 * t),
            "b_sem": dma(2, 2 * t),
            "send": dma(8, self.sends),
            "recv": dma(8, chunks),
            "small_send": dma(2 + rest),
            "small_recv": dma(2 + rest),
        }
        ins = {n: (a, ANY) for n, a in operands.items()} | {"small": (small, VMEM)}
        outs = {n: (s, VMEM) for n, s in outs.items()}
        return call("weight_gradient_sum", self.kernel, 0, ins, outs, scratch, SUM_VMEM_LIMIT)

    def results(self, sums, small, tables, ff):
        width = self.width
        sums = pltpu.with_memory_space_constraint(sums, pltpu.VMEM)
        ins = {"full": (sums, VMEM), "small": (small, VMEM)} | {f"table{i}": (a, ANY) for i, a in enumerate(tables)}
        outs = {
            "win": f32(2, width, 3 * width),
            "wout": f32(2, width, width),
            "up": f32(width, ff),
            "down": f32(ff, width),
        } | {f"out{i}": f32(*a.shape) for i, a in enumerate(tables)}
        outs = {n: (s, ANY) for n, s in outs.items()}
        outs |= {"gain": (f32(1, 3, width), VMEM), "missing": (f32(1, width), VMEM)}
        scratch = {f"table_v{i}": VMEM(a.shape, F32) for i, a in enumerate(tables)}
        scratch |= {"sem": dma(self.chunks), "in_sem": dma(len(tables)), "out_sem": dma(len(tables))}

        def body(r):
            buffers = [getattr(r, f"table_v{i}") for i in range(len(tables))]
            loads = [start(getattr(r, f"table{i}"), v, r.in_sem.at[i]) for i, v in enumerate(buffers)]
            stores = []
            for first, stop, *_, out, site, across in self.groups:
                dst = getattr(r, out) if site is None else getattr(r, out).at[site]
                for c in range(first * self.PARTS, stop * self.PARTS):
                    q = c // self.PARTS - first
                    row = q // across * self.ROWS + c % self.PARTS * self.rows
                    at = (slice(row, row + self.rows), slice(q % across * self.COLS, (q % across + 1) * self.COLS))
                    stores.append(start(r.full.at[c], dst.at[at], r.sem.at[c]))
            r.gain[0] = r.small[0:3, :]
            r.missing[...] = r.small[3:4, :]
            for i, v in enumerate(buffers):
                loads[i].wait()
                stores.append(start(v, getattr(r, f"out{i}"), r.out_sem.at[i]))
            for copy in stores:
                copy.wait()

        return call("results", body, None, ins, outs, scratch, SUM_VMEM_LIMIT)


def local(
    cells,
    missing_mask,
    missing_embed,
    context_rows,
    norm_gains,
    attn_in,
    attn_out,
    mlp_up,
    mlp_down,
    cotangent,
):
    tables, rows, feat, width = cells.shape
    ff = mlp_up.shape[2]
    layers = Layers(tables, rows, feat, width, ff)

    def flat(tables_of_cells):
        return jnp.swapaxes(tables_of_cells, 1, 2).reshape(tables, rows * feat, -1)

    def unflat(cells_of_tables):
        return jnp.swapaxes(cells_of_tables.reshape(tables, feat, rows, width), 1, 2)[None]

    mask = jnp.pad(flat(missing_mask == 1).astype(F32), ((0, 0), (0, layers.cells - rows * feat), (0, 0)))
    weights = (attn_in[0], attn_out[0], mlp_up[0], mlp_down[0])
    done = layers(flat(cells), mask, missing_embed[None], context_rows, norm_gains[0], weights, flat(cotangent))
    operands = {n: done[n] for n in ("as_", "os", "gs", "dys", "dzs", "dhs", "dqkvs")}
    grad_sum = GradSum(lax.axis_size("dp"), tables, layers.cells, width, ff)
    sums = grad_sum(operands, done["small"])
    got = grad_sum.results(sums["full"], sums["small_out"], (done["out"], done["din"]), ff)
    return (
        unflat(got["out0"]),
        unflat(got["out1"]),
        got["gain"],
        got["win"][None],
        got["wout"][None],
        got["up"][None],
        got["down"][None],
        got["missing"][0],
    )


def solution(mesh):
    in_specs = (
        P("dp", None, None, None),
        P("dp", None, None),
        P(),
        P("dp"),
        P("section", None, None),
        P("section", None, None, None),
        P("section", None, None, None),
        P("section", None, None),
        P("section", None, None),
        P("dp", None, None, None),
    )
    out_specs = (
        P("section", "dp", None, None, None),
        P("section", "dp", None, None, None),
        P("section", None, None),
        P("section", None, None, None),
        P("section", None, None, None),
        P("section", None, None),
        P("section", None, None),
        P(),
    )
    return jax.shard_map(local, mesh=mesh, in_specs=in_specs, out_specs=out_specs, check_vma=False)
```

```python
import functools
from types import SimpleNamespace

import jax
import jax.numpy as jnp
from jax import lax
from jax.experimental import pallas as pl
from jax.experimental.pallas import tpu as pltpu
from jax.sharding import PartitionSpec as P

HEADS = 4
EPSILON = 1e-05
NEG = -1e30
INV_SQRT2PI = 0.3989422804014327
LOG2E = 1.4426950408889634
LN2 = 0.6931471805599453
ERFC_P = 0.33
ERFC_C = (0.1863578482, 0.1829552331, 0.2012284886, 0.0472047191, 0.4085317677, -0.3511862269, 0.4602596132, -0.1353514118)
VMEM_LIMIT = 62 * 1024 * 1024
SUM_VMEM_LIMIT = 38 * 1024 * 1024
TILE = 512
F32, BF16 = jnp.float32, jnp.bfloat16


def dot(a, b, contract=((1,), (0,))):
    return lax.dot_general(a, b, (contract, ((), ())), preferred_element_type=F32)


def split(v):
    hi = v.astype(BF16)
    return hi, (v - hi.astype(F32)).astype(BF16)


def put(ref, index, v):
    hi, lo = split(v)
    ref[(0, *index)] = hi
    ref[(1, *index)] = lo


def parts(ref, *index):
    return ref[(0, *index)], ref[(1, *index)]


def wide(a, b, ca, cb):
    (ah, al), (bh, bl) = a, b
    if ah.shape[ca] < 512:
        return dot(jnp.concatenate([ah, ah, al], ca), jnp.concatenate([bh, bl, bh], cb), ((ca,), (cb,)))
    rows = ah.shape[1 - ca]
    both = dot(jnp.concatenate([ah, al], 1 - ca), bh, ((ca,), (cb,)))
    return both[:rows] + both[rows:] + dot(ah, bl, ((ca,), (cb,)))


def side(a, b):
    (ah, al), (bh, bl) = a, b
    width = bh.shape[1]
    both = dot(ah, jnp.concatenate([bh, bl], 1))
    return both[:, :width] + both[:, width:] + dot(al, bh)


def normalized(h):
    centred = h - jnp.mean(h, axis=-1, keepdims=True)
    rstd = lax.rsqrt(jnp.mean(centred * centred, axis=-1, keepdims=True) + EPSILON)
    return centred * rstd, rstd


def norm_back(n, rstd, gain, da):
    dn = da * gain
    return rstd * (dn - jnp.mean(dn, axis=-1, keepdims=True) - n * jnp.mean(dn * n, axis=-1, keepdims=True))


def cell_ids(start, count, inner, along):
    shape = (count, 1) if along == 0 else (1, count)
    at = lax.broadcasted_iota(jnp.int32, shape, along) + start
    outer = lax.shift_right_logical(at * ((1 << 20) // inner + 1), 20)
    return outer, at - outer * inner


def up16(n):
    return (n + 15) // 16 * 16


def blocks(outer, inner):
    cells = up16(outer * inner)
    half = up16((outer + 1) // 2 * inner)
    first_keys = min(cells, up16((((half - 1) // inner) + 1) * inner))
    second_keys = ((half // inner) * inner) // 16 * 16
    return ((slice(0, half), slice(0, first_keys)), (slice(half, cells), slice(second_keys, cells)))


def when(cond):
    if isinstance(cond, bool):
        return (lambda action: action()) if cond else (lambda action: None)
    return pl.when(cond)


def over(count, action):
    if count <= 4:
        for i in range(count):
            action(i)
    else:
        pl.loop(0, count)(action)


def staggered(units, *steps):
    state = [None] * len(units)
    for i in range(len(units) + 1):
        if i < len(units):
            state[i] = steps[0](*units[i])
        if i > 0:
            for step in steps[1:]:
                state[i - 1] = step(*units[i - 1], state[i - 1])


def lanes(j, width):
    return pl.ds(pl.multiple_of(j * width, width), width)


def start(src, dst, sem):
    copy = pltpu.make_async_copy(src, dst, sem)
    copy.start()
    return copy


def fill_biases(outer, inner, limit, refs, keys_along):
    for (queries, keys), ref in zip(blocks(outer, inner), refs):
        q_outer, _ = cell_ids(queries.start, queries.stop - queries.start, inner, 1 - keys_along)
        k_outer, k_inner = cell_ids(keys.start, keys.stop - keys.start, inner, keys_along)
        ref[...] = jnp.where((q_outer == k_outer) & (k_inner < limit), 0.0, NEG)


def gelu_parts(z):
    size = jnp.abs(z)
    below = 1.0 + (ERFC_P * 0.7071067811865476) * size
    t = pl.reciprocal(below, approx=True)
    t = t * (2.0 - below * t)
    series = jnp.full_like(t, ERFC_C[-1])
    for c in ERFC_C[-2::-1]:
        series = series * t + c
    bell = jnp.exp(-0.5 * z * z)
    tail = 0.5 * (series * t) * bell
    phi = jnp.where(z >= 0.0, 1.0 - tail, tail)
    return z * phi, phi + z * (INV_SQRT2PI * bell)


SMEM, VMEM, ANY = pltpu.SMEM, pltpu.VMEM, pl.ANY


def f32(*shape):
    return jax.ShapeDtypeStruct(shape, F32)


def b16(*shape):
    return jax.ShapeDtypeStruct(shape, BF16)


def dma(*shape):
    return pltpu.SemaphoreType.DMA(shape)


def remote(src, dst, send, recv, device):
    return pltpu.make_async_remote_copy(
        src_ref=src, dst_ref=dst, send_sem=send, recv_sem=recv, device_id=device, device_id_type=pl.DeviceIdType.MESH
    )


def call(name, body, collective_id, ins, outs, scratch, limit):
    names = [*ins, *outs, *scratch]

    def kernel(*refs):
        body(SimpleNamespace(**dict(zip(names, refs))))

    results = pl.pallas_call(
        kernel,
        out_shape=[t for t, _ in outs.values()],
        in_specs=[pl.BlockSpec(memory_space=s) for _, s in ins.values()],
        out_specs=[pl.BlockSpec(memory_space=s) for _, s in outs.values()],
        scratch_shapes=list(scratch.values()),
        compiler_params=pltpu.CompilerParams(
            vmem_limit_bytes=limit, collective_id=collective_id, has_side_effects=collective_id is not None
        ),
        name=name,
    )(*(a for a, _ in ins.values()))
    return dict(zip(outs, results))


class Layers:
    SPLIT_ROWS = 64

    def __init__(self, tables, rows, feat, width, ff):
        self.tables, self.rows, self.feat, self.width, self.ff = tables, rows, feat, width, ff
        self.real, self.cells = rows * feat, up16(rows * feat)
        self.hd = width // HEADS
        self.scale = self.hd ** (-0.5)

    def sites(self, r, site, keys_along):
        if site == 1:
            ranges, biases = blocks(self.feat, self.rows), r.col_bias
        else:
            ranges, biases = blocks(self.rows, self.feat), r.row_bias
        return [(*unit, bias) for unit, bias in zip(ranges, biases[keys_along])]

    def missing(self, r, table):
        mask = r.mask[table]
        return [(slice(f * self.rows, (f + 1) * self.rows), mask[:, f : f + 1] == 1) for f in range(self.feat)]

    def set_out(self, r, src, count):
        for k in range(self.width // 128):
            r.perm_v[k, 0:count] = src[0:count, k * 128 : (k + 1) * 128]

    def by_rows(self, r, dst):
        for row in range(self.rows):
            for k in range(self.width // 128):
                at = (slice(row * self.feat, (row + 1) * self.feat), slice(k * 128, (k + 1) * 128))
                dst[at] = r.perm_v[k, pl.ds(row, self.feat, stride=self.rows), :]

    def by_features(self, r, dst):
        for feat in range(self.feat):
            for k in range(self.width // 128):
                at = (slice(feat * self.rows, (feat + 1) * self.rows), slice(k * 128, (k + 1) * 128))
                dst[at] = r.perm_v[k, pl.ds(feat, self.rows, stride=self.feat), :]

    def __call__(self, cells, mask, embed, context, gains, weights, cotangent):
        t, c, w, ff, real = self.tables, self.cells, self.width, self.ff, self.real
        rows, feat = self.rows, self.feat
        ins = {
            "cells": (cells, ANY),
            "mask": (mask, VMEM),
            "embed": (embed, VMEM),
            "ctx": (context, SMEM),
            "gains": (gains, VMEM),
            "cot": (cotangent, ANY),
        }
        names = ("win", "wout", "wup", "wdown")
        ins |= {n: (a, ANY) for n, a in zip(names, weights)}
        outs = {
            "out": f32(t, real, w),
            "din": f32(t, real, w),
            "ns": f32(t, 3, c, w),
            "qkvs": b16(t, 2, 2, c, 3 * w),
            "gps": f32(t, c, ff),
            "as_": b16(t, 2, 3, c, w),
            "os": b16(t, 2, 2, c, w),
            "gs": b16(t, 2, c, ff),
            "dys": b16(t, 2, c, w),
            "dzs": b16(t, 2, c, ff),
            "dhs": b16(t, 2, 2, c, w),
            "dqkvs": b16(t, 2, 2, c, 3 * w),
        }
        outs = {n: (s, ANY) for n, s in outs.items()} | {"small": (f32(8, w), VMEM)}
        scratch = {n + "_v": VMEM((2, *a.shape), BF16) for n, a in zip(names, weights)}
        scratch |= {
            "h_v": VMEM((2, c, w), F32),
            "n_v": VMEM((3, c, w), F32),
            "qkv_v": VMEM((2, 2, c, 3 * w), BF16),
            "o_v": VMEM((2, 2, c, w), BF16),
            "gp_v": VMEM((c, ff), F32),
            "g_v": VMEM((2, c, ff), BF16),
            "a_v": VMEM((2, 3, c, w), BF16),
            "y_v": VMEM((t, c, w), F32),
            "dqkv_f": VMEM((c, 3 * w), F32),
            "perm_v": VMEM((w // 128, c, 128), F32),
            "dys_v": VMEM((2, c, w), BF16),
            "dy_v": VMEM((c, w), F32),
            "do_v": VMEM((2, c, w), BF16),
            "got": VMEM((t, real, w), F32),
            "stat_v": VMEM((t, c, 128), F32),
            "lse_v": VMEM((t, 2 * HEADS, c), F32),
            "spare_v": VMEM((w // 2, w), F32),
            "raw_sem": pltpu.SemaphoreType.DMA((20,)),
            "in_sem": pltpu.SemaphoreType.DMA((4,)),
            "out_sem": pltpu.SemaphoreType.DMA((18,)),
            "send": pltpu.SemaphoreType.DMA((t, 2)),
            "recv": pltpu.SemaphoreType.DMA((t, 2)),
        }
        for name, ranges in (("col_bias", blocks(feat, rows)), ("row_bias", blocks(rows, feat))):
            for i, (queries, keys) in enumerate(ranges):
                shape = (queries.stop - queries.start, keys.stop - keys.start)
                scratch[f"{name}0{i}"] = VMEM(shape[::-1], F32)
                scratch[f"{name}1{i}"] = VMEM(shape, F32)

        def body(r):
            for n in ("col_bias", "row_bias"):
                setattr(r, n, [[getattr(r, f"{n}{along}{i}") for i in range(2)] for along in range(2)])
            self.kernel(r)

        return call("layers", body, 1, ins, outs, scratch, VMEM_LIMIT)

    def raw_pieces(self, r):
        w, ff = self.width, self.ff
        half, wide_in, step = w // 2, 3 * w, self.SPLIT_ROWS
        top, rest, whole = slice(0, half), slice(half, w), slice(None)
        big, bigger = r.dqkv_f.at[top], r.gp_v.at[top]
        pieces = [
            (r.win.at[0, top], big, r.win_v, (0,), 0, whole, 0),
            (r.win.at[0, rest], bigger.at[:, 0:wide_in], r.win_v, (0,), half, whole, 1),
            (r.wout.at[0, top], r.h_v.at[0, top], r.wout_v, (0,), 0, whole, 2),
            (r.wout.at[0, rest], r.h_v.at[1, top], r.wout_v, (0,), half, whole, 3),
            (r.win.at[1, top], big, r.win_v, (1,), 0, whole, 0),
            (r.win.at[1, rest], bigger.at[:, 0:wide_in], r.win_v, (1,), half, whole, 1),
            (r.wout.at[1, top], r.n_v.at[0, top], r.wout_v, (1,), 0, whole, 4),
            (r.wout.at[1, rest], r.spare_v, r.wout_v, (1,), half, whole, 5),
        ]
        self.attention_pieces = len(pieces)
        pieces.append((r.wup.at[top], bigger, r.wup_v, (), 0, whole, 1))
        pieces.append((r.wup.at[rest, 0:wide_in], big, r.wup_v, (), half, slice(0, wide_in), 0))
        pieces.append((r.wup.at[rest, wide_in:ff], r.spare_v, r.wup_v, (), half, slice(wide_in, ff), 5))
        high = self.cells // step * step
        buffers = [r.y_v.at[0, 0:high], r.y_v.at[1, 0:high]]
        low = slice(half, half + (self.cells - half) // step * step)
        for k in range(3):
            buffers.append(r.dqkv_f.at[low, k * w : (k + 1) * w])
        for k in range(ff // w):
            buffers.append(r.gp_v.at[low, k * w : (k + 1) * w])
        at = 0
        for i, buffer in enumerate(buffers):
            size = min(buffer.shape[0], ff - at)
            if size:
                pieces.append((r.wdown.at[at : at + size], buffer.at[0:size], r.wdown_v, (), at, whole, 6 + i))
            at += size
        assert at == ff
        return pieces

    def raw_copy(self, r, i):
        src, buffer = self.raw_pieces(r)[i][:2]
        return pltpu.make_async_copy(src, buffer, r.raw_sem.at[i])

    def split_piece(self, r, i):
        pieces = self.raw_pieces(r)
        _, buffer, v, lead, at, columns, user = pieces[i]
        step = self.SPLIT_ROWS
        self.raw_copy(r, i).wait()

        @pl.loop(0, buffer.shape[0] // step)
        def _(j):
            src = pl.ds(pl.multiple_of(j * step, step), step)
            dst = pl.ds(pl.multiple_of(at + j * step, step), step)
            put(v, (*lead, dst, columns), buffer[src])

        later = [k for k in range(i + 1, len(pieces)) if pieces[k][-1] == user]
        if later:
            self.raw_copy(r, later[0]).start()

    def start_raw(self, r):
        seen = set()
        for i, piece in enumerate(self.raw_pieces(r)):
            if piece[-1] not in seen:
                self.raw_copy(r, i).start()
            seen.add(piece[-1])

    def split_attention(self, r):
        for i in range(self.attention_pieces):
            self.split_piece(r, i)

    def split_mlp(self, r):
        for i in range(self.attention_pieces, len(self.raw_pieces(r))):
            self.split_piece(r, i)

    def kernel(self, r):
        t, real, c = self.tables, self.real, self.cells
        section = lax.axis_index("section")
        other = {"section": 1 - section}
        barrier = pltpu.get_barrier_semaphore()
        pl.semaphore_signal(barrier, inc=1, device_id=other, device_id_type=pl.DeviceIdType.MESH)
        self.start_raw(r)

        @pl.when(section == 0)
        def _():
            start(r.cells.at[0], r.dy_v.at[0:real], r.in_sem.at[0])

        self.split_attention(r)

        @pl.when(section == 1)
        def _():
            self.split_mlp(r)

        for along in range(2):
            fill_biases(self.rows, self.feat, self.feat, r.row_bias[along], along)
        r.small[...] = jnp.zeros_like(r.small)
        pl.semaphore_wait(barrier, 1)

        def relay(table, half):
            at = slice(half * self.width // 2, (half + 1) * self.width // 2)
            src, dst = r.y_v.at[table, 0:real, at], r.got.at[table, :, at]
            return remote(src, dst, r.send.at[table, half], r.recv.at[table, half], other)

        @pl.loop(0, 2 * t)
        def _(step):
            forward = (1 - section) * (1 - step // t) + section * (1 - step % 2)
            table = (1 - section) * (step % t) + section * (step // 2)

            @pl.when(forward == 1)
            def _():
                self.forward(r, table, section, relay, step)

            @pl.when(forward == 0)
            def _():
                self.backward(r, table, section, relay)

        @pl.when(section == 1)
        def _():
            for table in range(t):
                for half in range(2):
                    relay(table, half).wait_send()

    def forward(self, r, table, section, relay, step):
        c, w, ff, hd, real = self.cells, self.width, self.ff, self.hd, self.real
        stores, held = [], []

        def keep(src, dst, to_reload=False):
            copy = pltpu.make_async_copy(src, dst, r.out_sem.at[len(stores) + len(held)])
            if to_reload:
                held.append(copy)
                pl.when(section == 0)(copy.start)
            else:
                stores.append(copy)
                copy.start()

        for level in range(2):
            r.h_v[level, real:, :] = jnp.zeros((c - real, w), F32)

        def keep_column(k, at, value):
            column = lax.broadcasted_iota(jnp.int32, (1, r.stat_v.shape[2]), 1) == k
            r.stat_v[table, at, :] = jnp.where(column, value, r.stat_v[table, at, :])

        def norm(site):
            n, rstd = normalized(r.h_v[site % 2])
            r.n_v[site] = n
            keep(r.n_v.at[site], r.ns.at[table, site], True)
            keep_column(2 * HEADS + site, slice(None), rstd)
            put(r.a_v, (site,), n * r.gains[site])
            keep(r.a_v.at[:, site], r.as_.at[table, :, site])

        fill_biases(self.feat, self.rows, r.ctx[table], r.col_bias[1], 1)

        @pl.when(section == 0)
        def _():
            load = pltpu.make_async_copy(r.cells.at[table], r.dy_v.at[0:real], r.in_sem.at[0])
            pl.when(step > 0)(load.start)
            load.wait()
            for at, missing in self.missing(r, table):
                r.dy_v[at] = jnp.where(missing, r.embed[...], r.dy_v[at])
            self.set_out(r, r.dy_v, real)

        @pl.when(section == 1)
        def _():
            start(r.cot.at[table], r.dy_v.at[0:real], r.in_sem.at[1])
            for half in range(2):
                relay(table, half).wait_recv()
            self.set_out(r, r.got.at[table], real)

        self.by_rows(r, r.h_v.at[0])
        for site in range(2):
            norm(site)

            def project(j):
                at = slice(j * TILE, (j + 1) * TILE)
                return wide(parts(r.a_v, site), parts(r.win_v, site, slice(None), at), 1, 0)

            def keep_projected(j, out):
                if j < w // TILE:
                    out = out * (self.scale * LOG2E)
                put(r.qkv_v, (site, slice(None), slice(j * TILE, (j + 1) * TILE)), out)

            staggered([(j,) for j in range(3 * w // TILE)], project, keep_projected)
            keep(r.qkv_v.at[:, site], r.qkvs.at[table, :, site], True)

            def scores(head, queries, keys, bias):
                q = parts(r.qkv_v, site, queries, lanes(head, hd))
                k = parts(r.qkv_v, site, keys, lanes(HEADS + head, hd))
                return wide(q, k, 1, 1)

            def softmax(head, queries, keys, bias, s):
                s = s + bias[...]
                top = jnp.max(s, axis=-1, keepdims=True)
                e = jnp.exp2(s - top)
                total = jnp.sum(e, axis=-1, keepdims=True)
                keep_column(site * HEADS + head, queries, top + jnp.log2(total))
                return split(e), 1.0 / total

            def blend(head, queries, keys, bias, state):
                e, inverse = state
                v = parts(r.qkv_v, site, keys, lanes(2 * HEADS + head, hd))
                put(r.o_v, (site, queries, lanes(head, hd)), side(e, v) * inverse)

            @pl.loop(0, HEADS // 2)
            def _(two):
                units = [(head, *unit) for head in (2 * two, 2 * two + 1) for unit in self.sites(r, site, 1)]
                staggered(units, scores, softmax, blend)

            keep(r.o_v.at[:, site], r.os.at[table, :, site])
            after = r.h_v[site] + wide(parts(r.o_v, site), parts(r.wout_v, site), 1, 0)
            if site == 0:
                self.set_out(r, after, c)
                self.by_features(r, r.h_v.at[1])
            else:
                r.h_v[0] = after
        r.lse_v[table] = r.stat_v[table].T[0 : 2 * HEADS]
        norm(2)

        @pl.when((section == 0) & (step == 0))
        def _():
            self.split_mlp(r)

        def up(j):
            return wide(parts(r.a_v, 2), parts(r.wup_v, slice(None), slice(j * TILE, (j + 1) * TILE)), 1, 0)

        tiles = ff // TILE
        z = up(0)
        for j in range(tiles):
            at = slice(j * TILE, (j + 1) * TILE)
            following = up(j + 1) if j + 1 < tiles else None
            g, gp = gelu_parts(z)
            put(r.g_v, (slice(None), at), g)
            r.gp_v[:, at] = gp
            z = following
        keep(r.g_v, r.gs.at[table])
        keep(r.gp_v, r.gps.at[table], True)
        for half in range(2):
            at = slice(half * w // 2, (half + 1) * w // 2)
            r.y_v[table, :, at] = r.h_v[0, :, at] + wide(parts(r.g_v), parts(r.wdown_v, slice(None), at), 1, 0)

            @pl.when(section == 0)
            def _():
                relay(table, half).start()

        keep(r.y_v.at[table, 0:real], r.out.at[table])
        for copy in stores:
            copy.wait()

        @pl.when(section == 0)
        def _():
            for copy in held:
                copy.wait()

    def backward(self, r, table, section, relay):
        c, w, ff, hd, real = self.cells, self.width, self.ff, self.hd, self.real
        stores = []

        def keep(src, dst):
            stores.append(start(src, dst, r.out_sem.at[len(stores)]))

        fill_biases(self.feat, self.rows, r.ctx[table], r.col_bias[0], 0)

        @pl.when(section == 0)
        def _():
            loads = [
                start(r.ns.at[table], r.n_v, r.in_sem.at[0]),
                start(r.qkvs.at[table], r.qkv_v, r.in_sem.at[1]),
                start(r.gps.at[table], r.gp_v, r.in_sem.at[2]),
            ]
            for half in range(2):
                relay(table, half).wait()
            r.dy_v[0:real] = r.got[table]
            for copy in loads:
                copy.wait()

        @pl.when(section == 1)
        def _():
            pltpu.make_async_copy(r.cot.at[table], r.dy_v.at[0:real], r.in_sem.at[1]).wait()

        r.dy_v[real:, :] = jnp.zeros((c - real, w), F32)
        put(r.dys_v, (), r.dy_v[...])
        keep(r.dys_v, r.dys.at[table])

        def down(j):
            return wide(parts(r.dys_v), parts(r.wdown_v, slice(j * TILE, (j + 1) * TILE)), 1, 1)

        tiles = ff // TILE
        dg = down(0)
        for j in range(tiles):
            at = slice(j * TILE, (j + 1) * TILE)
            following = down(j + 1) if j + 1 < tiles else None
            put(r.g_v, (slice(None), at), dg * r.gp_v[:, at])
            dg = following
        keep(r.g_v, r.dzs.at[table])
        da = wide(parts(r.g_v), parts(r.wup_v), 1, 1)

        def through_norm(site, da):
            n, k = r.n_v[site], 2 * HEADS + site
            rstd = r.stat_v[table, :, k : k + 1]
            r.small[site : site + 1, :] += jnp.sum(da * n, axis=0, keepdims=True)
            return norm_back(n, rstd, r.gains[site], da)

        r.dy_v[...] += through_norm(2, da)
        for site in (1, 0):
            if site == 0:
                self.set_out(r, r.dy_v, real)
                self.by_rows(r, r.dy_v)
            put(r.o_v, (site,), r.dy_v[...])
            keep(r.o_v.at[:, site], r.dhs.at[table, :, site])
            put(r.do_v, (), wide(parts(r.o_v, site), parts(r.wout_v, site), 1, 1))

            def part_of(which, head, span):
                return parts(r.qkv_v, site, span, lanes(which * HEADS + head, hd))

            def products(head, queries, keys, bias):
                do = parts(r.do_v, queries, lanes(head, hd))
                s = wide(part_of(1, head, keys), part_of(0, head, queries), 1, 1)
                return s, wide(part_of(2, head, keys), do, 1, 1)

            def gradients(head, queries, keys, bias, state):
                s, dp = state
                p = jnp.exp2(s + bias[...] - r.lse_v[table, pl.ds(site * HEADS + head, 1), queries])
                ds = p * (dp - jnp.sum(p * dp, axis=0, keepdims=True))
                return split(p), split(ds)

            def back(head, queries, keys, bias, state):
                p, ds = state
                k = part_of(1, head, keys)
                r.dqkv_f[queries, lanes(head, hd)] = (wide(tuple(x.T for x in k), ds, 1, 0) * self.scale).T
                dk = side(ds, part_of(0, head, queries)) * LN2
                dv = side(p, parts(r.do_v, queries, lanes(head, hd)))
                for which, term in ((1, dk), (2, dv)):
                    at = lanes(which * HEADS + head, hd)
                    if keys.start == 0:
                        r.dqkv_f[keys, at] = term
                    else:
                        known = overlap - keys.start
                        if known:
                            r.dqkv_f[keys.start : overlap, at] += term[:known]
                        r.dqkv_f[overlap : keys.stop, at] = term[known:]

            overlap = self.sites(r, site, 0)[0][1].stop

            @pl.loop(0, HEADS // 2)
            def _(two):
                units = [(head, *unit) for head in (2 * two, 2 * two + 1) for unit in self.sites(r, site, 0)]
                staggered(units, products, gradients, back)

            for j in range(3 * w // TILE):
                at = slice(j * TILE, (j + 1) * TILE)
                put(r.qkv_v, (site, slice(None), at), r.dqkv_f[:, at])
            keep(r.qkv_v.at[:, site], r.dqkvs.at[table, :, site])
            da = wide(parts(r.qkv_v, site), parts(r.win_v, site), 1, 1)
            r.dy_v[...] += through_norm(site, da)

        self.set_out(r, r.dy_v, real)
        self.by_features(r, r.dy_v)

        @pl.when(section == 0)
        def _():
            total = jnp.zeros((1, w), F32)
            for at, missing in self.missing(r, table):
                total += jnp.sum(jnp.where(missing, r.dy_v[at], 0.0), axis=0, keepdims=True)
                r.y_v[table, at] = jnp.where(missing, 0.0, r.dy_v[at])
            r.small[3:4, :] += total

        @pl.when(section == 1)
        def _():
            r.y_v[table] = r.dy_v[...]
            for half in range(2):
                relay(table, half).start()

        keep(r.y_v.at[table, 0:real], r.din.at[table])
        for copy in stores:
            copy.wait()


class GradSum:
    ROWS, COLS = 512, 256
    PARTS = 2
    SLACK = 2

    def __init__(self, count, tables, cells, width, ff):
        self.count, self.tables, self.cells, self.width = count, tables, cells, width
        self.rest = count // 4
        shapes = [("gs", None, "dys", None, "down", None, ff, width), ("as_", 2, "dzs", None, "up", None, width, ff)]
        for site in (1, 0):
            shapes.append(("as_", site, "dqkvs", site, "win", site, width, 3 * width))
            shapes.append(("os", site, "dhs", site, "wout", site, width, width))
        self.groups, at = [], 0
        for *which, k, n in shapes:
            blocks = (k // self.ROWS) * (n // self.COLS)
            self.groups.append((at, at + blocks, *which, n // self.COLS))
            at += blocks
        self.blocks = at
        self.chunks = self.blocks * self.PARTS
        self.hops = self.rest // 2 - 1
        self.sends = self.SLACK * (self.hops + 1) + 2
        self.rows = self.ROWS // self.PARTS
        self.ring = self.SLACK // self.PARTS + 2
        self.depth = (cells + 127) // 128 * 128

    def select(self, q, action):
        for group in self.groups:
            first, stop, *_, across = group

            @pl.when((q >= first) & (q < stop))
            def _():
                action(group, (q - first) // across, (q - first) % across)

    def starts_row(self, q):
        found = False
        for first, stop, *_, across in self.groups:
            found = found | ((q >= first) & (q < stop) & ((q - first) % across == 0))
        return found

    def load(self, r, q):
        slot = q % 2

        def action(group, i, j):
            _, _, left, left_site, right, right_site, *_ = group
            a, b = getattr(r, left), getattr(r, right)

            def at(t, part, site):
                return (t, part, slice(None)) if site is None else (t, part, site, slice(None))

            for t in range(self.tables):
                rows = slice(t * self.depth, t * self.depth + self.cells)
                for part in range(2):
                    sem = 2 * t + part
                    start(b.at[(*at(t, part, right_site), lanes(j, self.COLS))], r.b_v.at[slot, part, rows], r.b_sem.at[slot, sem])

                    @pl.when(j == 0)
                    def _():
                        start(a.at[(*at(t, part, left_site), lanes(i, self.ROWS))], r.a_v.at[part, rows], r.a_sem.at[sem])

        self.select(q, action)

    def each_operand(self):
        return [(2 * t + part, part, slice(t * self.depth, t * self.depth + self.cells)) for t in range(self.tables) for part in range(2)]

    def product(self, r, q):
        slot = q % 2

        @pl.when(self.starts_row(q))
        def _():
            for sem, part, rows in self.each_operand():
                a = r.a_v.at[part, rows]
                pltpu.make_async_copy(a, a, r.a_sem.at[sem]).wait()
            for part in range(2):
                r.left_v[part] = r.a_v[part].T

        for sem, part, rows in self.each_operand():
            b = r.b_v.at[slot, part, rows]
            pltpu.make_async_copy(b, b, r.b_sem.at[slot, sem]).wait()

        @pl.when(q + 1 < self.blocks)
        def _():
            self.load(r, q + 1)

        r.products[q % self.ring] = side(parts(r.left_v), parts(r.b_v.at[slot]))

    def kernel(self, r):
        rest, rows, ring = self.rest, self.rows, self.ring
        half = rows // 2
        quart = half // 2
        me, section = lax.axis_index("dp"), lax.axis_index("section")
        core, pair, place = me % 2, me // 2 % 2, me // 4
        sibling, neighbour = {"dp": me + 1 - 2 * core}, {"dp": me + 2 - 4 * pair}
        far = place // (rest // 2)
        along = (1 - far) * place + far * (rest - 1 - place)
        inward, outward = {"dp": me + 4 - 8 * far}, {"dp": me - 4 + 8 * far}
        hops = self.hops

        def peer(j):
            return {"dp": lax.rem(place + j, rest) * 4 + me % 4}

        def span(at, size):
            return pl.ds(pl.multiple_of(at, size), size)

        mine = core * half
        own, other = pair * quart, (1 - pair) * quart
        keeps, gives = far * quart, (1 - far) * quart

        barrier = pltpu.get_barrier_semaphore()

        def greet(device):
            pl.semaphore_signal(barrier, inc=1, device_id=device, device_id_type=pl.DeviceIdType.MESH)

        greet(sibling)
        greet(neighbour)

        @pl.loop(1, rest)
        def _(j):
            greet(peer(j))

        for t in range(self.tables):
            pad = slice(t * self.depth + self.cells, (t + 1) * self.depth)
            for part in range(2):
                r.a_v[part, pad] = jnp.zeros_like(r.a_v[part, pad])
                for slot in range(2):
                    r.b_v[slot, part, pad] = jnp.zeros_like(r.b_v[slot, part, pad])
        self.load(r, 0)
        passing = [
            start(getattr(r, f"table{i}"), getattr(r, f"out{i}"), r.table_sem.at[i]) for i in range(self.passed)
        ]

        @pl.when(section == 1)
        def _():
            greet({"section": 0})

        pl.semaphore_wait(barrier, rest + 2 - section)

        def copy(which, c, src, dst, device):
            return remote(src, dst, r.send.at[which, c % self.sends], r.recv.at[which, c], device)

        def product_rows(c, which):
            return c // self.PARTS % ring, span(c % self.PARTS * rows + which * half, half)

        def halve(c):
            return copy(0, c, r.products.at[product_rows(c, 1 - core)], r.sums.at[c], sibling)

        def gather_half(c):
            at = r.full.at[c, span(mine, half)]
            return copy(1, c, at, at, sibling)

        def quarter(c):
            return copy(2, c, r.sums.at[c, span(other, quart)], r.got_near.at[c], neighbour)

        def gather_quarter(c):
            at = r.full.at[c, span(mine + own, quart)]
            return copy(3, c, at, at, neighbour)

        def add_up(c):
            return copy(2, c, r.sums.at[c, span(keeps, quart)], r.got_near.at[c], neighbour)

        def come(kind, c):
            if kind == 0:
                return copy(4, c, r.sums.at[c, span(own, quart)], r.got_in.at[c, 0:quart], inward)
            return copy(4, c, r.sums.at[c], r.got_in.at[c], inward)

        def meet(kind, c):
            at = span(own if kind == 0 else gives, quart)
            return copy(5, c, r.sums.at[c, at], r.got_mid.at[c], inward)

        def give_back(c):
            at = r.full.at[c, span(mine + keeps, quart)]
            return copy(6, c, at, at, inward)

        def leave(kind, c):
            at = r.full.at[c, span(mine + own, quart) if kind == 0 else span(mine, half)]
            return copy(7, c, at, at, outward)

        def reduced(kind, c, h, at_end):
            @pl.when((along == h) & (h < hops))
            def _():
                come(kind, c).start()

            @pl.when((along == h) & (h == hops))
            def _():
                at_end(c)

        def come_hop(kind, c, h):
            @pl.when(along == h)
            def _():
                come(kind, c).wait_send()

            @pl.when(along == h + 1)
            def _():
                come(kind, c).wait_recv()
                if kind == 0:
                    r.sums[c, span(own, quart)] += r.got_in[c, 0:quart]
                else:
                    r.sums[c] += r.got_in[c]

            reduced(kind, c, h + 1, lambda c: meet(kind, c).start())

        def pass_out(kind, c, h):
            @pl.when((along == h) & (h > 0))
            def _():
                leave(kind, c).start()

            if kind == 0:

                @pl.when(along == h)
                def _():
                    gather_quarter(c).start()

        def leave_hop(kind, c, g):
            h = hops - g

            @pl.when(along == h)
            def _():
                leave(kind, c).wait_send()

            @pl.when(along == h - 1)
            def _():
                leave(kind, c).wait_recv()

            pass_out(kind, c, h - 1)

        def after_halve(c):
            halve(c).wait()
            r.sums[c] += r.products[product_rows(c, core)]

            @pl.when(core == 0)
            def _():
                quarter(c).start()

            @pl.when(core == 1)
            def _():
                reduced(1, c, 0, lambda c: meet(1, c).start())

        def after_quarter(c):
            quarter(c).wait()
            r.sums[c, span(own, quart)] += r.got_near[c]
            reduced(0, c, 0, lambda c: meet(0, c).start())

        def after_meet(kind, c):
            @pl.when(along == hops)
            def _():
                meet(kind, c).wait()
                if kind == 0:
                    r.full[c, span(mine + own, quart)] = r.sums[c, span(own, quart)] + r.got_mid[c]
                else:
                    r.sums[c, span(keeps, quart)] += r.got_mid[c]
                    add_up(c).start()

            if kind == 0:
                pass_out(0, c, hops)

        def after_add_up(c):
            @pl.when(along == hops)
            def _():
                add_up(c).wait()
                r.full[c, span(mine + keeps, quart)] = r.sums[c, span(keeps, quart)] + r.got_near[c]
                give_back(c).start()

        def after_give_back(c):
            @pl.when(along == hops)
            def _():
                give_back(c).wait()

            pass_out(1, c, hops)

        def gathered(c):
            @pl.when(core == 0)
            def _():
                gather_quarter(c).wait()

            gather_half(c).start()

        def after_gather_half(c):
            gather_half(c).wait()

        def small_copy(k, device):
            return remote(r.small_v.at[k], r.got_small.at[k], r.small_send.at[k], r.small_recv.at[k], device)

        def small_rest(j):
            dst = r.got_small.at[2 + j]
            return remote(r.small_v.at[3], dst, r.small_send.at[2 + j], r.small_recv.at[2 + j], peer(j))

        def small_step(step):
            @pl.when(step == 2)
            def _():
                r.small_v[1] = r.small[...]
                small_copy(1, sibling).start()

            @pl.when(step == 4)
            def _():
                small_copy(1, sibling).wait()
                r.small_v[2] = r.small_v[1] + r.got_small[1]
                small_copy(2, neighbour).start()

            @pl.when(step == 6)
            def _():
                small_copy(2, neighbour).wait()
                r.small_v[3] = r.small_v[2] + r.got_small[2]
                pl.loop(1, rest)(lambda j: small_rest(j).start())

            @pl.when(step == 8)
            def _():
                pl.loop(1, rest)(lambda j: small_rest(j).wait())
                total = r.small_v[3]
                for j in range(1, rest):
                    total += r.got_small[2 + j]
                r.small_v[0] = total

                @pl.when(section == 0)
                def _():
                    small_copy(0, {"section": 1}).start()

        last = 2 * hops + 5

        def delay(time):
            return self.SLACK * time - (1 if time < last else 2)

        @pl.loop(0, self.chunks + delay(last))
        def _(step):
            def stage(time, action):
                c = step - (delay(time) if isinstance(time, int) else self.SLACK * time - 1)

                @pl.when((c >= 0) & (c < self.chunks))
                def _():
                    action(c)

            stage(last, after_gather_half)

            @pl.when(core == 0)
            def _():
                over(hops, lambda g: stage(hops + 4 + g, lambda c: leave_hop(0, c, g)))
                stage(hops + 3, lambda c: after_meet(0, c))
                over(hops, lambda h: stage(3 + h, lambda c: come_hop(0, c, h)))
                stage(2, after_quarter)

            @pl.when(core == 1)
            def _():
                over(hops, lambda g: stage(hops + 5 + g, lambda c: leave_hop(1, c, g)))
                stage(hops + 4, after_give_back)
                stage(hops + 3, after_add_up)
                stage(hops + 2, lambda c: after_meet(1, c))
                over(hops, lambda h: stage(2 + h, lambda c: come_hop(1, c, h)))

            stage(last - 1, gathered)
            stage(1, after_halve)
            small_step(step)

            @pl.when(step < self.chunks)
            def _():
                @pl.when(step % self.PARTS == 0)
                def _():
                    self.product(r, step // self.PARTS)

                halve(step).start()

        for load in passing:
            load.wait()
        r.small_out[...] = r.small_v[0]

        @pl.when(section == 0)
        def _():
            small_copy(0, {"section": 1}).wait_send()

        @pl.when(section == 1)
        def _():
            small_copy(0, {"section": 1}).wait_recv()
            r.small_out[3:4] = r.got_small[0, 3:4]

    def __call__(self, operands, small, tables):
        t, width, deep = self.tables, self.width, self.tables * self.depth
        rest, chunks, rows, ring, cols = self.rest, self.chunks, self.rows, self.ring, self.COLS
        outs = {"full": VMEM((chunks, rows, cols), F32), "small_out": f32(8, width)}
        outs |= {f"out{i}": VMEM(a.shape, F32) for i, a in enumerate(tables)}
        scratch = {
            "products": VMEM((ring, self.ROWS, cols), F32),
            "sums": VMEM((chunks, rows // 2, cols), F32),
            "got_near": VMEM((chunks, rows // 4, cols), F32),
            "got_mid": VMEM((chunks, rows // 4, cols), F32),
            "got_in": VMEM((chunks, rows // 2, cols), F32),
            "a_v": VMEM((2, deep, self.ROWS), BF16),
            "left_v": VMEM((2, self.ROWS, deep), BF16),
            "b_v": VMEM((2, 2, deep, cols), BF16),
            "small_v": VMEM((4, 8, width), F32),
            "got_small": VMEM((2 + rest, 8, width), F32),
            "a_sem": dma(2 * t),
            "b_sem": dma(2, 2 * t),
            "send": dma(8, self.sends),
            "recv": dma(8, chunks),
            "small_send": dma(2 + rest),
            "small_recv": dma(2 + rest),
        }
        ins = {n: (a, ANY) for n, a in operands.items()} | {"small": (small, VMEM)}
        ins |= {f"table{i}": (a, ANY) for i, a in enumerate(tables)}
        scratch["table_sem"] = dma(len(tables))
        self.passed = len(tables)
        outs = {n: (s, VMEM) for n, s in outs.items()}
        return call("weight_gradient_sum", self.kernel, 0, ins, outs, scratch, SUM_VMEM_LIMIT)

    def results(self, sums, small, tables, ff):
        width = self.width

        def here(a):
            return (pltpu.with_memory_space_constraint(a, pltpu.VMEM), VMEM)

        ins = {"full": here(sums), "small": (small, VMEM)} | {f"table{i}": here(a) for i, a in enumerate(tables)}
        outs = {
            "win": f32(2, width, 3 * width),
            "wout": f32(2, width, width),
            "up": f32(width, ff),
            "down": f32(ff, width),
        } | {f"out{i}": f32(*a.shape) for i, a in enumerate(tables)}
        outs = {n: (s, ANY) for n, s in outs.items()}
        outs |= {"gain": (f32(3, 1, width), VMEM), "missing": (f32(1, width), VMEM)}
        scratch = {"sem": dma(self.chunks), "out_sem": dma(len(tables))}

        def body(r):
            stores = [
                start(getattr(r, f"table{i}"), getattr(r, f"out{i}"), r.out_sem.at[i]) for i in range(len(tables))
            ]
            for first, stop, *_, out, site, across in self.groups:
                dst = getattr(r, out) if site is None else getattr(r, out).at[site]
                for c in range(first * self.PARTS, stop * self.PARTS):
                    q = c // self.PARTS - first
                    row = q // across * self.ROWS + c % self.PARTS * self.rows
                    at = (slice(row, row + self.rows), slice(q % across * self.COLS, (q % across + 1) * self.COLS))
                    stores.append(start(r.full.at[c], dst.at[at], r.sem.at[c]))
            for k in range(3):
                r.gain[k] = r.small[k : k + 1, :]
            r.missing[...] = r.small[3:4, :]
            for copy in stores:
                copy.wait()

        return call("results", body, None, ins, outs, scratch, SUM_VMEM_LIMIT)


def local(
    cells,
    missing_mask,
    missing_embed,
    context_rows,
    norm_gains,
    attn_in,
    attn_out,
    mlp_up,
    mlp_down,
    cotangent,
):
    tables, rows, feat, width = cells.shape
    ff = mlp_up.shape[2]
    layers = Layers(tables, rows, feat, width, ff)

    def flat(tables_of_cells):
        return jnp.swapaxes(tables_of_cells, 1, 2).reshape(tables, rows * feat, -1)

    def unflat(cells_of_tables):
        return jnp.swapaxes(cells_of_tables.reshape(tables, feat, rows, width), 1, 2)[None]

    weights = (attn_in[0], attn_out[0], mlp_up[0], mlp_down[0])
    gains = jnp.swapaxes(norm_gains, 0, 1)
    done = layers(flat(cells), missing_mask, missing_embed[None], context_rows, gains, weights, flat(cotangent))
    operands = {n: done[n] for n in ("as_", "os", "gs", "dys", "dzs", "dhs", "dqkvs")}
    grad_sum = GradSum(lax.axis_size("dp"), tables, layers.cells, width, ff)
    sums = grad_sum(operands, done["small"], (done["out"], done["din"]))
    got = grad_sum.results(sums["full"], sums["small_out"], (sums["out0"], sums["out1"]), ff)
    return (
        unflat(got["out0"]),
        unflat(got["out1"]),
        jnp.swapaxes(got["gain"], 0, 1),
        got["win"][None],
        got["wout"][None],
        got["up"][None],
        got["down"][None],
        got["missing"][0],
    )


def solution(mesh):
    in_specs = (
        P("dp", None, None, None),
        P("dp", None, None),
        P(),
        P("dp"),
        P("section", None, None),
        P("section", None, None, None),
        P("section", None, None, None),
        P("section", None, None),
        P("section", None, None),
        P("dp", None, None, None),
    )
    out_specs = (
        P("section", "dp", None, None, None),
        P("section", "dp", None, None, None),
        P("section", None, None),
        P("section", None, None, None),
        P("section", None, None, None),
        P("section", None, None),
        P("section", None, None),
        P(),
    )
    return jax.shard_map(local, mesh=mesh, in_specs=in_specs, out_specs=out_specs, check_vma=False)
```

```python
import functools
from types import SimpleNamespace

import jax
import jax.numpy as jnp
from jax import lax
from jax.experimental import pallas as pl
from jax.experimental.pallas import tpu as pltpu
from jax.sharding import PartitionSpec as P

HEADS = 4
EPSILON = 1e-05
NEG = -1e30
INV_SQRT2PI = 0.3989422804014327
LOG2E = 1.4426950408889634
LN2 = 0.6931471805599453
ERFC_P = 0.33
ERFC_C = (0.1863578482, 0.1829552331, 0.2012284886, 0.0472047191, 0.4085317677, -0.3511862269, 0.4602596132, -0.1353514118)
VMEM_LIMIT = 62 * 1024 * 1024
SUM_VMEM_LIMIT = 38 * 1024 * 1024
TILE = 512
F32, BF16 = jnp.float32, jnp.bfloat16


def dot(a, b, contract=((1,), (0,))):
    return lax.dot_general(a, b, (contract, ((), ())), preferred_element_type=F32)


def split(v):
    hi = v.astype(BF16)
    return hi, (v - hi.astype(F32)).astype(BF16)


def put(ref, index, v):
    hi, lo = split(v)
    ref[(0, *index)] = hi
    ref[(1, *index)] = lo


def parts(ref, *index):
    return ref[(0, *index)], ref[(1, *index)]


def wide(a, b, ca, cb):
    (ah, al), (bh, bl) = a, b
    rows = ah.shape[1 - ca]
    both = dot(jnp.concatenate([ah, al], 1 - ca), bh, ((ca,), (cb,)))
    return both[:rows] + both[rows:] + dot(ah, bl, ((ca,), (cb,)))


def near(a, b):
    (ah, al), (bh, bl) = a, b
    return dot(jnp.concatenate([ah, ah, al, al], 1), jnp.concatenate([bh, bl, bh, bl], 1), ((1,), (1,)))


def side(a, b):
    (ah, al), (bh, bl) = a, b
    rows, width = ah.shape[0], bh.shape[1]
    four = dot(jnp.concatenate([ah, al], 0), jnp.concatenate([bh, bl], 1))
    high, low = four[:rows], four[rows:]
    return high[:, :width] + (high[:, width:] + low[:, :width] + low[:, width:])


def normalized(h):
    centred = h - jnp.mean(h, axis=-1, keepdims=True)
    rstd = lax.rsqrt(jnp.mean(centred * centred, axis=-1, keepdims=True) + EPSILON)
    return centred * rstd, rstd


def norm_back(n, rstd, gain, da):
    dn = da * gain
    return rstd * (dn - jnp.mean(dn, axis=-1, keepdims=True) - n * jnp.mean(dn * n, axis=-1, keepdims=True))


def cell_ids(start, count, inner, along):
    shape = (count, 1) if along == 0 else (1, count)
    at = lax.broadcasted_iota(jnp.int32, shape, along) + start
    outer = lax.shift_right_logical(at * ((1 << 20) // inner + 1), 20)
    return outer, at - outer * inner


def up16(n):
    return (n + 15) // 16 * 16


def blocks(outer, inner):
    cells = up16(outer * inner)
    half = up16((outer + 1) // 2 * inner)
    first_keys = min(cells, up16((((half - 1) // inner) + 1) * inner))
    second_keys = ((half // inner) * inner) // 16 * 16
    return ((slice(0, half), slice(0, first_keys)), (slice(half, cells), slice(second_keys, cells)))


def when(cond):
    if isinstance(cond, bool):
        return (lambda action: action()) if cond else (lambda action: None)
    return pl.when(cond)


def over(count, action):
    if count <= 4:
        for i in range(count):
            action(i)
    else:
        pl.loop(0, count)(action)


def staggered(units, *steps):
    state = [None] * len(units)
    for i in range(len(units) + 1):
        if i < len(units):
            state[i] = steps[0](*units[i])
        if i > 0:
            for step in steps[1:]:
                state[i - 1] = step(*units[i - 1], state[i - 1])


def lanes(j, width):
    return pl.ds(pl.multiple_of(j * width, width), width)


def start(src, dst, sem):
    copy = pltpu.make_async_copy(src, dst, sem)
    copy.start()
    return copy


def fill_biases(outer, inner, limit, refs, keys_along):
    for (queries, keys), ref in zip(blocks(outer, inner), refs):
        q_outer, _ = cell_ids(queries.start, queries.stop - queries.start, inner, 1 - keys_along)
        k_outer, k_inner = cell_ids(keys.start, keys.stop - keys.start, inner, keys_along)
        ref[...] = jnp.where((q_outer == k_outer) & (k_inner < limit), 0.0, NEG)


def gelu_parts(z):
    size = jnp.abs(z)
    below = 1.0 + (ERFC_P * 0.7071067811865476) * size
    t = pl.reciprocal(below, approx=True)
    t = t * (2.0 - below * t)
    series = jnp.full_like(t, ERFC_C[-1])
    for c in ERFC_C[-2::-1]:
        series = series * t + c
    bell = jnp.exp(-0.5 * z * z)
    tail = 0.5 * (series * t) * bell
    phi = jnp.where(z >= 0.0, 1.0 - tail, tail)
    return z * phi, phi + z * (INV_SQRT2PI * bell)


SMEM, VMEM, ANY = pltpu.SMEM, pltpu.VMEM, pl.ANY


def f32(*shape):
    return jax.ShapeDtypeStruct(shape, F32)


def b16(*shape):
    return jax.ShapeDtypeStruct(shape, BF16)


def dma(*shape):
    return pltpu.SemaphoreType.DMA(shape)


def remote(src, dst, send, recv, device):
    return pltpu.make_async_remote_copy(
        src_ref=src, dst_ref=dst, send_sem=send, recv_sem=recv, device_id=device, device_id_type=pl.DeviceIdType.MESH
    )


def call(name, body, collective_id, ins, outs, scratch, limit):
    names = [*ins, *outs, *scratch]

    def kernel(*refs):
        body(SimpleNamespace(**dict(zip(names, refs))))

    results = pl.pallas_call(
        kernel,
        out_shape=[t for t, _ in outs.values()],
        in_specs=[pl.BlockSpec(memory_space=s) for _, s in ins.values()],
        out_specs=[pl.BlockSpec(memory_space=s) for _, s in outs.values()],
        scratch_shapes=list(scratch.values()),
        compiler_params=pltpu.CompilerParams(
            vmem_limit_bytes=limit, collective_id=collective_id, has_side_effects=collective_id is not None
        ),
        name=name,
    )(*(a for a, _ in ins.values()))
    return dict(zip(outs, results))


class Layers:
    SPLIT_ROWS = 64

    def __init__(self, tables, rows, feat, width, ff):
        self.tables, self.rows, self.feat, self.width, self.ff = tables, rows, feat, width, ff
        self.real, self.cells = rows * feat, up16(rows * feat)
        self.hd = width // HEADS
        self.scale = self.hd ** (-0.5)
        self.halves = [queries for queries, _ in blocks(feat, rows)]

    def sites(self, r, site, keys_along):
        if site == 1:
            ranges, biases = blocks(self.feat, self.rows), r.col_bias
        else:
            ranges, biases = blocks(self.rows, self.feat), r.row_bias
        return [(*unit, bias) for unit, bias in zip(ranges, biases[keys_along])]

    def missing(self, r, table):
        mask = r.mask[table]
        return [(slice(f * self.rows, (f + 1) * self.rows), mask[:, f : f + 1] == 1) for f in range(self.feat)]

    def set_out(self, r, src, count):
        for k in range(self.width // 128):
            r.perm_v[k, 0:count] = src[0:count, k * 128 : (k + 1) * 128]

    def by_rows(self, r, dst):
        for row in range(self.rows):
            for k in range(self.width // 128):
                at = (slice(row * self.feat, (row + 1) * self.feat), slice(k * 128, (k + 1) * 128))
                dst[at] = r.perm_v[k, pl.ds(row, self.feat, stride=self.rows), :]

    def by_features(self, r, dst):
        for feat in range(self.feat):
            for k in range(self.width // 128):
                at = (slice(feat * self.rows, (feat + 1) * self.rows), slice(k * 128, (k + 1) * 128))
                dst[at] = r.perm_v[k, pl.ds(feat, self.rows, stride=self.feat), :]

    def __call__(self, cells, mask, embed, context, gains, weights, cotangent):
        t, c, w, ff, real = self.tables, self.cells, self.width, self.ff, self.real
        rows, feat = self.rows, self.feat
        ins = {
            "cells": (cells, ANY),
            "mask": (mask, VMEM),
            "embed": (embed, VMEM),
            "ctx": (context, SMEM),
            "gains": (gains, VMEM),
            "cot": (cotangent, ANY),
        }
        names = ("win", "wout", "wup", "wdown")
        ins |= {n: (a, ANY) for n, a in zip(names, weights)}
        outs = {
            "out": f32(t, real, w),
            "din": f32(t, real, w),
            "ns": f32(t, 3, c, w),
            "qkvs": b16(t, 2, 2, c, 3 * w),
            "gps": f32(t, c, ff),
            "as_": b16(t, 2, 3, c, w),
            "os": b16(t, 2, 2, c, w),
            "gs": b16(t, 2, c, ff),
            "dys": b16(t, 2, c, w),
            "dzs": b16(t, 2, c, ff),
            "dhs": b16(t, 2, 2, c, w),
            "dqkvs": b16(t, 2, 2, c, 3 * w),
        }
        outs = {n: (s, ANY) for n, s in outs.items()} | {"small": (f32(8, w), VMEM)}
        scratch = {n + "_v": VMEM((2, *a.shape), BF16) for n, a in zip(names, weights)}
        scratch |= {
            "h_v": VMEM((2, c, w), F32),
            "n_v": VMEM((3, c, w), F32),
            "qkv_v": VMEM((2, 2, c, 3 * w), BF16),
            "o_v": VMEM((2, 2, c, w), BF16),
            "gp_v": VMEM((c, ff), F32),
            "g_v": VMEM((2, c, ff), BF16),
            "a_v": VMEM((2, 3, c, w), BF16),
            "y_v": VMEM((t, c, w), F32),
            "dqkv_f": VMEM((c, 3 * w), F32),
            "perm_v": VMEM((w // 128, c, 128), F32),
            "dys_v": VMEM((2, c, w), BF16),
            "dy_v": VMEM((c, w), F32),
            "do_v": VMEM((2, c, w), BF16),
            "got": VMEM((t, real, w), F32),
            "stat_v": VMEM((t, c, 128), F32),
            "lse_v": VMEM((t, 2 * HEADS, c), F32),
            "spare_v": VMEM((w // 2, w), F32),
            "raw_sem": pltpu.SemaphoreType.DMA((20,)),
            "in_sem": pltpu.SemaphoreType.DMA((4,)),
            "out_sem": pltpu.SemaphoreType.DMA((18,)),
            "send": pltpu.SemaphoreType.DMA((t, 2)),
            "recv": pltpu.SemaphoreType.DMA((t, 2)),
        }
        for name, ranges in (("col_bias", blocks(feat, rows)), ("row_bias", blocks(rows, feat))):
            for i, (queries, keys) in enumerate(ranges):
                shape = (queries.stop - queries.start, keys.stop - keys.start)
                scratch[f"{name}0{i}"] = VMEM(shape[::-1], F32)
                scratch[f"{name}1{i}"] = VMEM(shape, F32)

        def body(r):
            for n in ("col_bias", "row_bias"):
                setattr(r, n, [[getattr(r, f"{n}{along}{i}") for i in range(2)] for along in range(2)])
            self.kernel(r)

        return call("layers", body, 1, ins, outs, scratch, VMEM_LIMIT)

    def raw_pieces(self, r):
        w, ff = self.width, self.ff
        half, wide_in, step = w // 2, 3 * w, self.SPLIT_ROWS
        top, rest, whole = slice(0, half), slice(half, w), slice(None)
        big, bigger = r.dqkv_f.at[top], r.gp_v.at[top]
        pieces = [
            (r.win.at[0, top], big, r.win_v, (0,), 0, whole, 0),
            (r.win.at[0, rest], bigger.at[:, 0:wide_in], r.win_v, (0,), half, whole, 1),
            (r.wout.at[0, top], r.h_v.at[0, top], r.wout_v, (0,), 0, whole, 2),
            (r.wout.at[0, rest], r.h_v.at[1, top], r.wout_v, (0,), half, whole, 3),
            (r.win.at[1, top], big, r.win_v, (1,), 0, whole, 0),
            (r.win.at[1, rest], bigger.at[:, 0:wide_in], r.win_v, (1,), half, whole, 1),
            (r.wout.at[1, top], r.n_v.at[0, top], r.wout_v, (1,), 0, whole, 4),
            (r.wout.at[1, rest], r.spare_v, r.wout_v, (1,), half, whole, 5),
        ]
        self.attention_pieces = len(pieces)
        pieces.append((r.wup.at[top], bigger, r.wup_v, (), 0, whole, 1))
        pieces.append((r.wup.at[rest, 0:wide_in], big, r.wup_v, (), half, slice(0, wide_in), 0))
        pieces.append((r.wup.at[rest, wide_in:ff], r.spare_v, r.wup_v, (), half, slice(wide_in, ff), 5))
        high = self.cells // step * step
        buffers = [r.y_v.at[0, 0:high], r.y_v.at[1, 0:high]]
        low = slice(half, half + (self.cells - half) // step * step)
        for k in range(3):
            buffers.append(r.dqkv_f.at[low, k * w : (k + 1) * w])
        for k in range(ff // w):
            buffers.append(r.gp_v.at[low, k * w : (k + 1) * w])
        at = 0
        for i, buffer in enumerate(buffers):
            size = min(buffer.shape[0], ff - at)
            if size:
                pieces.append((r.wdown.at[at : at + size], buffer.at[0:size], r.wdown_v, (), at, whole, 6 + i))
            at += size
        assert at == ff
        return pieces

    def raw_copy(self, r, i):
        src, buffer = self.raw_pieces(r)[i][:2]
        return pltpu.make_async_copy(src, buffer, r.raw_sem.at[i])

    def split_piece(self, r, i):
        pieces = self.raw_pieces(r)
        _, buffer, v, lead, at, columns, user = pieces[i]
        step = self.SPLIT_ROWS
        self.raw_copy(r, i).wait()

        @pl.loop(0, buffer.shape[0] // step)
        def _(j):
            src = pl.ds(pl.multiple_of(j * step, step), step)
            dst = pl.ds(pl.multiple_of(at + j * step, step), step)
            put(v, (*lead, dst, columns), buffer[src])

        later = [k for k in range(i + 1, len(pieces)) if pieces[k][-1] == user]
        if later:
            self.raw_copy(r, later[0]).start()

    def start_raw(self, r):
        seen = set()
        for i, piece in enumerate(self.raw_pieces(r)):
            if piece[-1] not in seen:
                self.raw_copy(r, i).start()
            seen.add(piece[-1])

    def split_attention(self, r):
        for i in range(self.attention_pieces):
            self.split_piece(r, i)

    def split_mlp(self, r):
        for i in range(self.attention_pieces, len(self.raw_pieces(r))):
            self.split_piece(r, i)

    def kernel(self, r):
        t, real, c = self.tables, self.real, self.cells
        section = lax.axis_index("section")
        other = {"section": 1 - section}
        barrier = pltpu.get_barrier_semaphore()
        pl.semaphore_signal(barrier, inc=1, device_id=other, device_id_type=pl.DeviceIdType.MESH)
        self.start_raw(r)

        @pl.when(section == 0)
        def _():
            start(r.cells.at[0], r.dy_v.at[0:real], r.in_sem.at[0])

        self.split_attention(r)

        @pl.when(section == 1)
        def _():
            self.split_mlp(r)

        for along in range(2):
            fill_biases(self.rows, self.feat, self.feat, r.row_bias[along], along)
        r.small[...] = jnp.zeros_like(r.small)
        pl.semaphore_wait(barrier, 1)

        def relay(table, half):
            at = self.halves[half]
            at = slice(at.start, min(at.stop, real))
            return remote(r.y_v.at[table, at], r.got.at[table, at], r.send.at[table, half], r.recv.at[table, half], other)

        @pl.loop(0, 2 * t)
        def _(step):
            forward = (1 - section) * (1 - step // t) + section * (1 - step % 2)
            table = (1 - section) * (step % t) + section * (step // 2)

            @pl.when(forward == 1)
            def _():
                self.forward(r, table, section, relay, step)

            @pl.when(forward == 0)
            def _():
                self.backward(r, table, section, relay)

        @pl.when(section == 1)
        def _():
            for table in range(t):
                for half in range(2):
                    relay(table, half).wait_send()

    def forward(self, r, table, section, relay, step):
        c, w, ff, hd, real = self.cells, self.width, self.ff, self.hd, self.real
        stores, held = [], []

        def keep(src, dst, to_reload=False):
            copy = pltpu.make_async_copy(src, dst, r.out_sem.at[len(stores) + len(held)])
            if to_reload:
                held.append(copy)
                pl.when(section == 0)(copy.start)
            else:
                stores.append(copy)
                copy.start()

        for level in range(2):
            r.h_v[level, real:, :] = jnp.zeros((c - real, w), F32)

        def keep_column(k, at, value):
            column = lax.broadcasted_iota(jnp.int32, (1, r.stat_v.shape[2]), 1) == k
            r.stat_v[table, at, :] = jnp.where(column, value, r.stat_v[table, at, :])

        def norm(site):
            n, rstd = normalized(r.h_v[site % 2])
            r.n_v[site] = n
            keep(r.n_v.at[site], r.ns.at[table, site], True)
            keep_column(2 * HEADS + site, slice(None), rstd)
            put(r.a_v, (site,), n * r.gains[site])
            keep(r.a_v.at[:, site], r.as_.at[table, :, site])

        fill_biases(self.feat, self.rows, r.ctx[table], r.col_bias[1], 1)

        @pl.when(section == 0)
        def _():
            load = pltpu.make_async_copy(r.cells.at[table], r.dy_v.at[0:real], r.in_sem.at[0])
            pl.when(step > 0)(load.start)
            load.wait()
            for at, missing in self.missing(r, table):
                r.dy_v[at] = jnp.where(missing, r.embed[...], r.dy_v[at])
            self.set_out(r, r.dy_v, real)

        @pl.when(section == 1)
        def _():
            start(r.cot.at[table], r.dy_v.at[0:real], r.in_sem.at[1])
            for half in range(2):
                relay(table, half).wait_recv()
            self.set_out(r, r.got.at[table], real)

        self.by_rows(r, r.h_v.at[0])
        for site in range(2):
            norm(site)

            def project(j):
                at = slice(j * TILE, (j + 1) * TILE)
                return wide(parts(r.a_v, site), parts(r.win_v, site, slice(None), at), 1, 0)

            def keep_projected(j, out):
                if j < w // TILE:
                    out = out * (self.scale * LOG2E)
                put(r.qkv_v, (site, slice(None), slice(j * TILE, (j + 1) * TILE)), out)

            staggered([(j,) for j in range(3 * w // TILE)], project, keep_projected)
            keep(r.qkv_v.at[:, site], r.qkvs.at[table, :, site], True)

            def scores(head, queries, keys, bias):
                q = parts(r.qkv_v, site, queries, lanes(head, hd))
                k = parts(r.qkv_v, site, keys, lanes(HEADS + head, hd))
                return near(q, k)

            def softmax(head, queries, keys, bias, s):
                s = s + bias[...]
                top = jnp.max(s, axis=-1, keepdims=True)
                e = jnp.exp2(s - top)
                total = jnp.sum(e, axis=-1, keepdims=True)
                keep_column(site * HEADS + head, queries, top + jnp.log2(total))
                return split(e), 1.0 / total

            def blend(head, queries, keys, bias, state):
                e, inverse = state
                v = parts(r.qkv_v, site, keys, lanes(2 * HEADS + head, hd))
                put(r.o_v, (site, queries, lanes(head, hd)), side(e, v) * inverse)

            @pl.loop(0, HEADS // 2)
            def _(two):
                units = [(head, *unit) for head in (2 * two, 2 * two + 1) for unit in self.sites(r, site, 1)]
                staggered(units, scores, softmax, blend)

            keep(r.o_v.at[:, site], r.os.at[table, :, site])
            after = r.h_v[site] + wide(parts(r.o_v, site), parts(r.wout_v, site), 1, 0)
            if site == 0:
                self.set_out(r, after, c)
                self.by_features(r, r.h_v.at[1])
            else:
                r.h_v[0] = after
        r.lse_v[table] = r.stat_v[table].T[0 : 2 * HEADS]
        norm(2)

        @pl.when((section == 0) & (step == 0))
        def _():
            self.split_mlp(r)

        def feed_forward(cells):
            def up(at):
                return wide(parts(r.a_v, 2, cells), parts(r.wup_v, slice(None), at), 1, 0)

            def activate(at, z):
                g, gp = gelu_parts(z)
                put(r.g_v, (cells, at), g)
                r.gp_v[cells, at] = gp

            staggered([(slice(j, j + TILE),) for j in range(0, ff, TILE)], up, activate)
            r.y_v[table, cells] = r.h_v[0, cells] + wide(parts(r.g_v, cells), parts(r.wdown_v), 1, 0)

        @pl.when(section == 0)
        def _():
            for half, cells in enumerate(self.halves):
                feed_forward(cells)
                relay(table, half).start()

        @pl.when(section == 1)
        def _():
            feed_forward(slice(0, c))

        keep(r.g_v, r.gs.at[table])
        keep(r.gp_v, r.gps.at[table], True)
        keep(r.y_v.at[table, 0:real], r.out.at[table])
        for copy in stores:
            copy.wait()

        @pl.when(section == 0)
        def _():
            for copy in held:
                copy.wait()

    def backward(self, r, table, section, relay):
        c, w, ff, hd, real = self.cells, self.width, self.ff, self.hd, self.real
        stores = []

        def keep(src, dst):
            stores.append(start(src, dst, r.out_sem.at[len(stores)]))

        fill_biases(self.feat, self.rows, r.ctx[table], r.col_bias[0], 0)

        def through_norm(site, cells, da):
            n, k = r.n_v[site, cells], 2 * HEADS + site
            rstd = r.stat_v[table, cells, k : k + 1]
            r.small[site : site + 1, :] += jnp.sum(da * n, axis=0, keepdims=True)
            r.dy_v[cells] += norm_back(n, rstd, r.gains[site], da)

        def mlp_back(cells):
            put(r.dys_v, (cells,), r.dy_v[cells])

            def down(at):
                return wide(parts(r.dys_v, cells), parts(r.wdown_v, at), 1, 1)

            def deactivate(at, dg):
                put(r.g_v, (cells, at), dg * r.gp_v[cells, at])

            staggered([(slice(j, j + TILE),) for j in range(0, ff, TILE)], down, deactivate)
            through_norm(2, cells, wide(parts(r.g_v, cells), parts(r.wup_v), 1, 1))

        r.dy_v[real:, :] = jnp.zeros((c - real, w), F32)

        @pl.when(section == 0)
        def _():
            loads = [
                start(r.ns.at[table], r.n_v, r.in_sem.at[0]),
                start(r.qkvs.at[table], r.qkv_v, r.in_sem.at[1]),
                start(r.gps.at[table], r.gp_v, r.in_sem.at[2]),
            ]
            for copy in loads:
                copy.wait()
            for half, cells in enumerate(self.halves):
                relay(table, half).wait()
                came = slice(cells.start, min(cells.stop, real))
                r.dy_v[came] = r.got[table, came]
                mlp_back(cells)

        @pl.when(section == 1)
        def _():
            pltpu.make_async_copy(r.cot.at[table], r.dy_v.at[0:real], r.in_sem.at[1]).wait()
            mlp_back(slice(0, c))

        keep(r.dys_v, r.dys.at[table])
        keep(r.g_v, r.dzs.at[table])
        for site in (1, 0):
            if site == 0:
                self.set_out(r, r.dy_v, real)
                self.by_rows(r, r.dy_v)
            put(r.o_v, (site,), r.dy_v[...])
            keep(r.o_v.at[:, site], r.dhs.at[table, :, site])
            put(r.do_v, (), wide(parts(r.o_v, site), parts(r.wout_v, site), 1, 1))

            def part_of(which, head, span):
                return parts(r.qkv_v, site, span, lanes(which * HEADS + head, hd))

            def products(head, queries, keys, bias):
                do = parts(r.do_v, queries, lanes(head, hd))
                return near(part_of(1, head, keys), part_of(0, head, queries)), near(part_of(2, head, keys), do)

            def gradients(head, queries, keys, bias, state):
                s, dp = state
                p = jnp.exp2(s + bias[...] - r.lse_v[table, pl.ds(site * HEADS + head, 1), queries])
                ds = p * (dp - jnp.sum(p * dp, axis=0, keepdims=True))
                return split(p), split(ds)

            def back(head, queries, keys, bias, state):
                p, ds = state
                k = part_of(1, head, keys)
                r.dqkv_f[queries, lanes(head, hd)] = (wide(tuple(x.T for x in k), ds, 1, 0) * self.scale).T
                dk = side(ds, part_of(0, head, queries)) * LN2
                dv = side(p, parts(r.do_v, queries, lanes(head, hd)))
                for which, term in ((1, dk), (2, dv)):
                    at = lanes(which * HEADS + head, hd)
                    if keys.start == 0:
                        r.dqkv_f[keys, at] = term
                    else:
                        known = overlap - keys.start
                        if known:
                            r.dqkv_f[keys.start : overlap, at] += term[:known]
                        r.dqkv_f[overlap : keys.stop, at] = term[known:]

            overlap = self.sites(r, site, 0)[0][1].stop

            @pl.loop(0, HEADS // 2)
            def _(two):
                units = [(head, *unit) for head in (2 * two, 2 * two + 1) for unit in self.sites(r, site, 0)]
                staggered(units, products, gradients, back)

            for j in range(3 * w // TILE):
                at = slice(j * TILE, (j + 1) * TILE)
                put(r.qkv_v, (site, slice(None), at), r.dqkv_f[:, at])
            keep(r.qkv_v.at[:, site], r.dqkvs.at[table, :, site])
            da = wide(parts(r.qkv_v, site), parts(r.win_v, site), 1, 1)
            through_norm(site, slice(None), da)

        self.set_out(r, r.dy_v, real)
        self.by_features(r, r.dy_v)

        @pl.when(section == 0)
        def _():
            total = jnp.zeros((1, w), F32)
            for at, missing in self.missing(r, table):
                total += jnp.sum(jnp.where(missing, r.dy_v[at], 0.0), axis=0, keepdims=True)
                r.y_v[table, at] = jnp.where(missing, 0.0, r.dy_v[at])
            r.small[3:4, :] += total

        @pl.when(section == 1)
        def _():
            r.y_v[table] = r.dy_v[...]
            for half in range(2):
                relay(table, half).start()

        keep(r.y_v.at[table, 0:real], r.din.at[table])
        for copy in stores:
            copy.wait()


class GradSum:
    ROWS, COLS = 512, 256
    PARTS = 2
    SLACK = 2

    def __init__(self, count, tables, cells, width, ff):
        self.count, self.tables, self.cells, self.width = count, tables, cells, width
        self.rest = count // 4
        shapes = [("gs", None, "dys", None, "down", None, ff, width), ("as_", 2, "dzs", None, "up", None, width, ff)]
        for site in (1, 0):
            shapes.append(("as_", site, "dqkvs", site, "win", site, width, 3 * width))
            shapes.append(("os", site, "dhs", site, "wout", site, width, width))
        self.groups, at = [], 0
        for *which, k, n in shapes:
            blocks = (k // self.ROWS) * (n // self.COLS)
            self.groups.append((at, at + blocks, *which, n // self.COLS))
            at += blocks
        self.blocks = at
        self.chunks = self.blocks * self.PARTS
        self.hops = self.rest // 2 - 1
        self.sends = self.SLACK * (self.hops + 1) + 2
        self.rows = self.ROWS // self.PARTS
        self.ring = self.SLACK // self.PARTS + 2
        self.depth = (cells + 127) // 128 * 128

    def select(self, q, action):
        for group in self.groups:
            first, stop, *_, across = group

            @pl.when((q >= first) & (q < stop))
            def _():
                action(group, (q - first) // across, (q - first) % across)

    def starts_row(self, q):
        found = False
        for first, stop, *_, across in self.groups:
            found = found | ((q >= first) & (q < stop) & ((q - first) % across == 0))
        return found

    def load(self, r, q):
        slot = q % 2

        def action(group, i, j):
            _, _, left, left_site, right, right_site, *_ = group
            a, b = getattr(r, left), getattr(r, right)

            def at(t, part, site):
                return (t, part, slice(None)) if site is None else (t, part, site, slice(None))

            for t in range(self.tables):
                rows = slice(t * self.depth, t * self.depth + self.cells)
                for part in range(2):
                    sem = 2 * t + part
                    start(b.at[(*at(t, part, right_site), lanes(j, self.COLS))], r.b_v.at[slot, part, rows], r.b_sem.at[slot, sem])

                    @pl.when(j == 0)
                    def _():
                        start(a.at[(*at(t, part, left_site), lanes(i, self.ROWS))], r.a_v.at[part, rows], r.a_sem.at[sem])

        self.select(q, action)

    def each_operand(self):
        return [(2 * t + part, part, slice(t * self.depth, t * self.depth + self.cells)) for t in range(self.tables) for part in range(2)]

    def product(self, r, q):
        slot = q % 2

        @pl.when(self.starts_row(q))
        def _():
            for sem, part, rows in self.each_operand():
                a = r.a_v.at[part, rows]
                pltpu.make_async_copy(a, a, r.a_sem.at[sem]).wait()
            for part in range(2):
                r.left_v[part] = r.a_v[part].T

        for sem, part, rows in self.each_operand():
            b = r.b_v.at[slot, part, rows]
            pltpu.make_async_copy(b, b, r.b_sem.at[slot, sem]).wait()

        @pl.when(q + 1 < self.blocks)
        def _():
            self.load(r, q + 1)

        r.products[q % self.ring] = side(parts(r.left_v), parts(r.b_v.at[slot]))

    def kernel(self, r):
        rest, rows, ring = self.rest, self.rows, self.ring
        half = rows // 2
        quart = half // 2
        me, section = lax.axis_index("dp"), lax.axis_index("section")
        core, pair, place = me % 2, me // 2 % 2, me // 4
        sibling, neighbour = {"dp": me + 1 - 2 * core}, {"dp": me + 2 - 4 * pair}
        far = place // (rest // 2)
        along = (1 - far) * place + far * (rest - 1 - place)
        inward, outward = {"dp": me + 4 - 8 * far}, {"dp": me - 4 + 8 * far}
        hops = self.hops

        def peer(j):
            return {"dp": lax.rem(place + j, rest) * 4 + me % 4}

        def span(at, size):
            return pl.ds(pl.multiple_of(at, size), size)

        mine = core * half
        own, other = pair * quart, (1 - pair) * quart
        keeps, gives = far * quart, (1 - far) * quart

        barrier = pltpu.get_barrier_semaphore()

        def greet(device):
            pl.semaphore_signal(barrier, inc=1, device_id=device, device_id_type=pl.DeviceIdType.MESH)

        greet(sibling)
        greet(neighbour)

        @pl.loop(1, rest)
        def _(j):
            greet(peer(j))

        for t in range(self.tables):
            pad = slice(t * self.depth + self.cells, (t + 1) * self.depth)
            for part in range(2):
                r.a_v[part, pad] = jnp.zeros_like(r.a_v[part, pad])
                for slot in range(2):
                    r.b_v[slot, part, pad] = jnp.zeros_like(r.b_v[slot, part, pad])
        self.load(r, 0)
        passing = [
            start(getattr(r, f"table{i}"), getattr(r, f"out{i}"), r.table_sem.at[i]) for i in range(self.passed)
        ]

        @pl.when(section == 1)
        def _():
            greet({"section": 0})

        pl.semaphore_wait(barrier, rest + 2 - section)

        def copy(which, c, src, dst, device):
            return remote(src, dst, r.send.at[which, c % self.sends], r.recv.at[which, c], device)

        def product_rows(c, which):
            return c // self.PARTS % ring, span(c % self.PARTS * rows + which * half, half)

        def halve(c):
            return copy(0, c, r.products.at[product_rows(c, 1 - core)], r.sums.at[c], sibling)

        def gather_half(c):
            at = r.full.at[c, span(mine, half)]
            return copy(1, c, at, at, sibling)

        def quarter(c):
            return copy(2, c, r.sums.at[c, span(other, quart)], r.got_near.at[c], neighbour)

        def gather_quarter(c):
            at = r.full.at[c, span(mine + own, quart)]
            return copy(3, c, at, at, neighbour)

        def add_up(c):
            return copy(2, c, r.sums.at[c, span(keeps, quart)], r.got_near.at[c], neighbour)

        def come(kind, c):
            if kind == 0:
                return copy(4, c, r.sums.at[c, span(own, quart)], r.got_in.at[c, 0:quart], inward)
            return copy(4, c, r.sums.at[c], r.got_in.at[c], inward)

        def meet(kind, c):
            at = span(own if kind == 0 else gives, quart)
            return copy(5, c, r.sums.at[c, at], r.got_mid.at[c], inward)

        def give_back(c):
            at = r.full.at[c, span(mine + keeps, quart)]
            return copy(6, c, at, at, inward)

        def leave(kind, c):
            at = r.full.at[c, span(mine + own, quart) if kind == 0 else span(mine, half)]
            return copy(7, c, at, at, outward)

        def reduced(kind, c, h, at_end):
            @pl.when((along == h) & (h < hops))
            def _():
                come(kind, c).start()

            @pl.when((along == h) & (h == hops))
            def _():
                at_end(c)

        def come_hop(kind, c, h):
            @pl.when(along == h)
            def _():
                come(kind, c).wait_send()

            @pl.when(along == h + 1)
            def _():
                come(kind, c).wait_recv()
                if kind == 0:
                    r.sums[c, span(own, quart)] += r.got_in[c, 0:quart]
                else:
                    r.sums[c] += r.got_in[c]

            reduced(kind, c, h + 1, lambda c: meet(kind, c).start())

        def pass_out(kind, c, h):
            @pl.when((along == h) & (h > 0))
            def _():
                leave(kind, c).start()

            if kind == 0:

                @pl.when(along == h)
                def _():
                    gather_quarter(c).start()

        def leave_hop(kind, c, g):
            h = hops - g

            @pl.when(along == h)
            def _():
                leave(kind, c).wait_send()

            @pl.when(along == h - 1)
            def _():
                leave(kind, c).wait_recv()

            pass_out(kind, c, h - 1)

        def after_halve(c):
            halve(c).wait()
            r.sums[c] += r.products[product_rows(c, core)]

            @pl.when(core == 0)
            def _():
                quarter(c).start()

            @pl.when(core == 1)
            def _():
                reduced(1, c, 0, lambda c: meet(1, c).start())

        def after_quarter(c):
            quarter(c).wait()
            r.sums[c, span(own, quart)] += r.got_near[c]
            reduced(0, c, 0, lambda c: meet(0, c).start())

        def after_meet(kind, c):
            @pl.when(along == hops)
            def _():
                meet(kind, c).wait()
                if kind == 0:
                    r.full[c, span(mine + own, quart)] = r.sums[c, span(own, quart)] + r.got_mid[c]
                else:
                    r.sums[c, span(keeps, quart)] += r.got_mid[c]
                    add_up(c).start()

            if kind == 0:
                pass_out(0, c, hops)

        def after_add_up(c):
            @pl.when(along == hops)
            def _():
                add_up(c).wait()
                r.full[c, span(mine + keeps, quart)] = r.sums[c, span(keeps, quart)] + r.got_near[c]
                give_back(c).start()

        def after_give_back(c):
            @pl.when(along == hops)
            def _():
                give_back(c).wait()

            pass_out(1, c, hops)

        def gathered(c):
            @pl.when(core == 0)
            def _():
                gather_quarter(c).wait()

            gather_half(c).start()

        def after_gather_half(c):
            gather_half(c).wait()

        def small_copy(k, device):
            return remote(r.small_v.at[k], r.got_small.at[k], r.small_send.at[k], r.small_recv.at[k], device)

        def small_rest(j):
            dst = r.got_small.at[2 + j]
            return remote(r.small_v.at[3], dst, r.small_send.at[2 + j], r.small_recv.at[2 + j], peer(j))

        def small_step(step):
            @pl.when(step == 2)
            def _():
                r.small_v[1] = r.small[...]
                small_copy(1, sibling).start()

            @pl.when(step == 4)
            def _():
                small_copy(1, sibling).wait()
                r.small_v[2] = r.small_v[1] + r.got_small[1]
                small_copy(2, neighbour).start()

            @pl.when(step == 6)
            def _():
                small_copy(2, neighbour).wait()
                r.small_v[3] = r.small_v[2] + r.got_small[2]
                pl.loop(1, rest)(lambda j: small_rest(j).start())

            @pl.when(step == 8)
            def _():
                pl.loop(1, rest)(lambda j: small_rest(j).wait())
                total = r.small_v[3]
                for j in range(1, rest):
                    total += r.got_small[2 + j]
                r.small_v[0] = total

                @pl.when(section == 0)
                def _():
                    small_copy(0, {"section": 1}).start()

        last = 2 * hops + 5

        def delay(time):
            return self.SLACK * time - (1 if time < last else 2)

        @pl.loop(0, self.chunks + delay(last))
        def _(step):
            def stage(time, action):
                c = step - (delay(time) if isinstance(time, int) else self.SLACK * time - 1)

                @pl.when((c >= 0) & (c < self.chunks))
                def _():
                    action(c)

            stage(last, after_gather_half)

            @pl.when(core == 0)
            def _():
                over(hops, lambda g: stage(hops + 4 + g, lambda c: leave_hop(0, c, g)))
                stage(hops + 3, lambda c: after_meet(0, c))
                over(hops, lambda h: stage(3 + h, lambda c: come_hop(0, c, h)))
                stage(2, after_quarter)

            @pl.when(core == 1)
            def _():
                over(hops, lambda g: stage(hops + 5 + g, lambda c: leave_hop(1, c, g)))
                stage(hops + 4, after_give_back)
                stage(hops + 3, after_add_up)
                stage(hops + 2, lambda c: after_meet(1, c))
                over(hops, lambda h: stage(2 + h, lambda c: come_hop(1, c, h)))

            stage(last - 1, gathered)
            stage(1, after_halve)
            small_step(step)

            @pl.when(step < self.chunks)
            def _():
                @pl.when(step % self.PARTS == 0)
                def _():
                    self.product(r, step // self.PARTS)

                halve(step).start()

        for load in passing:
            load.wait()
        r.small_out[...] = r.small_v[0]

        @pl.when(section == 0)
        def _():
            small_copy(0, {"section": 1}).wait_send()

        @pl.when(section == 1)
        def _():
            small_copy(0, {"section": 1}).wait_recv()
            r.small_out[3:4] = r.got_small[0, 3:4]

    def __call__(self, operands, small, tables):
        t, width, deep = self.tables, self.width, self.tables * self.depth
        rest, chunks, rows, ring, cols = self.rest, self.chunks, self.rows, self.ring, self.COLS
        outs = {"full": VMEM((chunks, rows, cols), F32), "small_out": f32(8, width)}
        outs |= {f"out{i}": VMEM(a.shape, F32) for i, a in enumerate(tables)}
        scratch = {
            "products": VMEM((ring, self.ROWS, cols), F32),
            "sums": VMEM((chunks, rows // 2, cols), F32),
            "got_near": VMEM((chunks, rows // 4, cols), F32),
            "got_mid": VMEM((chunks, rows // 4, cols), F32),
            "got_in": VMEM((chunks, rows // 2, cols), F32),
            "a_v": VMEM((2, deep, self.ROWS), BF16),
            "left_v": VMEM((2, self.ROWS, deep), BF16),
            "b_v": VMEM((2, 2, deep, cols), BF16),
            "small_v": VMEM((4, 8, width), F32),
            "got_small": VMEM((2 + rest, 8, width), F32),
            "a_sem": dma(2 * t),
            "b_sem": dma(2, 2 * t),
            "send": dma(8, self.sends),
            "recv": dma(8, chunks),
            "small_send": dma(2 + rest),
            "small_recv": dma(2 + rest),
        }
        ins = {n: (a, ANY) for n, a in operands.items()} | {"small": (small, VMEM)}
        ins |= {f"table{i}": (a, ANY) for i, a in enumerate(tables)}
        scratch["table_sem"] = dma(len(tables))
        self.passed = len(tables)
        outs = {n: (s, VMEM) for n, s in outs.items()}
        return call("weight_gradient_sum", self.kernel, 0, ins, outs, scratch, SUM_VMEM_LIMIT)

    def results(self, sums, small, tables, ff):
        width = self.width

        def here(a):
            return (pltpu.with_memory_space_constraint(a, pltpu.VMEM), VMEM)

        ins = {"full": here(sums), "small": (small, VMEM)} | {f"table{i}": here(a) for i, a in enumerate(tables)}
        outs = {
            "win": f32(2, width, 3 * width),
            "wout": f32(2, width, width),
            "up": f32(width, ff),
            "down": f32(ff, width),
        } | {f"out{i}": f32(*a.shape) for i, a in enumerate(tables)}
        outs = {n: (s, ANY) for n, s in outs.items()}
        outs |= {"gain": (f32(3, 1, width), VMEM), "missing": (f32(1, width), VMEM)}
        scratch = {"sem": dma(self.chunks), "out_sem": dma(len(tables))}

        def body(r):
            stores = [
                start(getattr(r, f"table{i}"), getattr(r, f"out{i}"), r.out_sem.at[i]) for i in range(len(tables))
            ]
            for first, stop, *_, out, site, across in self.groups:
                dst = getattr(r, out) if site is None else getattr(r, out).at[site]
                for c in range(first * self.PARTS, stop * self.PARTS):
                    q = c // self.PARTS - first
                    row = q // across * self.ROWS + c % self.PARTS * self.rows
                    at = (slice(row, row + self.rows), slice(q % across * self.COLS, (q % across + 1) * self.COLS))
                    stores.append(start(r.full.at[c], dst.at[at], r.sem.at[c]))
            for k in range(3):
                r.gain[k] = r.small[k : k + 1, :]
            r.missing[...] = r.small[3:4, :]
            for copy in stores:
                copy.wait()

        return call("results", body, None, ins, outs, scratch, SUM_VMEM_LIMIT)


def local(
    cells,
    missing_mask,
    missing_embed,
    context_rows,
    norm_gains,
    attn_in,
    attn_out,
    mlp_up,
    mlp_down,
    cotangent,
):
    tables, rows, feat, width = cells.shape
    ff = mlp_up.shape[2]
    layers = Layers(tables, rows, feat, width, ff)

    def flat(tables_of_cells):
        return jnp.swapaxes(tables_of_cells, 1, 2).reshape(tables, rows * feat, -1)

    def unflat(cells_of_tables):
        return jnp.swapaxes(cells_of_tables.reshape(tables, feat, rows, width), 1, 2)[None]

    weights = (attn_in[0], attn_out[0], mlp_up[0], mlp_down[0])
    gains = jnp.swapaxes(norm_gains, 0, 1)
    done = layers(flat(cells), missing_mask, missing_embed[None], context_rows, gains, weights, flat(cotangent))
    operands = {n: done[n] for n in ("as_", "os", "gs", "dys", "dzs", "dhs", "dqkvs")}
    grad_sum = GradSum(lax.axis_size("dp"), tables, layers.cells, width, ff)
    sums = grad_sum(operands, done["small"], (done["out"], done["din"]))
    got = grad_sum.results(sums["full"], sums["small_out"], (sums["out0"], sums["out1"]), ff)
    return (
        unflat(got["out0"]),
        unflat(got["out1"]),
        jnp.swapaxes(got["gain"], 0, 1),
        got["win"][None],
        got["wout"][None],
        got["up"][None],
        got["down"][None],
        got["missing"][0],
    )


def solution(mesh):
    in_specs = (
        P("dp", None, None, None),
        P("dp", None, None),
        P(),
        P("dp"),
        P("section", None, None),
        P("section", None, None, None),
        P("section", None, None, None),
        P("section", None, None),
        P("section", None, None),
        P("dp", None, None, None),
    )
    out_specs = (
        P("section", "dp", None, None, None),
        P("section", "dp", None, None, None),
        P("section", None, None),
        P("section", None, None, None),
        P("section", None, None, None),
        P("section", None, None),
        P("section", None, None),
        P(),
    )
    return jax.shard_map(local, mesh=mesh, in_specs=in_specs, out_specs=out_specs, check_vma=False)
```

```python
import functools
from types import SimpleNamespace

import jax
import jax.numpy as jnp
from jax import lax
from jax.experimental import pallas as pl
from jax.experimental.pallas import tpu as pltpu
from jax.sharding import PartitionSpec as P

HEADS = 4
EPSILON = 1e-05
NEG = -1e30
INV_SQRT2PI = 0.3989422804014327
LOG2E = 1.4426950408889634
LN2 = 0.6931471805599453
ERFC_P = 0.33
ERFC_C = (0.1863578482, 0.1829552331, 0.2012284886, 0.0472047191, 0.4085317677, -0.3511862269, 0.4602596132, -0.1353514118)
VMEM_LIMIT = 62 * 1024 * 1024
SUM_VMEM_LIMIT = 38 * 1024 * 1024
TILE = 512
F32, BF16 = jnp.float32, jnp.bfloat16


def dot(a, b, contract=((1,), (0,))):
    return lax.dot_general(a, b, (contract, ((), ())), preferred_element_type=F32)


def split(v):
    hi = v.astype(BF16)
    return hi, (v - hi.astype(F32)).astype(BF16)


def put(ref, index, v):
    hi, lo = split(v)
    ref[(0, *index)] = hi
    ref[(1, *index)] = lo


def parts(ref, *index):
    return ref[(0, *index)], ref[(1, *index)]


def wide(a, b, ca, cb):
    (ah, al), (bh, bl) = a, b
    if ah.shape[ca] < 512:
        return dot(jnp.concatenate([ah, ah, al], ca), jnp.concatenate([bh, bl, bh], cb), ((ca,), (cb,)))
    rows = ah.shape[1 - ca]
    both = dot(jnp.concatenate([ah, al], 1 - ca), bh, ((ca,), (cb,)))
    return both[:rows] + both[rows:] + dot(ah, bl, ((ca,), (cb,)))


def near(a, b):
    (ah, al), (bh, bl) = a, b
    return dot(jnp.concatenate([ah, ah, al, al], 1), jnp.concatenate([bh, bl, bh, bl], 1), ((1,), (1,)))


def side(a, b):
    (ah, al), (bh, bl) = a, b
    width = bh.shape[1]
    both = dot(ah, jnp.concatenate([bh, bl], 1))
    return both[:, :width] + both[:, width:] + dot(al, bh)


def normalized(h):
    centred = h - jnp.mean(h, axis=-1, keepdims=True)
    rstd = lax.rsqrt(jnp.mean(centred * centred, axis=-1, keepdims=True) + EPSILON)
    return centred * rstd, rstd


def norm_back(n, rstd, gain, da):
    dn = da * gain
    return rstd * (dn - jnp.mean(dn, axis=-1, keepdims=True) - n * jnp.mean(dn * n, axis=-1, keepdims=True))


def cell_ids(start, count, inner, along):
    shape = (count, 1) if along == 0 else (1, count)
    at = lax.broadcasted_iota(jnp.int32, shape, along) + start
    outer = lax.shift_right_logical(at * ((1 << 20) // inner + 1), 20)
    return outer, at - outer * inner


def up16(n):
    return (n + 15) // 16 * 16


def blocks(outer, inner):
    cells = up16(outer * inner)
    half = up16((outer + 1) // 2 * inner)
    first_keys = min(cells, up16((((half - 1) // inner) + 1) * inner))
    second_keys = ((half // inner) * inner) // 16 * 16
    return ((slice(0, half), slice(0, first_keys)), (slice(half, cells), slice(second_keys, cells)))


def when(cond):
    if isinstance(cond, bool):
        return (lambda action: action()) if cond else (lambda action: None)
    return pl.when(cond)


def over(count, action):
    if count <= 4:
        for i in range(count):
            action(i)
    else:
        pl.loop(0, count)(action)


def staggered(units, *steps):
    state = [None] * len(units)
    for i in range(len(units) + 1):
        if i < len(units):
            state[i] = steps[0](*units[i])
        if i > 0:
            for step in steps[1:]:
                state[i - 1] = step(*units[i - 1], state[i - 1])


def lanes(j, width):
    return pl.ds(pl.multiple_of(j * width, width), width)


def start(src, dst, sem):
    copy = pltpu.make_async_copy(src, dst, sem)
    copy.start()
    return copy


def fill_biases(outer, inner, limit, refs, keys_along):
    for (queries, keys), ref in zip(blocks(outer, inner), refs):
        q_outer, _ = cell_ids(queries.start, queries.stop - queries.start, inner, 1 - keys_along)
        k_outer, k_inner = cell_ids(keys.start, keys.stop - keys.start, inner, keys_along)
        ref[...] = jnp.where((q_outer == k_outer) & (k_inner < limit), 0.0, NEG)


def gelu_parts(z):
    size = jnp.abs(z)
    below = 1.0 + (ERFC_P * 0.7071067811865476) * size
    t = pl.reciprocal(below, approx=True)
    t = t * (2.0 - below * t)
    series = jnp.full_like(t, ERFC_C[-1])
    for c in ERFC_C[-2::-1]:
        series = series * t + c
    bell = jnp.exp(-0.5 * z * z)
    tail = 0.5 * (series * t) * bell
    phi = jnp.where(z >= 0.0, 1.0 - tail, tail)
    return z * phi, phi + z * (INV_SQRT2PI * bell)


SMEM, VMEM, ANY = pltpu.SMEM, pltpu.VMEM, pl.ANY


def f32(*shape):
    return jax.ShapeDtypeStruct(shape, F32)


def b16(*shape):
    return jax.ShapeDtypeStruct(shape, BF16)


def dma(*shape):
    return pltpu.SemaphoreType.DMA(shape)


def remote(src, dst, send, recv, device):
    return pltpu.make_async_remote_copy(
        src_ref=src, dst_ref=dst, send_sem=send, recv_sem=recv, device_id=device, device_id_type=pl.DeviceIdType.MESH
    )


def call(name, body, collective_id, ins, outs, scratch, limit):
    names = [*ins, *outs, *scratch]

    def kernel(*refs):
        body(SimpleNamespace(**dict(zip(names, refs))))

    results = pl.pallas_call(
        kernel,
        out_shape=[t for t, _ in outs.values()],
        in_specs=[pl.BlockSpec(memory_space=s) for _, s in ins.values()],
        out_specs=[pl.BlockSpec(memory_space=s) for _, s in outs.values()],
        scratch_shapes=list(scratch.values()),
        compiler_params=pltpu.CompilerParams(
            vmem_limit_bytes=limit, collective_id=collective_id, has_side_effects=collective_id is not None
        ),
        name=name,
    )(*(a for a, _ in ins.values()))
    return dict(zip(outs, results))


class Layers:
    SPLIT_ROWS = 64

    def __init__(self, tables, rows, feat, width, ff):
        self.tables, self.rows, self.feat, self.width, self.ff = tables, rows, feat, width, ff
        self.real, self.cells = rows * feat, up16(rows * feat)
        self.hd = width // HEADS
        self.scale = self.hd ** (-0.5)

    def sites(self, r, site, keys_along):
        if site == 1:
            ranges, biases = blocks(self.feat, self.rows), r.col_bias
        else:
            ranges, biases = blocks(self.rows, self.feat), r.row_bias
        return [(*unit, bias) for unit, bias in zip(ranges, biases[keys_along])]

    def missing(self, r, table):
        mask = r.mask[table]
        return [(slice(f * self.rows, (f + 1) * self.rows), mask[:, f : f + 1] == 1) for f in range(self.feat)]

    def set_out(self, r, src, count):
        for k in range(self.width // 128):
            r.perm_v[k, 0:count] = src[0:count, k * 128 : (k + 1) * 128]

    def by_rows(self, r, dst):
        for row in range(self.rows):
            for k in range(self.width // 128):
                at = (slice(row * self.feat, (row + 1) * self.feat), slice(k * 128, (k + 1) * 128))
                dst[at] = r.perm_v[k, pl.ds(row, self.feat, stride=self.rows), :]

    def by_features(self, r, dst):
        for feat in range(self.feat):
            for k in range(self.width // 128):
                at = (slice(feat * self.rows, (feat + 1) * self.rows), slice(k * 128, (k + 1) * 128))
                dst[at] = r.perm_v[k, pl.ds(feat, self.rows, stride=self.feat), :]

    def __call__(self, cells, mask, embed, context, gains, weights, cotangent):
        t, c, w, ff, real = self.tables, self.cells, self.width, self.ff, self.real
        rows, feat = self.rows, self.feat
        ins = {
            "cells": (cells, ANY),
            "mask": (mask, VMEM),
            "embed": (embed, VMEM),
            "ctx": (context, SMEM),
            "gains": (gains, VMEM),
            "cot": (cotangent, ANY),
        }
        names = ("win", "wout", "wup", "wdown")
        ins |= {n: (a, ANY) for n, a in zip(names, weights)}
        outs = {
            "out": f32(t, real, w),
            "din": f32(t, real, w),
            "ns": f32(t, 3, c, w),
            "qkvs": b16(t, 2, 2, c, 3 * w),
            "gps": f32(t, c, ff),
            "as_": b16(t, 2, 3, c, w),
            "os": b16(t, 2, 2, c, w),
            "gs": b16(t, 2, c, ff),
            "dys": b16(t, 2, c, w),
            "dzs": b16(t, 2, c, ff),
            "dhs": b16(t, 2, 2, c, w),
            "dqkvs": b16(t, 2, 2, c, 3 * w),
        }
        outs = {n: (s, ANY) for n, s in outs.items()} | {"small": (f32(8, w), VMEM)}
        scratch = {n + "_v": VMEM((2, *a.shape), BF16) for n, a in zip(names, weights)}
        scratch |= {
            "h_v": VMEM((2, c, w), F32),
            "n_v": VMEM((3, c, w), F32),
            "qkv_v": VMEM((2, 2, c, 3 * w), BF16),
            "o_v": VMEM((2, 2, c, w), BF16),
            "gp_v": VMEM((c, ff), F32),
            "g_v": VMEM((2, c, ff), BF16),
            "a_v": VMEM((2, 3, c, w), BF16),
            "y_v": VMEM((t, c, w), F32),
            "dqkv_f": VMEM((c, 3 * w), F32),
            "perm_v": VMEM((w // 128, c, 128), F32),
            "dys_v": VMEM((2, c, w), BF16),
            "dy_v": VMEM((c, w), F32),
            "do_v": VMEM((2, c, w), BF16),
            "got": VMEM((t, real, w), F32),
            "stat_v": VMEM((t, c, 128), F32),
            "lse_v": VMEM((t, 2 * HEADS, c), F32),
            "spare_v": VMEM((w // 2, w), F32),
            "raw_sem": pltpu.SemaphoreType.DMA((20,)),
            "in_sem": pltpu.SemaphoreType.DMA((4,)),
            "out_sem": pltpu.SemaphoreType.DMA((18,)),
            "send": pltpu.SemaphoreType.DMA((t, 2)),
            "recv": pltpu.SemaphoreType.DMA((t, 2)),
        }
        for name, ranges in (("col_bias", blocks(feat, rows)), ("row_bias", blocks(rows, feat))):
            for i, (queries, keys) in enumerate(ranges):
                shape = (queries.stop - queries.start, keys.stop - keys.start)
                scratch[f"{name}0{i}"] = VMEM(shape[::-1], F32)
                scratch[f"{name}1{i}"] = VMEM(shape, F32)

        def body(r):
            for n in ("col_bias", "row_bias"):
                setattr(r, n, [[getattr(r, f"{n}{along}{i}") for i in range(2)] for along in range(2)])
            self.kernel(r)

        return call("layers", body, 1, ins, outs, scratch, VMEM_LIMIT)

    attention_pieces = 8

    def raw_pieces(self, r):
        w, ff = self.width, self.ff
        half, wide_in, step = w // 2, 3 * w, self.SPLIT_ROWS
        top, rest, whole = slice(0, half), slice(half, w), slice(None)
        big, bigger = r.dqkv_f.at[top], r.gp_v.at[top]
        pieces = [
            (r.win.at[0, top], big, r.win_v, (0,), 0, whole, 0),
            (r.win.at[0, rest], bigger.at[:, 0:wide_in], r.win_v, (0,), half, whole, 1),
            (r.wout.at[0, top], r.h_v.at[0, top], r.wout_v, (0,), 0, whole, 2),
            (r.wout.at[0, rest], r.h_v.at[1, top], r.wout_v, (0,), half, whole, 3),
            (r.win.at[1, top], big, r.win_v, (1,), 0, whole, 0),
            (r.win.at[1, rest], bigger.at[:, 0:wide_in], r.win_v, (1,), half, whole, 1),
            (r.wout.at[1, top], r.n_v.at[0, top], r.wout_v, (1,), 0, whole, 4),
            (r.wout.at[1, rest], r.spare_v, r.wout_v, (1,), half, whole, 5),
        ]
        assert len(pieces) == self.attention_pieces
        pieces.append((r.wup.at[top], bigger, r.wup_v, (), 0, whole, 1))
        pieces.append((r.wup.at[rest, 0:wide_in], big, r.wup_v, (), half, slice(0, wide_in), 0))
        pieces.append((r.wup.at[rest, wide_in:ff], r.spare_v, r.wup_v, (), half, slice(wide_in, ff), 5))
        high = self.cells // step * step
        buffers = [r.y_v.at[0, 0:high], r.y_v.at[1, 0:high]]
        low = slice(half, half + (self.cells - half) // step * step)
        for k in range(3):
            buffers.append(r.dqkv_f.at[low, k * w : (k + 1) * w])
        for k in range(ff // w):
            buffers.append(r.gp_v.at[low, k * w : (k + 1) * w])
        at = 0
        for i, buffer in enumerate(buffers):
            size = min(buffer.shape[0], ff - at)
            if size:
                pieces.append((r.wdown.at[at : at + size], buffer.at[0:size], r.wdown_v, (), at, whole, 6 + i))
            at += size
        assert at == ff
        return pieces

    def raw_copy(self, r, i):
        src, buffer = self.raw_pieces(r)[i][:2]
        return pltpu.make_async_copy(src, buffer, r.raw_sem.at[i])

    def split_piece(self, r, i):
        pieces = self.raw_pieces(r)
        _, buffer, v, lead, at, columns, user = pieces[i]
        step = self.SPLIT_ROWS
        self.raw_copy(r, i).wait()

        @pl.loop(0, buffer.shape[0] // step)
        def _(j):
            src = pl.ds(pl.multiple_of(j * step, step), step)
            dst = pl.ds(pl.multiple_of(at + j * step, step), step)
            put(v, (*lead, dst, columns), buffer[src])

        later = [k for k in range(i + 1, len(pieces)) if pieces[k][-1] == user]
        if later:
            self.raw_copy(r, later[0]).start()

    def start_raw(self, r, mlp):
        seen = set()
        for i, piece in enumerate(self.raw_pieces(r)):
            if piece[-1] not in seen and mlp == (i >= self.attention_pieces):
                self.raw_copy(r, i).start()
            seen.add(piece[-1])

    def split_attention(self, r):
        self.start_raw(r, False)
        for i in range(self.attention_pieces):
            self.split_piece(r, i)
        self.start_raw(r, True)

    def split_mlp(self, r):
        for i in range(self.attention_pieces, len(self.raw_pieces(r))):
            self.split_piece(r, i)

    def kernel(self, r):
        t, real, c = self.tables, self.real, self.cells
        section = lax.axis_index("section")
        other = {"section": 1 - section}
        barrier = pltpu.get_barrier_semaphore()
        pl.semaphore_signal(barrier, inc=1, device_id=other, device_id_type=pl.DeviceIdType.MESH)

        @pl.when(section == 0)
        def _():
            start(r.cells.at[0], r.dy_v.at[0:real], r.in_sem.at[0])

        self.split_attention(r)

        @pl.when(section == 1)
        def _():
            self.split_mlp(r)

        for along in range(2):
            fill_biases(self.rows, self.feat, self.feat, r.row_bias[along], along)
        r.small[...] = jnp.zeros_like(r.small)
        pl.semaphore_wait(barrier, 1)

        def relay(table, half):
            at = slice(half * self.width // 2, (half + 1) * self.width // 2)
            src, dst = r.y_v.at[table, 0:real, at], r.got.at[table, :, at]
            return remote(src, dst, r.send.at[table, half], r.recv.at[table, half], other)

        @pl.loop(0, 2 * t)
        def _(step):
            forward = (1 - section) * (1 - step // t) + section * (1 - step % 2)
            table = (1 - section) * (step % t) + section * (step // 2)

            @pl.when(forward == 1)
            def _():
                self.forward(r, table, section, relay, step)

            @pl.when(forward == 0)
            def _():
                self.backward(r, table, section, relay)

        @pl.when(section == 1)
        def _():
            for table in range(t):
                for half in range(2):
                    relay(table, half).wait_send()

    def forward(self, r, table, section, relay, step):
        c, w, ff, hd, real = self.cells, self.width, self.ff, self.hd, self.real
        stores, held = [], []

        def keep(src, dst, to_reload=False):
            copy = pltpu.make_async_copy(src, dst, r.out_sem.at[len(stores) + len(held)])
            if to_reload:
                held.append(copy)
                pl.when(section == 0)(copy.start)
            else:
                stores.append(copy)
                copy.start()

        for level in range(2):
            r.h_v[level, real:, :] = jnp.zeros((c - real, w), F32)

        def keep_column(k, at, value):
            column = lax.broadcasted_iota(jnp.int32, (1, r.stat_v.shape[2]), 1) == k
            r.stat_v[table, at, :] = jnp.where(column, value, r.stat_v[table, at, :])

        def norm(site):
            n, rstd = normalized(r.h_v[site % 2])
            r.n_v[site] = n
            keep(r.n_v.at[site], r.ns.at[table, site], True)
            keep_column(2 * HEADS + site, slice(None), rstd)
            put(r.a_v, (site,), n * r.gains[site])
            keep(r.a_v.at[:, site], r.as_.at[table, :, site])

        fill_biases(self.feat, self.rows, r.ctx[table], r.col_bias[1], 1)

        @pl.when(section == 0)
        def _():
            load = pltpu.make_async_copy(r.cells.at[table], r.dy_v.at[0:real], r.in_sem.at[0])
            pl.when(step > 0)(load.start)
            load.wait()
            for at, missing in self.missing(r, table):
                r.dy_v[at] = jnp.where(missing, r.embed[...], r.dy_v[at])
            self.set_out(r, r.dy_v, real)

        @pl.when(section == 1)
        def _():
            start(r.cot.at[table], r.dy_v.at[0:real], r.in_sem.at[1])
            for half in range(2):
                relay(table, half).wait_recv()
            self.set_out(r, r.got.at[table], real)

        self.by_rows(r, r.h_v.at[0])
        for site in range(2):
            norm(site)

            def project(j):
                at = slice(j * TILE, (j + 1) * TILE)
                return wide(parts(r.a_v, site), parts(r.win_v, site, slice(None), at), 1, 0)

            def keep_projected(j, out):
                if j < w // TILE:
                    out = out * (self.scale * LOG2E)
                put(r.qkv_v, (site, slice(None), slice(j * TILE, (j + 1) * TILE)), out)

            staggered([(j,) for j in range(3 * w // TILE)], project, keep_projected)
            keep(r.qkv_v.at[:, site], r.qkvs.at[table, :, site], True)

            def scores(head, queries, keys, bias):
                q = parts(r.qkv_v, site, queries, lanes(head, hd))
                k = parts(r.qkv_v, site, keys, lanes(HEADS + head, hd))
                return near(q, k)

            def softmax(head, queries, keys, bias, s):
                s = s + bias[...]
                top = jnp.max(s, axis=-1, keepdims=True)
                e = jnp.exp2(s - top)
                total = jnp.sum(e, axis=-1, keepdims=True)
                keep_column(site * HEADS + head, queries, top + jnp.log2(total))
                return split(e), 1.0 / total

            def blend(head, queries, keys, bias, state):
                e, inverse = state
                v = parts(r.qkv_v, site, keys, lanes(2 * HEADS + head, hd))
                put(r.o_v, (site, queries, lanes(head, hd)), side(e, v) * inverse)

            @pl.loop(0, HEADS // 2)
            def _(two):
                units = [(head, *unit) for head in (2 * two, 2 * two + 1) for unit in self.sites(r, site, 1)]
                staggered(units, scores, softmax, blend)

            keep(r.o_v.at[:, site], r.os.at[table, :, site])
            after = r.h_v[site] + wide(parts(r.o_v, site), parts(r.wout_v, site), 1, 0)
            if site == 0:
                self.set_out(r, after, c)
                self.by_features(r, r.h_v.at[1])
            else:
                r.h_v[0] = after
        r.lse_v[table] = r.stat_v[table].T[0 : 2 * HEADS]
        norm(2)

        @pl.when((section == 0) & (step == 0))
        def _():
            self.split_mlp(r)

        def up(j):
            return wide(parts(r.a_v, 2), parts(r.wup_v, slice(None), slice(j * TILE, (j + 1) * TILE)), 1, 0)

        tiles = ff // TILE
        z = up(0)
        for j in range(tiles):
            at = slice(j * TILE, (j + 1) * TILE)
            following = up(j + 1) if j + 1 < tiles else None
            g, gp = gelu_parts(z)
            put(r.g_v, (slice(None), at), g)
            r.gp_v[:, at] = gp
            z = following
        keep(r.g_v, r.gs.at[table])
        keep(r.gp_v, r.gps.at[table], True)
        for half in range(2):
            at = slice(half * w // 2, (half + 1) * w // 2)
            r.y_v[table, :, at] = r.h_v[0, :, at] + wide(parts(r.g_v), parts(r.wdown_v, slice(None), at), 1, 0)

            @pl.when(section == 0)
            def _():
                relay(table, half).start()

        keep(r.y_v.at[table, 0:real], r.out.at[table])
        for copy in stores:
            copy.wait()

        @pl.when(section == 0)
        def _():
            for copy in held:
                copy.wait()

    def backward(self, r, table, section, relay):
        c, w, ff, hd, real = self.cells, self.width, self.ff, self.hd, self.real
        stores = []

        def keep(src, dst):
            stores.append(start(src, dst, r.out_sem.at[len(stores)]))

        fill_biases(self.feat, self.rows, r.ctx[table], r.col_bias[0], 0)

        @pl.when(section == 0)
        def _():
            loads = [
                start(r.ns.at[table], r.n_v, r.in_sem.at[0]),
                start(r.qkvs.at[table], r.qkv_v, r.in_sem.at[1]),
                start(r.gps.at[table], r.gp_v, r.in_sem.at[2]),
            ]
            for half in range(2):
                relay(table, half).wait()
            r.dy_v[0:real] = r.got[table]
            for copy in loads:
                copy.wait()

        @pl.when(section == 1)
        def _():
            pltpu.make_async_copy(r.cot.at[table], r.dy_v.at[0:real], r.in_sem.at[1]).wait()

        r.dy_v[real:, :] = jnp.zeros((c - real, w), F32)
        put(r.dys_v, (), r.dy_v[...])
        keep(r.dys_v, r.dys.at[table])

        column_tiles = [slice(j, j + 256) for j in range(0, w, 256)]

        def down(j):
            return wide(parts(r.dys_v), parts(r.wdown_v, slice(j * TILE, (j + 1) * TILE)), 1, 1)

        tiles = ff // TILE
        dg = down(0)
        for j in range(tiles):
            at = slice(j * TILE, (j + 1) * TILE)
            following = down(j + 1) if j + 1 < tiles else None
            put(r.g_v, (slice(None), at), dg * r.gp_v[:, at])
            dg = following
        keep(r.g_v, r.dzs.at[table])
        da = jnp.concatenate([wide(parts(r.g_v), parts(r.wup_v, at), 1, 1) for at in column_tiles], 1)

        def through_norm(site, da):
            n, k = r.n_v[site], 2 * HEADS + site
            rstd = r.stat_v[table, :, k : k + 1]
            r.small[site : site + 1, :] += jnp.sum(da * n, axis=0, keepdims=True)
            return norm_back(n, rstd, r.gains[site], da)

        r.dy_v[...] += through_norm(2, da)
        for site in (1, 0):
            if site == 0:
                self.set_out(r, r.dy_v, real)
                self.by_rows(r, r.dy_v)
            put(r.o_v, (site,), r.dy_v[...])
            keep(r.o_v.at[:, site], r.dhs.at[table, :, site])
            put(r.do_v, (), wide(parts(r.o_v, site), parts(r.wout_v, site), 1, 1))

            def part_of(which, head, span):
                return parts(r.qkv_v, site, span, lanes(which * HEADS + head, hd))

            def products(head, queries, keys, bias):
                do = parts(r.do_v, queries, lanes(head, hd))
                return near(part_of(1, head, keys), part_of(0, head, queries)), near(part_of(2, head, keys), do)

            def gradients(head, queries, keys, bias, state):
                s, dp = state
                p = jnp.exp2(s + bias[...] - r.lse_v[table, pl.ds(site * HEADS + head, 1), queries])
                ds = p * (dp - jnp.sum(p * dp, axis=0, keepdims=True))
                return split(p), split(ds)

            def back(head, queries, keys, bias, state):
                p, ds = state
                k = part_of(1, head, keys)
                r.dqkv_f[queries, lanes(head, hd)] = (wide(tuple(x.T for x in k), ds, 1, 0) * self.scale).T
                dk = side(ds, part_of(0, head, queries)) * LN2
                dv = side(p, parts(r.do_v, queries, lanes(head, hd)))
                for which, term in ((1, dk), (2, dv)):
                    at = lanes(which * HEADS + head, hd)
                    if keys.start == 0:
                        r.dqkv_f[keys, at] = term
                    else:
                        known = overlap - keys.start
                        if known:
                            r.dqkv_f[keys.start : overlap, at] += term[:known]
                        r.dqkv_f[overlap : keys.stop, at] = term[known:]

            overlap = self.sites(r, site, 0)[0][1].stop

            @pl.loop(0, HEADS // 2)
            def _(two):
                units = [(head, *unit) for head in (2 * two, 2 * two + 1) for unit in self.sites(r, site, 0)]
                staggered(units, products, gradients, back)

            for j in range(3 * w // TILE):
                at = slice(j * TILE, (j + 1) * TILE)
                put(r.qkv_v, (site, slice(None), at), r.dqkv_f[:, at])
            keep(r.qkv_v.at[:, site], r.dqkvs.at[table, :, site])
            da = jnp.concatenate([wide(parts(r.qkv_v, site), parts(r.win_v, site, at), 1, 1) for at in column_tiles], 1)
            r.dy_v[...] += through_norm(site, da)

        self.set_out(r, r.dy_v, real)
        self.by_features(r, r.dy_v)

        @pl.when(section == 0)
        def _():
            total = jnp.zeros((1, w), F32)
            for at, missing in self.missing(r, table):
                total += jnp.sum(jnp.where(missing, r.dy_v[at], 0.0), axis=0, keepdims=True)
                r.y_v[table, at] = jnp.where(missing, 0.0, r.dy_v[at])
            r.small[3:4, :] += total

        @pl.when(section == 1)
        def _():
            r.y_v[table] = r.dy_v[...]
            for half in range(2):
                relay(table, half).start()

        keep(r.y_v.at[table, 0:real], r.din.at[table])
        for copy in stores:
            copy.wait()


class GradSum:
    ROWS, COLS = 512, 256
    PARTS = 2
    SLACK = 2

    def __init__(self, count, tables, cells, width, ff):
        self.count, self.tables, self.cells, self.width = count, tables, cells, width
        self.rest = count // 4
        shapes = [("gs", None, "dys", None, "down", None, ff, width), ("as_", 2, "dzs", None, "up", None, width, ff)]
        for site in (1, 0):
            shapes.append(("as_", site, "dqkvs", site, "win", site, width, 3 * width))
            shapes.append(("os", site, "dhs", site, "wout", site, width, width))
        self.groups, at = [], 0
        for *which, k, n in shapes:
            blocks = (k // self.ROWS) * (n // self.COLS)
            self.groups.append((at, at + blocks, *which, n // self.COLS))
            at += blocks
        self.blocks = at
        self.chunks = self.blocks * self.PARTS
        self.hops = self.rest // 2 - 1
        self.sends = self.SLACK * (self.hops + 1) + 2
        self.rows = self.ROWS // self.PARTS
        self.ring = self.SLACK // self.PARTS + 2
        self.depth = (cells + 127) // 128 * 128

    def select(self, q, action):
        for group in self.groups:
            first, stop, *_, across = group

            @pl.when((q >= first) & (q < stop))
            def _():
                action(group, (q - first) // across, (q - first) % across)

    def starts_row(self, q):
        found = False
        for first, stop, *_, across in self.groups:
            found = found | ((q >= first) & (q < stop) & ((q - first) % across == 0))
        return found

    def load(self, r, q):
        slot = q % 2

        def action(group, i, j):
            _, _, left, left_site, right, right_site, *_ = group
            a, b = getattr(r, left), getattr(r, right)

            def at(t, part, site):
                return (t, part, slice(None)) if site is None else (t, part, site, slice(None))

            for t in range(self.tables):
                rows = slice(t * self.depth, t * self.depth + self.cells)
                for part in range(2):
                    sem = 2 * t + part
                    start(b.at[(*at(t, part, right_site), lanes(j, self.COLS))], r.b_v.at[slot, part, rows], r.b_sem.at[slot, sem])

                    @pl.when(j == 0)
                    def _():
                        start(a.at[(*at(t, part, left_site), lanes(i, self.ROWS))], r.a_v.at[part, rows], r.a_sem.at[sem])

        self.select(q, action)

    def each_operand(self):
        return [(2 * t + part, part, slice(t * self.depth, t * self.depth + self.cells)) for t in range(self.tables) for part in range(2)]

    def product(self, r, q):
        slot = q % 2

        @pl.when(self.starts_row(q))
        def _():
            for sem, part, rows in self.each_operand():
                a = r.a_v.at[part, rows]
                pltpu.make_async_copy(a, a, r.a_sem.at[sem]).wait()
            for part in range(2):
                r.left_v[part] = r.a_v[part].T

        for sem, part, rows in self.each_operand():
            b = r.b_v.at[slot, part, rows]
            pltpu.make_async_copy(b, b, r.b_sem.at[slot, sem]).wait()

        @pl.when(q + 1 < self.blocks)
        def _():
            self.load(r, q + 1)

        r.products[q % self.ring] = side(parts(r.left_v), parts(r.b_v.at[slot]))

    def kernel(self, r):
        rest, rows, ring = self.rest, self.rows, self.ring
        half = rows // 2
        quart = half // 2
        me, section = lax.axis_index("dp"), lax.axis_index("section")
        core, pair, place = me % 2, me // 2 % 2, me // 4
        sibling, neighbour = {"dp": me + 1 - 2 * core}, {"dp": me + 2 - 4 * pair}
        far = place // (rest // 2)
        along = (1 - far) * place + far * (rest - 1 - place)
        inward, outward = {"dp": me + 4 - 8 * far}, {"dp": me - 4 + 8 * far}
        hops = self.hops

        def peer(j):
            return {"dp": lax.rem(place + j, rest) * 4 + me % 4}

        def span(at, size):
            return pl.ds(pl.multiple_of(at, size), size)

        mine = core * half
        own, other = pair * quart, (1 - pair) * quart
        keeps, gives = far * quart, (1 - far) * quart

        barrier = pltpu.get_barrier_semaphore()

        def greet(device):
            pl.semaphore_signal(barrier, inc=1, device_id=device, device_id_type=pl.DeviceIdType.MESH)

        greet(sibling)
        greet(neighbour)

        @pl.loop(1, rest)
        def _(j):
            greet(peer(j))

        for t in range(self.tables):
            pad = slice(t * self.depth + self.cells, (t + 1) * self.depth)
            for part in range(2):
                r.a_v[part, pad] = jnp.zeros_like(r.a_v[part, pad])
                for slot in range(2):
                    r.b_v[slot, part, pad] = jnp.zeros_like(r.b_v[slot, part, pad])
        self.load(r, 0)
        passing = [
            start(getattr(r, f"table{i}"), getattr(r, f"out{i}"), r.table_sem.at[i]) for i in range(self.passed)
        ]

        @pl.when(section == 1)
        def _():
            greet({"section": 0})

        pl.semaphore_wait(barrier, rest + 2 - section)

        def copy(which, c, src, dst, device):
            return remote(src, dst, r.send.at[which, c % self.sends], r.recv.at[which, c], device)

        def product_rows(c, which):
            return c // self.PARTS % ring, span(c % self.PARTS * rows + which * half, half)

        def halve(c):
            return copy(0, c, r.products.at[product_rows(c, 1 - core)], r.sums.at[c], sibling)

        def gather_half(c):
            at = r.full.at[c, span(mine, half)]
            return copy(1, c, at, at, sibling)

        def quarter(c):
            return copy(2, c, r.sums.at[c, span(other, quart)], r.got_near.at[c], neighbour)

        def gather_quarter(c):
            at = r.full.at[c, span(mine + own, quart)]
            return copy(3, c, at, at, neighbour)

        def add_up(c):
            return copy(2, c, r.sums.at[c, span(keeps, quart)], r.got_near.at[c], neighbour)

        def come(kind, c):
            if kind == 0:
                return copy(4, c, r.sums.at[c, span(own, quart)], r.got_in.at[c, 0:quart], inward)
            return copy(4, c, r.sums.at[c], r.got_in.at[c], inward)

        def meet(kind, c):
            at = span(own if kind == 0 else gives, quart)
            return copy(5, c, r.sums.at[c, at], r.got_mid.at[c], inward)

        def give_back(c):
            at = r.full.at[c, span(mine + keeps, quart)]
            return copy(6, c, at, at, inward)

        def leave(kind, c):
            at = r.full.at[c, span(mine + own, quart) if kind == 0 else span(mine, half)]
            return copy(7, c, at, at, outward)

        def reduced(kind, c, h, at_end):
            @pl.when((along == h) & (h < hops))
            def _():
                come(kind, c).start()

            @pl.when((along == h) & (h == hops))
            def _():
                at_end(c)

        def come_hop(kind, c, h):
            @pl.when(along == h)
            def _():
                come(kind, c).wait_send()

            @pl.when(along == h + 1)
            def _():
                come(kind, c).wait_recv()
                if kind == 0:
                    r.sums[c, span(own, quart)] += r.got_in[c, 0:quart]
                else:
                    r.sums[c] += r.got_in[c]

            reduced(kind, c, h + 1, lambda c: meet(kind, c).start())

        def pass_out(kind, c, h):
            @pl.when((along == h) & (h > 0))
            def _():
                leave(kind, c).start()

            if kind == 0:

                @pl.when(along == h)
                def _():
                    gather_quarter(c).start()

        def leave_hop(kind, c, g):
            h = hops - g

            @pl.when(along == h)
            def _():
                leave(kind, c).wait_send()

            @pl.when(along == h - 1)
            def _():
                leave(kind, c).wait_recv()

            pass_out(kind, c, h - 1)

        def after_halve(c):
            halve(c).wait()
            r.sums[c] += r.products[product_rows(c, core)]

            @pl.when(core == 0)
            def _():
                quarter(c).start()

            @pl.when(core == 1)
            def _():
                reduced(1, c, 0, lambda c: meet(1, c).start())

        def after_quarter(c):
            quarter(c).wait()
            r.sums[c, span(own, quart)] += r.got_near[c]
            reduced(0, c, 0, lambda c: meet(0, c).start())

        def after_meet(kind, c):
            @pl.when(along == hops)
            def _():
                meet(kind, c).wait()
                if kind == 0:
                    r.full[c, span(mine + own, quart)] = r.sums[c, span(own, quart)] + r.got_mid[c]
                else:
                    r.sums[c, span(keeps, quart)] += r.got_mid[c]
                    add_up(c).start()

            if kind == 0:
                pass_out(0, c, hops)

        def after_add_up(c):
            @pl.when(along == hops)
            def _():
                add_up(c).wait()
                r.full[c, span(mine + keeps, quart)] = r.sums[c, span(keeps, quart)] + r.got_near[c]
                give_back(c).start()

        def after_give_back(c):
            @pl.when(along == hops)
            def _():
                give_back(c).wait()

            pass_out(1, c, hops)

        def gathered(c):
            @pl.when(core == 0)
            def _():
                gather_quarter(c).wait()

            gather_half(c).start()

        def after_gather_half(c):
            gather_half(c).wait()

        def small_copy(k, device):
            return remote(r.small_v.at[k], r.got_small.at[k], r.small_send.at[k], r.small_recv.at[k], device)

        def small_rest(j):
            dst = r.got_small.at[2 + j]
            return remote(r.small_v.at[3], dst, r.small_send.at[2 + j], r.small_recv.at[2 + j], peer(j))

        def small_step(step):
            @pl.when(step == 2)
            def _():
                r.small_v[1] = r.small[...]
                small_copy(1, sibling).start()

            @pl.when(step == 4)
            def _():
                small_copy(1, sibling).wait()
                r.small_v[2] = r.small_v[1] + r.got_small[1]
                small_copy(2, neighbour).start()

            @pl.when(step == 6)
            def _():
                small_copy(2, neighbour).wait()
                r.small_v[3] = r.small_v[2] + r.got_small[2]
                pl.loop(1, rest)(lambda j: small_rest(j).start())

            @pl.when(step == 8)
            def _():
                pl.loop(1, rest)(lambda j: small_rest(j).wait())
                total = r.small_v[3]
                for j in range(1, rest):
                    total += r.got_small[2 + j]
                r.small_v[0] = total

                @pl.when(section == 0)
                def _():
                    small_copy(0, {"section": 1}).start()

        last = 2 * hops + 5

        def delay(time):
            return self.SLACK * time - (1 if time < last else 2)

        @pl.loop(0, self.chunks + delay(last))
        def _(step):
            def stage(time, action):
                c = step - (delay(time) if isinstance(time, int) else self.SLACK * time - 1)

                @pl.when((c >= 0) & (c < self.chunks))
                def _():
                    action(c)

            stage(last, after_gather_half)

            @pl.when(core == 0)
            def _():
                over(hops, lambda g: stage(hops + 4 + g, lambda c: leave_hop(0, c, g)))
                stage(hops + 3, lambda c: after_meet(0, c))
                over(hops, lambda h: stage(3 + h, lambda c: come_hop(0, c, h)))
                stage(2, after_quarter)

            @pl.when(core == 1)
            def _():
                over(hops, lambda g: stage(hops + 5 + g, lambda c: leave_hop(1, c, g)))
                stage(hops + 4, after_give_back)
                stage(hops + 3, after_add_up)
                stage(hops + 2, lambda c: after_meet(1, c))
                over(hops, lambda h: stage(2 + h, lambda c: come_hop(1, c, h)))

            stage(last - 1, gathered)
            stage(1, after_halve)
            small_step(step)

            @pl.when(step < self.chunks)
            def _():
                @pl.when(step % self.PARTS == 0)
                def _():
                    self.product(r, step // self.PARTS)

                halve(step).start()

        for load in passing:
            load.wait()
        r.small_out[...] = r.small_v[0]

        @pl.when(section == 0)
        def _():
            small_copy(0, {"section": 1}).wait_send()

        @pl.when(section == 1)
        def _():
            small_copy(0, {"section": 1}).wait_recv()
            r.small_out[3:4] = r.got_small[0, 3:4]

    def __call__(self, operands, small, tables):
        t, width, deep = self.tables, self.width, self.tables * self.depth
        rest, chunks, rows, ring, cols = self.rest, self.chunks, self.rows, self.ring, self.COLS
        outs = {"full": VMEM((chunks, rows, cols), F32), "small_out": f32(8, width)}
        outs |= {f"out{i}": VMEM(a.shape, F32) for i, a in enumerate(tables)}
        scratch = {
            "products": VMEM((ring, self.ROWS, cols), F32),
            "sums": VMEM((chunks, rows // 2, cols), F32),
            "got_near": VMEM((chunks, rows // 4, cols), F32),
            "got_mid": VMEM((chunks, rows // 4, cols), F32),
            "got_in": VMEM((chunks, rows // 2, cols), F32),
            "a_v": VMEM((2, deep, self.ROWS), BF16),
            "left_v": VMEM((2, self.ROWS, deep), BF16),
            "b_v": VMEM((2, 2, deep, cols), BF16),
            "small_v": VMEM((4, 8, width), F32),
            "got_small": VMEM((2 + rest, 8, width), F32),
            "a_sem": dma(2 * t),
            "b_sem": dma(2, 2 * t),
            "send": dma(8, self.sends),
            "recv": dma(8, chunks),
            "small_send": dma(2 + rest),
            "small_recv": dma(2 + rest),
        }
        ins = {n: (a, ANY) for n, a in operands.items()} | {"small": (small, VMEM)}
        ins |= {f"table{i}": (a, ANY) for i, a in enumerate(tables)}
        scratch["table_sem"] = dma(len(tables))
        self.passed = len(tables)
        outs = {n: (s, VMEM) for n, s in outs.items()}
        return call("weight_gradient_sum", self.kernel, 0, ins, outs, scratch, SUM_VMEM_LIMIT)

    def results(self, sums, small, tables, ff):
        width = self.width

        def here(a):
            return (pltpu.with_memory_space_constraint(a, pltpu.VMEM), VMEM)

        ins = {"full": here(sums), "small": (small, VMEM)} | {f"table{i}": here(a) for i, a in enumerate(tables)}
        outs = {
            "win": f32(2, width, 3 * width),
            "wout": f32(2, width, width),
            "up": f32(width, ff),
            "down": f32(ff, width),
        } | {f"out{i}": f32(*a.shape) for i, a in enumerate(tables)}
        outs = {n: (s, ANY) for n, s in outs.items()}
        outs |= {"gain": (f32(3, 1, width), VMEM), "missing": (f32(1, width), VMEM)}
        scratch = {"sem": dma(self.chunks), "out_sem": dma(len(tables))}

        def body(r):
            stores = [
                start(getattr(r, f"table{i}"), getattr(r, f"out{i}"), r.out_sem.at[i]) for i in range(len(tables))
            ]
            for first, stop, *_, out, site, across in self.groups:
                dst = getattr(r, out) if site is None else getattr(r, out).at[site]
                for c in range(first * self.PARTS, stop * self.PARTS):
                    q = c // self.PARTS - first
                    row = q // across * self.ROWS + c % self.PARTS * self.rows
                    at = (slice(row, row + self.rows), slice(q % across * self.COLS, (q % across + 1) * self.COLS))
                    stores.append(start(r.full.at[c], dst.at[at], r.sem.at[c]))
            for k in range(3):
                r.gain[k] = r.small[k : k + 1, :]
            r.missing[...] = r.small[3:4, :]
            for copy in stores:
                copy.wait()

        return call("results", body, None, ins, outs, scratch, SUM_VMEM_LIMIT)


def local(
    cells,
    missing_mask,
    missing_embed,
    context_rows,
    norm_gains,
    attn_in,
    attn_out,
    mlp_up,
    mlp_down,
    cotangent,
):
    tables, rows, feat, width = cells.shape
    ff = mlp_up.shape[2]
    layers = Layers(tables, rows, feat, width, ff)

    def flat(tables_of_cells):
        return jnp.swapaxes(tables_of_cells, 1, 2).reshape(tables, rows * feat, -1)

    def unflat(cells_of_tables):
        return jnp.swapaxes(cells_of_tables.reshape(tables, feat, rows, width), 1, 2)[None]

    weights = (attn_in[0], attn_out[0], mlp_up[0], mlp_down[0])
    gains = jnp.swapaxes(norm_gains, 0, 1)
    done = layers(flat(cells), missing_mask, missing_embed[None], context_rows, gains, weights, flat(cotangent))
    operands = {n: done[n] for n in ("as_", "os", "gs", "dys", "dzs", "dhs", "dqkvs")}
    grad_sum = GradSum(lax.axis_size("dp"), tables, layers.cells, width, ff)
    sums = grad_sum(operands, done["small"], (done["out"], done["din"]))
    got = grad_sum.results(sums["full"], sums["small_out"], (sums["out0"], sums["out1"]), ff)
    return (
        unflat(got["out0"]),
        unflat(got["out1"]),
        jnp.swapaxes(got["gain"], 0, 1),
        got["win"][None],
        got["wout"][None],
        got["up"][None],
        got["down"][None],
        got["missing"][0],
    )


def solution(mesh):
    in_specs = (
        P("dp", None, None, None),
        P("dp", None, None),
        P(),
        P("dp"),
        P("section", None, None),
        P("section", None, None, None),
        P("section", None, None, None),
        P("section", None, None),
        P("section", None, None),
        P("dp", None, None, None),
    )
    out_specs = (
        P("section", "dp", None, None, None),
        P("section", "dp", None, None, None),
        P("section", None, None),
        P("section", None, None, None),
        P("section", None, None, None),
        P("section", None, None),
        P("section", None, None),
        P(),
    )
    return jax.shard_map(local, mesh=mesh, in_specs=in_specs, out_specs=out_specs, check_vma=False)
```

```python
import functools
from types import SimpleNamespace

import jax
import jax.numpy as jnp
from jax import lax
from jax.experimental import pallas as pl
from jax.experimental.pallas import tpu as pltpu
from jax.sharding import PartitionSpec as P

HEADS = 4
EPSILON = 1e-05
NEG = -1e30
INV_SQRT2PI = 0.3989422804014327
LOG2E = 1.4426950408889634
LN2 = 0.6931471805599453
ERFC_P = 0.33
ERFC_C = (0.1863578482, 0.1829552331, 0.2012284886, 0.0472047191, 0.4085317677, -0.3511862269, 0.4602596132, -0.1353514118)
VMEM_LIMIT = 62 * 1024 * 1024
SUM_VMEM_LIMIT = 38 * 1024 * 1024
TILE = 512
F32, BF16 = jnp.float32, jnp.bfloat16


def dot(a, b, contract=((1,), (0,))):
    return lax.dot_general(a, b, (contract, ((), ())), preferred_element_type=F32)


def split(v):
    hi = v.astype(BF16)
    return hi, (v - hi.astype(F32)).astype(BF16)


def put(ref, index, v):
    hi, lo = split(v)
    ref[(0, *index)] = hi
    ref[(1, *index)] = lo


def parts(ref, *index):
    return ref[(0, *index)], ref[(1, *index)]


def wide(a, b, ca, cb):
    (ah, al), (bh, bl) = a, b
    if ah.shape[ca] < 512:
        return dot(jnp.concatenate([ah, ah, al], ca), jnp.concatenate([bh, bl, bh], cb), ((ca,), (cb,)))
    rows = ah.shape[1 - ca]
    both = dot(jnp.concatenate([ah, al], 1 - ca), bh, ((ca,), (cb,)))
    return both[:rows] + both[rows:] + dot(ah, bl, ((ca,), (cb,)))


def near(a, b):
    (ah, al), (bh, bl) = a, b
    return dot(jnp.concatenate([ah, ah, al, al], 1), jnp.concatenate([bh, bl, bh, bl], 1), ((1,), (1,)))


def side(a, b):
    (ah, al), (bh, bl) = a, b
    width = bh.shape[1]
    both = dot(ah, jnp.concatenate([bh, bl], 1))
    return both[:, :width] + both[:, width:] + dot(al, bh)


def normalized(h):
    centred = h - jnp.mean(h, axis=-1, keepdims=True)
    rstd = lax.rsqrt(jnp.mean(centred * centred, axis=-1, keepdims=True) + EPSILON)
    return centred * rstd, rstd


def norm_back(n, rstd, gain, da):
    dn = da * gain
    return rstd * (dn - jnp.mean(dn, axis=-1, keepdims=True) - n * jnp.mean(dn * n, axis=-1, keepdims=True))


def cell_ids(start, count, inner, along):
    shape = (count, 1) if along == 0 else (1, count)
    at = lax.broadcasted_iota(jnp.int32, shape, along) + start
    outer = lax.shift_right_logical(at * ((1 << 20) // inner + 1), 20)
    return outer, at - outer * inner


def up16(n):
    return (n + 15) // 16 * 16


def blocks(outer, inner):
    cells = up16(outer * inner)
    half = up16((outer + 1) // 2 * inner)
    first_keys = min(cells, up16((((half - 1) // inner) + 1) * inner))
    second_keys = ((half // inner) * inner) // 16 * 16
    return ((slice(0, half), slice(0, first_keys)), (slice(half, cells), slice(second_keys, cells)))


def when(cond):
    if isinstance(cond, bool):
        return (lambda action: action()) if cond else (lambda action: None)
    return pl.when(cond)


def over(count, action):
    if count <= 4:
        for i in range(count):
            action(i)
    else:
        pl.loop(0, count)(action)


def staggered(units, *steps):
    state = [None] * len(units)
    for i in range(len(units) + 1):
        if i < len(units):
            state[i] = steps[0](*units[i])
        if i > 0:
            for step in steps[1:]:
                state[i - 1] = step(*units[i - 1], state[i - 1])


def lanes(j, width):
    return pl.ds(pl.multiple_of(j * width, width), width)


def start(src, dst, sem):
    copy = pltpu.make_async_copy(src, dst, sem)
    copy.start()
    return copy


def fill_biases(outer, inner, limit, refs, keys_along):
    for (queries, keys), ref in zip(blocks(outer, inner), refs):
        q_outer, _ = cell_ids(queries.start, queries.stop - queries.start, inner, 1 - keys_along)
        k_outer, k_inner = cell_ids(keys.start, keys.stop - keys.start, inner, keys_along)
        ref[...] = jnp.where((q_outer == k_outer) & (k_inner < limit), 0.0, NEG)


def gelu_parts(z):
    size = jnp.abs(z)
    below = 1.0 + (ERFC_P * 0.7071067811865476) * size
    t = pl.reciprocal(below, approx=True)
    t = t * (2.0 - below * t)
    series = jnp.full_like(t, ERFC_C[-1])
    for c in ERFC_C[-2::-1]:
        series = series * t + c
    bell = jnp.exp(-0.5 * z * z)
    tail = 0.5 * (series * t) * bell
    phi = jnp.where(z >= 0.0, 1.0 - tail, tail)
    return z * phi, phi + z * (INV_SQRT2PI * bell)


SMEM, VMEM, ANY = pltpu.SMEM, pltpu.VMEM, pl.ANY


def f32(*shape):
    return jax.ShapeDtypeStruct(shape, F32)


def b16(*shape):
    return jax.ShapeDtypeStruct(shape, BF16)


def dma(*shape):
    return pltpu.SemaphoreType.DMA(shape)


def remote(src, dst, send, recv, device):
    return pltpu.make_async_remote_copy(
        src_ref=src, dst_ref=dst, send_sem=send, recv_sem=recv, device_id=device, device_id_type=pl.DeviceIdType.MESH
    )


def call(name, body, collective_id, ins, outs, scratch, limit):
    names = [*ins, *outs, *scratch]

    def kernel(*refs):
        body(SimpleNamespace(**dict(zip(names, refs))))

    results = pl.pallas_call(
        kernel,
        out_shape=[t for t, _ in outs.values()],
        in_specs=[pl.BlockSpec(memory_space=s) for _, s in ins.values()],
        out_specs=[pl.BlockSpec(memory_space=s) for _, s in outs.values()],
        scratch_shapes=list(scratch.values()),
        compiler_params=pltpu.CompilerParams(
            vmem_limit_bytes=limit, collective_id=collective_id, has_side_effects=collective_id is not None
        ),
        name=name,
    )(*(a for a, _ in ins.values()))
    return dict(zip(outs, results))


class Layers:
    SPLIT_ROWS = 64

    def __init__(self, tables, rows, feat, width, ff):
        self.tables, self.rows, self.feat, self.width, self.ff = tables, rows, feat, width, ff
        self.real, self.cells = rows * feat, up16(rows * feat)
        self.hd = width // HEADS
        self.scale = self.hd ** (-0.5)
        self.halves = [queries for queries, _ in blocks(feat, rows)]

    def sites(self, r, site, keys_along):
        if site == 1:
            ranges, biases = blocks(self.feat, self.rows), r.col_bias
        else:
            ranges, biases = blocks(self.rows, self.feat), r.row_bias
        return [(*unit, bias) for unit, bias in zip(ranges, biases[keys_along])]

    def missing(self, r, table):
        mask = r.mask[table]
        return [(slice(f * self.rows, (f + 1) * self.rows), mask[:, f : f + 1] == 1) for f in range(self.feat)]

    def set_out(self, r, src, count):
        for k in range(self.width // 128):
            r.perm_v[k, 0:count] = src[0:count, k * 128 : (k + 1) * 128]

    def by_rows(self, r, dst):
        for row in range(self.rows):
            for k in range(self.width // 128):
                at = (slice(row * self.feat, (row + 1) * self.feat), slice(k * 128, (k + 1) * 128))
                dst[at] = r.perm_v[k, pl.ds(row, self.feat, stride=self.rows), :]

    def by_features(self, r, dst):
        for feat in range(self.feat):
            for k in range(self.width // 128):
                at = (slice(feat * self.rows, (feat + 1) * self.rows), slice(k * 128, (k + 1) * 128))
                dst[at] = r.perm_v[k, pl.ds(feat, self.rows, stride=self.feat), :]

    def __call__(self, cells, mask, embed, context, gains, weights, cotangent):
        t, c, w, ff, real = self.tables, self.cells, self.width, self.ff, self.real
        rows, feat = self.rows, self.feat
        ins = {
            "cells": (cells, ANY),
            "mask": (mask, VMEM),
            "embed": (embed, VMEM),
            "ctx": (context, SMEM),
            "gains": (gains, VMEM),
            "cot": (cotangent, ANY),
        }
        names = ("win", "wout", "wup", "wdown")
        ins |= {n: (a, ANY) for n, a in zip(names, weights)}
        outs = {
            "out": f32(t, real, w),
            "din": f32(t, real, w),
            "ns": f32(t, 3, c, w),
            "qkvs": b16(t, 2, 2, c, 3 * w),
            "gps": f32(t, c, ff),
            "as_": b16(t, 2, 3, c, w),
            "os": b16(t, 2, 2, c, w),
            "gs": b16(t, 2, c, ff),
            "dys": b16(t, 2, c, w),
            "dzs": b16(t, 2, c, ff),
            "dhs": b16(t, 2, 2, c, w),
            "dqkvs": b16(t, 2, 2, c, 3 * w),
        }
        outs = {n: (s, ANY) for n, s in outs.items()} | {"small": (f32(8, w), VMEM)}
        scratch = {n + "_v": VMEM((2, *a.shape), BF16) for n, a in zip(names, weights)}
        scratch |= {
            "h_v": VMEM((2, c, w), F32),
            "n_v": VMEM((3, c, w), F32),
            "qkv_v": VMEM((2, 2, c, 3 * w), BF16),
            "o_v": VMEM((2, 2, c, w), BF16),
            "gp_v": VMEM((c, ff), F32),
            "g_v": VMEM((2, c, ff), BF16),
            "a_v": VMEM((2, 3, c, w), BF16),
            "y_v": VMEM((t, c, w), F32),
            "dqkv_f": VMEM((c, 3 * w), F32),
            "perm_v": VMEM((w // 128, c, 128), F32),
            "dys_v": VMEM((2, c, w), BF16),
            "dy_v": VMEM((c, w), F32),
            "do_v": VMEM((2, c, w), BF16),
            "got": VMEM((t, real, w), F32),
            "stat_v": VMEM((t, c, 128), F32),
            "lse_v": VMEM((t, 2 * HEADS, c), F32),
            "spare_v": VMEM((w // 2, w), F32),
            "raw_sem": pltpu.SemaphoreType.DMA((20,)),
            "in_sem": pltpu.SemaphoreType.DMA((4,)),
            "out_sem": pltpu.SemaphoreType.DMA((18,)),
            "send": pltpu.SemaphoreType.DMA((t, 2)),
            "recv": pltpu.SemaphoreType.DMA((t, 2)),
        }
        for name, ranges in (("col_bias", blocks(feat, rows)), ("row_bias", blocks(rows, feat))):
            for i, (queries, keys) in enumerate(ranges):
                shape = (queries.stop - queries.start, keys.stop - keys.start)
                scratch[f"{name}0{i}"] = VMEM(shape[::-1], F32)
                scratch[f"{name}1{i}"] = VMEM(shape, F32)

        def body(r):
            for n in ("col_bias", "row_bias"):
                setattr(r, n, [[getattr(r, f"{n}{along}{i}") for i in range(2)] for along in range(2)])
            self.kernel(r)

        return call("layers", body, 1, ins, outs, scratch, VMEM_LIMIT)

    attention_pieces = 8

    def raw_pieces(self, r):
        w, ff = self.width, self.ff
        half, wide_in, step = w // 2, 3 * w, self.SPLIT_ROWS
        top, rest, whole = slice(0, half), slice(half, w), slice(None)
        big, bigger = r.dqkv_f.at[top], r.gp_v.at[top]
        pieces = [
            (r.win.at[0, top], big, r.win_v, (0,), 0, whole, 0),
            (r.win.at[0, rest], bigger.at[:, 0:wide_in], r.win_v, (0,), half, whole, 1),
            (r.wout.at[0, top], r.h_v.at[0, top], r.wout_v, (0,), 0, whole, 2),
            (r.wout.at[0, rest], r.h_v.at[1, top], r.wout_v, (0,), half, whole, 3),
            (r.win.at[1, top], big, r.win_v, (1,), 0, whole, 0),
            (r.win.at[1, rest], bigger.at[:, 0:wide_in], r.win_v, (1,), half, whole, 1),
            (r.wout.at[1, top], r.n_v.at[0, top], r.wout_v, (1,), 0, whole, 4),
            (r.wout.at[1, rest], r.spare_v, r.wout_v, (1,), half, whole, 5),
        ]
        assert len(pieces) == self.attention_pieces
        pieces.append((r.wup.at[top], bigger, r.wup_v, (), 0, whole, 1))
        pieces.append((r.wup.at[rest, 0:wide_in], big, r.wup_v, (), half, slice(0, wide_in), 0))
        pieces.append((r.wup.at[rest, wide_in:ff], r.spare_v, r.wup_v, (), half, slice(wide_in, ff), 5))
        high = self.cells // step * step
        buffers = [r.y_v.at[0, 0:high], r.y_v.at[1, 0:high]]
        low = slice(half, half + (self.cells - half) // step * step)
        for k in range(3):
            buffers.append(r.dqkv_f.at[low, k * w : (k + 1) * w])
        for k in range(ff // w):
            buffers.append(r.gp_v.at[low, k * w : (k + 1) * w])
        at = 0
        for i, buffer in enumerate(buffers):
            size = min(buffer.shape[0], ff - at)
            if size:
                pieces.append((r.wdown.at[at : at + size], buffer.at[0:size], r.wdown_v, (), at, whole, 6 + i))
            at += size
        assert at == ff
        return pieces

    def raw_copy(self, r, i):
        src, buffer = self.raw_pieces(r)[i][:2]
        return pltpu.make_async_copy(src, buffer, r.raw_sem.at[i])

    def split_piece(self, r, i):
        pieces = self.raw_pieces(r)
        _, buffer, v, lead, at, columns, user = pieces[i]
        step = self.SPLIT_ROWS
        self.raw_copy(r, i).wait()

        @pl.loop(0, buffer.shape[0] // step)
        def _(j):
            src = pl.ds(pl.multiple_of(j * step, step), step)
            dst = pl.ds(pl.multiple_of(at + j * step, step), step)
            put(v, (*lead, dst, columns), buffer[src])

        later = [k for k in range(i + 1, len(pieces)) if pieces[k][-1] == user]
        if later:
            self.raw_copy(r, later[0]).start()

    def start_raw(self, r, mlp):
        seen = set()
        for i, piece in enumerate(self.raw_pieces(r)):
            if piece[-1] not in seen and mlp == (i >= self.attention_pieces):
                self.raw_copy(r, i).start()
            seen.add(piece[-1])

    def split_attention(self, r):
        self.start_raw(r, False)
        for i in range(self.attention_pieces):
            self.split_piece(r, i)
        self.start_raw(r, True)

    def split_mlp(self, r):
        for i in range(self.attention_pieces, len(self.raw_pieces(r))):
            self.split_piece(r, i)

    def kernel(self, r):
        t, real, c = self.tables, self.real, self.cells
        section = lax.axis_index("section")
        other = {"section": 1 - section}
        barrier = pltpu.get_barrier_semaphore()
        pl.semaphore_signal(barrier, inc=1, device_id=other, device_id_type=pl.DeviceIdType.MESH)

        @pl.when(section == 0)
        def _():
            start(r.cells.at[0], r.dy_v.at[0:real], r.in_sem.at[0])

        self.split_attention(r)

        @pl.when(section == 1)
        def _():
            self.split_mlp(r)

        for along in range(2):
            fill_biases(self.rows, self.feat, self.feat, r.row_bias[along], along)
        r.small[...] = jnp.zeros_like(r.small)
        pl.semaphore_wait(barrier, 1)

        def relay(table, half, back):
            at = self.halves[half]
            at = (slice(at.start, min(at.stop, real)),)
            if not back:
                at = (slice(0, real), slice(half * self.width // 2, (half + 1) * self.width // 2))
            src, dst = r.y_v.at[(table, *at)], r.got.at[(table, *at)]
            return remote(src, dst, r.send.at[table, half], r.recv.at[table, half], other)

        @pl.loop(0, 2 * t)
        def _(step):
            forward = (1 - section) * (1 - step // t) + section * (1 - step % 2)
            table = (1 - section) * (step % t) + section * (step // 2)

            @pl.when(forward == 1)
            def _():
                self.forward(r, table, section, relay, step)

            @pl.when(forward == 0)
            def _():
                self.backward(r, table, section, relay)

        @pl.when(section == 1)
        def _():
            for table in range(t):
                for half in range(2):
                    relay(table, half, True).wait_send()

    def forward(self, r, table, section, relay, step):
        c, w, ff, hd, real = self.cells, self.width, self.ff, self.hd, self.real
        stores, held = [], []

        def keep(src, dst, to_reload=False):
            copy = pltpu.make_async_copy(src, dst, r.out_sem.at[len(stores) + len(held)])
            if to_reload:
                held.append(copy)
                pl.when(section == 0)(copy.start)
            else:
                stores.append(copy)
                copy.start()

        for level in range(2):
            r.h_v[level, real:, :] = jnp.zeros((c - real, w), F32)

        def keep_column(k, at, value):
            column = lax.broadcasted_iota(jnp.int32, (1, r.stat_v.shape[2]), 1) == k
            r.stat_v[table, at, :] = jnp.where(column, value, r.stat_v[table, at, :])

        def norm(site):
            n, rstd = normalized(r.h_v[site % 2])
            r.n_v[site] = n
            keep(r.n_v.at[site], r.ns.at[table, site], True)
            keep_column(2 * HEADS + site, slice(None), rstd)
            put(r.a_v, (site,), n * r.gains[site])
            keep(r.a_v.at[:, site], r.as_.at[table, :, site])

        fill_biases(self.feat, self.rows, r.ctx[table], r.col_bias[1], 1)

        @pl.when(section == 0)
        def _():
            load = pltpu.make_async_copy(r.cells.at[table], r.dy_v.at[0:real], r.in_sem.at[0])
            pl.when(step > 0)(load.start)
            load.wait()
            for at, missing in self.missing(r, table):
                r.dy_v[at] = jnp.where(missing, r.embed[...], r.dy_v[at])
            self.set_out(r, r.dy_v, real)

        @pl.when(section == 1)
        def _():
            start(r.cot.at[table], r.dy_v.at[0:real], r.in_sem.at[1])
            for half in range(2):
                relay(table, half, False).wait_recv()
            self.set_out(r, r.got.at[table], real)

        self.by_rows(r, r.h_v.at[0])
        for site in range(2):
            norm(site)

            def project(j):
                at = slice(j * TILE, (j + 1) * TILE)
                return wide(parts(r.a_v, site), parts(r.win_v, site, slice(None), at), 1, 0)

            def keep_projected(j, out):
                if j < w // TILE:
                    out = out * (self.scale * LOG2E)
                put(r.qkv_v, (site, slice(None), slice(j * TILE, (j + 1) * TILE)), out)

            staggered([(j,) for j in range(3 * w // TILE)], project, keep_projected)
            keep(r.qkv_v.at[:, site], r.qkvs.at[table, :, site], True)

            def scores(head, queries, keys, bias):
                q = parts(r.qkv_v, site, queries, lanes(head, hd))
                k = parts(r.qkv_v, site, keys, lanes(HEADS + head, hd))
                return near(q, k)

            def softmax(head, queries, keys, bias, s):
                s = s + bias[...]
                top = jnp.max(s, axis=-1, keepdims=True)
                e = jnp.exp2(s - top)
                total = jnp.sum(e, axis=-1, keepdims=True)
                keep_column(site * HEADS + head, queries, top + jnp.log2(total))
                return split(e), 1.0 / total

            def blend(head, queries, keys, bias, state):
                e, inverse = state
                v = parts(r.qkv_v, site, keys, lanes(2 * HEADS + head, hd))
                put(r.o_v, (site, queries, lanes(head, hd)), side(e, v) * inverse)

            @pl.loop(0, HEADS // 2)
            def _(two):
                units = [(head, *unit) for head in (2 * two, 2 * two + 1) for unit in self.sites(r, site, 1)]
                staggered(units, scores, softmax, blend)

            keep(r.o_v.at[:, site], r.os.at[table, :, site])
            after = r.h_v[site] + wide(parts(r.o_v, site), parts(r.wout_v, site), 1, 0)
            if site == 0:
                self.set_out(r, after, c)
                self.by_features(r, r.h_v.at[1])
            else:
                r.h_v[0] = after
        r.lse_v[table] = r.stat_v[table].T[0 : 2 * HEADS]
        norm(2)

        @pl.when((section == 0) & (step == 0))
        def _():
            self.split_mlp(r)

        def up(j):
            return wide(parts(r.a_v, 2), parts(r.wup_v, slice(None), slice(j * TILE, (j + 1) * TILE)), 1, 0)

        tiles = ff // TILE
        z = up(0)
        for j in range(tiles):
            at = slice(j * TILE, (j + 1) * TILE)
            following = up(j + 1) if j + 1 < tiles else None
            g, gp = gelu_parts(z)
            put(r.g_v, (slice(None), at), g)
            r.gp_v[:, at] = gp
            z = following
        keep(r.g_v, r.gs.at[table])
        keep(r.gp_v, r.gps.at[table], True)
        for half in range(2):
            at = slice(half * w // 2, (half + 1) * w // 2)
            r.y_v[table, :, at] = r.h_v[0, :, at] + wide(parts(r.g_v), parts(r.wdown_v, slice(None), at), 1, 0)

            @pl.when(section == 0)
            def _():
                relay(table, half, False).start()

        keep(r.y_v.at[table, 0:real], r.out.at[table])
        for copy in stores:
            copy.wait()

        @pl.when(section == 0)
        def _():
            for copy in held:
                copy.wait()

    def backward(self, r, table, section, relay):
        c, w, ff, hd, real = self.cells, self.width, self.ff, self.hd, self.real
        stores = []

        def keep(src, dst):
            stores.append(start(src, dst, r.out_sem.at[len(stores)]))

        fill_biases(self.feat, self.rows, r.ctx[table], r.col_bias[0], 0)

        column_tiles = [slice(j, j + 256) for j in range(0, w, 256)]

        def through_norm(site, cells, da):
            n, k = r.n_v[site, cells], 2 * HEADS + site
            rstd = r.stat_v[table, cells, k : k + 1]
            r.small[site : site + 1, :] += jnp.sum(da * n, axis=0, keepdims=True)
            r.dy_v[cells] += norm_back(n, rstd, r.gains[site], da)

        def mlp_back(cells):
            put(r.dys_v, (cells,), r.dy_v[cells])

            def down(at):
                return wide(parts(r.dys_v, cells), parts(r.wdown_v, at), 1, 1)

            def deactivate(at, dg):
                put(r.g_v, (cells, at), dg * r.gp_v[cells, at])

            staggered([(slice(j, j + TILE),) for j in range(0, ff, TILE)], down, deactivate)
            da = [wide(parts(r.g_v, cells), parts(r.wup_v, at), 1, 1) for at in column_tiles]
            through_norm(2, cells, jnp.concatenate(da, 1))

        r.dy_v[real:, :] = jnp.zeros((c - real, w), F32)

        @pl.when(section == 0)
        def _():
            loads = [
                start(r.ns.at[table], r.n_v, r.in_sem.at[0]),
                start(r.qkvs.at[table], r.qkv_v, r.in_sem.at[1]),
                start(r.gps.at[table], r.gp_v, r.in_sem.at[2]),
            ]
            for half in range(2):
                relay(table, half, False).wait_send()
            for copy in loads:
                copy.wait()
            for half, cells in enumerate(self.halves):
                relay(table, half, True).wait_recv()
                came = slice(cells.start, min(cells.stop, real))
                r.dy_v[came] = r.got[table, came]
                mlp_back(cells)

        @pl.when(section == 1)
        def _():
            pltpu.make_async_copy(r.cot.at[table], r.dy_v.at[0:real], r.in_sem.at[1]).wait()
            mlp_back(slice(0, c))

        keep(r.dys_v, r.dys.at[table])
        keep(r.g_v, r.dzs.at[table])
        for site in (1, 0):
            if site == 0:
                self.set_out(r, r.dy_v, real)
                self.by_rows(r, r.dy_v)
            put(r.o_v, (site,), r.dy_v[...])
            keep(r.o_v.at[:, site], r.dhs.at[table, :, site])
            put(r.do_v, (), wide(parts(r.o_v, site), parts(r.wout_v, site), 1, 1))

            def part_of(which, head, span):
                return parts(r.qkv_v, site, span, lanes(which * HEADS + head, hd))

            def products(head, queries, keys, bias):
                do = parts(r.do_v, queries, lanes(head, hd))
                return near(part_of(1, head, keys), part_of(0, head, queries)), near(part_of(2, head, keys), do)

            def gradients(head, queries, keys, bias, state):
                s, dp = state
                p = jnp.exp2(s + bias[...] - r.lse_v[table, pl.ds(site * HEADS + head, 1), queries])
                ds = p * (dp - jnp.sum(p * dp, axis=0, keepdims=True))
                return split(p), split(ds)

            def back(head, queries, keys, bias, state):
                p, ds = state
                k = part_of(1, head, keys)
                r.dqkv_f[queries, lanes(head, hd)] = (wide(tuple(x.T for x in k), ds, 1, 0) * self.scale).T
                dk = side(ds, part_of(0, head, queries)) * LN2
                dv = side(p, parts(r.do_v, queries, lanes(head, hd)))
                for which, term in ((1, dk), (2, dv)):
                    at = lanes(which * HEADS + head, hd)
                    if keys.start == 0:
                        r.dqkv_f[keys, at] = term
                    else:
                        known = overlap - keys.start
                        if known:
                            r.dqkv_f[keys.start : overlap, at] += term[:known]
                        r.dqkv_f[overlap : keys.stop, at] = term[known:]

            overlap = self.sites(r, site, 0)[0][1].stop

            @pl.loop(0, HEADS // 2)
            def _(two):
                units = [(head, *unit) for head in (2 * two, 2 * two + 1) for unit in self.sites(r, site, 0)]
                staggered(units, products, gradients, back)

            for j in range(3 * w // TILE):
                at = slice(j * TILE, (j + 1) * TILE)
                put(r.qkv_v, (site, slice(None), at), r.dqkv_f[:, at])
            keep(r.qkv_v.at[:, site], r.dqkvs.at[table, :, site])
            da = jnp.concatenate([wide(parts(r.qkv_v, site), parts(r.win_v, site, at), 1, 1) for at in column_tiles], 1)
            through_norm(site, slice(None), da)

        self.set_out(r, r.dy_v, real)
        self.by_features(r, r.dy_v)

        @pl.when(section == 0)
        def _():
            total = jnp.zeros((1, w), F32)
            for at, missing in self.missing(r, table):
                total += jnp.sum(jnp.where(missing, r.dy_v[at], 0.0), axis=0, keepdims=True)
                r.y_v[table, at] = jnp.where(missing, 0.0, r.dy_v[at])
            r.small[3:4, :] += total

        @pl.when(section == 1)
        def _():
            r.y_v[table] = r.dy_v[...]
            for half in range(2):
                relay(table, half, True).start()

        keep(r.y_v.at[table, 0:real], r.din.at[table])
        for copy in stores:
            copy.wait()


class GradSum:
    ROWS, COLS = 512, 256
    PARTS = 2
    SLACK = 2

    def __init__(self, count, tables, cells, width, ff):
        self.count, self.tables, self.cells, self.width = count, tables, cells, width
        self.rest = count // 4
        shapes = [("gs", None, "dys", None, "down", None, ff, width), ("as_", 2, "dzs", None, "up", None, width, ff)]
        for site in (1, 0):
            shapes.append(("as_", site, "dqkvs", site, "win", site, width, 3 * width))
            shapes.append(("os", site, "dhs", site, "wout", site, width, width))
        self.groups, at = [], 0
        for *which, k, n in shapes:
            blocks = (k // self.ROWS) * (n // self.COLS)
            self.groups.append((at, at + blocks, *which, n // self.COLS))
            at += blocks
        self.blocks = at
        self.chunks = self.blocks * self.PARTS
        self.hops = self.rest // 2 - 1
        self.sends = self.SLACK * (self.hops + 1) + 2
        self.rows = self.ROWS // self.PARTS
        self.ring = self.SLACK // self.PARTS + 2
        self.depth = (cells + 127) // 128 * 128

    def select(self, q, action):
        for group in self.groups:
            first, stop, *_, across = group

            @pl.when((q >= first) & (q < stop))
            def _():
                action(group, (q - first) // across, (q - first) % across)

    def starts_row(self, q):
        found = False
        for first, stop, *_, across in self.groups:
            found = found | ((q >= first) & (q < stop) & ((q - first) % across == 0))
        return found

    def load(self, r, q):
        slot = q % 2

        def action(group, i, j):
            _, _, left, left_site, right, right_site, *_ = group
            a, b = getattr(r, left), getattr(r, right)

            def at(t, part, site):
                return (t, part, slice(None)) if site is None else (t, part, site, slice(None))

            for t in range(self.tables):
                rows = slice(t * self.depth, t * self.depth + self.cells)
                for part in range(2):
                    sem = 2 * t + part
                    start(b.at[(*at(t, part, right_site), lanes(j, self.COLS))], r.b_v.at[slot, part, rows], r.b_sem.at[slot, sem])

                    @pl.when(j == 0)
                    def _():
                        start(a.at[(*at(t, part, left_site), lanes(i, self.ROWS))], r.a_v.at[part, rows], r.a_sem.at[sem])

        self.select(q, action)

    def each_operand(self):
        return [(2 * t + part, part, slice(t * self.depth, t * self.depth + self.cells)) for t in range(self.tables) for part in range(2)]

    def product(self, r, q):
        slot = q % 2

        @pl.when(self.starts_row(q))
        def _():
            for sem, part, rows in self.each_operand():
                a = r.a_v.at[part, rows]
                pltpu.make_async_copy(a, a, r.a_sem.at[sem]).wait()
            for part in range(2):
                r.left_v[part] = r.a_v[part].T

        for sem, part, rows in self.each_operand():
            b = r.b_v.at[slot, part, rows]
            pltpu.make_async_copy(b, b, r.b_sem.at[slot, sem]).wait()

        @pl.when(q + 1 < self.blocks)
        def _():
            self.load(r, q + 1)

        r.products[q % self.ring] = side(parts(r.left_v), parts(r.b_v.at[slot]))

    def kernel(self, r):
        rest, rows, ring = self.rest, self.rows, self.ring
        half = rows // 2
        quart = half // 2
        me, section = lax.axis_index("dp"), lax.axis_index("section")
        core, pair, place = me % 2, me // 2 % 2, me // 4
        sibling, neighbour = {"dp": me + 1 - 2 * core}, {"dp": me + 2 - 4 * pair}
        far = place // (rest // 2)
        along = (1 - far) * place + far * (rest - 1 - place)
        inward, outward = {"dp": me + 4 - 8 * far}, {"dp": me - 4 + 8 * far}
        hops = self.hops

        def peer(j):
            return {"dp": lax.rem(place + j, rest) * 4 + me % 4}

        def span(at, size):
            return pl.ds(pl.multiple_of(at, size), size)

        mine = core * half
        own, other = pair * quart, (1 - pair) * quart
        keeps, gives = far * quart, (1 - far) * quart

        barrier = pltpu.get_barrier_semaphore()

        def greet(device):
            pl.semaphore_signal(barrier, inc=1, device_id=device, device_id_type=pl.DeviceIdType.MESH)

        greet(sibling)
        greet(neighbour)

        @pl.loop(1, rest)
        def _(j):
            greet(peer(j))

        for t in range(self.tables):
            pad = slice(t * self.depth + self.cells, (t + 1) * self.depth)
            for part in range(2):
                r.a_v[part, pad] = jnp.zeros_like(r.a_v[part, pad])
                for slot in range(2):
                    r.b_v[slot, part, pad] = jnp.zeros_like(r.b_v[slot, part, pad])
        self.load(r, 0)
        passing = [
            start(getattr(r, f"table{i}"), getattr(r, f"out{i}"), r.table_sem.at[i]) for i in range(self.passed)
        ]

        @pl.when(section == 1)
        def _():
            greet({"section": 0})

        pl.semaphore_wait(barrier, rest + 2 - section)

        def copy(which, c, src, dst, device):
            return remote(src, dst, r.send.at[which, c % self.sends], r.recv.at[which, c], device)

        def product_rows(c, which):
            return c // self.PARTS % ring, span(c % self.PARTS * rows + which * half, half)

        def halve(c):
            return copy(0, c, r.products.at[product_rows(c, 1 - core)], r.sums.at[c], sibling)

        def gather_half(c):
            at = r.full.at[c, span(mine, half)]
            return copy(1, c, at, at, sibling)

        def quarter(c):
            return copy(2, c, r.sums.at[c, span(other, quart)], r.got_near.at[c], neighbour)

        def gather_quarter(c):
            at = r.full.at[c, span(mine + own, quart)]
            return copy(3, c, at, at, neighbour)

        def add_up(c):
            return copy(2, c, r.sums.at[c, span(keeps, quart)], r.got_near.at[c], neighbour)

        def come(kind, c):
            if kind == 0:
                return copy(4, c, r.sums.at[c, span(own, quart)], r.got_in.at[c, 0:quart], inward)
            return copy(4, c, r.sums.at[c], r.got_in.at[c], inward)

        def meet(kind, c):
            at = span(own if kind == 0 else gives, quart)
            return copy(5, c, r.sums.at[c, at], r.got_mid.at[c], inward)

        def give_back(c):
            at = r.full.at[c, span(mine + keeps, quart)]
            return copy(6, c, at, at, inward)

        def leave(kind, c):
            at = r.full.at[c, span(mine + own, quart) if kind == 0 else span(mine, half)]
            return copy(7, c, at, at, outward)

        def reduced(kind, c, h, at_end):
            @pl.when((along == h) & (h < hops))
            def _():
                come(kind, c).start()

            @pl.when((along == h) & (h == hops))
            def _():
                at_end(c)

        def come_hop(kind, c, h):
            @pl.when(along == h)
            def _():
                come(kind, c).wait_send()

            @pl.when(along == h + 1)
            def _():
                come(kind, c).wait_recv()
                if kind == 0:
                    r.sums[c, span(own, quart)] += r.got_in[c, 0:quart]
                else:
                    r.sums[c] += r.got_in[c]

            reduced(kind, c, h + 1, lambda c: meet(kind, c).start())

        def pass_out(kind, c, h):
            @pl.when((along == h) & (h > 0))
            def _():
                leave(kind, c).start()

            if kind == 0:

                @pl.when(along == h)
                def _():
                    gather_quarter(c).start()

        def leave_hop(kind, c, g):
            h = hops - g

            @pl.when(along == h)
            def _():
                leave(kind, c).wait_send()

            @pl.when(along == h - 1)
            def _():
                leave(kind, c).wait_recv()

            pass_out(kind, c, h - 1)

        def after_halve(c):
            halve(c).wait()
            r.sums[c] += r.products[product_rows(c, core)]

            @pl.when(core == 0)
            def _():
                quarter(c).start()

            @pl.when(core == 1)
            def _():
                reduced(1, c, 0, lambda c: meet(1, c).start())

        def after_quarter(c):
            quarter(c).wait()
            r.sums[c, span(own, quart)] += r.got_near[c]
            reduced(0, c, 0, lambda c: meet(0, c).start())

        def after_meet(kind, c):
            @pl.when(along == hops)
            def _():
                meet(kind, c).wait()
                if kind == 0:
                    r.full[c, span(mine + own, quart)] = r.sums[c, span(own, quart)] + r.got_mid[c]
                else:
                    r.sums[c, span(keeps, quart)] += r.got_mid[c]
                    add_up(c).start()

            if kind == 0:
                pass_out(0, c, hops)

        def after_add_up(c):
            @pl.when(along == hops)
            def _():
                add_up(c).wait()
                r.full[c, span(mine + keeps, quart)] = r.sums[c, span(keeps, quart)] + r.got_near[c]
                give_back(c).start()

        def after_give_back(c):
            @pl.when(along == hops)
            def _():
                give_back(c).wait()

            pass_out(1, c, hops)

        def gathered(c):
            @pl.when(core == 0)
            def _():
                gather_quarter(c).wait()

            gather_half(c).start()

        def after_gather_half(c):
            gather_half(c).wait()

        def small_copy(k, device):
            return remote(r.small_v.at[k], r.got_small.at[k], r.small_send.at[k], r.small_recv.at[k], device)

        def small_rest(j):
            dst = r.got_small.at[2 + j]
            return remote(r.small_v.at[3], dst, r.small_send.at[2 + j], r.small_recv.at[2 + j], peer(j))

        def small_step(step):
            @pl.when(step == 2)
            def _():
                r.small_v[1] = r.small[...]
                small_copy(1, sibling).start()

            @pl.when(step == 4)
            def _():
                small_copy(1, sibling).wait()
                r.small_v[2] = r.small_v[1] + r.got_small[1]
                small_copy(2, neighbour).start()

            @pl.when(step == 6)
            def _():
                small_copy(2, neighbour).wait()
                r.small_v[3] = r.small_v[2] + r.got_small[2]
                pl.loop(1, rest)(lambda j: small_rest(j).start())

            @pl.when(step == 8)
            def _():
                pl.loop(1, rest)(lambda j: small_rest(j).wait())
                total = r.small_v[3]
                for j in range(1, rest):
                    total += r.got_small[2 + j]
                r.small_v[0] = total

                @pl.when(section == 0)
                def _():
                    small_copy(0, {"section": 1}).start()

        last = 2 * hops + 5

        def delay(time):
            return self.SLACK * time - (1 if time < last else 2)

        @pl.loop(0, self.chunks + delay(last))
        def _(step):
            def stage(time, action):
                c = step - (delay(time) if isinstance(time, int) else self.SLACK * time - 1)

                @pl.when((c >= 0) & (c < self.chunks))
                def _():
                    action(c)

            stage(last, after_gather_half)

            @pl.when(core == 0)
            def _():
                over(hops, lambda g: stage(hops + 4 + g, lambda c: leave_hop(0, c, g)))
                stage(hops + 3, lambda c: after_meet(0, c))
                over(hops, lambda h: stage(3 + h, lambda c: come_hop(0, c, h)))
                stage(2, after_quarter)

            @pl.when(core == 1)
            def _():
                over(hops, lambda g: stage(hops + 5 + g, lambda c: leave_hop(1, c, g)))
                stage(hops + 4, after_give_back)
                stage(hops + 3, after_add_up)
                stage(hops + 2, lambda c: after_meet(1, c))
                over(hops, lambda h: stage(2 + h, lambda c: come_hop(1, c, h)))

            stage(last - 1, gathered)
            stage(1, after_halve)
            small_step(step)

            @pl.when(step < self.chunks)
            def _():
                @pl.when(step % self.PARTS == 0)
                def _():
                    self.product(r, step // self.PARTS)

                halve(step).start()

        for load in passing:
            load.wait()
        r.small_out[...] = r.small_v[0]

        @pl.when(section == 0)
        def _():
            small_copy(0, {"section": 1}).wait_send()

        @pl.when(section == 1)
        def _():
            small_copy(0, {"section": 1}).wait_recv()
            r.small_out[3:4] = r.got_small[0, 3:4]

    def __call__(self, operands, small, tables):
        t, width, deep = self.tables, self.width, self.tables * self.depth
        rest, chunks, rows, ring, cols = self.rest, self.chunks, self.rows, self.ring, self.COLS
        outs = {"full": VMEM((chunks, rows, cols), F32), "small_out": f32(8, width)}
        outs |= {f"out{i}": VMEM(a.shape, F32) for i, a in enumerate(tables)}
        scratch = {
            "products": VMEM((ring, self.ROWS, cols), F32),
            "sums": VMEM((chunks, rows // 2, cols), F32),
            "got_near": VMEM((chunks, rows // 4, cols), F32),
            "got_mid": VMEM((chunks, rows // 4, cols), F32),
            "got_in": VMEM((chunks, rows // 2, cols), F32),
            "a_v": VMEM((2, deep, self.ROWS), BF16),
            "left_v": VMEM((2, self.ROWS, deep), BF16),
            "b_v": VMEM((2, 2, deep, cols), BF16),
            "small_v": VMEM((4, 8, width), F32),
            "got_small": VMEM((2 + rest, 8, width), F32),
            "a_sem": dma(2 * t),
            "b_sem": dma(2, 2 * t),
            "send": dma(8, self.sends),
            "recv": dma(8, chunks),
            "small_send": dma(2 + rest),
            "small_recv": dma(2 + rest),
        }
        ins = {n: (a, ANY) for n, a in operands.items()} | {"small": (small, VMEM)}
        ins |= {f"table{i}": (a, ANY) for i, a in enumerate(tables)}
        scratch["table_sem"] = dma(len(tables))
        self.passed = len(tables)
        outs = {n: (s, VMEM) for n, s in outs.items()}
        return call("weight_gradient_sum", self.kernel, 0, ins, outs, scratch, SUM_VMEM_LIMIT)

    def results(self, sums, small, tables, ff):
        width = self.width

        def here(a):
            return (pltpu.with_memory_space_constraint(a, pltpu.VMEM), VMEM)

        ins = {"full": here(sums), "small": (small, VMEM)} | {f"table{i}": here(a) for i, a in enumerate(tables)}
        outs = {
            "win": f32(2, width, 3 * width),
            "wout": f32(2, width, width),
            "up": f32(width, ff),
            "down": f32(ff, width),
        } | {f"out{i}": f32(*a.shape) for i, a in enumerate(tables)}
        outs = {n: (s, ANY) for n, s in outs.items()}
        outs |= {"gain": (f32(3, 1, width), VMEM), "missing": (f32(1, width), VMEM)}
        scratch = {"sem": dma(self.chunks), "out_sem": dma(len(tables))}

        def body(r):
            stores = [
                start(getattr(r, f"table{i}"), getattr(r, f"out{i}"), r.out_sem.at[i]) for i in range(len(tables))
            ]
            for first, stop, *_, out, site, across in self.groups:
                dst = getattr(r, out) if site is None else getattr(r, out).at[site]
                for c in range(first * self.PARTS, stop * self.PARTS):
                    q = c // self.PARTS - first
                    row = q // across * self.ROWS + c % self.PARTS * self.rows
                    at = (slice(row, row + self.rows), slice(q % across * self.COLS, (q % across + 1) * self.COLS))
                    stores.append(start(r.full.at[c], dst.at[at], r.sem.at[c]))
            for k in range(3):
                r.gain[k] = r.small[k : k + 1, :]
            r.missing[...] = r.small[3:4, :]
            for copy in stores:
                copy.wait()

        return call("results", body, None, ins, outs, scratch, SUM_VMEM_LIMIT)


def local(
    cells,
    missing_mask,
    missing_embed,
    context_rows,
    norm_gains,
    attn_in,
    attn_out,
    mlp_up,
    mlp_down,
    cotangent,
):
    tables, rows, feat, width = cells.shape
    ff = mlp_up.shape[2]
    layers = Layers(tables, rows, feat, width, ff)

    def flat(tables_of_cells):
        return jnp.swapaxes(tables_of_cells, 1, 2).reshape(tables, rows * feat, -1)

    def unflat(cells_of_tables):
        return jnp.swapaxes(cells_of_tables.reshape(tables, feat, rows, width), 1, 2)[None]

    weights = (attn_in[0], attn_out[0], mlp_up[0], mlp_down[0])
    gains = jnp.swapaxes(norm_gains, 0, 1)
    done = layers(flat(cells), missing_mask, missing_embed[None], context_rows, gains, weights, flat(cotangent))
    operands = {n: done[n] for n in ("as_", "os", "gs", "dys", "dzs", "dhs", "dqkvs")}
    grad_sum = GradSum(lax.axis_size("dp"), tables, layers.cells, width, ff)
    sums = grad_sum(operands, done["small"], (done["out"], done["din"]))
    got = grad_sum.results(sums["full"], sums["small_out"], (sums["out0"], sums["out1"]), ff)
    return (
        unflat(got["out0"]),
        unflat(got["out1"]),
        jnp.swapaxes(got["gain"], 0, 1),
        got["win"][None],
        got["wout"][None],
        got["up"][None],
        got["down"][None],
        got["missing"][0],
    )


def solution(mesh):
    in_specs = (
        P("dp", None, None, None),
        P("dp", None, None),
        P(),
        P("dp"),
        P("section", None, None),
        P("section", None, None, None),
        P("section", None, None, None),
        P("section", None, None),
        P("section", None, None),
        P("dp", None, None, None),
    )
    out_specs = (
        P("section", "dp", None, None, None),
        P("section", "dp", None, None, None),
        P("section", None, None),
        P("section", None, None, None),
        P("section", None, None, None),
        P("section", None, None),
        P("section", None, None),
        P(),
    )
    return jax.shard_map(local, mesh=mesh, in_specs=in_specs, out_specs=out_specs, check_vma=False)
```
